32 devices in a mesh: groups: 2 (over x), sample: 16 (over z, y, core).
Axes of the slice: x: 2, y: 2, z: 4, core: 2. Of those that a mesh axis runs over, the one named last changes fastest.
Arguments:
- prompt_states: bfloat16 [16384, 8192], P(('groups', 'sample')), parts along dimension 0, may hold values from -6 to 6
- page_table: int32 [128], P('groups'), parts along dimension 0, may hold values from 0 to 63, each once
- step_states: bfloat16 [2, 64, 8192], P(None, 'groups'), parts along dimension 1, may hold values from -15 to 15
- sample_order: int32 [64], P('groups'), parts along dimension 0, may hold values from 0 to 31, each once
- key_weight: bfloat16 [8192, 512], P('sample'), may hold values from -0.088388348 to 0.088388348
- value_weight: bfloat16 [8192, 512], P('sample'), may hold values from -0.0625 to 0.0625
- query_weight: bfloat16 [8192, 4096], P(None, 'sample'), may hold values from -0.121533978 to 0.121533978
- out_weight: bfloat16 [4096, 8192], P('sample'), may hold values from -0.125 to 0.125
Outputs:
- attn_out: bfloat16 [2, 64, 8192], P(None, 'groups', 'sample'), parts along dimension 1
The draws below stay inside these ranges and needn't reach their ends.
There are 2 independent parts, one for each index of `groups`. The reference program is written for one: setup_inputs(seed, part) draws one part's arguments, and reference() takes and returns one part's arrays. A program takes and returns all parts, laid end to end along the dimension named above; an argument that names none is the same for every part. Nothing has to cross between parts.
Inputs may be any that keep to these rules, and one draw needn't show every extreme that they name: `page_table`: A permutation: entry p * 64 + j is the physical page that holds logical page j of prompt p; physical page r is rows r * 128 to (r + 1) * 128 - 1 of prompt_states. `sample_order`: A permutation; completion i continues prompt sample_order[i] // 32.
All inputs are finite; a program needn't handle non-finite values.
Results may differ from the reference program's by a relative error of at most 0.034.
Values may be sent and summed in bfloat16 or wider, within the bound.
No kernel may reach another device: no remote copies, remote signals or barrier semaphores. Data moves between devices by JAX's collectives and lax.ppermute only.
A program may use at most 128 MiB of HBM per device.

```python
import jax
import jax.numpy as jnp
from jax import lax

D = 8192
HEAD_DIM = 128
HEADS = 32
KV_HEADS = 4
GQA = 8
PAGE = 128
PROMPT_PAGES = 64
GROUP = 32
PAGES = 64
PROMPTS = 1
PROMPT_LEN = 8192
SAMPLES = 32
N_SAMPLE = 16


def weight_pair(key):
    base_part = jnp.clip(jax.random.normal(jax.random.fold_in(key, 31), (D, KV_HEADS, 1, HEAD_DIM), jnp.float32), -5.0, 5.0)
    base_part = base_part * (1.6 / D ** 0.5)
    noise_part = jnp.clip(jax.random.normal(jax.random.fold_in(key, 32), (D, KV_HEADS, GQA, HEAD_DIM), jnp.float32), -5.0, 5.0)
    noise_part = noise_part * (1.45 / D ** 0.5)
    query_part = 0.42 * base_part + noise_part
    return (base_part.reshape(D, KV_HEADS * HEAD_DIM), query_part.reshape(D, HEADS * HEAD_DIM))


def draw_key_weight(key, part):
    return weight_pair(key)[0].astype(jnp.bfloat16)


def draw_query_weight(key, part):
    return weight_pair(key)[1].astype(jnp.bfloat16)


def draw_step_states(key, part):
    first_part = jnp.clip(jax.random.normal(jax.random.fold_in(key, 41), (SAMPLES, D), jnp.float32), -5.0, 5.0)
    fresh_part = jnp.clip(jax.random.normal(jax.random.fold_in(key, 42), (SAMPLES, D), jnp.float32), -5.0, 5.0)
    second_part = 0.8 * first_part + 0.6 * fresh_part
    return jnp.stack([first_part, second_part]).astype(jnp.bfloat16)


def spiked(result, rng, source, target, shards_of, factor):
    owner, partner = [(jnp.arange(result.shape[axis_at]) // (result.shape[axis_at] // shards_of)).reshape([-1 if axis == axis_at else 1 for axis in range(result.ndim)]) for axis_at in (source, target)]
    chosen = jax.random.permutation(rng, shards_of)[partner]
    strong = (owner == chosen) | (owner == (partner + shards_of // 2) % shards_of)
    return jnp.where(strong, factor * result, result)


def levels(own_key, shape, split, smallest, largest):
    def one(axis_at, parts):
        heights = jax.random.uniform(jax.random.fold_in(jax.random.fold_in(own_key, 6), axis_at), (parts,), jnp.float32, smallest / len(split), largest / len(split))
        return jnp.repeat(jnp.exp(heights), shape[axis_at] // parts).reshape((-1,) + (1,) * (len(shape) - axis_at - 1))

    level = one(*split[0])
    for cut in split[1:]:
        level = level * one(*cut)
    return level


def noise(rng, shape, width, most, split=(), held_as=jnp.bfloat16):
    level = levels(rng, shape, split, -0.22, 0.18) if split else 1.0
    values = jax.random.normal(rng, shape, jnp.float32) * width * level
    return jnp.minimum(jnp.maximum(values, -most), most).astype(held_as)


def gaussian_with(stream_key, shape, width, most, split, heavy, kind=jnp.bfloat16):
    entries = width * jax.random.normal(stream_key, shape, jnp.float32)
    if split:
        entries = entries * levels(stream_key, shape, split, -0.22, 0.18)
    return jnp.clip(spiked(entries, jax.random.fold_in(stream_key, 3), *heavy), -most, most).astype(kind)


def setup_inputs(seed: int = 0, part: int = 0) -> dict:
    arg_keys = jax.random.split(jax.random.key(seed), 9)
    part_splits = jax.random.split(jax.random.fold_in(arg_keys[8], part), 9)
    prompt_states = noise(part_splits[0], (PAGES * PAGE, D), 1.0, 6.0, ((0, 16),))
    page_table = jax.random.permutation(part_splits[1], PAGES).astype(jnp.int32)
    step_states = draw_step_states(jax.random.fold_in(jax.random.fold_in(arg_keys[8], part), 71), part)
    sample_order = jax.random.permutation(part_splits[3], SAMPLES).astype(jnp.int32)
    key_weight = draw_key_weight(jax.random.fold_in(arg_keys[8], 71), part)
    value_weight = noise(arg_keys[5], (D, KV_HEADS * HEAD_DIM), D ** -0.5, 0.0625, ((0, 16),))
    query_weight = draw_query_weight(jax.random.fold_in(arg_keys[8], 71), part)
    out_weight = gaussian_with(arg_keys[7], (HEADS * HEAD_DIM, D), (HEADS * HEAD_DIM) ** -0.5, 0.125, ((0, 16),), (0, 1, 16, 2.0))
    return {"prompt_states": prompt_states, "page_table": page_table, "step_states": step_states, "sample_order": sample_order, "key_weight": key_weight, "value_weight": value_weight, "query_weight": query_weight, "out_weight": out_weight}


rope_base = 1000000.0


def rotate(vector, position):
    half_dim = vector.shape[-1] // 2
    frequency = rope_base ** (-jnp.arange(half_dim, dtype=jnp.float32) * 2.0 / vector.shape[-1])
    angles = position.astype(jnp.float32)[..., None] * frequency
    cosine = jnp.cos(angles)
    sine_part = jnp.sin(angles)
    first_half = vector[..., :half_dim]
    second_half = vector[..., half_dim:]
    return jnp.concatenate([first_half * cosine - second_half * sine_part, second_half * cosine + first_half * sine_part], axis=-1)


def finish_heads(prefix_top, prefix_total, prefix_sum, queries, new_keys, new_values):
    score_scale = queries.shape[-1] ** -0.5
    query_wide = queries.astype(jnp.float32)
    key_wide = new_keys.astype(jnp.float32)
    value_wide = new_values.astype(jnp.float32)
    own_score = jnp.sum(query_wide * key_wide, axis=-1) * score_scale
    back_score = jnp.sum(query_wide[1] * key_wide[0], axis=-1) * score_scale
    first_high = jnp.maximum(prefix_top[0], own_score[0])
    first_old = jnp.exp(prefix_top[0] - first_high)
    first_own = jnp.exp(own_score[0] - first_high)
    first_out = (first_old[..., None] * prefix_sum[0] + first_own[..., None] * value_wide[0]) / (first_old * prefix_total[0] + first_own)[..., None]
    second_high = jnp.maximum(jnp.maximum(prefix_top[1], own_score[1]), back_score)
    second_old = jnp.exp(prefix_top[1] - second_high)
    second_back = jnp.exp(back_score - second_high)
    second_own = jnp.exp(own_score[1] - second_high)
    second_num = second_old[..., None] * prefix_sum[1] + second_back[..., None] * value_wide[0] + second_own[..., None] * value_wide[1]
    second_out = second_num / (second_old * prefix_total[1] + second_back + second_own)[..., None]
    return jnp.stack([first_out, second_out]).astype(jnp.bfloat16)


def reference(prompt_states, page_table, step_states, sample_order, key_weight, value_weight, query_weight, out_weight):
    score_scale = HEAD_DIM ** -0.5
    page_rows = prompt_states.reshape(PAGES, PAGE, D)
    logical = page_table.reshape(PROMPTS, PROMPT_PAGES)
    token_place = jnp.arange(PROMPT_LEN, dtype=jnp.int32)

    def prefill(prompt):
        states = page_rows[logical[prompt]].reshape(PROMPT_LEN, D)
        keys = jnp.dot(states, key_weight, preferred_element_type=jnp.float32).reshape(PROMPT_LEN, KV_HEADS, HEAD_DIM)
        keys = rotate(keys, token_place[:, None]).astype(jnp.bfloat16)
        values = jnp.dot(states, value_weight, preferred_element_type=jnp.float32).astype(jnp.bfloat16)
        return keys, values.reshape(PROMPT_LEN, KV_HEADS, HEAD_DIM)

    prefix_keys, prefix_values = lax.map(prefill, jnp.arange(PROMPTS, dtype=jnp.int32))
    flat_states = step_states.reshape(2 * SAMPLES, D)
    step_place = (PROMPT_LEN + jnp.arange(2, dtype=jnp.int32))[:, None, None]
    queries = jnp.dot(flat_states, query_weight, preferred_element_type=jnp.float32).reshape(2, SAMPLES, HEADS, HEAD_DIM)
    queries = rotate(queries, step_place).astype(jnp.bfloat16)
    new_keys = jnp.dot(flat_states, key_weight, preferred_element_type=jnp.float32).reshape(2, SAMPLES, KV_HEADS, HEAD_DIM)
    new_keys = rotate(new_keys, step_place).astype(jnp.bfloat16)
    new_values = jnp.dot(flat_states, value_weight, preferred_element_type=jnp.float32).astype(jnp.bfloat16)
    new_values = new_values.reshape(2, SAMPLES, KV_HEADS, HEAD_DIM)
    inverse = jnp.zeros((SAMPLES,), jnp.int32).at[sample_order].set(jnp.arange(SAMPLES, dtype=jnp.int32))
    grouped = queries[:, inverse].reshape(2, PROMPTS, GROUP, KV_HEADS, GQA, HEAD_DIM)

    def attend(prompt):
        block_query = grouped[:, prompt].astype(jnp.float32)
        keys = prefix_keys[prompt].astype(jnp.float32)
        values = prefix_values[prompt].astype(jnp.float32)
        scores = jnp.einsum("smcgd,lcd->smcgl", block_query, keys) * score_scale
        prefix_top = jnp.max(scores, axis=-1)
        weights = jnp.exp(scores - prefix_top[..., None])
        prefix_total = jnp.sum(weights, axis=-1)
        rounded = lax.optimization_barrier(weights.astype(jnp.bfloat16)).astype(jnp.float32)
        prefix_sum = jnp.einsum("smcgl,lcd->smcgd", rounded, values)
        return prefix_top, prefix_total, prefix_sum

    prefix_top, prefix_total, prefix_sum = lax.map(attend, jnp.arange(PROMPTS, dtype=jnp.int32))
    prefix_top = jnp.moveaxis(prefix_top, 0, 1).reshape(2, SAMPLES, HEADS)[:, sample_order]
    prefix_total = jnp.moveaxis(prefix_total, 0, 1).reshape(2, SAMPLES, HEADS)[:, sample_order]
    prefix_sum = jnp.moveaxis(prefix_sum, 0, 1).reshape(2, SAMPLES, HEADS, HEAD_DIM)[:, sample_order]
    head_out = finish_heads(prefix_top, prefix_total, prefix_sum, queries, jnp.repeat(new_keys, GQA, axis=2), jnp.repeat(new_values, GQA, axis=2))
    flat_out = head_out.reshape(2 * SAMPLES, HEADS * HEAD_DIM)
    block_width = (HEADS // N_SAMPLE) * HEAD_DIM

    def add_block(running, block):
        start_col = (block * block_width).astype(jnp.int32)
        piece = lax.dynamic_slice_in_dim(flat_out, start_col, block_width, 1)
        weight_rows = lax.dynamic_slice_in_dim(out_weight, start_col, block_width, 0)
        term = jnp.dot(piece, weight_rows, preferred_element_type=jnp.float32).astype(jnp.bfloat16)
        term = lax.optimization_barrier(term).astype(jnp.float32)
        return running + term, None

    total_out, unused = lax.scan(add_block, jnp.zeros((2 * SAMPLES, D), jnp.float32), jnp.arange(N_SAMPLE, dtype=jnp.int32))
    return total_out.astype(jnp.bfloat16).reshape(2, SAMPLES, D)
```

```python
import jax
import jax.numpy as jnp
from jax import lax
from jax.sharding import PartitionSpec as P

D = 8192
HEAD_DIM = 128
KV_HEADS = 4
GQA = 8
PAGE = 128
PROMPT_PAGES = 64
LINE = 4

rope_base = 1000000.0


def rope_tables(position):
    half_dim = HEAD_DIM // 2
    frequency = rope_base ** (-jnp.arange(half_dim, dtype=jnp.float32) * 2.0 / HEAD_DIM)
    angles = position.astype(jnp.float32)[..., None] * frequency
    return jnp.cos(angles), jnp.sin(angles)


def turn(vector, tables):
    cosine, sine_part = tables
    half_dim = HEAD_DIM // 2
    first_half = vector[..., :half_dim]
    second_half = vector[..., half_dim:]
    return jnp.concatenate(
        [
            first_half * cosine - second_half * sine_part,
            second_half * cosine + first_half * sine_part,
        ],
        axis=-1,
    )


def finish_heads(prefix_top, prefix_total, prefix_sum, queries, new_keys, new_values):
    score_scale = queries.shape[-1] ** (-0.5)
    query_wide = queries.astype(jnp.float32)
    key_wide = new_keys.astype(jnp.float32)
    value_wide = new_values.astype(jnp.float32)
    own_score = jnp.sum(query_wide * key_wide, axis=-1) * score_scale
    back_score = jnp.sum(query_wide[1] * key_wide[0], axis=-1) * score_scale
    first_high = jnp.maximum(prefix_top[0], own_score[0])
    first_old = jnp.exp(prefix_top[0] - first_high)
    first_own = jnp.exp(own_score[0] - first_high)
    first_out = (first_old[..., None] * prefix_sum[0] + first_own[..., None] * value_wide[0]) / (
        first_old * prefix_total[0] + first_own
    )[..., None]
    second_high = jnp.maximum(jnp.maximum(prefix_top[1], own_score[1]), back_score)
    second_old = jnp.exp(prefix_top[1] - second_high)
    second_back = jnp.exp(back_score - second_high)
    second_own = jnp.exp(own_score[1] - second_high)
    second_num = (
        second_old[..., None] * prefix_sum[1]
        + second_back[..., None] * value_wide[0]
        + second_own[..., None] * value_wide[1]
    )
    second_out = second_num / (second_old * prefix_total[1] + second_back + second_own)[..., None]
    return jnp.stack([first_out, second_out]).astype(jnp.bfloat16)


def mover(groups, devices):
    deep = devices // LINE

    def move(value, step):
        pairs = []
        for g in range(groups):
            for s in range(devices):
                a, b, c = s // LINE, s // 2 % 2, s % 2
                to_g, to_a, to_b, to_c = step(g, a, b, c)
                to_s = (to_a % deep) * LINE + to_b * 2 + to_c
                pairs.append((g * devices + s, to_g * devices + to_s))
        return lax.ppermute(value, ("groups", "sample"), pairs)

    along_z = lambda v: move(v, lambda g, a, b, c: (g, a + 1, b, c))
    along_y = lambda v: move(v, lambda g, a, b, c: (g, a, 1 - b, c))
    along_x = lambda v: move(v, lambda g, a, b, c: (g ^ 1, a, b, c))
    in_chip = lambda v: move(v, lambda g, a, b, c: (g, a, b, 1 - c))
    return along_z, along_y, along_x, in_chip


def on_device(
    prompt_states,
    page_table,
    step_states,
    sample_order,
    key_weight,
    value_weight,
    query_weight,
    out_weight,
):
    devices = lax.axis_size("sample")
    groups = lax.axis_size("groups")
    own_index = lax.axis_index("sample")
    plane = lax.axis_index("groups") % 2
    deep = devices // LINE
    own_a, own_b, own_c = own_index // LINE, own_index // 2 % 2, own_index % 2
    along_z, along_y, along_x, in_chip = mover(groups, devices)
    row_count = prompt_states.shape[0]
    pages_here = row_count // PAGE
    heads_here = query_weight.shape[1] // HEAD_DIM
    total_pages = page_table.shape[0]
    prompts = total_pages // PROMPT_PAGES
    samples = sample_order.shape[0]
    group_size = samples // prompts
    score_scale = HEAD_DIM ** (-0.5)
    own_kv = own_index * heads_here // GQA
    wide_states = step_states.reshape(2 * samples, D)
    width = key_weight.shape[0]
    kv_cols = key_weight.shape[1]
    half = kv_cols // 2
    quarter = kv_cols // 4

    first = plane == 0
    key_mine = jnp.where(first, key_weight[:, :half], key_weight[:, half:])
    key_other = jnp.where(first, key_weight[:, half:], key_weight[:, :half])
    value_mine = jnp.concatenate(
        [
            jnp.where(first, value_weight[:, :quarter], value_weight[:, quarter:half]),
            value_weight[:, half:],
        ],
        axis=1,
    )
    value_other = jnp.where(first, value_weight[:, quarter:half], value_weight[:, :quarter])

    def columns(source, k, flip, core):
        block = ((own_a + deep - k) % deep) * LINE + (own_b ^ flip) * 2 + core
        return lax.dynamic_slice_in_dim(source, block * width, width, 1)

    places = [(k, flip) for k in range(deep) for flip in (0, 1)]
    sent = jnp.stack([columns(prompt_states, k, flip, 1 - own_c) for k, flip in places])
    got = in_chip(sent)
    left = {
        place: jnp.concatenate(
            [columns(prompt_states, *place, own_c), got[i], columns(wide_states, *place, own_c)]
        )
        for i, place in enumerate(places)
    }

    def gather(mine, other, swapped):
        pieces = {}
        held = mine
        for k in range(deep):
            if k:
                held = along_z(held)
            pieces[k, 0] = held
            pieces[k, 1] = along_y(held)
        others = {}
        for place in places:
            others[place] = other if place == (0, 0) else along_x(pieces[place][:, :swapped])
        mine_acc = other_acc = 0.0
        for place in places:
            mine_acc = mine_acc + jnp.dot(
                left[place], pieces[place], preferred_element_type=jnp.float32
            )
            other_acc = other_acc + jnp.dot(
                left[place], others[place], preferred_element_type=jnp.float32
            )
        return mine_acc, other_acc

    def close(acc):
        back = in_chip(acc[row_count:])
        return jnp.concatenate([acc[:row_count] + back[:row_count], acc[2 * row_count :] + back[row_count:]])

    step_place = PROMPT_PAGES * PAGE + jnp.arange(2, dtype=jnp.int32)
    step_tables = tuple(t[:, None, :] for t in rope_tables(step_place))
    queries = jnp.dot(wide_states, query_weight, preferred_element_type=jnp.float32)
    queries = queries.reshape(2, samples, heads_here, HEAD_DIM).transpose(2, 0, 1, 3)
    queries = turn(queries, step_tables).astype(jnp.bfloat16)
    rows = heads_here * 2 * samples
    all_queries = lax.all_gather(queries.reshape(rows, HEAD_DIM), "sample", axis=0, tiled=True)
    all_queries = all_queries.reshape(KV_HEADS, devices // KV_HEADS * rows, HEAD_DIM)

    own_pages = own_index * pages_here + jnp.arange(pages_here, dtype=jnp.int32)
    slots = jnp.sum(
        jnp.where(
            page_table[None, :] == own_pages[:, None],
            jnp.arange(total_pages, dtype=jnp.int32)[None, :],
            0,
        ),
        axis=1,
    )
    positions = (slots % PROMPT_PAGES * PAGE)[:, None] + jnp.arange(PAGE, dtype=jnp.int32)[None, :]
    cosine, sine_part = rope_tables(positions.reshape(row_count))

    key_m, key_o = gather(key_mine, key_other, half)
    keys = close(jnp.concatenate([key_m, key_o], axis=1))
    keys = jnp.where(
        first, keys, jnp.concatenate([keys[:, half:], keys[:, :half]], axis=1)
    ).reshape(-1, KV_HEADS, HEAD_DIM)
    prefix_keys = turn(keys[:row_count], (cosine[:, None], sine_part[:, None])).astype(jnp.bfloat16)
    key_step = lax.dynamic_slice_in_dim(keys[row_count:], own_kv, 1, 1)
    new_keys = turn(key_step.reshape(2, samples, HEAD_DIM), step_tables).astype(jnp.bfloat16)

    scores = (
        jnp.einsum("krd,lkd->krl", all_queries, prefix_keys, preferred_element_type=jnp.float32)
        * score_scale
    )
    if prompts > 1:
        token_prompt = jnp.repeat(slots // PROMPT_PAGES, PAGE)
        row_prompt = jnp.tile(sample_order // group_size, scores.shape[1] // samples)
        scores = jnp.where(row_prompt[:, None] == token_prompt[None, :], scores, -1e30)
    top = jnp.max(scores, axis=-1)
    weights = jnp.exp(scores - top[..., None])
    total = jnp.sum(weights, axis=-1)
    stats = jnp.stack([top.reshape(devices, rows), total.reshape(devices, rows)], axis=1)
    stats = lax.all_to_all(stats, "sample", split_axis=0, concat_axis=0, tiled=True)
    tops, totals = stats[:, 0], stats[:, 1]
    prefix_top = jnp.max(tops, axis=0)
    factors = jnp.exp(tops - prefix_top[None])
    prefix_total = jnp.sum(factors * totals, axis=0)

    value_m, value_o = gather(value_mine, value_other, quarter)
    values = close(jnp.concatenate([value_m[:, :quarter], value_o, value_m[:, quarter:]], axis=1))
    values = jnp.where(
        first,
        values,
        jnp.concatenate([values[:, quarter:half], values[:, :quarter], values[:, half:]], axis=1),
    ).astype(jnp.bfloat16).reshape(-1, KV_HEADS, HEAD_DIM)
    new_values = lax.dynamic_slice_in_dim(values[row_count:], own_kv, 1, 1)
    new_values = new_values.reshape(2, samples, HEAD_DIM)

    partial = jnp.einsum(
        "krl,lkd->krd",
        weights.astype(jnp.bfloat16),
        values[:row_count],
        preferred_element_type=jnp.float32,
    ).astype(jnp.bfloat16)
    partial = lax.all_to_all(
        partial.reshape(devices, rows, HEAD_DIM), "sample", split_axis=0, concat_axis=0, tiled=True
    )
    prefix_sum = jnp.sum(partial.astype(jnp.float32) * factors[..., None], axis=0)

    by_head = (heads_here, 2, samples)
    head_out = finish_heads(
        prefix_top.reshape(by_head).swapaxes(0, 1),
        prefix_total.reshape(by_head).swapaxes(0, 1),
        prefix_sum.reshape(by_head + (HEAD_DIM,)).swapaxes(0, 1),
        queries.swapaxes(0, 1),
        new_keys[:, None],
        new_values[:, None],
    )
    flat_heads = head_out.transpose(0, 2, 1, 3).reshape(2 * samples, heads_here * HEAD_DIM)
    terms = jnp.dot(flat_heads, out_weight, preferred_element_type=jnp.float32).astype(jnp.bfloat16)
    terms = terms.reshape(2 * samples, devices, -1).swapaxes(0, 1)
    terms = lax.all_to_all(terms, "sample", split_axis=0, concat_axis=0, tiled=True)
    attn_out = jnp.sum(terms.astype(jnp.float32), axis=0).astype(jnp.bfloat16)
    return attn_out.reshape(2, samples, -1)


def solution(mesh):
    in_specs = (
        P(("groups", "sample"), None),
        P("groups"),
        P(None, "groups", None),
        P("groups"),
        P("sample", None),
        P("sample", None),
        P(None, "sample"),
        P("sample", None),
    )
    out_specs = P(None, "groups", "sample")
    return jax.shard_map(
        on_device, mesh=mesh, in_specs=in_specs, out_specs=out_specs, check_vma=False
    )
```

```python
import jax
import jax.numpy as jnp
from jax import lax
from jax.sharding import PartitionSpec as P

D = 8192
HEAD_DIM = 128
KV_HEADS = 4
GQA = 8
PAGE = 128
PROMPT_PAGES = 64
CORES = 2

rope_base = 1000000.0


def rope_tables(position):
    half_dim = HEAD_DIM // 2
    frequency = rope_base ** (-jnp.arange(half_dim, dtype=jnp.float32) * 2.0 / HEAD_DIM)
    angles = position.astype(jnp.float32)[..., None] * frequency
    return jnp.cos(angles), jnp.sin(angles)


def turn(vector, tables):
    cosine, sine_part = tables
    half_dim = HEAD_DIM // 2
    first_half = vector[..., :half_dim]
    second_half = vector[..., half_dim:]
    return jnp.concatenate(
        [
            first_half * cosine - second_half * sine_part,
            second_half * cosine + first_half * sine_part,
        ],
        axis=-1,
    )


def finish_heads(prefix_top, prefix_total, prefix_sum, queries, new_keys, new_values):
    score_scale = queries.shape[-1] ** (-0.5)
    query_wide = queries.astype(jnp.float32)
    key_wide = new_keys.astype(jnp.float32)
    value_wide = new_values.astype(jnp.float32)
    own_score = jnp.sum(query_wide * key_wide, axis=-1) * score_scale
    back_score = jnp.sum(query_wide[1] * key_wide[0], axis=-1) * score_scale
    first_high = jnp.maximum(prefix_top[0], own_score[0])
    first_old = jnp.exp(prefix_top[0] - first_high)
    first_own = jnp.exp(own_score[0] - first_high)
    first_out = (first_old[..., None] * prefix_sum[0] + first_own[..., None] * value_wide[0]) / (
        first_old * prefix_total[0] + first_own
    )[..., None]
    second_high = jnp.maximum(jnp.maximum(prefix_top[1], own_score[1]), back_score)
    second_old = jnp.exp(prefix_top[1] - second_high)
    second_back = jnp.exp(back_score - second_high)
    second_own = jnp.exp(own_score[1] - second_high)
    second_num = (
        second_old[..., None] * prefix_sum[1]
        + second_back[..., None] * value_wide[0]
        + second_own[..., None] * value_wide[1]
    )
    second_out = second_num / (second_old * prefix_total[1] + second_back + second_own)[..., None]
    return jnp.stack([first_out, second_out]).astype(jnp.bfloat16)


def on_device(
    prompt_states,
    page_table,
    step_states,
    sample_order,
    key_weight,
    value_weight,
    query_weight,
    out_weight,
):
    devices = lax.axis_size("sample")
    groups = lax.axis_size("groups")
    own_index = lax.axis_index("sample")
    core = own_index % CORES
    chips = devices // CORES
    first_core = core == 0
    first_plane = lax.axis_index("groups") % 2 == 0
    same_core = [[c + CORES * i for i in range(chips)] for c in range(CORES)]
    core_pairs = [(s, s ^ 1) for s in range(devices)]
    plane_pairs = [(g, g ^ 1) for g in range(groups)]

    def in_chip(value):
        return lax.ppermute(value, "sample", core_pairs)

    def across(value):
        return lax.ppermute(value, "groups", plane_pairs)

    def gather(value):
        return lax.all_gather(value, "sample", axis=0, tiled=True, axis_index_groups=same_core)

    def exchange(value):
        return lax.all_to_all(
            value, "sample", split_axis=0, concat_axis=0, tiled=True, axis_index_groups=same_core
        )

    row_count = prompt_states.shape[0]
    pages_here = row_count // PAGE
    heads_here = query_weight.shape[1] // HEAD_DIM
    total_pages = page_table.shape[0]
    prompts = total_pages // PROMPT_PAGES
    samples = sample_order.shape[0]
    group_size = samples // prompts
    score_scale = HEAD_DIM ** (-0.5)
    own_kv = own_index * heads_here // GQA
    wide_states = step_states.reshape(2 * samples, D)
    rows = heads_here * 2 * samples

    def weight_parts(weight):
        quarter = weight.shape[1] // 4
        low, high = weight[:, :quarter], weight[:, quarter : 2 * quarter]
        mine = gather(jnp.where(first_plane, low, high))
        other = across(mine)
        both = gather(weight[:, 2 * quarter :])
        return mine, other, both

    def project(left, parts):
        mine, other, both = (
            jnp.dot(left, part, preferred_element_type=jnp.float32) for part in parts
        )
        low = jnp.where(first_plane, mine, other)
        high = jnp.where(first_plane, other, mine)
        return jnp.concatenate([low, high, both], axis=1)

    key_parts = weight_parts(key_weight)
    value_parts = weight_parts(value_weight)

    def halves(source):
        parts = jnp.split(source, devices, axis=1)
        kept = [jnp.where(first_core, *parts[i : i + 2]) for i in range(0, devices, 2)]
        sent = [jnp.where(first_core, *parts[i : i + 2][::-1]) for i in range(0, devices, 2)]
        return kept, sent

    kept, sent = (jnp.concatenate(part, axis=1) for part in halves(prompt_states))
    kept_step = jnp.concatenate(halves(wide_states)[0], axis=1)
    left = jnp.concatenate([kept, in_chip(sent), kept_step])

    step_place = PROMPT_PAGES * PAGE + jnp.arange(2, dtype=jnp.int32)
    step_tables = tuple(t[:, None, :] for t in rope_tables(step_place))
    queries = jnp.dot(wide_states, query_weight, preferred_element_type=jnp.float32)
    queries = queries.reshape(2, samples, heads_here, HEAD_DIM).transpose(2, 0, 1, 3)
    queries = turn(queries, step_tables).astype(jnp.bfloat16)
    flat_queries = queries.reshape(1, rows, HEAD_DIM)
    core_queries = exchange(jnp.broadcast_to(flat_queries, (chips, rows, HEAD_DIM)))
    core_queries = core_queries.reshape(KV_HEADS, chips // KV_HEADS * rows, HEAD_DIM)
    owned = core_queries.shape[1]
    all_queries = jnp.concatenate([core_queries, in_chip(core_queries)], axis=1)

    own_pages = jnp.concatenate(
        [
            holder * pages_here + jnp.arange(pages_here, dtype=jnp.int32)
            for holder in (own_index, own_index ^ 1)
        ]
    )
    slots = jnp.sum(
        jnp.where(
            page_table[None, :] == own_pages[:, None],
            jnp.arange(total_pages, dtype=jnp.int32)[None, :],
            0,
        ),
        axis=1,
    )
    positions = (slots % PROMPT_PAGES * PAGE)[:, None] + jnp.arange(PAGE, dtype=jnp.int32)[None, :]
    chip_rows = 2 * row_count
    cosine, sine_part = rope_tables(positions.reshape(chip_rows))

    keys = project(left, key_parts)
    back = in_chip(keys)
    keys = keys + jnp.concatenate([back[row_count:chip_rows], back[:row_count], back[chip_rows:]])
    keys = keys.reshape(-1, KV_HEADS, HEAD_DIM)
    prefix_keys = turn(keys[:chip_rows], (cosine[:, None], sine_part[:, None])).astype(jnp.bfloat16)
    key_step = lax.dynamic_slice_in_dim(keys[chip_rows:], own_kv, 1, 1)
    new_keys = turn(key_step.reshape(2, samples, HEAD_DIM), step_tables).astype(jnp.bfloat16)

    scores = (
        jnp.einsum("krd,lkd->krl", all_queries, prefix_keys, preferred_element_type=jnp.float32)
        * score_scale
    )
    if prompts > 1:
        token_prompt = jnp.repeat(slots // PROMPT_PAGES, PAGE)
        row_prompt = jnp.tile(sample_order // group_size, scores.shape[1] // samples)
        scores = jnp.where(row_prompt[:, None] == token_prompt[None, :], scores, -1e30)
    top = jnp.max(scores, axis=-1)
    weights = jnp.exp(scores - top[..., None])
    total = jnp.sum(weights, axis=-1)
    stats = jnp.stack(
        [top[:, :owned].reshape(chips, rows), total[:, :owned].reshape(chips, rows)], axis=1
    )
    stats = exchange(stats)
    tops, totals = stats[:, 0], stats[:, 1]
    prefix_top = jnp.max(tops, axis=0)
    factors = jnp.exp(tops - prefix_top[None])
    prefix_total = jnp.sum(factors * totals, axis=0)

    values = project(left, value_parts)
    step_values = values[chip_rows:]
    step_values = step_values + in_chip(step_values)
    new_values = lax.dynamic_slice_in_dim(step_values.reshape(-1, KV_HEADS, HEAD_DIM), own_kv, 1, 1)
    new_values = new_values.reshape(2, samples, HEAD_DIM).astype(jnp.bfloat16)
    values = values[:chip_rows].astype(jnp.bfloat16).reshape(chip_rows, KV_HEADS, HEAD_DIM)
    partial = jnp.einsum(
        "krl,lkd->krd", weights.astype(jnp.bfloat16), values, preferred_element_type=jnp.float32
    )
    partial = partial[:, :owned] + in_chip(partial[:, owned:].astype(jnp.bfloat16)).astype(
        jnp.float32
    )
    partial = exchange(partial.astype(jnp.bfloat16).reshape(chips, rows, HEAD_DIM))
    prefix_sum = jnp.sum(partial.astype(jnp.float32) * factors[..., None], axis=0)

    by_head = (heads_here, 2, samples)
    head_out = finish_heads(
        prefix_top.reshape(by_head).swapaxes(0, 1),
        prefix_total.reshape(by_head).swapaxes(0, 1),
        prefix_sum.reshape(by_head + (HEAD_DIM,)).swapaxes(0, 1),
        queries.swapaxes(0, 1),
        new_keys[:, None],
        new_values[:, None],
    )
    flat_heads = head_out.transpose(0, 2, 1, 3).reshape(2 * samples, heads_here * HEAD_DIM)
    terms = jnp.dot(flat_heads, out_weight, preferred_element_type=jnp.float32).astype(jnp.bfloat16)
    kept, sent = (jnp.stack(part) for part in halves(terms))
    terms = kept.astype(jnp.float32) + in_chip(sent).astype(jnp.float32)
    terms = exchange(terms.astype(jnp.bfloat16))
    attn_out = jnp.sum(terms.astype(jnp.float32), axis=0).astype(jnp.bfloat16)
    return attn_out.reshape(2, samples, -1)


def solution(mesh):
    in_specs = (
        P(("groups", "sample"), None),
        P("groups"),
        P(None, "groups", None),
        P("groups"),
        P("sample", None),
        P("sample", None),
        P(None, "sample"),
        P("sample", None),
    )
    out_specs = P(None, "groups", "sample")
    return jax.shard_map(
        on_device, mesh=mesh, in_specs=in_specs, out_specs=out_specs, check_vma=False
    )
```

```python
import jax
import jax.numpy as jnp
from jax import lax
from jax.experimental import pallas as pl
from jax.experimental.pallas import tpu as pltpu
from jax.sharding import PartitionSpec as P

D = 8192
HEAD_DIM = 128
KV_HEADS = 4
GQA = 8
PAGE = 128
PROMPT_PAGES = 64
LINE = 4

rope_base = 1000000.0


def rope_tables(position):
    half_dim = HEAD_DIM // 2
    frequency = rope_base ** (-jnp.arange(half_dim, dtype=jnp.float32) * 2.0 / HEAD_DIM)
    angles = position.astype(jnp.float32)[..., None] * frequency
    return jnp.cos(angles), jnp.sin(angles)


def turn(vector, tables):
    cosine, sine_part = tables
    half_dim = HEAD_DIM // 2
    first_half = vector[..., :half_dim]
    second_half = vector[..., half_dim:]
    return jnp.concatenate(
        [
            first_half * cosine - second_half * sine_part,
            second_half * cosine + first_half * sine_part,
        ],
        axis=-1,
    )


def finish_heads(prefix_top, prefix_total, prefix_sum, queries, new_keys, new_values):
    score_scale = queries.shape[-1] ** (-0.5)
    query_wide = queries.astype(jnp.float32)
    key_wide = new_keys.astype(jnp.float32)
    value_wide = new_values.astype(jnp.float32)
    own_score = jnp.sum(query_wide * key_wide, axis=-1) * score_scale
    back_score = jnp.sum(query_wide[1] * key_wide[0], axis=-1) * score_scale
    first_high = jnp.maximum(prefix_top[0], own_score[0])
    first_old = jnp.exp(prefix_top[0] - first_high)
    first_own = jnp.exp(own_score[0] - first_high)
    first_out = (first_old[..., None] * prefix_sum[0] + first_own[..., None] * value_wide[0]) / (
        first_old * prefix_total[0] + first_own
    )[..., None]
    second_high = jnp.maximum(jnp.maximum(prefix_top[1], own_score[1]), back_score)
    second_old = jnp.exp(prefix_top[1] - second_high)
    second_back = jnp.exp(back_score - second_high)
    second_own = jnp.exp(own_score[1] - second_high)
    second_num = (
        second_old[..., None] * prefix_sum[1]
        + second_back[..., None] * value_wide[0]
        + second_own[..., None] * value_wide[1]
    )
    second_out = second_num / (second_old * prefix_total[1] + second_back + second_own)[..., None]
    return jnp.stack([first_out, second_out]).astype(jnp.bfloat16)


def mover(groups, devices):
    deep = devices // LINE

    def move(value, step):
        pairs = []
        for g in range(groups):
            for s in range(devices):
                a, b, c = s // LINE, s // 2 % 2, s % 2
                to_g, to_a, to_b, to_c = step(g, a, b, c)
                to_s = (to_a % deep) * LINE + to_b * 2 + to_c
                pairs.append((g * devices + s, to_g * devices + to_s))
        return lax.ppermute(value, ("groups", "sample"), pairs)

    along_z = lambda v, k=1: move(v, lambda g, a, b, c: (g, a + k, b, c))
    along_y = lambda v: move(v, lambda g, a, b, c: (g, a, 1 - b, c))
    along_x = lambda v: move(v, lambda g, a, b, c: (g ^ 1, a, b, c))
    in_chip = lambda v: move(v, lambda g, a, b, c: (g, a, b, 1 - c))
    return along_z, along_y, along_x, in_chip


def after(value, done):
    return lax.optimization_barrier((value, done))[0]


def pick(sources, blocks, width):
    heights = [source.shape[0] for source in sources]
    height = sum(heights)

    def body(block_ref, *refs):
        start = 0
        for ref, rows in zip(refs[:-1], heights):
            refs[-1][start : start + rows, :] = ref[...]
            start += rows

    return pl.pallas_call(
        body,
        grid_spec=pltpu.PrefetchScalarGridSpec(
            num_scalar_prefetch=1,
            grid=(blocks.shape[0],),
            in_specs=[
                pl.BlockSpec((rows, width), lambda i, block_ref: (0, block_ref[i]))
                for rows in heights
            ],
            out_specs=pl.BlockSpec((height, width), lambda i, block_ref: (0, i)),
        ),
        out_shape=jax.ShapeDtypeStruct((height, blocks.shape[0] * width), sources[0].dtype),
        cost_estimate=pl.CostEstimate(
            flops=0, bytes_accessed=4 * height * blocks.shape[0] * width, transcendentals=0
        ),
    )(blocks, *sources)


def on_device(
    prompt_states,
    page_table,
    step_states,
    sample_order,
    key_weight,
    value_weight,
    query_weight,
    out_weight,
):
    devices = lax.axis_size("sample")
    groups = lax.axis_size("groups")
    own_index = lax.axis_index("sample")
    first = lax.axis_index("groups") % 2 == 0
    deep = devices // LINE
    own_a, own_b, own_c = own_index // LINE, own_index // 2 % 2, own_index % 2
    along_z, along_y, along_x, in_chip = mover(groups, devices)
    row_count = prompt_states.shape[0]
    chip_rows = 2 * row_count
    pages_here = row_count // PAGE
    heads_here = query_weight.shape[1] // HEAD_DIM
    total_pages = page_table.shape[0]
    prompts = total_pages // PROMPT_PAGES
    samples = sample_order.shape[0]
    steps = 2 * samples
    group_size = samples // prompts
    score_scale = HEAD_DIM ** (-0.5)
    own_kv = own_index * heads_here // GQA
    wide_states = step_states.reshape(steps, D)
    rows = heads_here * steps
    width = key_weight.shape[0]
    half = key_weight.shape[1] // 2

    def in_order(mine, other):
        return jnp.where(
            first,
            jnp.concatenate([mine, other], axis=1),
            jnp.concatenate([other, mine], axis=1),
        )

    places = [(k, flip) for k in range(deep) for flip in (0, 1)]

    def blocks(core, turns):
        return jnp.stack(
            [
                ((own_a + deep + k) % deep) * LINE + (own_b ^ flip) * 2 + core
                for k, flip in turns
            ]
        )

    back = [(-k, flip) for k, flip in places]
    sent = pick([prompt_states], blocks(1 - own_c, back), width)
    got = in_chip(sent)
    kept = pick([prompt_states, wide_states], after(blocks(own_c, back), sent), width)

    key_mine = jnp.where(first, key_weight[:, :half], key_weight[:, half:])
    value_mine = jnp.where(first, value_weight[:, :half], value_weight[:, half:])
    value_other = jnp.where(first, value_weight[:, half:], value_weight[:, :half])
    done = {0: [got]}

    def send(move, value, turn_at):
        if turn_at > 1:
            value = after(value, done[turn_at - 2])
        done.setdefault(turn_at, []).append(move(value))
        return done[turn_at][-1]

    key_z, key_full, key_y = {0: key_mine}, {0: key_weight}, {}
    value_pairs, other_pairs = {}, {}
    for r in range(2 * deep - 1):
        late = r - deep + 2
        if r + 1 < deep:
            key_z[r + 1] = send(along_z, key_z[r], r)
        elif late < deep:
            value_pairs[late] = send(along_z, value_pairs[late - 1], r)
        if r == 0:
            value_y = send(along_y, value_mine, r)
            value_pairs[0] = jnp.concatenate([value_mine, value_y])
        elif r == 1:
            key_y[0] = send(along_y, key_weight, r)
        if 0 < r < deep:
            key_full[r] = in_order(key_z[r], send(along_x, key_z[r], r))
        elif r:
            other_pairs[late - 1] = send(along_x, value_pairs[late - 1], r)
        if r == deep - 1:
            other_pairs[0] = jnp.concatenate([value_other, send(along_x, value_y, r)])
        if 0 < late < deep:
            key_y[late] = send(along_y, key_full[late], r)

    step_place = PROMPT_PAGES * PAGE + jnp.arange(2, dtype=jnp.int32)
    step_tables = tuple(t[:, None, :] for t in rope_tables(step_place))
    queries = jnp.dot(after(wide_states, sent), query_weight, preferred_element_type=jnp.float32)
    queries = queries.reshape(2, samples, heads_here, HEAD_DIM).transpose(2, 0, 1, 3)
    queries = turn(queries, step_tables).astype(jnp.bfloat16)
    flat_queries = queries.reshape(rows, HEAD_DIM)
    pair_queries = jnp.stack([flat_queries, along_y(flat_queries)])
    ring = [pair_queries] + [along_z(pair_queries, deep - j) for j in range(1, deep)]
    line = lax.dynamic_slice_in_dim(jnp.stack(ring + ring), deep - own_a, deep)
    all_queries = jnp.stack([line, in_chip(line)], axis=1)
    by_owner = (deep, 2, 2, rows)
    all_queries = all_queries.reshape(KV_HEADS, -1, HEAD_DIM)

    own_pages = jnp.concatenate(
        [
            holder * pages_here + jnp.arange(pages_here, dtype=jnp.int32)
            for holder in (own_index, own_index ^ 1)
        ]
    )
    slots = jnp.sum(
        jnp.where(
            page_table[None, :] == own_pages[:, None],
            jnp.arange(total_pages, dtype=jnp.int32)[None, :],
            0,
        ),
        axis=1,
    )
    positions = (slots % PROMPT_PAGES * PAGE)[:, None] + jnp.arange(PAGE, dtype=jnp.int32)[None, :]
    cosine, sine_part = rope_tables(positions.reshape(chip_rows))

    turns = [(k, flip) for flip in (0, 1) for k in range(deep)]
    out_width = out_weight.shape[1] // devices
    out_sent = pick([out_weight], after(blocks(1 - own_c, turns), key_y[0]), out_width)
    out_kept = pick([out_weight], after(blocks(own_c, turns), out_sent), out_width)
    out_got = in_chip(out_sent)

    def columns(source, start, count):
        return lax.slice_in_dim(source, start * width, (start + count) * width, axis=1)

    key_own = key_sib = 0.0
    for i, (k, flip) in enumerate(places):
        piece = key_y[k] if flip else key_full[k]
        key_own += jnp.dot(columns(kept, i, 1), piece, preferred_element_type=jnp.float32)
        key_sib += jnp.dot(columns(got, i, 1), piece, preferred_element_type=jnp.float32)
    own_back, sib_back = in_chip(key_own), in_chip(key_sib)
    step_keys = key_own[row_count:] + own_back[row_count:]
    prefix_keys = jnp.concatenate([key_own[:row_count] + sib_back, key_sib + own_back[:row_count]])
    prefix_keys = turn(
        prefix_keys.reshape(chip_rows, KV_HEADS, HEAD_DIM), (cosine[:, None], sine_part[:, None])
    ).astype(jnp.bfloat16)
    step_keys = lax.dynamic_slice_in_dim(step_keys, own_kv * HEAD_DIM, HEAD_DIM, 1)
    new_keys = turn(step_keys.reshape(2, samples, HEAD_DIM), step_tables).astype(jnp.bfloat16)

    scores = (
        jnp.einsum("krd,lkd->krl", all_queries, prefix_keys, preferred_element_type=jnp.float32)
        * score_scale
    )
    if prompts > 1:
        token_prompt = jnp.repeat(slots // PROMPT_PAGES, PAGE)
        row_prompt = jnp.tile(sample_order // group_size, scores.shape[1] // samples)
        scores = jnp.where(row_prompt[:, None] == token_prompt[None, :], scores, -1e30)
    top = jnp.max(scores, axis=-1)
    weights = jnp.exp(scores - top[..., None])
    total = jnp.sum(weights, axis=-1)
    weights = weights.astype(jnp.bfloat16)

    stats = jnp.stack([top.reshape(by_owner), total.reshape(by_owner)])
    stats = jnp.stack([stats, along_y(stats)[:, :, :, ::-1]])
    stats = jnp.concatenate([stats] + [along_z(stats, k) for k in range(1, deep)])
    prefix_top = jnp.max(stats[:, 0], axis=0)
    prefix_total = jnp.sum(jnp.exp(stats[:, 0] - prefix_top) * stats[:, 1], axis=0)
    factor = jnp.exp(top.reshape(by_owner) - prefix_top)
    prefix_top = lax.dynamic_index_in_dim(prefix_top, own_a, 0, False)[0, 0]
    prefix_total = lax.dynamic_index_in_dim(prefix_total, own_a, 0, False)[0, 0]

    def project(pieces):
        own = sib = 0.0
        for k in range(deep):
            own += jnp.dot(columns(kept, 2 * k, 2), pieces[k], preferred_element_type=jnp.float32)
            sib += jnp.dot(columns(got, 2 * k, 2), pieces[k], preferred_element_type=jnp.float32)
        return own, sib

    own_m, sib_m = project(value_pairs)
    own_o, sib_o = project(other_pairs)
    step_values = in_order(own_m[row_count:], own_o[row_count:])
    step_values = step_values + in_chip(step_values)
    new_values = lax.dynamic_slice_in_dim(step_values, own_kv * HEAD_DIM, HEAD_DIM, 1)
    new_values = new_values.reshape(2, samples, HEAD_DIM).astype(jnp.bfloat16)
    values = in_order(
        jnp.concatenate([own_m[:row_count], sib_m]).astype(jnp.bfloat16),
        jnp.concatenate([own_o[:row_count], sib_o]).astype(jnp.bfloat16),
    ).reshape(chip_rows, KV_HEADS, HEAD_DIM)
    partial = jnp.einsum("krl,lkd->krd", weights, values, preferred_element_type=jnp.float32)
    partial = partial.reshape(by_owner + (HEAD_DIM,)) * factor[..., None]

    def narrow(value):
        return value.astype(jnp.bfloat16)

    partial = partial[:, 0] + in_chip(narrow(partial[:, 1])).astype(jnp.float32)
    partial = partial[:, 0] + along_y(narrow(partial[:, 1])).astype(jnp.float32)
    narrowed = narrow(partial)
    prefix_sum = lax.dynamic_index_in_dim(partial, own_a, 0, False)
    for k in range(1, deep):
        piece = lax.dynamic_index_in_dim(narrowed, (own_a + k) % deep, 0, False)
        prefix_sum = prefix_sum + along_z(piece, k).astype(jnp.float32)

    by_head = (heads_here, 2, samples)
    head_out = finish_heads(
        prefix_top.reshape(by_head).swapaxes(0, 1),
        prefix_total.reshape(by_head).swapaxes(0, 1),
        prefix_sum.reshape(by_head + (HEAD_DIM,)).swapaxes(0, 1),
        queries.swapaxes(0, 1),
        new_keys[:, None],
        new_values[:, None],
    )
    flat_heads = head_out.transpose(0, 2, 1, 3).reshape(steps, heads_here * HEAD_DIM)
    terms = jnp.dot(flat_heads, out_kept, preferred_element_type=jnp.float32)
    terms += jnp.dot(in_chip(flat_heads), out_got, preferred_element_type=jnp.float32)
    share = deep * out_width
    terms = terms[:, :share] + along_y(narrow(terms[:, share:])).astype(jnp.float32)
    attn_out = terms[:, :out_width]
    for k in range(1, deep):
        piece = narrow(terms[:, k * out_width : (k + 1) * out_width])
        attn_out = attn_out + along_z(piece, k).astype(jnp.float32)
    return narrow(attn_out).reshape(2, samples, -1)


def solution(mesh):
    in_specs = (
        P(("groups", "sample"), None),
        P("groups"),
        P(None, "groups", None),
        P("groups"),
        P("sample", None),
        P("sample", None),
        P(None, "sample"),
        P("sample", None),
    )
    out_specs = P(None, "groups", "sample")
    return jax.shard_map(
        on_device, mesh=mesh, in_specs=in_specs, out_specs=out_specs, check_vma=False
    )
```

```python
import jax
import jax.numpy as jnp
from jax import lax
from jax.experimental import pallas as pl
from jax.experimental.pallas import tpu as pltpu
from jax.sharding import PartitionSpec as P

D = 8192
HEAD_DIM = 128
KV_HEADS = 4
GQA = 8
PAGE = 128
PROMPT_PAGES = 64
LINE = 4

rope_base = 1000000.0


def rope_tables(position):
    half_dim = HEAD_DIM // 2
    frequency = rope_base ** (-jnp.arange(half_dim, dtype=jnp.float32) * 2.0 / HEAD_DIM)
    angles = position.astype(jnp.float32)[..., None] * frequency
    return jnp.cos(angles), jnp.sin(angles)


def turn(vector, tables):
    cosine, sine_part = tables
    half_dim = HEAD_DIM // 2
    first_half = vector[..., :half_dim]
    second_half = vector[..., half_dim:]
    return jnp.concatenate(
        [
            first_half * cosine - second_half * sine_part,
            second_half * cosine + first_half * sine_part,
        ],
        axis=-1,
    )


def finish_heads(prefix_top, prefix_total, prefix_sum, queries, new_keys, new_values):
    score_scale = queries.shape[-1] ** (-0.5)
    query_wide = queries.astype(jnp.float32)
    key_wide = new_keys.astype(jnp.float32)
    value_wide = new_values.astype(jnp.float32)
    own_score = jnp.sum(query_wide * key_wide, axis=-1) * score_scale
    back_score = jnp.sum(query_wide[1] * key_wide[0], axis=-1) * score_scale
    first_high = jnp.maximum(prefix_top[0], own_score[0])
    first_old = jnp.exp(prefix_top[0] - first_high)
    first_own = jnp.exp(own_score[0] - first_high)
    first_out = (first_old[..., None] * prefix_sum[0] + first_own[..., None] * value_wide[0]) / (
        first_old * prefix_total[0] + first_own
    )[..., None]
    second_high = jnp.maximum(jnp.maximum(prefix_top[1], own_score[1]), back_score)
    second_old = jnp.exp(prefix_top[1] - second_high)
    second_back = jnp.exp(back_score - second_high)
    second_own = jnp.exp(own_score[1] - second_high)
    second_num = (
        second_old[..., None] * prefix_sum[1]
        + second_back[..., None] * value_wide[0]
        + second_own[..., None] * value_wide[1]
    )
    second_out = second_num / (second_old * prefix_total[1] + second_back + second_own)[..., None]
    return jnp.stack([first_out, second_out]).astype(jnp.bfloat16)


def mover(groups, devices):
    deep = devices // LINE

    def move(value, step):
        pairs = []
        for g in range(groups):
            for s in range(devices):
                a, b, c = s // LINE, s // 2 % 2, s % 2
                to_g, to_a, to_b, to_c = step(g, a, b, c)
                to_s = (to_a % deep) * LINE + to_b * 2 + to_c
                pairs.append((g * devices + s, to_g * devices + to_s))
        return lax.ppermute(value, ("groups", "sample"), pairs)

    along_z = lambda v, k=1: move(v, lambda g, a, b, c: (g, a + k, b, c))
    along_y = lambda v: move(v, lambda g, a, b, c: (g, a, 1 - b, c))
    along_x = lambda v: move(v, lambda g, a, b, c: (g ^ 1, a, b, c))
    in_chip = lambda v: move(v, lambda g, a, b, c: (g, a, b, 1 - c))
    return along_z, along_y, along_x, in_chip


def after(value, done):
    return lax.optimization_barrier((value, done))[0]


VMEM_LIMIT = 48 * 1024 * 1024


def pick(source, blocks, width):
    count = blocks.shape[0]

    def body(block_ref, source_ref, out_ref, sems):
        copies = []
        for i in range(count):
            start = pl.multiple_of(block_ref[i] * width, width)
            copies.append(
                pltpu.make_async_copy(
                    source_ref.at[:, pl.ds(start, width)],
                    out_ref.at[:, pl.ds(i * width, width)],
                    sems.at[i],
                )
            )
            copies[-1].start()
        for copy in copies:
            copy.wait()

    rows = source.shape[0]
    return pl.pallas_call(
        body,
        in_specs=[pl.BlockSpec(memory_space=pltpu.SMEM), pl.BlockSpec(memory_space=pl.ANY)],
        out_specs=pl.BlockSpec(memory_space=pl.ANY),
        out_shape=jax.ShapeDtypeStruct((rows, count * width), source.dtype),
        scratch_shapes=[pltpu.SemaphoreType.DMA((count,))],
        cost_estimate=pl.CostEstimate(
            flops=0, bytes_accessed=4 * rows * count * width, transcendentals=0
        ),
    )(blocks, source)


def project(prompt, steps, got, blocks, begin, pieces, acc):
    arrays = []
    for piece in pieces:
        for array, _ in piece:
            if not any(array is held for held in arrays):
                arrays.append(array)
    width = pieces[0][0][0].shape[0] if len(pieces[0]) == 1 else pieces[0][0][0].shape[0] // 2
    columns = sum(array.shape[1] for array, _ in pieces[0])
    row_count, step_count = prompt.shape[0], steps.shape[0]
    height = 2 * row_count + step_count
    extra = [] if acc is None else [acc]

    def body(block_ref, prompt_ref, got_ref, step_ref, *refs):
        weights, held = refs[: len(arrays)], refs[-1]
        out_ref = refs[-2]
        step = pl.program_id(0)
        for i, piece in enumerate(pieces):

            @pl.when(step == i)
            def _():
                column = 0
                for array, first in piece:
                    ref = weights[[array is other for other in arrays].index(True)]
                    held[:, column : column + array.shape[1]] = ref[first : first + width, :]
                    column += array.shape[1]

        @pl.when(step == 0)
        def _():
            if acc is None:
                out_ref[...] = jnp.zeros_like(out_ref)
            else:
                out_ref[...] = refs[len(arrays)][...]

        start = 0
        for ref, rows in (
            (prompt_ref, row_count),
            (got_ref, row_count),
            (step_ref, step_count),
        ):
            out_ref[start : start + rows, :] += jnp.dot(
                ref[...], held[...], preferred_element_type=jnp.float32
            )
            start += rows

    whole = pl.BlockSpec(memory_space=pltpu.VMEM)
    return pl.pallas_call(
        body,
        grid_spec=pltpu.PrefetchScalarGridSpec(
            num_scalar_prefetch=1,
            grid=(len(pieces),),
            in_specs=[
                pl.BlockSpec((row_count, width), lambda i, ref: (0, ref[i])),
                pl.BlockSpec((row_count, width), lambda i, ref: (0, begin + i)),
                pl.BlockSpec((step_count, width), lambda i, ref: (0, ref[i])),
            ]
            + [whole] * (len(arrays) + len(extra)),
            out_specs=pl.BlockSpec((height, columns), lambda i, ref: (0, 0)),
            scratch_shapes=[pltpu.VMEM((width, columns), jnp.bfloat16)],
        ),
        out_shape=jax.ShapeDtypeStruct((height, columns), jnp.float32),
        compiler_params=pltpu.CompilerParams(vmem_limit_bytes=VMEM_LIMIT),
        cost_estimate=pl.CostEstimate(
            flops=2 * height * width * len(pieces) * columns,
            bytes_accessed=2 * height * width * len(pieces) + 8 * height * columns,
            transcendentals=0,
        ),
    )(blocks, prompt, got, steps, *arrays, *extra)


def attend(places, queries, own, other, cosine, sine, token_prompt, row_prompt):
    kv_heads, count, _ = queries.shape
    tokens = cosine.shape[0]
    half = tokens // 2
    height = own.shape[0]
    masks = [] if token_prompt is None else [token_prompt, row_prompt]

    def body(place_ref, query_ref, own_ref, other_ref, cosine_ref, sine_ref, *refs):
        weight_ref, top_ref, total_ref = refs[-3:]
        keys = jnp.concatenate(
            [
                own_ref[:half, :] + other_ref[half:tokens, :],
                own_ref[half:tokens, :] + other_ref[:half, :],
            ],
            axis=0,
        )
        swapped = pltpu.roll(keys, HEAD_DIM // 2, 1)
        keys = (keys * cosine_ref[...] + swapped * sine_ref[...]).astype(jnp.bfloat16)
        scores = lax.dot_general(
            keys, query_ref[0], (((1,), (1,)), ((), ())), preferred_element_type=jnp.float32
        ) * (HEAD_DIM**-0.5)
        if masks:
            scores = jnp.where(refs[0][...] == refs[1][...], scores, -1e30)
        top = jnp.max(scores, axis=0, keepdims=True)
        weights = jnp.exp(scores - top)
        top_ref[0] = top
        total_ref[0] = jnp.sum(weights, axis=0, keepdims=True)
        weight_ref[0] = weights.astype(jnp.bfloat16)

    row = jax.ShapeDtypeStruct((kv_heads, 1, count), jnp.float32)
    row_spec = pl.BlockSpec((1, 1, count), lambda j, ref: (j, 0, 0))
    fixed = lambda j, ref: (0, 0)
    return pl.pallas_call(
        body,
        grid_spec=pltpu.PrefetchScalarGridSpec(
            num_scalar_prefetch=1,
            grid=(kv_heads,),
            in_specs=[
                pl.BlockSpec((1, count, HEAD_DIM), lambda j, ref: (j, 0, 0)),
                pl.BlockSpec((height, HEAD_DIM), lambda j, ref: (0, ref[j])),
                pl.BlockSpec((height, HEAD_DIM), lambda j, ref: (0, ref[j])),
                pl.BlockSpec((tokens, HEAD_DIM), fixed),
                pl.BlockSpec((tokens, HEAD_DIM), fixed),
            ]
            + [pl.BlockSpec(mask.shape, fixed) for mask in masks],
            out_specs=[
                pl.BlockSpec((1, tokens, count), lambda j, ref: (j, 0, 0)),
                row_spec,
                row_spec,
            ],
        ),
        out_shape=[
            jax.ShapeDtypeStruct((kv_heads, tokens, count), jnp.bfloat16),
            row,
            row,
        ],
        compiler_params=pltpu.CompilerParams(vmem_limit_bytes=VMEM_LIMIT),
        cost_estimate=pl.CostEstimate(
            flops=2 * kv_heads * tokens * count * HEAD_DIM,
            bytes_accessed=8 * height * kv_heads * HEAD_DIM + 2 * kv_heads * tokens * count,
            transcendentals=kv_heads * tokens * count,
        ),
    )(places, queries, own, other, cosine, sine, *masks)


def apply_weights(places, weights, values, factor):
    kv_heads, tokens, count = weights.shape

    def body(place_ref, weight_ref, value_ref, factor_ref, out_ref):
        summed = lax.dot_general(
            value_ref[:tokens, :].astype(jnp.bfloat16),
            weight_ref[0],
            (((0,), (0,)), ((), ())),
            preferred_element_type=jnp.float32,
        )
        out_ref[0] = (summed * factor_ref[0]).T.astype(jnp.bfloat16)

    return pl.pallas_call(
        body,
        grid_spec=pltpu.PrefetchScalarGridSpec(
            num_scalar_prefetch=1,
            grid=(kv_heads,),
            in_specs=[
                pl.BlockSpec((1, tokens, count), lambda j, ref: (j, 0, 0)),
                pl.BlockSpec((values.shape[0], HEAD_DIM), lambda j, ref: (0, ref[j])),
                pl.BlockSpec((1, 1, count), lambda j, ref: (j, 0, 0)),
            ],
            out_specs=pl.BlockSpec((1, count, HEAD_DIM), lambda j, ref: (j, 0, 0)),
        ),
        out_shape=jax.ShapeDtypeStruct((kv_heads, count, HEAD_DIM), jnp.bfloat16),
        compiler_params=pltpu.CompilerParams(vmem_limit_bytes=VMEM_LIMIT),
        cost_estimate=pl.CostEstimate(
            flops=2 * kv_heads * tokens * count * HEAD_DIM,
            bytes_accessed=2 * kv_heads * tokens * count,
            transcendentals=0,
        ),
    )(places, weights, values, factor)


def out_project(blocks, heads, weight, width):
    def body(block_ref, head_ref, weight_ref, out_ref):
        for i in range(blocks.shape[0]):
            start = pl.multiple_of(block_ref[i] * width, width)
            out_ref[:, i * width : (i + 1) * width] = jnp.dot(
                head_ref[...], weight_ref[:, pl.ds(start, width)], preferred_element_type=jnp.float32
            ).astype(jnp.bfloat16)

    whole = pl.BlockSpec(memory_space=pltpu.VMEM)
    shape = (heads.shape[0], weight.shape[1])
    return pl.pallas_call(
        body,
        in_specs=[pl.BlockSpec(memory_space=pltpu.SMEM), whole, whole],
        out_specs=whole,
        out_shape=jax.ShapeDtypeStruct(shape, jnp.bfloat16),
        compiler_params=pltpu.CompilerParams(vmem_limit_bytes=VMEM_LIMIT),
        cost_estimate=pl.CostEstimate(
            flops=2 * heads.shape[1] * shape[0] * shape[1],
            bytes_accessed=2 * (weight.size + heads.size + shape[0] * shape[1]),
            transcendentals=0,
        ),
    )(blocks, heads, weight)


def on_device(
    prompt_states,
    page_table,
    step_states,
    sample_order,
    key_weight,
    value_weight,
    query_weight,
    out_weight,
):
    devices = lax.axis_size("sample")
    groups = lax.axis_size("groups")
    own_index = lax.axis_index("sample")
    first = lax.axis_index("groups") % 2 == 0
    deep = devices // LINE
    own_a, own_b, own_c = own_index // LINE, own_index // 2 % 2, own_index % 2
    along_z, along_y, along_x, in_chip = mover(groups, devices)
    row_count = prompt_states.shape[0]
    chip_rows = 2 * row_count
    pages_here = row_count // PAGE
    heads_here = query_weight.shape[1] // HEAD_DIM
    total_pages = page_table.shape[0]
    prompts = total_pages // PROMPT_PAGES
    samples = sample_order.shape[0]
    steps = 2 * samples
    group_size = samples // prompts
    own_kv = own_index * heads_here // GQA
    wide_states = step_states.reshape(steps, D)
    rows = heads_here * steps
    width = key_weight.shape[0]
    half = key_weight.shape[1] // 2
    kv_places = jnp.where(first, 0, KV_HEADS // 2) + jnp.arange(KV_HEADS, dtype=jnp.int32)
    kv_places = kv_places % KV_HEADS

    def block(turn_z, flip, core):
        return ((own_a + deep + turn_z) % deep) * LINE + (own_b ^ flip) * 2 + core

    def halves(weight):
        low, high = weight[:, :half], weight[:, half:]
        return jnp.where(first, low, high), jnp.where(first, high, low)

    key_mine, key_other = halves(key_weight)
    value_mine, value_other = halves(value_weight)

    places = [(k, flip) for k in range(deep) for flip in (0, 1)]
    own_blocks = jnp.stack([block(-k, flip, own_c) for k, flip in places])
    sent_blocks = jnp.stack([block(-k, flip, 1 - own_c) for k, flip in places])
    sent = pick(prompt_states, after(sent_blocks, (key_mine, value_mine)), width)
    got = in_chip(sent)
    done = {0: [got]}

    def send(move, value, turn_at):
        if turn_at > 1:
            value = after(value, done[turn_at - 2])
        done.setdefault(turn_at, []).append(move(value))
        return done[turn_at][-1]

    step_place = PROMPT_PAGES * PAGE + jnp.arange(2, dtype=jnp.int32)
    step_tables = tuple(t[:, None, :] for t in rope_tables(step_place))
    queries = jnp.dot(after(wide_states, sent), query_weight, preferred_element_type=jnp.float32)
    queries = queries.reshape(2, samples, heads_here, HEAD_DIM).transpose(2, 0, 1, 3)
    queries = turn(queries, step_tables).astype(jnp.bfloat16)
    flat_queries = queries.reshape(rows, HEAD_DIM)

    key_z, key_y = {0: key_mine}, {}
    key_full = {0: jnp.concatenate([key_mine, key_other], axis=1)}
    value_pairs, other_pairs = {}, {}
    ring = {}
    for r in range(2 * deep - 1):
        late = r - deep + 2
        if r + 1 < deep:
            key_z[r + 1] = send(along_z, key_z[r], r)
        elif late < deep:
            value_pairs[late] = send(along_z, value_pairs[late - 1], r)
        if r == 0:
            value_y = send(along_y, value_mine, r)
            value_pairs[0] = jnp.concatenate([value_mine, value_y])
        elif r == 1:
            key_y[0] = send(along_y, key_full[0], r)
            pair_queries = jnp.stack([flat_queries, send(along_y, flat_queries, r)])
        if 0 < r < deep:
            key_full[r] = jnp.concatenate([key_z[r], send(along_x, key_z[r], r)], axis=1)
        elif r:
            other_pairs[late - 1] = send(along_x, value_pairs[late - 1], r)
        if r == deep - 1:
            other_pairs[0] = jnp.concatenate([value_other, send(along_x, value_y, r)])
        if 0 < late < deep:
            key_y[late] = send(along_y, key_full[late], r)
        if 1 < r <= deep:
            ring[r - 1] = send(lambda v: along_z(v, deep - r + 1), pair_queries, r)
    ring = [pair_queries] + [ring[j] for j in range(1, deep)]
    line = lax.dynamic_slice_in_dim(jnp.stack(ring + ring), deep - own_a, deep)
    all_queries = jnp.stack([line, in_chip(line)], axis=1)
    by_owner = (deep, 2, 2, rows)
    all_queries = all_queries.reshape(KV_HEADS, -1, HEAD_DIM)

    own_pages = jnp.concatenate(
        [
            holder * pages_here + jnp.arange(pages_here, dtype=jnp.int32)
            for holder in (own_index, own_index ^ 1)
        ]
    )
    slots = jnp.sum(
        jnp.where(
            page_table[None, :] == own_pages[:, None],
            jnp.arange(total_pages, dtype=jnp.int32)[None, :],
            0,
        ),
        axis=1,
    )
    positions = (slots % PROMPT_PAGES * PAGE)[:, None] + jnp.arange(PAGE, dtype=jnp.int32)[None, :]
    cosine, sine_part = rope_tables(positions.reshape(chip_rows))
    cosine = jnp.concatenate([cosine, cosine], axis=1)
    sine_part = jnp.concatenate([-sine_part, sine_part], axis=1)

    def pieces_of(k_range, key):
        if key:
            return [[((key_y if flip else key_full)[k], 0)] for k in k_range for flip in (0, 1)]
        return [
            [(value_pairs[k], flip * width), (other_pairs[k], flip * width)]
            for k in k_range
            for flip in (0, 1)
        ]

    def project_all(key):
        split = 2 * (deep - 1)
        early = project(
            prompt_states, wide_states, got, own_blocks[:split], 0,
            pieces_of(range(deep - 1), key), None,
        )
        return project(
            prompt_states, wide_states, got, own_blocks[split:], split,
            pieces_of([deep - 1], key), early,
        )

    key_sum = project_all(True)
    key_back = in_chip(key_sum)
    own_place = lax.dynamic_index_in_dim(kv_places, own_kv, 0, False) * HEAD_DIM

    def own_head(sums):
        return lax.dynamic_slice_in_dim(sums, own_place, HEAD_DIM, 1).reshape(2, samples, HEAD_DIM)

    new_keys = own_head(key_sum[chip_rows:]) + own_head(key_back[chip_rows:])
    new_keys = turn(new_keys, step_tables).astype(jnp.bfloat16)
    masks = (None, None)
    if prompts > 1:
        token_prompt = jnp.repeat(slots // PROMPT_PAGES, PAGE)
        row_prompt = jnp.tile(sample_order // group_size, all_queries.shape[1] // samples)
        masks = (token_prompt[:, None], row_prompt[None, :])
    weights, top, total = attend(
        kv_places, all_queries, key_sum, key_back, cosine, sine_part, *masks
    )

    stats = jnp.stack([top.reshape(by_owner), total.reshape(by_owner)])
    stats = jnp.stack([stats, along_y(stats)[:, :, :, ::-1]])
    stats = jnp.concatenate([stats] + [along_z(stats, k) for k in range(1, deep)])
    prefix_top = jnp.max(stats[:, 0], axis=0)
    prefix_total = jnp.sum(jnp.exp(stats[:, 0] - prefix_top) * stats[:, 1], axis=0)
    factor = jnp.exp(top.reshape(by_owner) - prefix_top).reshape(top.shape)
    prefix_top = lax.dynamic_index_in_dim(prefix_top, own_a, 0, False)[0, 0]
    prefix_total = lax.dynamic_index_in_dim(prefix_total, own_a, 0, False)[0, 0]

    value_sum = project_all(False)
    step_values = own_head(value_sum[chip_rows:])
    step_back = lax.dynamic_slice_in_dim(
        in_chip(value_sum[chip_rows:]), own_place, HEAD_DIM, 1
    ).reshape(step_values.shape)
    new_values = (step_values + step_back).astype(jnp.bfloat16)
    partial = apply_weights(kv_places, weights, value_sum, factor)
    partial = partial.reshape(by_owner + (HEAD_DIM,))

    def narrow(value):
        return value.astype(jnp.bfloat16)

    def wide(value):
        return value.astype(jnp.float32)

    partial = narrow(wide(partial[:, 0]) + wide(in_chip(partial[:, 1])))
    partial = narrow(wide(partial[:, 0]) + wide(along_y(partial[:, 1])))
    prefix_sum = wide(lax.dynamic_index_in_dim(partial, own_a, 0, False))
    for k in range(1, deep):
        piece = lax.dynamic_index_in_dim(partial, (own_a + k) % deep, 0, False)
        prefix_sum = prefix_sum + wide(along_z(piece, k))

    by_head = (heads_here, 2, samples)
    head_out = finish_heads(
        prefix_top.reshape(by_head).swapaxes(0, 1),
        prefix_total.reshape(by_head).swapaxes(0, 1),
        prefix_sum.reshape(by_head + (HEAD_DIM,)).swapaxes(0, 1),
        queries.swapaxes(0, 1),
        new_keys[:, None],
        new_values[:, None],
    )
    flat_heads = head_out.transpose(0, 2, 1, 3).reshape(steps, heads_here * HEAD_DIM)

    out_width = out_weight.shape[1] // devices
    out_blocks = jnp.stack(
        [
            block(k, flip, own_c ^ turned)
            for turned in (0, 1)
            for flip in (0, 1)
            for k in range(deep)
        ]
    )
    terms = out_project(out_blocks, flat_heads, out_weight, out_width)
    for move in (in_chip, along_y):
        share = terms.shape[1] // 2
        terms = narrow(wide(terms[:, :share]) + wide(move(terms[:, share:])))
    attn_out = wide(terms[:, :out_width])
    for k in range(1, deep):
        attn_out = attn_out + wide(along_z(terms[:, k * out_width : (k + 1) * out_width], k))
    return narrow(attn_out).reshape(2, samples, -1)


def solution(mesh):
    in_specs = (
        P(("groups", "sample"), None),
        P("groups"),
        P(None, "groups", None),
        P("groups"),
        P("sample", None),
        P("sample", None),
        P(None, "sample"),
        P("sample", None),
    )
    out_specs = P(None, "groups", "sample")
    return jax.shard_map(
        on_device, mesh=mesh, in_specs=in_specs, out_specs=out_specs, check_vma=False
    )
```

```python
import jax
import jax.numpy as jnp
from jax import lax
from jax.experimental import pallas as pl
from jax.experimental.pallas import tpu as pltpu
from jax.sharding import PartitionSpec as P

D = 8192
HEAD_DIM = 128
KV_HEADS = 4
GQA = 8
PAGE = 128
PROMPT_PAGES = 64
LINE = 4

rope_base = 1000000.0


def rope_tables(position):
    half_dim = HEAD_DIM // 2
    frequency = rope_base ** (-jnp.arange(half_dim, dtype=jnp.float32) * 2.0 / HEAD_DIM)
    angles = position.astype(jnp.float32)[..., None] * frequency
    return jnp.cos(angles), jnp.sin(angles)


def turn(vector, tables):
    cosine, sine_part = tables
    half_dim = HEAD_DIM // 2
    first_half = vector[..., :half_dim]
    second_half = vector[..., half_dim:]
    return jnp.concatenate(
        [
            first_half * cosine - second_half * sine_part,
            second_half * cosine + first_half * sine_part,
        ],
        axis=-1,
    )


def finish_heads(prefix_top, prefix_total, prefix_sum, queries, new_keys, new_values):
    score_scale = queries.shape[-1] ** (-0.5)
    query_wide = queries.astype(jnp.float32)
    key_wide = new_keys.astype(jnp.float32)
    value_wide = new_values.astype(jnp.float32)
    own_score = jnp.sum(query_wide * key_wide, axis=-1) * score_scale
    back_score = jnp.sum(query_wide[1] * key_wide[0], axis=-1) * score_scale
    first_high = jnp.maximum(prefix_top[0], own_score[0])
    first_old = jnp.exp(prefix_top[0] - first_high)
    first_own = jnp.exp(own_score[0] - first_high)
    first_out = (first_old[..., None] * prefix_sum[0] + first_own[..., None] * value_wide[0]) / (
        first_old * prefix_total[0] + first_own
    )[..., None]
    second_high = jnp.maximum(jnp.maximum(prefix_top[1], own_score[1]), back_score)
    second_old = jnp.exp(prefix_top[1] - second_high)
    second_back = jnp.exp(back_score - second_high)
    second_own = jnp.exp(own_score[1] - second_high)
    second_num = (
        second_old[..., None] * prefix_sum[1]
        + second_back[..., None] * value_wide[0]
        + second_own[..., None] * value_wide[1]
    )
    second_out = second_num / (second_old * prefix_total[1] + second_back + second_own)[..., None]
    return jnp.stack([first_out, second_out]).astype(jnp.bfloat16)


def ring_order(deep):
    return [*range(0, deep, 2), *range(deep - 1 - deep % 2, 0, -2)]


def mover(groups, devices):
    deep = devices // LINE
    order = ring_order(deep)

    def move(value, step):
        pairs = []
        for g in range(groups):
            for s in range(devices):
                a, b, c = s // LINE, s // 2 % 2, s % 2
                to_g, to_a, to_b, to_c = step(g, a, b, c)
                to_s = (to_a % deep) * LINE + to_b * 2 + to_c
                pairs.append((g * devices + s, to_g * devices + to_s))
        return lax.ppermute(value, ("groups", "sample"), pairs)

    def next_on_ring(a):
        return order[(order.index(a) + 1) % deep]

    along_ring = lambda v: move(v, lambda g, a, b, c: (g, next_on_ring(a), b, c))
    along_z = lambda v, k: move(v, lambda g, a, b, c: (g, a + k, b, c))
    along_y = lambda v: move(v, lambda g, a, b, c: (g, a, 1 - b, c))
    along_x = lambda v: move(v, lambda g, a, b, c: (g ^ 1, a, b, c))
    in_chip = lambda v: move(v, lambda g, a, b, c: (g, a, b, 1 - c))
    return along_ring, along_z, along_y, along_x, in_chip


def after(value, done):
    return lax.optimization_barrier((value, done))[0]


MIB = 1024 * 1024


def pick(source, blocks, width):
    count = blocks.shape[0]
    rows = source.shape[0]

    def body(block_ref, source_ref, out_ref, sems):
        copies = []
        for i in range(count):
            start = pl.multiple_of(block_ref[i] * width, width)
            copies.append(
                pltpu.make_async_copy(
                    source_ref.at[:, pl.ds(start, width)],
                    out_ref.at[:, pl.ds(i * width, width)],
                    sems.at[i],
                )
            )
            copies[-1].start()
        for copy in copies:
            copy.wait()

    return pl.pallas_call(
        body,
        in_specs=[pl.BlockSpec(memory_space=pltpu.SMEM), pl.BlockSpec(memory_space=pl.ANY)],
        out_specs=pl.BlockSpec(memory_space=pltpu.VMEM),
        out_shape=jax.ShapeDtypeStruct((rows, count * width), source.dtype),
        scratch_shapes=[pltpu.SemaphoreType.DMA((count,))],
        compiler_params=pltpu.CompilerParams(vmem_limit_bytes=16 * MIB),
        cost_estimate=pl.CostEstimate(
            flops=0, bytes_accessed=4 * rows * count * width, transcendentals=0
        ),
    )(blocks, source)


def project(prompt, steps, got, blocks, begin, pieces, acc):
    arrays = []
    for piece in pieces:
        for array, _ in piece:
            if not any(array is held for held in arrays):
                arrays.append(array)
    width = got.shape[1] // (begin + len(pieces)) if acc is not None else None
    width = width or prompt.shape[1] // (2 * (len(pieces) + 2))
    count = len(pieces)
    columns = sum(array.shape[1] for array, _ in pieces[0])
    row_count, step_count = prompt.shape[0], steps.shape[0]
    height = 2 * row_count + step_count
    extra = [] if acc is None else [acc]

    def body(block_ref, prompt_ref, got_ref, step_ref, *refs):
        weight_refs = refs[: len(arrays)]
        out_ref, left, held, sems = refs[-4:]
        copies = []
        for i, piece in enumerate(pieces):
            start = pl.multiple_of(block_ref[i] * width, width)
            column = pl.ds(start, width)
            group = [
                pltpu.make_async_copy(
                    prompt_ref.at[:, column], left.at[i, pl.ds(0, row_count), :], sems.at[i, 0]
                ),
                pltpu.make_async_copy(
                    got_ref.at[:, pl.ds((begin + i) * width, width)],
                    left.at[i, pl.ds(row_count, row_count), :],
                    sems.at[i, 1],
                ),
                pltpu.make_async_copy(
                    step_ref.at[:, column],
                    left.at[i, pl.ds(2 * row_count, step_count), :],
                    sems.at[i, 2],
                ),
            ]
            side = 0
            for j, (array, first) in enumerate(piece):
                ref = weight_refs[[array is other for other in arrays].index(True)]
                group.append(
                    pltpu.make_async_copy(
                        ref.at[pl.ds(first, width), :],
                        held.at[i, :, pl.ds(side, array.shape[1])],
                        sems.at[i, 3 + j],
                    )
                )
                side += array.shape[1]
            for copy in group:
                copy.start()
            copies.append(group)
        for i, group in enumerate(copies):
            for copy in group:
                copy.wait()
            product = jnp.dot(left[i], held[i], preferred_element_type=jnp.float32)
            if i:
                out_ref[...] += product
            elif acc is not None:
                out_ref[...] = refs[len(arrays)][...] + product
            else:
                out_ref[...] = product

    anywhere = pl.BlockSpec(memory_space=pl.ANY)
    whole = pl.BlockSpec(memory_space=pltpu.VMEM)
    return pl.pallas_call(
        body,
        in_specs=[pl.BlockSpec(memory_space=pltpu.SMEM)]
        + [anywhere] * (3 + len(arrays))
        + [whole] * len(extra),
        out_specs=whole,
        out_shape=jax.ShapeDtypeStruct((height, columns), jnp.float32),
        scratch_shapes=[
            pltpu.VMEM((count, height, width), jnp.bfloat16),
            pltpu.VMEM((count, width, columns), jnp.bfloat16),
            pltpu.SemaphoreType.DMA((count, 5)),
        ],
        compiler_params=pltpu.CompilerParams(vmem_limit_bytes=24 * MIB),
        cost_estimate=pl.CostEstimate(
            flops=2 * height * width * count * columns,
            bytes_accessed=2 * height * width * count + 8 * height * columns,
            transcendentals=0,
        ),
    )(blocks, prompt, got, steps, *arrays, *extra)


def attend(places, queries, own, other, cosine, sine, token_prompt, row_prompt):
    kv_heads, count, _ = queries.shape
    tokens = cosine.shape[0]
    half = tokens // 2
    height = own.shape[0]
    masks = [] if token_prompt is None else [token_prompt, row_prompt]

    def body(place_ref, query_ref, own_ref, other_ref, cosine_ref, sine_ref, *refs):
        weight_ref, top_ref, total_ref = refs[-3:]
        keys = jnp.concatenate(
            [
                own_ref[:half, :] + other_ref[half:tokens, :],
                own_ref[half:tokens, :] + other_ref[:half, :],
            ],
            axis=0,
        )
        swapped = pltpu.roll(keys, HEAD_DIM // 2, 1)
        keys = (keys * cosine_ref[...] + swapped * sine_ref[...]).astype(jnp.bfloat16)
        scores = lax.dot_general(
            keys, query_ref[0], (((1,), (1,)), ((), ())), preferred_element_type=jnp.float32
        ) * (HEAD_DIM**-0.5)
        if masks:
            scores = jnp.where(refs[0][...] == refs[1][...], scores, -1e30)
        top = jnp.max(scores, axis=0, keepdims=True)
        weights = jnp.exp(scores - top)
        top_ref[0] = top
        total_ref[0] = jnp.sum(weights, axis=0, keepdims=True)
        weight_ref[0] = weights.astype(jnp.bfloat16)

    row = jax.ShapeDtypeStruct((kv_heads, 1, count), jnp.float32)
    row_spec = pl.BlockSpec((1, 1, count), lambda j, ref: (j, 0, 0))
    fixed = lambda j, ref: (0, 0)
    return pl.pallas_call(
        body,
        grid_spec=pltpu.PrefetchScalarGridSpec(
            num_scalar_prefetch=1,
            grid=(kv_heads,),
            in_specs=[
                pl.BlockSpec((1, count, HEAD_DIM), lambda j, ref: (j, 0, 0)),
                pl.BlockSpec((height, HEAD_DIM), lambda j, ref: (0, ref[j])),
                pl.BlockSpec((height, HEAD_DIM), lambda j, ref: (0, ref[j])),
                pl.BlockSpec((tokens, HEAD_DIM), fixed),
                pl.BlockSpec((tokens, HEAD_DIM), fixed),
            ]
            + [pl.BlockSpec(mask.shape, fixed) for mask in masks],
            out_specs=[
                pl.BlockSpec((1, tokens, count), lambda j, ref: (j, 0, 0)),
                row_spec,
                row_spec,
            ],
        ),
        out_shape=[
            jax.ShapeDtypeStruct((kv_heads, tokens, count), jnp.bfloat16),
            row,
            row,
        ],
        compiler_params=pltpu.CompilerParams(vmem_limit_bytes=20 * MIB),
        cost_estimate=pl.CostEstimate(
            flops=2 * kv_heads * tokens * count * HEAD_DIM,
            bytes_accessed=8 * height * kv_heads * HEAD_DIM + 2 * kv_heads * tokens * count,
            transcendentals=kv_heads * tokens * count,
        ),
    )(places, queries, own, other, cosine, sine, *masks)


def apply_weights(places, weights, values):
    kv_heads, tokens, count = weights.shape

    def body(place_ref, weight_ref, value_ref, out_ref):
        summed = lax.dot_general(
            value_ref[:tokens, :].astype(jnp.bfloat16),
            weight_ref[0],
            (((0,), (0,)), ((), ())),
            preferred_element_type=jnp.float32,
        )
        out_ref[0] = summed.T.astype(jnp.bfloat16)

    return pl.pallas_call(
        body,
        grid_spec=pltpu.PrefetchScalarGridSpec(
            num_scalar_prefetch=1,
            grid=(kv_heads,),
            in_specs=[
                pl.BlockSpec((1, tokens, count), lambda j, ref: (j, 0, 0)),
                pl.BlockSpec((values.shape[0], HEAD_DIM), lambda j, ref: (0, ref[j])),
            ],
            out_specs=pl.BlockSpec((1, count, HEAD_DIM), lambda j, ref: (j, 0, 0)),
        ),
        out_shape=jax.ShapeDtypeStruct((kv_heads, count, HEAD_DIM), jnp.bfloat16),
        compiler_params=pltpu.CompilerParams(vmem_limit_bytes=20 * MIB),
        cost_estimate=pl.CostEstimate(
            flops=2 * kv_heads * tokens * count * HEAD_DIM,
            bytes_accessed=2 * kv_heads * tokens * count,
            transcendentals=0,
        ),
    )(places, weights, values)


def out_project(blocks, heads, weight, width):
    def body(block_ref, head_ref, weight_ref, out_ref):
        for i in range(blocks.shape[0]):
            start = pl.multiple_of(block_ref[i] * width, width)
            out_ref[:, i * width : (i + 1) * width] = jnp.dot(
                head_ref[...], weight_ref[:, pl.ds(start, width)], preferred_element_type=jnp.float32
            ).astype(jnp.bfloat16)

    whole = pl.BlockSpec(memory_space=pltpu.VMEM)
    shape = (heads.shape[0], weight.shape[1])
    return pl.pallas_call(
        body,
        in_specs=[pl.BlockSpec(memory_space=pltpu.SMEM), whole, whole],
        out_specs=whole,
        out_shape=jax.ShapeDtypeStruct(shape, jnp.bfloat16),
        compiler_params=pltpu.CompilerParams(vmem_limit_bytes=20 * MIB),
        cost_estimate=pl.CostEstimate(
            flops=2 * heads.shape[1] * shape[0] * shape[1],
            bytes_accessed=2 * (weight.size + heads.size + shape[0] * shape[1]),
            transcendentals=0,
        ),
    )(blocks, heads, weight)


def on_device(
    prompt_states,
    page_table,
    step_states,
    sample_order,
    key_weight,
    value_weight,
    query_weight,
    out_weight,
):
    devices = lax.axis_size("sample")
    groups = lax.axis_size("groups")
    own_index = lax.axis_index("sample")
    first = lax.axis_index("groups") % 2 == 0
    deep = devices // LINE
    own_a, own_b, own_c = own_index // LINE, own_index // 2 % 2, own_index % 2
    along_ring, along_z, along_y, along_x, in_chip = mover(groups, devices)
    row_count = prompt_states.shape[0]
    chip_rows = 2 * row_count
    pages_here = row_count // PAGE
    heads_here = query_weight.shape[1] // HEAD_DIM
    total_pages = page_table.shape[0]
    prompts = total_pages // PROMPT_PAGES
    samples = sample_order.shape[0]
    steps = 2 * samples
    group_size = samples // prompts
    own_kv = own_index * heads_here // GQA
    wide_states = step_states.reshape(steps, D)
    rows = heads_here * steps
    width = key_weight.shape[0]
    half = key_weight.shape[1] // 2
    kv_places = jnp.where(first, 0, KV_HEADS // 2) + jnp.arange(KV_HEADS, dtype=jnp.int32)
    kv_places = kv_places % KV_HEADS

    order = ring_order(deep)

    def by_place(table):
        return sum(jnp.where(own_a == a, table[a], 0) for a in range(deep))

    own_turn = by_place([order.index(a) for a in range(deep)])

    def block(place_z, flip, core):
        return place_z * LINE + (own_b ^ flip) * 2 + core

    def behind(k):
        return by_place([order[(order.index(a) - k) % deep] for a in range(deep)])

    def halves(weight):
        low, high = weight[:, :half], weight[:, half:]
        return jnp.where(first, low, high), jnp.where(first, high, low)

    key_mine, key_other = halves(key_weight)
    value_mine, value_other = halves(value_weight)

    step_place = PROMPT_PAGES * PAGE + jnp.arange(2, dtype=jnp.int32)
    step_tables = tuple(t[:, None, :] for t in rope_tables(step_place))
    queries = jnp.dot(wide_states, query_weight, preferred_element_type=jnp.float32)
    queries = queries.reshape(2, samples, heads_here, HEAD_DIM).transpose(2, 0, 1, 3)
    queries = turn(queries, step_tables).astype(jnp.bfloat16)
    flat_queries = queries.reshape(rows, HEAD_DIM)

    places = [(k, flip) for k in range(deep) for flip in (0, 1)]
    own_blocks = jnp.stack([block(behind(k), flip, own_c) for k, flip in places])
    done = {}

    def send(move, value, turn_at):
        if turn_at:
            value = after(value, done[turn_at - 2] if turn_at > 1 else flat_queries)
        done.setdefault(turn_at, []).append(move(value))
        return done[turn_at][-1]

    key_z, key_y = {0: key_mine}, {}
    key_full = {0: jnp.concatenate([key_mine, key_other], axis=1)}
    value_pairs, other_pairs = {}, {}
    for r in range(2 * deep - 1):
        late = r - deep + 2
        if r + 1 < deep:
            key_z[r + 1] = send(along_ring, key_z[r], r)
        elif late < deep:
            value_pairs[late] = send(along_ring, value_pairs[late - 1], r)
        if r == 0:
            value_y = send(along_y, value_mine, r)
        elif r == 1:
            sent_blocks = jnp.stack([block(behind(k), flip, 1 - own_c) for k, flip in places])
            sent = pick(prompt_states, after(sent_blocks, done[0]), width)
            got = in_chip(sent)
            key_y[0] = send(
                along_y,
                jnp.concatenate([key_full[0], flat_queries.reshape(-1, key_full[0].shape[1])]),
                r,
            )
            query_pair = jnp.stack([flat_queries, key_y[0][width:].reshape(rows, HEAD_DIM)])
            value_pairs[0] = jnp.concatenate([value_mine, value_y, query_pair.reshape(-1, half)])
        elif r == 2:
            done[r].append(got)
        if 0 < r < deep:
            key_full[r] = jnp.concatenate([key_z[r], send(along_x, key_z[r], r)], axis=1)
        elif r:
            other_pairs[late - 1] = send(along_x, value_pairs[late - 1][: 2 * width], r)
        if r == deep - 1:
            other_pairs[0] = jnp.concatenate([value_other, send(along_x, value_y, r)])
        if 0 < late < deep:
            key_y[late] = send(along_y, key_full[late], r)
    ring = [
        value_pairs[(deep - j) % deep][2 * width :].reshape(query_pair.shape) for j in range(deep)
    ]
    line = lax.dynamic_slice_in_dim(jnp.stack(ring + ring), deep - own_turn, deep)
    line = jnp.stack([line[order.index(a)] for a in range(deep)])
    all_queries = jnp.stack([line, in_chip(line)], axis=1)
    by_owner = (deep, 2, 2, rows)
    all_queries = all_queries.reshape(KV_HEADS, -1, HEAD_DIM)

    own_pages = jnp.concatenate(
        [
            holder * pages_here + jnp.arange(pages_here, dtype=jnp.int32)
            for holder in (own_index, own_index ^ 1)
        ]
    )
    slots = jnp.sum(
        jnp.where(
            page_table[None, :] == own_pages[:, None],
            jnp.arange(total_pages, dtype=jnp.int32)[None, :],
            0,
        ),
        axis=1,
    )
    positions = (slots % PROMPT_PAGES * PAGE)[:, None] + jnp.arange(PAGE, dtype=jnp.int32)[None, :]
    cosine, sine_part = rope_tables(positions.reshape(chip_rows))
    cosine = jnp.concatenate([cosine, cosine], axis=1)
    sine_part = jnp.concatenate([-sine_part, sine_part], axis=1)

    def pieces_of(k_range, key):
        if key:
            return [[((key_y if flip else key_full)[k], 0)] for k in k_range for flip in (0, 1)]
        return [
            [(value_pairs[k], flip * width), (other_pairs[k], flip * width)]
            for k in k_range
            for flip in (0, 1)
        ]

    def project_all(key, ready):
        split = 2 * (deep - 1)
        early = project(
            prompt_states, wide_states, got, own_blocks[:split], 0,
            pieces_of(range(deep - 1), key), None,
        )
        return project(
            prompt_states, wide_states, got, after(own_blocks[split:], ready), split,
            pieces_of([deep - 1], key), early,
        )

    key_sum = project_all(True, got)
    key_back = in_chip(key_sum)
    own_place = lax.dynamic_index_in_dim(kv_places, own_kv, 0, False) * HEAD_DIM

    def own_head(sums):
        return lax.dynamic_slice_in_dim(sums, own_place, HEAD_DIM, 1).reshape(2, samples, HEAD_DIM)

    new_keys = own_head(key_sum[chip_rows:]) + own_head(key_back[chip_rows:])
    new_keys = turn(new_keys, step_tables).astype(jnp.bfloat16)
    masks = (None, None)
    if prompts > 1:
        token_prompt = jnp.repeat(slots // PROMPT_PAGES, PAGE)
        row_prompt = jnp.tile(sample_order // group_size, all_queries.shape[1] // samples)
        masks = (token_prompt[:, None], row_prompt[None, :])
    weights, top, total = attend(
        kv_places, all_queries, key_sum, key_back, cosine, sine_part, *masks
    )

    stats = jnp.stack([top.reshape(by_owner), total.reshape(by_owner)])
    stats = jnp.stack([stats, along_y(stats)[:, :, :, ::-1]])
    stats = jnp.concatenate([stats] + [along_z(stats, k) for k in range(1, deep)])
    prefix_top = jnp.max(stats[:, 0], axis=0)
    prefix_total = jnp.sum(jnp.exp(stats[:, 0] - prefix_top) * stats[:, 1], axis=0)
    factor = jnp.exp(top.reshape(by_owner) - prefix_top)[:, 0]
    prefix_top = lax.dynamic_index_in_dim(prefix_top, own_a, 0, False)[0, 0]
    prefix_total = lax.dynamic_index_in_dim(prefix_total, own_a, 0, False)[0, 0]

    value_sum = project_all(False, weights)
    step_values = own_head(value_sum[chip_rows:])
    step_back = lax.dynamic_slice_in_dim(
        in_chip(value_sum[chip_rows:]), own_place, HEAD_DIM, 1
    ).reshape(step_values.shape)
    new_values = (step_values + step_back).astype(jnp.bfloat16)
    partial = apply_weights(kv_places, weights, value_sum)
    partial = partial.reshape(by_owner + (HEAD_DIM,))

    def narrow(value):
        return value.astype(jnp.bfloat16)

    def wide(value):
        return value.astype(jnp.float32)

    partial = wide(partial[:, 0]) + wide(in_chip(partial[:, 1]))
    partial = narrow(partial * factor[..., None])
    partial = narrow(wide(partial[:, 0]) + wide(along_y(partial[:, 1])))
    prefix_sum = wide(lax.dynamic_index_in_dim(partial, own_a, 0, False))
    for k in range(1, deep):
        piece = lax.dynamic_index_in_dim(partial, (own_a + k) % deep, 0, False)
        prefix_sum = prefix_sum + wide(along_z(piece, k))

    by_head = (heads_here, 2, samples)
    head_out = finish_heads(
        prefix_top.reshape(by_head).swapaxes(0, 1),
        prefix_total.reshape(by_head).swapaxes(0, 1),
        prefix_sum.reshape(by_head + (HEAD_DIM,)).swapaxes(0, 1),
        queries.swapaxes(0, 1),
        new_keys[:, None],
        new_values[:, None],
    )
    flat_heads = head_out.transpose(0, 2, 1, 3).reshape(steps, heads_here * HEAD_DIM)

    out_width = out_weight.shape[1] // devices
    out_blocks = jnp.stack(
        [
            block((own_a + k) % deep, flip, own_c ^ turned)
            for turned in (0, 1)
            for flip in (0, 1)
            for k in range(deep)
        ]
    )
    terms = out_project(out_blocks, flat_heads, out_weight, out_width)
    for move in (in_chip, along_y):
        share = terms.shape[1] // 2
        terms = narrow(wide(terms[:, :share]) + wide(move(terms[:, share:])))
    attn_out = wide(terms[:, :out_width])
    for k in range(1, deep):
        attn_out = attn_out + wide(along_z(terms[:, k * out_width : (k + 1) * out_width], k))
    return narrow(attn_out).reshape(2, samples, -1)


def solution(mesh):
    in_specs = (
        P(("groups", "sample"), None),
        P("groups"),
        P(None, "groups", None),
        P("groups"),
        P("sample", None),
        P("sample", None),
        P(None, "sample"),
        P("sample", None),
    )
    out_specs = P(None, "groups", "sample")
    return jax.shard_map(
        on_device, mesh=mesh, in_specs=in_specs, out_specs=out_specs, check_vma=False
    )
```

```python
import jax
import jax.numpy as jnp
from jax import lax
from jax.experimental import pallas as pl
from jax.experimental.pallas import tpu as pltpu
from jax.sharding import PartitionSpec as P

D = 8192
HEAD_DIM = 128
KV_HEADS = 4
GQA = 8
PAGE = 128
PROMPT_PAGES = 64
LINE = 4

rope_base = 1000000.0


def rope_tables(position):
    half_dim = HEAD_DIM // 2
    frequency = rope_base ** (-jnp.arange(half_dim, dtype=jnp.float32) * 2.0 / HEAD_DIM)
    angles = position.astype(jnp.float32)[..., None] * frequency
    return jnp.cos(angles), jnp.sin(angles)


def turn(vector, tables):
    cosine, sine_part = tables
    half_dim = HEAD_DIM // 2
    first_half = vector[..., :half_dim]
    second_half = vector[..., half_dim:]
    return jnp.concatenate(
        [
            first_half * cosine - second_half * sine_part,
            second_half * cosine + first_half * sine_part,
        ],
        axis=-1,
    )


def finish_heads(prefix_top, prefix_total, prefix_sum, queries, new_keys, new_values):
    score_scale = queries.shape[-1] ** (-0.5)
    query_wide = queries.astype(jnp.float32)
    key_wide = new_keys.astype(jnp.float32)
    value_wide = new_values.astype(jnp.float32)
    own_score = jnp.sum(query_wide * key_wide, axis=-1) * score_scale
    back_score = jnp.sum(query_wide[1] * key_wide[0], axis=-1) * score_scale
    first_high = jnp.maximum(prefix_top[0], own_score[0])
    first_old = jnp.exp(prefix_top[0] - first_high)
    first_own = jnp.exp(own_score[0] - first_high)
    first_out = (first_old[..., None] * prefix_sum[0] + first_own[..., None] * value_wide[0]) / (
        first_old * prefix_total[0] + first_own
    )[..., None]
    second_high = jnp.maximum(jnp.maximum(prefix_top[1], own_score[1]), back_score)
    second_old = jnp.exp(prefix_top[1] - second_high)
    second_back = jnp.exp(back_score - second_high)
    second_own = jnp.exp(own_score[1] - second_high)
    second_num = (
        second_old[..., None] * prefix_sum[1]
        + second_back[..., None] * value_wide[0]
        + second_own[..., None] * value_wide[1]
    )
    second_out = second_num / (second_old * prefix_total[1] + second_back + second_own)[..., None]
    return jnp.stack([first_out, second_out]).astype(jnp.bfloat16)


def ring_order(deep):
    return [*range(0, deep, 2), *range(deep - 1 - deep % 2, 0, -2)]


def mover(groups, devices):
    deep = devices // LINE
    order = ring_order(deep)

    def move(value, step):
        pairs = []
        for g in range(groups):
            for s in range(devices):
                a, b, c = s // LINE, s // 2 % 2, s % 2
                to_g, to_a, to_b, to_c = step(g, a, b, c)
                to_s = (to_a % deep) * LINE + to_b * 2 + to_c
                pairs.append((g * devices + s, to_g * devices + to_s))
        return lax.ppermute(value, ("groups", "sample"), pairs)

    def next_on_ring(a):
        return order[(order.index(a) + 1) % deep]

    along_ring = lambda v: move(v, lambda g, a, b, c: (g, next_on_ring(a), b, c))
    along_z = lambda v, k: move(v, lambda g, a, b, c: (g, a + k, b, c))
    along_y = lambda v: move(v, lambda g, a, b, c: (g, a, 1 - b, c))
    along_x = lambda v: move(v, lambda g, a, b, c: (g ^ 1, a, b, c))
    in_chip = lambda v: move(v, lambda g, a, b, c: (g, a, b, 1 - c))
    return along_ring, along_z, along_y, along_x, in_chip


def after(value, done):
    return lax.optimization_barrier((value, done))[0]


MIB = 1024 * 1024


def pick(source, blocks, width):
    count = blocks.shape[0]
    rows = source.shape[0]

    def body(block_ref, source_ref, out_ref, sems):
        copies = []
        for i in range(count):
            start = pl.multiple_of(block_ref[i] * width, width)
            copies.append(
                pltpu.make_async_copy(
                    source_ref.at[:, pl.ds(start, width)],
                    out_ref.at[:, pl.ds(i * width, width)],
                    sems.at[i],
                )
            )
            copies[-1].start()
        for copy in copies:
            copy.wait()

    return pl.pallas_call(
        body,
        in_specs=[pl.BlockSpec(memory_space=pltpu.SMEM), pl.BlockSpec(memory_space=pltpu.HBM)],
        out_specs=pl.BlockSpec(memory_space=pltpu.VMEM),
        out_shape=jax.ShapeDtypeStruct((rows, count * width), source.dtype),
        scratch_shapes=[pltpu.SemaphoreType.DMA((count,))],
        compiler_params=pltpu.CompilerParams(vmem_limit_bytes=57 * MIB),
        cost_estimate=pl.CostEstimate(
            flops=0, bytes_accessed=4 * rows * count * width, transcendentals=0
        ),
    )(blocks, source)


def project_queries(steps, weight, cosine, sine):
    count, depth = steps.shape
    parts = 8
    piece = depth // parts

    def body(step_ref, weight_ref, cosine_ref, sine_ref, out_ref, held, sems):
        copies = []
        for i in range(parts):
            copies.append(
                pltpu.make_async_copy(
                    weight_ref.at[pl.ds(i * piece, piece), :], held.at[i], sems.at[i]
                )
            )
            copies[-1].start()
        total = None
        for i in range(parts):
            copies[i].wait()
            product = jnp.dot(
                step_ref[:, i * piece : (i + 1) * piece],
                held[i],
                preferred_element_type=jnp.float32,
            )
            total = product if total is None else total + product
        for start in range(0, weight.shape[1], HEAD_DIM):
            head = total[:, start : start + HEAD_DIM]
            turned = head * cosine_ref[...] + pltpu.roll(head, HEAD_DIM // 2, 1) * sine_ref[...]
            out_ref[:, start : start + HEAD_DIM] = turned.astype(jnp.bfloat16)

    whole = pl.BlockSpec(memory_space=pltpu.VMEM)
    return pl.pallas_call(
        body,
        in_specs=[whole, pl.BlockSpec(memory_space=pltpu.HBM), whole, whole],
        out_specs=whole,
        out_shape=jax.ShapeDtypeStruct((count, weight.shape[1]), jnp.bfloat16),
        scratch_shapes=[
            pltpu.VMEM((parts, piece, weight.shape[1]), weight.dtype),
            pltpu.SemaphoreType.DMA((parts,)),
        ],
        compiler_params=pltpu.CompilerParams(vmem_limit_bytes=10 * MIB),
        cost_estimate=pl.CostEstimate(
            flops=2 * count * weight.size, bytes_accessed=2 * weight.size, transcendentals=0
        ),
    )(steps, weight, cosine, sine)


def collect(arrays, first, height):
    columns = arrays[0].shape[1]

    def body(*refs):
        out_ref, sems = refs[-2:]
        copies = [
            pltpu.make_async_copy(ref.at[pl.ds(first, height), :], out_ref.at[i], sems.at[i])
            for i, ref in enumerate(refs[:-2])
        ]
        for copy in copies:
            copy.start()
        for copy in copies:
            copy.wait()

    return pl.pallas_call(
        body,
        in_specs=[pl.BlockSpec(memory_space=pl.ANY)] * len(arrays),
        out_specs=pl.BlockSpec(memory_space=pltpu.VMEM),
        out_shape=jax.ShapeDtypeStruct((len(arrays), height, columns), arrays[0].dtype),
        scratch_shapes=[pltpu.SemaphoreType.DMA((len(arrays),))],
        compiler_params=pltpu.CompilerParams(vmem_limit_bytes=4 * MIB),
        cost_estimate=pl.CostEstimate(
            flops=0, bytes_accessed=4 * len(arrays) * height * columns, transcendentals=0
        ),
    )(*arrays)


def project(prompt, steps, got, width, blocks, begin, pieces, acc):
    arrays = []
    for piece in pieces:
        for array, _ in piece:
            if not any(array is held for held in arrays):
                arrays.append(array)
    count = len(pieces)
    columns = sum(array.shape[1] for array, _ in pieces[0])
    row_count, step_count = prompt.shape[0], steps.shape[0]
    height = 2 * row_count + step_count
    extra = [] if acc is None else [acc]

    def body(block_ref, prompt_ref, got_ref, step_ref, *refs):
        weight_refs = refs[: len(arrays)]
        out_ref, left, held, sems = refs[-4:]
        copies = []
        for i, piece in enumerate(pieces):
            start = pl.multiple_of(block_ref[i] * width, width)
            column = pl.ds(start, width)
            group = [
                pltpu.make_async_copy(
                    prompt_ref.at[:, column], left.at[i, pl.ds(0, row_count), :], sems.at[i, 0]
                ),
                pltpu.make_async_copy(
                    got_ref.at[:, pl.ds((begin + i) * width, width)],
                    left.at[i, pl.ds(row_count, row_count), :],
                    sems.at[i, 1],
                ),
                pltpu.make_async_copy(
                    step_ref.at[:, column],
                    left.at[i, pl.ds(2 * row_count, step_count), :],
                    sems.at[i, 2],
                ),
            ]
            side = 0
            for j, (array, first) in enumerate(piece):
                ref = weight_refs[[array is other for other in arrays].index(True)]
                group.append(
                    pltpu.make_async_copy(
                        ref.at[pl.ds(first, width), :],
                        held.at[i, :, pl.ds(side, array.shape[1])],
                        sems.at[i, 3 + j],
                    )
                )
                side += array.shape[1]
            for copy in group:
                copy.start()
            copies.append(group)
        for i, group in enumerate(copies):
            for copy in group:
                copy.wait()
            product = jnp.dot(left[i], held[i], preferred_element_type=jnp.float32)
            if i:
                out_ref[...] += product
            elif acc is not None:
                out_ref[...] = refs[len(arrays)][...] + product
            else:
                out_ref[...] = product

    anywhere = pl.BlockSpec(memory_space=pl.ANY)
    whole = pl.BlockSpec(memory_space=pltpu.VMEM)
    return pl.pallas_call(
        body,
        in_specs=[pl.BlockSpec(memory_space=pltpu.SMEM), pl.BlockSpec(memory_space=pltpu.HBM)]
        + [anywhere] * (2 + len(arrays))
        + [whole] * len(extra),
        out_specs=whole,
        out_shape=jax.ShapeDtypeStruct((height, columns), jnp.float32),
        scratch_shapes=[
            pltpu.VMEM((count, height, width), jnp.bfloat16),
            pltpu.VMEM((count, width, columns), jnp.bfloat16),
            pltpu.SemaphoreType.DMA((count, 5)),
        ],
        compiler_params=pltpu.CompilerParams(vmem_limit_bytes=57 * MIB),
        cost_estimate=pl.CostEstimate(
            flops=2 * height * width * count * columns,
            bytes_accessed=2 * height * width * count + 8 * height * columns,
            transcendentals=0,
        ),
    )(blocks, prompt, got, steps, *arrays, *extra)


def attend(places, turns, queries, own, other, cosine, sine, token_prompt, row_prompt):
    kv_heads = places.shape[0]
    deep, packed, lanes = queries[0].shape
    share = deep // kv_heads
    count = 2 * share * packed * lanes // HEAD_DIM
    tokens = cosine.shape[0]
    half = tokens // 2
    height = own.shape[0]
    masks = [] if token_prompt is None else [token_prompt, row_prompt]

    def body(place_ref, turn_ref, *refs):
        query_refs = refs[: 2 * share]
        own_ref, other_ref, cosine_ref, sine_ref = refs[2 * share : 2 * share + 4]
        mask_refs = refs[2 * share + 4 : -3]
        weight_ref, top_ref, total_ref = refs[-3:]
        keys = jnp.concatenate(
            [
                own_ref[:half, :] + other_ref[half:tokens, :],
                own_ref[half:tokens, :] + other_ref[:half, :],
            ],
            axis=0,
        )
        swapped = pltpu.roll(keys, HEAD_DIM // 2, 1)
        wide_cosine = jnp.concatenate([cosine_ref[...], cosine_ref[...]], axis=1)
        wide_sine = jnp.concatenate([-sine_ref[...], sine_ref[...]], axis=1)
        keys = (keys * wide_cosine + swapped * wide_sine).astype(jnp.bfloat16)
        unpacked = []
        for ref in query_refs:
            for low in range(0, packed, packed // 2):
                for left in range(0, lanes, HEAD_DIM):
                    unpacked.append(ref[0, low : low + packed // 2, left : left + HEAD_DIM])
        scores = lax.dot_general(
            keys,
            jnp.concatenate(unpacked, axis=0),
            (((1,), (1,)), ((), ())),
            preferred_element_type=jnp.float32,
        ) * (HEAD_DIM**-0.5)
        if masks:
            scores = jnp.where(mask_refs[0][...] == mask_refs[1][...], scores, -1e30)
        top = jnp.max(scores, axis=0, keepdims=True)
        weights = jnp.exp(scores - top)
        top_ref[0] = top
        total_ref[0] = jnp.sum(weights, axis=0, keepdims=True)
        weight_ref[0] = weights.astype(jnp.bfloat16)

    def query_spec(part):
        return pl.BlockSpec(
            (1, packed, lanes), lambda j, place, turn: (turn[j * share + part], 0, 0)
        )

    row = jax.ShapeDtypeStruct((kv_heads, 1, count), jnp.float32)
    row_spec = pl.BlockSpec((1, 1, count), lambda j, place, turn: (j, 0, 0))
    fixed = lambda j, place, turn: (0, 0)
    column = pl.BlockSpec((height, HEAD_DIM), lambda j, place, turn: (0, place[j]))
    return pl.pallas_call(
        body,
        grid_spec=pltpu.PrefetchScalarGridSpec(
            num_scalar_prefetch=2,
            grid=(kv_heads,),
            in_specs=[query_spec(part) for part in range(share) for _ in queries]
            + [column, column]
            + [pl.BlockSpec(cosine.shape, fixed)] * 2
            + [pl.BlockSpec(mask.shape, fixed) for mask in masks],
            out_specs=[
                pl.BlockSpec((1, tokens, count), lambda j, place, turn: (j, 0, 0)),
                row_spec,
                row_spec,
            ],
        ),
        out_shape=[
            jax.ShapeDtypeStruct((kv_heads, tokens, count), jnp.bfloat16),
            row,
            row,
        ],
        compiler_params=pltpu.CompilerParams(vmem_limit_bytes=20 * MIB),
        cost_estimate=pl.CostEstimate(
            flops=2 * kv_heads * tokens * count * HEAD_DIM,
            bytes_accessed=8 * height * kv_heads * HEAD_DIM + 2 * kv_heads * tokens * count,
            transcendentals=kv_heads * tokens * count,
        ),
    )(places, turns, *([*queries] * share), own, other, cosine, sine, *masks)


def apply_weights(places, weights, values):
    kv_heads, tokens, count = weights.shape

    def body(place_ref, weight_ref, value_ref, out_ref):
        summed = lax.dot_general(
            value_ref[:tokens, :].astype(jnp.bfloat16),
            weight_ref[0],
            (((0,), (0,)), ((), ())),
            preferred_element_type=jnp.float32,
        )
        out_ref[0] = summed.T.astype(jnp.bfloat16)

    return pl.pallas_call(
        body,
        grid_spec=pltpu.PrefetchScalarGridSpec(
            num_scalar_prefetch=1,
            grid=(kv_heads,),
            in_specs=[
                pl.BlockSpec((1, tokens, count), lambda j, ref: (j, 0, 0)),
                pl.BlockSpec((values.shape[0], HEAD_DIM), lambda j, ref: (0, ref[j])),
            ],
            out_specs=pl.BlockSpec((1, count, HEAD_DIM), lambda j, ref: (j, 0, 0)),
        ),
        out_shape=jax.ShapeDtypeStruct((kv_heads, count, HEAD_DIM), jnp.bfloat16),
        compiler_params=pltpu.CompilerParams(vmem_limit_bytes=20 * MIB),
        cost_estimate=pl.CostEstimate(
            flops=2 * kv_heads * tokens * count * HEAD_DIM,
            bytes_accessed=2 * kv_heads * tokens * count,
            transcendentals=0,
        ),
    )(places, weights, values)


def out_project(blocks, heads, weight, width):
    def body(block_ref, head_ref, weight_ref, out_ref):
        for i in range(blocks.shape[0]):
            start = pl.multiple_of(block_ref[i] * width, width)
            out_ref[:, i * width : (i + 1) * width] = jnp.dot(
                head_ref[...], weight_ref[:, pl.ds(start, width)], preferred_element_type=jnp.float32
            ).astype(jnp.bfloat16)

    whole = pl.BlockSpec(memory_space=pltpu.VMEM)
    shape = (heads.shape[0], weight.shape[1])
    return pl.pallas_call(
        body,
        in_specs=[pl.BlockSpec(memory_space=pltpu.SMEM), whole, whole],
        out_specs=whole,
        out_shape=jax.ShapeDtypeStruct(shape, jnp.bfloat16),
        compiler_params=pltpu.CompilerParams(vmem_limit_bytes=20 * MIB),
        cost_estimate=pl.CostEstimate(
            flops=2 * heads.shape[1] * shape[0] * shape[1],
            bytes_accessed=2 * (weight.size + heads.size + shape[0] * shape[1]),
            transcendentals=0,
        ),
    )(blocks, heads, weight)


def on_device(
    prompt_states,
    page_table,
    step_states,
    sample_order,
    key_weight,
    value_weight,
    query_weight,
    out_weight,
):
    devices = lax.axis_size("sample")
    groups = lax.axis_size("groups")
    own_index = lax.axis_index("sample")
    first = lax.axis_index("groups") % 2 == 0
    deep = devices // LINE
    own_a, own_b, own_c = own_index // LINE, own_index // 2 % 2, own_index % 2
    along_ring, along_z, along_y, along_x, in_chip = mover(groups, devices)
    row_count = prompt_states.shape[0]
    chip_rows = 2 * row_count
    pages_here = row_count // PAGE
    heads_here = query_weight.shape[1] // HEAD_DIM
    total_pages = page_table.shape[0]
    prompts = total_pages // PROMPT_PAGES
    samples = sample_order.shape[0]
    steps = 2 * samples
    group_size = samples // prompts
    own_kv = own_index * heads_here // GQA
    wide_states = step_states.reshape(steps, D)
    rows = heads_here * steps
    width = key_weight.shape[0]
    half = key_weight.shape[1] // 2
    kv_places = jnp.where(first, 0, KV_HEADS // 2) + jnp.arange(KV_HEADS, dtype=jnp.int32)
    kv_places = kv_places % KV_HEADS

    order = ring_order(deep)

    def by_place(table):
        return sum(jnp.where(own_a == a, table[a], 0) for a in range(deep))

    own_turn = by_place([order.index(a) for a in range(deep)])

    def block(place_z, flip, core):
        return place_z * LINE + (own_b ^ flip) * 2 + core

    def behind(k):
        return by_place([order[(order.index(a) - k) % deep] for a in range(deep)])

    def halves(weight):
        low, high = weight[:, :half], weight[:, half:]
        return jnp.where(first, low, high), jnp.where(first, high, low)

    key_mine, key_other = halves(key_weight)
    value_mine, value_other = halves(value_weight)

    step_place = PROMPT_PAGES * PAGE + jnp.arange(2, dtype=jnp.int32)
    step_tables = tuple(t[:, None, :] for t in rope_tables(step_place))
    flat_tables = [
        jnp.repeat(jnp.concatenate([sign * table, table], axis=-1)[:, 0], samples, axis=0)
        for sign, table in zip((1, -1), step_tables)
    ]
    queries = project_queries(wide_states, query_weight, *flat_tables)
    packed_queries = jnp.concatenate(
        jnp.split(queries, half // queries.shape[1], axis=0), axis=1
    )
    packed = packed_queries.shape[0]
    queries = queries.reshape(2, samples, heads_here, HEAD_DIM)

    places = [(k, flip) for k in range(deep) for flip in (0, 1)]
    own_blocks = jnp.stack([block(behind(k), flip, own_c) for k, flip in places])
    done = {}

    def send(move, value, turn_at):
        if turn_at > 1:
            value = after(value, done[turn_at - 2])
        done.setdefault(turn_at, []).append(move(value))
        return done[turn_at][-1]

    key_z, key_y = {0: key_mine}, {}
    key_full = {0: jnp.concatenate([key_mine, key_other, packed_queries])}
    value_pairs, other_pairs = {}, {}
    for r in range(2 * deep - 1):
        late = r - deep + 2
        if r + 1 < deep:
            key_z[r + 1] = send(along_ring, key_z[r], r)
        elif late < deep:
            value_pairs[late] = send(along_ring, value_pairs[late - 1], r)
        if r == 0:
            value_y = send(along_y, value_mine, r)
        elif r == 1:
            sent_blocks = jnp.stack([block(behind(k), flip, 1 - own_c) for k, flip in places])
            sent = pick(prompt_states, after(sent_blocks, (done[0], packed_queries)), width)
            got = in_chip(sent)
            key_y[0] = send(along_y, key_full[0], r)
            value_pairs[0] = jnp.concatenate(
                [value_mine, value_y, packed_queries, key_y[0][2 * width :]]
            )
        elif r == 2:
            done[r].append(got)
        if 0 < r < deep:
            key_full[r] = jnp.concatenate([key_z[r], send(along_x, key_z[r], r)])
        elif r:
            other_pairs[late - 1] = send(along_x, value_pairs[late - 1], r)
        if r == deep - 1:
            other_pairs[0] = jnp.concatenate([value_other, send(along_x, value_y, r)])
        if 0 < late < deep:
            key_y[late] = send(along_y, key_full[late], r)
    ring_queries = collect([value_pairs[k] for k in range(deep)], 2 * width, 2 * packed)
    ring_queries = [ring_queries, in_chip(ring_queries)]
    query_turns = jnp.stack([(own_turn + deep - order.index(a)) % deep for a in range(deep)])
    by_owner = (deep, 2, 2, rows)

    own_pages = jnp.concatenate(
        [
            holder * pages_here + jnp.arange(pages_here, dtype=jnp.int32)
            for holder in (own_index, own_index ^ 1)
        ]
    )
    slots = jnp.sum(
        jnp.where(
            page_table[None, :] == own_pages[:, None],
            jnp.arange(total_pages, dtype=jnp.int32)[None, :],
            0,
        ),
        axis=1,
    )
    positions = (slots % PROMPT_PAGES * PAGE)[:, None] + jnp.arange(PAGE, dtype=jnp.int32)[None, :]
    cosine, sine_part = rope_tables(positions.reshape(chip_rows))

    def pieces_of(k_range, key):
        if key:
            return [
                [((key_y if flip else key_full)[k], first) for first in (0, width)]
                for k in k_range
                for flip in (0, 1)
            ]
        return [
            [(value_pairs[k], flip * width), (other_pairs[k], flip * width)]
            for k in k_range
            for flip in (0, 1)
        ]

    def project_part(key, k_range, acc, ready):
        low, high = 2 * k_range[0], 2 * k_range[-1] + 2
        return project(
            prompt_states, wide_states, got, width, after(own_blocks[low:high], ready), low,
            pieces_of(k_range, key), acc,
        )

    every = range(deep)
    key_early = project_part(True, every[:-1], None, done[deep])
    value_early = project_part(False, every[:-2], None, (done[deep], key_early))
    key_sum = project_part(True, every[-1:], key_early, (done[deep + 1], value_early))
    key_back = in_chip(key_sum)
    own_place = lax.dynamic_index_in_dim(kv_places, own_kv, 0, False) * HEAD_DIM

    def own_head(sums):
        return lax.dynamic_slice_in_dim(sums, own_place, HEAD_DIM, 1).reshape(2, samples, HEAD_DIM)

    new_keys = own_head(key_sum[chip_rows:]) + own_head(key_back[chip_rows:])
    new_keys = turn(new_keys, step_tables).astype(jnp.bfloat16)
    masks = (None, None)
    if prompts > 1:
        token_prompt = jnp.repeat(slots // PROMPT_PAGES, PAGE)
        row_prompt = jnp.tile(sample_order // group_size, devices // KV_HEADS * rows // samples)
        masks = (token_prompt[:, None], row_prompt[None, :])
    weights, top, total = attend(
        kv_places, query_turns, ring_queries, key_sum, key_back, cosine, sine_part, *masks
    )

    stats = jnp.stack([top.reshape(by_owner), total.reshape(by_owner)])
    stats = jnp.stack([stats, along_y(stats)[:, :, :, ::-1]])
    weights = after(weights, stats)
    stats = jnp.concatenate([stats] + [along_z(stats, k) for k in range(1, deep)])
    prefix_top = jnp.max(stats[:, 0], axis=0)
    prefix_total = jnp.sum(jnp.exp(stats[:, 0] - prefix_top) * stats[:, 1], axis=0)
    factor = jnp.exp(top.reshape(by_owner) - prefix_top)[:, 0]
    prefix_top = lax.dynamic_index_in_dim(prefix_top, own_a, 0, False)[0, 0]
    prefix_total = lax.dynamic_index_in_dim(prefix_total, own_a, 0, False)[0, 0]

    value_sum = project_part(False, every[-2:], value_early, weights)
    step_values = own_head(value_sum[chip_rows:])
    step_back = lax.dynamic_slice_in_dim(
        in_chip(value_sum[chip_rows:]), own_place, HEAD_DIM, 1
    ).reshape(step_values.shape)
    new_values = (step_values + step_back).astype(jnp.bfloat16)
    partial = apply_weights(kv_places, weights, value_sum)
    partial = partial.reshape(by_owner + (HEAD_DIM,))

    def narrow(value):
        return value.astype(jnp.bfloat16)

    def wide(value):
        return value.astype(jnp.float32)

    partial = wide(partial[:, 0]) + wide(in_chip(partial[:, 1]))
    partial = narrow(partial * factor[..., None])
    partial = narrow(wide(partial[:, 0]) + wide(along_y(partial[:, 1])))
    prefix_sum = wide(lax.dynamic_index_in_dim(partial, own_a, 0, False))
    for k in range(1, deep):
        piece = lax.dynamic_index_in_dim(partial, (own_a + k) % deep, 0, False)
        prefix_sum = prefix_sum + wide(along_z(piece, k))

    by_head = (heads_here, 2, samples)
    head_out = finish_heads(
        prefix_top.reshape(by_head).swapaxes(0, 1),
        prefix_total.reshape(by_head).swapaxes(0, 1),
        prefix_sum.reshape(by_head + (HEAD_DIM,)).swapaxes(0, 1),
        queries.transpose(0, 2, 1, 3),
        new_keys[:, None],
        new_values[:, None],
    )
    flat_heads = head_out.transpose(0, 2, 1, 3).reshape(steps, heads_here * HEAD_DIM)

    out_width = out_weight.shape[1] // devices
    out_blocks = jnp.stack(
        [
            block((own_a + k) % deep, flip, own_c ^ turned)
            for turned in (0, 1)
            for flip in (0, 1)
            for k in range(deep)
        ]
    )
    terms = out_project(out_blocks, flat_heads, out_weight, out_width)
    for move in (in_chip, along_y):
        share = terms.shape[1] // 2
        terms = narrow(wide(terms[:, :share]) + wide(move(terms[:, share:])))
    attn_out = wide(terms[:, :out_width])
    for k in range(1, deep):
        attn_out = attn_out + wide(along_z(terms[:, k * out_width : (k + 1) * out_width], k))
    return narrow(attn_out).reshape(2, samples, -1)


def solution(mesh):
    in_specs = (
        P(("groups", "sample"), None),
        P("groups"),
        P(None, "groups", None),
        P("groups"),
        P("sample", None),
        P("sample", None),
        P(None, "sample"),
        P("sample", None),
    )
    out_specs = P(None, "groups", "sample")
    return jax.shard_map(
        on_device, mesh=mesh, in_specs=in_specs, out_specs=out_specs, check_vma=False
    )
```

```python
import jax
import jax.numpy as jnp
from jax import lax
from jax.experimental import pallas as pl
from jax.experimental.pallas import tpu as pltpu
from jax.sharding import PartitionSpec as P

D = 8192
HEAD_DIM = 128
KV_HEADS = 4
GQA = 8
PAGE = 128
PROMPT_PAGES = 64
LINE = 4

rope_base = 1000000.0


def rope_tables(position):
    half_dim = HEAD_DIM // 2
    frequency = rope_base ** (-jnp.arange(half_dim, dtype=jnp.float32) * 2.0 / HEAD_DIM)
    angles = position.astype(jnp.float32)[..., None] * frequency
    return jnp.cos(angles), jnp.sin(angles)


def turn(vector, tables):
    cosine, sine_part = tables
    half_dim = HEAD_DIM // 2
    first_half = vector[..., :half_dim]
    second_half = vector[..., half_dim:]
    return jnp.concatenate(
        [
            first_half * cosine - second_half * sine_part,
            second_half * cosine + first_half * sine_part,
        ],
        axis=-1,
    )


def finish_heads(prefix_top, prefix_total, prefix_sum, queries, new_keys, new_values):
    score_scale = queries.shape[-1] ** (-0.5)
    query_wide = queries.astype(jnp.float32)
    key_wide = new_keys.astype(jnp.float32)
    value_wide = new_values.astype(jnp.float32)
    own_score = jnp.sum(query_wide * key_wide, axis=-1) * score_scale
    back_score = jnp.sum(query_wide[1] * key_wide[0], axis=-1) * score_scale
    first_high = jnp.maximum(prefix_top[0], own_score[0])
    first_old = jnp.exp(prefix_top[0] - first_high)
    first_own = jnp.exp(own_score[0] - first_high)
    first_out = (first_old[..., None] * prefix_sum[0] + first_own[..., None] * value_wide[0]) / (
        first_old * prefix_total[0] + first_own
    )[..., None]
    second_high = jnp.maximum(jnp.maximum(prefix_top[1], own_score[1]), back_score)
    second_old = jnp.exp(prefix_top[1] - second_high)
    second_back = jnp.exp(back_score - second_high)
    second_own = jnp.exp(own_score[1] - second_high)
    second_num = (
        second_old[..., None] * prefix_sum[1]
        + second_back[..., None] * value_wide[0]
        + second_own[..., None] * value_wide[1]
    )
    second_out = second_num / (second_old * prefix_total[1] + second_back + second_own)[..., None]
    return jnp.stack([first_out, second_out]).astype(jnp.bfloat16)


def ring_order(deep):
    return [*range(0, deep, 2), *range(deep - 1 - deep % 2, 0, -2)]


def mover(groups, devices):
    deep = devices // LINE
    order = ring_order(deep)

    def move(value, step):
        pairs = []
        for g in range(groups):
            for s in range(devices):
                a, b, c = s // LINE, s // 2 % 2, s % 2
                to_g, to_a, to_b, to_c = step(g, a, b, c)
                to_s = (to_a % deep) * LINE + to_b * 2 + to_c
                pairs.append((g * devices + s, to_g * devices + to_s))
        return lax.ppermute(value, ("groups", "sample"), pairs)

    def next_on_ring(a):
        return order[(order.index(a) + 1) % deep]

    along_ring = lambda v: move(v, lambda g, a, b, c: (g, next_on_ring(a), b, c))
    along_z = lambda v, k: move(v, lambda g, a, b, c: (g, a + k, b, c))
    along_y = lambda v: move(v, lambda g, a, b, c: (g, a, 1 - b, c))
    along_x = lambda v: move(v, lambda g, a, b, c: (g ^ 1, a, b, c))
    in_chip = lambda v: move(v, lambda g, a, b, c: (g, a, b, 1 - c))
    return along_ring, along_z, along_y, along_x, in_chip


def after(value, done):
    return lax.optimization_barrier((value, done))[0]


MIB = 1024 * 1024
LIGHT = pl.CostEstimate(flops=1, bytes_accessed=1, transcendentals=0)


def pick(source, blocks, width):
    count = blocks.shape[0]
    rows = source.shape[0]

    def body(block_ref, source_ref, out_ref, sems):
        copies = []
        for i in range(count):
            start = pl.multiple_of(block_ref[i] * width, width)
            copies.append(
                pltpu.make_async_copy(
                    source_ref.at[:, pl.ds(start, width)],
                    out_ref.at[:, pl.ds(i * width, width)],
                    sems.at[i],
                )
            )
            copies[-1].start()
        for copy in copies:
            copy.wait()

    return pl.pallas_call(
        body,
        in_specs=[pl.BlockSpec(memory_space=pltpu.SMEM), pl.BlockSpec(memory_space=pltpu.HBM)],
        out_specs=pl.BlockSpec(memory_space=pltpu.VMEM),
        out_shape=jax.ShapeDtypeStruct((rows, count * width), source.dtype),
        scratch_shapes=[pltpu.SemaphoreType.DMA((count,))],
        compiler_params=pltpu.CompilerParams(vmem_limit_bytes=12 * MIB),
        cost_estimate=LIGHT,
    )(blocks, source)


def project_queries(steps, weight, cosine, sine):
    count, depth = steps.shape
    parts = 8
    piece = depth // parts

    def body(step_ref, weight_ref, cosine_ref, sine_ref, out_ref, held, sems):
        copies = []
        for i in range(parts):
            copies.append(
                pltpu.make_async_copy(
                    weight_ref.at[pl.ds(i * piece, piece), :], held.at[i], sems.at[i]
                )
            )
            copies[-1].start()
        total = None
        for i in range(parts):
            copies[i].wait()
            product = jnp.dot(
                step_ref[:, i * piece : (i + 1) * piece],
                held[i],
                preferred_element_type=jnp.float32,
            )
            total = product if total is None else total + product
        for start in range(0, weight.shape[1], HEAD_DIM):
            head = total[:, start : start + HEAD_DIM]
            turned = head * cosine_ref[...] + pltpu.roll(head, HEAD_DIM // 2, 1) * sine_ref[...]
            out_ref[:, start : start + HEAD_DIM] = turned.astype(jnp.bfloat16)

    whole = pl.BlockSpec(memory_space=pltpu.VMEM)
    return pl.pallas_call(
        body,
        in_specs=[whole, pl.BlockSpec(memory_space=pltpu.HBM), whole, whole],
        out_specs=whole,
        out_shape=jax.ShapeDtypeStruct((count, weight.shape[1]), jnp.bfloat16),
        scratch_shapes=[
            pltpu.VMEM((parts, piece, weight.shape[1]), weight.dtype),
            pltpu.SemaphoreType.DMA((parts,)),
        ],
        compiler_params=pltpu.CompilerParams(vmem_limit_bytes=10 * MIB),
        cost_estimate=LIGHT,
    )(steps, weight, cosine, sine)


def collect(arrays, first, height):
    columns = arrays[0].shape[1]

    def body(*refs):
        out_ref, sems = refs[-2:]
        copies = [
            pltpu.make_async_copy(ref.at[pl.ds(first, height), :], out_ref.at[i], sems.at[i])
            for i, ref in enumerate(refs[:-2])
        ]
        for copy in copies:
            copy.start()
        for copy in copies:
            copy.wait()

    return pl.pallas_call(
        body,
        in_specs=[pl.BlockSpec(memory_space=pl.ANY)] * len(arrays),
        out_specs=pl.BlockSpec(memory_space=pltpu.VMEM),
        out_shape=jax.ShapeDtypeStruct((len(arrays), height, columns), arrays[0].dtype),
        scratch_shapes=[pltpu.SemaphoreType.DMA((len(arrays),))],
        compiler_params=pltpu.CompilerParams(vmem_limit_bytes=4 * MIB),
        cost_estimate=LIGHT,
    )(*arrays)


def assemble(prompt, steps, got, blocks, width):
    count = blocks.shape[0]
    row_count, step_count = prompt.shape[0], steps.shape[0]
    height = 2 * row_count + step_count

    def body(block_ref, prompt_ref, got_ref, step_ref, out_ref, sems):
        copies = []
        for i in range(count):
            column = pl.ds(pl.multiple_of(block_ref[i] * width, width), width)
            for j, (source, start, rows) in enumerate(
                (
                    (prompt_ref.at[:, column], 0, row_count),
                    (got_ref.at[:, pl.ds(i * width, width)], row_count, row_count),
                    (step_ref.at[:, column], 2 * row_count, step_count),
                )
            ):
                copies.append(
                    pltpu.make_async_copy(
                        source, out_ref.at[i, pl.ds(start, rows), :], sems.at[i, j]
                    )
                )
                copies[-1].start()
        for copy in copies:
            copy.wait()

    anywhere = pl.BlockSpec(memory_space=pl.ANY)
    return pl.pallas_call(
        body,
        in_specs=[pl.BlockSpec(memory_space=pltpu.SMEM)] + [anywhere] * 3,
        out_specs=pl.BlockSpec(memory_space=pltpu.VMEM),
        out_shape=jax.ShapeDtypeStruct((count, height, width), prompt.dtype),
        scratch_shapes=[pltpu.SemaphoreType.DMA((count, 3))],
        compiler_params=pltpu.CompilerParams(vmem_limit_bytes=16 * MIB),
        cost_estimate=LIGHT,
    )(blocks, prompt, got, steps)


def project(left, which, pieces, acc):
    arrays = []
    for piece in pieces:
        for array, _ in piece:
            if not any(array is held for held in arrays):
                arrays.append(array)
    _, height, width = left.shape
    columns = sum(array.shape[1] for array, _ in pieces[0])
    extra = [] if acc is None else [acc]

    def body(left_ref, *refs):
        out_ref = refs[-1]
        for i, piece in enumerate(pieces):
            side = 0
            for array, first in piece:
                ref = refs[[array is other for other in arrays].index(True)]
                place = slice(side, side + array.shape[1])
                product = jnp.dot(
                    left_ref[which[i]],
                    ref[first : first + width, :],
                    preferred_element_type=jnp.float32,
                )
                if i:
                    out_ref[:, place] += product
                elif extra:
                    out_ref[:, place] = refs[len(arrays)][:, place] + product
                else:
                    out_ref[:, place] = product
                side += array.shape[1]

    whole = pl.BlockSpec(memory_space=pltpu.VMEM)
    return pl.pallas_call(
        body,
        in_specs=[whole] * (1 + len(arrays) + len(extra)),
        out_specs=whole,
        out_shape=jax.ShapeDtypeStruct((height, columns), jnp.float32),
        compiler_params=pltpu.CompilerParams(vmem_limit_bytes=28 * MIB),
        cost_estimate=LIGHT,
    )(left, *arrays, *extra)


def attend(places, turns, queries, own, other, cosine, sine, token_prompt, row_prompt):
    kv_heads = places.shape[0]
    deep, packed, lanes = queries[0].shape
    share = deep // kv_heads
    count = 2 * share * packed * lanes // HEAD_DIM
    tokens = cosine.shape[0]
    half = tokens // 2
    height = own.shape[0]
    masks = [] if token_prompt is None else [token_prompt, row_prompt]

    def body(place_ref, turn_ref, *refs):
        query_refs = refs[: 2 * share]
        own_ref, other_ref, cosine_ref, sine_ref = refs[2 * share : 2 * share + 4]
        mask_refs = refs[2 * share + 4 : -3]
        weight_ref, top_ref, total_ref = refs[-3:]
        keys = jnp.concatenate(
            [
                own_ref[:half, :] + other_ref[half:tokens, :],
                own_ref[half:tokens, :] + other_ref[:half, :],
            ],
            axis=0,
        )
        swapped = pltpu.roll(keys, HEAD_DIM // 2, 1)
        wide_cosine = jnp.concatenate([cosine_ref[...], cosine_ref[...]], axis=1)
        wide_sine = jnp.concatenate([-sine_ref[...], sine_ref[...]], axis=1)
        keys = (keys * wide_cosine + swapped * wide_sine).astype(jnp.bfloat16)
        unpacked = []
        for ref in query_refs:
            for low in range(0, packed, packed // 2):
                for left in range(0, lanes, HEAD_DIM):
                    unpacked.append(ref[0, low : low + packed // 2, left : left + HEAD_DIM])
        scores = lax.dot_general(
            keys,
            jnp.concatenate(unpacked, axis=0),
            (((1,), (1,)), ((), ())),
            preferred_element_type=jnp.float32,
        ) * (HEAD_DIM**-0.5)
        if masks:
            scores = jnp.where(mask_refs[0][...] == mask_refs[1][...], scores, -1e30)
        top = jnp.max(scores, axis=0, keepdims=True)
        weights = jnp.exp(scores - top)
        top_ref[0] = top
        total_ref[0] = jnp.sum(weights, axis=0, keepdims=True)
        weight_ref[0] = weights.astype(jnp.bfloat16)

    def query_spec(part):
        return pl.BlockSpec(
            (1, packed, lanes), lambda j, place, turn: (turn[j * share + part], 0, 0)
        )

    row = jax.ShapeDtypeStruct((kv_heads, 1, count), jnp.float32)
    row_spec = pl.BlockSpec((1, 1, count), lambda j, place, turn: (j, 0, 0))
    fixed = lambda j, place, turn: (0, 0)
    column = pl.BlockSpec((height, HEAD_DIM), lambda j, place, turn: (0, place[j]))
    return pl.pallas_call(
        body,
        grid_spec=pltpu.PrefetchScalarGridSpec(
            num_scalar_prefetch=2,
            grid=(kv_heads,),
            in_specs=[query_spec(part) for part in range(share) for _ in queries]
            + [column, column]
            + [pl.BlockSpec(cosine.shape, fixed)] * 2
            + [pl.BlockSpec(mask.shape, fixed) for mask in masks],
            out_specs=[
                pl.BlockSpec((1, tokens, count), lambda j, place, turn: (j, 0, 0)),
                row_spec,
                row_spec,
            ],
        ),
        out_shape=[
            jax.ShapeDtypeStruct((kv_heads, tokens, count), jnp.bfloat16),
            row,
            row,
        ],
        compiler_params=pltpu.CompilerParams(vmem_limit_bytes=20 * MIB),
        cost_estimate=LIGHT,
    )(places, turns, *([*queries] * share), own, other, cosine, sine, *masks)


def apply_weights(places, weights, values):
    kv_heads, tokens, count = weights.shape

    def body(place_ref, weight_ref, value_ref, out_ref):
        summed = lax.dot_general(
            value_ref[:tokens, :].astype(jnp.bfloat16),
            weight_ref[0],
            (((0,), (0,)), ((), ())),
            preferred_element_type=jnp.float32,
        )
        out_ref[0] = summed.T.astype(jnp.bfloat16)

    return pl.pallas_call(
        body,
        grid_spec=pltpu.PrefetchScalarGridSpec(
            num_scalar_prefetch=1,
            grid=(kv_heads,),
            in_specs=[
                pl.BlockSpec((1, tokens, count), lambda j, ref: (j, 0, 0)),
                pl.BlockSpec((values.shape[0], HEAD_DIM), lambda j, ref: (0, ref[j])),
            ],
            out_specs=pl.BlockSpec((1, count, HEAD_DIM), lambda j, ref: (j, 0, 0)),
        ),
        out_shape=jax.ShapeDtypeStruct((kv_heads, count, HEAD_DIM), jnp.bfloat16),
        compiler_params=pltpu.CompilerParams(vmem_limit_bytes=20 * MIB),
        cost_estimate=LIGHT,
    )(places, weights, values)


def out_project(blocks, heads, weight, width):
    def body(block_ref, head_ref, weight_ref, out_ref):
        for i in range(blocks.shape[0]):
            start = pl.multiple_of(block_ref[i] * width, width)
            out_ref[:, i * width : (i + 1) * width] = jnp.dot(
                head_ref[...], weight_ref[:, pl.ds(start, width)], preferred_element_type=jnp.float32
            ).astype(jnp.bfloat16)

    whole = pl.BlockSpec(memory_space=pltpu.VMEM)
    shape = (heads.shape[0], weight.shape[1])
    return pl.pallas_call(
        body,
        in_specs=[pl.BlockSpec(memory_space=pltpu.SMEM), whole, whole],
        out_specs=whole,
        out_shape=jax.ShapeDtypeStruct(shape, jnp.bfloat16),
        compiler_params=pltpu.CompilerParams(vmem_limit_bytes=20 * MIB),
        cost_estimate=LIGHT,
    )(blocks, heads, weight)


def on_device(
    prompt_states,
    page_table,
    step_states,
    sample_order,
    key_weight,
    value_weight,
    query_weight,
    out_weight,
):
    devices = lax.axis_size("sample")
    groups = lax.axis_size("groups")
    own_index = lax.axis_index("sample")
    first = lax.axis_index("groups") % 2 == 0
    deep = devices // LINE
    own_a, own_b, own_c = own_index // LINE, own_index // 2 % 2, own_index % 2
    along_ring, along_z, along_y, along_x, in_chip = mover(groups, devices)
    row_count = prompt_states.shape[0]
    chip_rows = 2 * row_count
    pages_here = row_count // PAGE
    heads_here = query_weight.shape[1] // HEAD_DIM
    total_pages = page_table.shape[0]
    prompts = total_pages // PROMPT_PAGES
    samples = sample_order.shape[0]
    steps = 2 * samples
    group_size = samples // prompts
    own_kv = own_index * heads_here // GQA
    wide_states = step_states.reshape(steps, D)
    rows = heads_here * steps
    width = key_weight.shape[0]
    half = key_weight.shape[1] // 2
    kv_places = jnp.where(first, 0, KV_HEADS // 2) + jnp.arange(KV_HEADS, dtype=jnp.int32)
    kv_places = kv_places % KV_HEADS

    order = ring_order(deep)

    def by_place(table):
        return sum(jnp.where(own_a == a, table[a], 0) for a in range(deep))

    own_turn = by_place([order.index(a) for a in range(deep)])

    def block(place_z, flip, core):
        return place_z * LINE + (own_b ^ flip) * 2 + core

    def behind(k):
        return by_place([order[(order.index(a) - k) % deep] for a in range(deep)])

    def halves(weight):
        low, high = weight[:, :half], weight[:, half:]
        return jnp.where(first, low, high), jnp.where(first, high, low)

    key_mine, key_other = halves(key_weight)
    value_mine, value_other = halves(value_weight)

    step_place = PROMPT_PAGES * PAGE + jnp.arange(2, dtype=jnp.int32)
    step_tables = tuple(t[:, None, :] for t in rope_tables(step_place))
    flat_tables = [
        jnp.repeat(jnp.concatenate([sign * table, table], axis=-1)[:, 0], samples, axis=0)
        for sign, table in zip((1, -1), step_tables)
    ]
    queries = project_queries(wide_states, query_weight, *flat_tables)
    packed_queries = jnp.concatenate(
        jnp.split(queries, half // queries.shape[1], axis=0), axis=1
    )
    packed = packed_queries.shape[0]
    queries = queries.reshape(2, samples, heads_here, HEAD_DIM)

    places = [(k, flip) for k in range(deep) for flip in (0, 1)]
    own_blocks = jnp.stack([block(behind(k), flip, own_c) for k, flip in places])
    done = {}

    def send(move, value):
        moved = done.setdefault(move, [])
        moved.append(move(after(value, moved[-2]) if len(moved) > 1 else value))
        return moved[-1]

    key_z, mine, theirs = {0: key_mine}, {0: value_mine}, {}
    key_z[1] = send(along_ring, key_z[0])
    mine[1] = send(along_ring, mine[0])
    value_y = send(along_y, value_mine)
    key_full = {0: jnp.concatenate([key_mine, key_other, packed_queries])}
    key_y = {0: send(along_y, after(key_full[0], (value_y, key_z[1])))}
    theirs[0] = jnp.concatenate([value_y, packed_queries, key_y[0][2 * width :]])
    mine_x, theirs_x = {0: value_other}, {}
    for k in range(1, deep):
        swapped = send(along_x, after(key_z[k], packed_queries))
        mine_x[k] = send(along_x, mine[k])
        if k == 1:
            theirs_x[0] = send(along_x, value_y)
        if k + 1 < deep:
            key_z[k + 1] = send(along_ring, key_z[k])
            mine[k + 1] = send(along_ring, mine[k])
        key_full[k] = jnp.concatenate([key_z[k], swapped])
        key_y[k] = send(along_y, after(key_full[k], key_y[k - 1]))
        if k == 1:
            sent_blocks = jnp.stack([block(behind(j), flip, 1 - own_c) for j, flip in places])
            sent = pick(prompt_states, after(sent_blocks, (key_z[2], swapped, mine[1])), width)
            got = in_chip(sent)
    for k in range(1, deep):
        theirs[k] = send(along_ring, theirs[k - 1])
        theirs_x[k] = send(along_x, theirs[k])
    left = assemble(prompt_states, wide_states, got, after(own_blocks, (key_y[1], mine[2])), width)

    ring_queries = collect([theirs[k] for k in range(deep)], width, 2 * packed)
    ring_queries = [ring_queries, in_chip(ring_queries)]
    query_turns = jnp.stack([(own_turn + deep - order.index(a)) % deep for a in range(deep)])
    by_owner = (deep, 2, 2, rows)

    own_pages = jnp.concatenate(
        [
            holder * pages_here + jnp.arange(pages_here, dtype=jnp.int32)
            for holder in (own_index, own_index ^ 1)
        ]
    )
    slots = jnp.sum(
        jnp.where(
            page_table[None, :] == own_pages[:, None],
            jnp.arange(total_pages, dtype=jnp.int32)[None, :],
            0,
        ),
        axis=1,
    )
    positions = (slots % PROMPT_PAGES * PAGE)[:, None] + jnp.arange(PAGE, dtype=jnp.int32)[None, :]
    cosine, sine_part = rope_tables(positions.reshape(chip_rows))

    key_pieces = [
        [((key_y if flip else key_full)[k], start) for start in (0, width)] for k, flip in places
    ]
    value_pieces = [
        [((theirs if flip else mine)[k], 0), ((theirs_x if flip else mine_x)[k], 0)]
        for k, flip in places
    ]

    def project_blocks(pieces, which, acc, ready):
        return project(after(left, ready), which, [pieces[i] for i in which], acc)

    last = 2 * deep - 2
    key_early = project_blocks(
        key_pieces, range(last), None, (theirs[1], mine_x[deep - 1], key_y[deep - 2])
    )
    early = [*range(0, 2 * deep, 2), 1]
    value_early = project_blocks(value_pieces, early, None, (key_early, theirs_x[1]))
    key_sum = project_blocks(
        key_pieces, [last, last + 1], key_early, (value_early, theirs[deep - 1], theirs_x[deep - 2])
    )
    key_back = in_chip(key_sum)
    own_place = lax.dynamic_index_in_dim(kv_places, own_kv, 0, False) * HEAD_DIM

    def own_head(sums):
        return lax.dynamic_slice_in_dim(sums, own_place, HEAD_DIM, 1).reshape(2, samples, HEAD_DIM)

    new_keys = own_head(key_sum[chip_rows:]) + own_head(key_back[chip_rows:])
    new_keys = turn(new_keys, step_tables).astype(jnp.bfloat16)
    masks = (None, None)
    if prompts > 1:
        token_prompt = jnp.repeat(slots // PROMPT_PAGES, PAGE)
        row_prompt = jnp.tile(sample_order // group_size, devices // KV_HEADS * rows // samples)
        masks = (token_prompt[:, None], row_prompt[None, :])
    weights, top, total = attend(
        kv_places, query_turns, ring_queries, key_sum, key_back, cosine, sine_part, *masks
    )

    stats = jnp.stack([top.reshape(by_owner), total.reshape(by_owner)])
    stats = jnp.stack([stats, along_y(stats)[:, :, :, ::-1]])
    weights = after(weights, stats)
    stats = jnp.concatenate([stats] + [along_z(stats, k) for k in range(1, deep)])
    prefix_top = jnp.max(stats[:, 0], axis=0)
    prefix_total = jnp.sum(jnp.exp(stats[:, 0] - prefix_top) * stats[:, 1], axis=0)
    factor = jnp.exp(top.reshape(by_owner) - prefix_top)[:, 0]
    prefix_top = lax.dynamic_index_in_dim(prefix_top, own_a, 0, False)[0, 0]
    prefix_total = lax.dynamic_index_in_dim(prefix_total, own_a, 0, False)[0, 0]

    late = [i for i in range(2 * deep) if i not in early]
    value_sum = project_blocks(value_pieces, late, value_early, weights)
    step_values = own_head(value_sum[chip_rows:])
    step_back = lax.dynamic_slice_in_dim(
        in_chip(value_sum[chip_rows:]), own_place, HEAD_DIM, 1
    ).reshape(step_values.shape)
    new_values = (step_values + step_back).astype(jnp.bfloat16)
    partial = apply_weights(kv_places, weights, value_sum)
    partial = partial.reshape(by_owner + (HEAD_DIM,))

    def narrow(value):
        return value.astype(jnp.bfloat16)

    def wide(value):
        return value.astype(jnp.float32)

    partial = wide(partial[:, 0]) + wide(in_chip(partial[:, 1]))
    partial = narrow(partial * factor[..., None])
    partial = narrow(wide(partial[:, 0]) + wide(along_y(partial[:, 1])))
    prefix_sum = wide(lax.dynamic_index_in_dim(partial, own_a, 0, False))
    for k in range(1, deep):
        piece = lax.dynamic_index_in_dim(partial, (own_a + k) % deep, 0, False)
        prefix_sum = prefix_sum + wide(along_z(piece, k))

    by_head = (heads_here, 2, samples)
    head_out = finish_heads(
        prefix_top.reshape(by_head).swapaxes(0, 1),
        prefix_total.reshape(by_head).swapaxes(0, 1),
        prefix_sum.reshape(by_head + (HEAD_DIM,)).swapaxes(0, 1),
        queries.transpose(0, 2, 1, 3),
        new_keys[:, None],
        new_values[:, None],
    )
    flat_heads = head_out.transpose(0, 2, 1, 3).reshape(steps, heads_here * HEAD_DIM)

    out_width = out_weight.shape[1] // devices
    out_blocks = jnp.stack(
        [
            block((own_a + k) % deep, flip, own_c ^ turned)
            for turned in (0, 1)
            for flip in (0, 1)
            for k in range(deep)
        ]
    )
    terms = out_project(out_blocks, flat_heads, out_weight, out_width)
    for move in (in_chip, along_y):
        share = terms.shape[1] // 2
        terms = narrow(wide(terms[:, :share]) + wide(move(terms[:, share:])))
    attn_out = wide(terms[:, :out_width])
    for k in range(1, deep):
        attn_out = attn_out + wide(along_z(terms[:, k * out_width : (k + 1) * out_width], k))
    return narrow(attn_out).reshape(2, samples, -1)


def solution(mesh):
    in_specs = (
        P(("groups", "sample"), None),
        P("groups"),
        P(None, "groups", None),
        P("groups"),
        P("sample", None),
        P("sample", None),
        P(None, "sample"),
        P("sample", None),
    )
    out_specs = P(None, "groups", "sample")
    return jax.shard_map(
        on_device, mesh=mesh, in_specs=in_specs, out_specs=out_specs, check_vma=False
    )
```

```python
import jax
import jax.numpy as jnp
from jax import lax
from jax.experimental import pallas as pl
from jax.experimental.pallas import tpu as pltpu
from jax.sharding import PartitionSpec as P

D = 8192
HEAD_DIM = 128
KV_HEADS = 4
GQA = 8
PAGE = 128
PROMPT_PAGES = 64
LINE = 4

rope_base = 1000000.0


def rope_tables(position):
    half_dim = HEAD_DIM // 2
    frequency = rope_base ** (-jnp.arange(half_dim, dtype=jnp.float32) * 2.0 / HEAD_DIM)
    angles = position.astype(jnp.float32)[..., None] * frequency
    return jnp.cos(angles), jnp.sin(angles)


def turn(vector, tables):
    cosine, sine_part = tables
    half_dim = HEAD_DIM // 2
    first_half = vector[..., :half_dim]
    second_half = vector[..., half_dim:]
    return jnp.concatenate(
        [
            first_half * cosine - second_half * sine_part,
            second_half * cosine + first_half * sine_part,
        ],
        axis=-1,
    )


def finish_heads(prefix_top, prefix_total, prefix_sum, queries, new_keys, new_values):
    score_scale = queries.shape[-1] ** (-0.5)
    query_wide = queries.astype(jnp.float32)
    key_wide = new_keys.astype(jnp.float32)
    value_wide = new_values.astype(jnp.float32)
    own_score = jnp.sum(query_wide * key_wide, axis=-1) * score_scale
    back_score = jnp.sum(query_wide[1] * key_wide[0], axis=-1) * score_scale
    first_high = jnp.maximum(prefix_top[0], own_score[0])
    first_old = jnp.exp(prefix_top[0] - first_high)
    first_own = jnp.exp(own_score[0] - first_high)
    first_out = (first_old[..., None] * prefix_sum[0] + first_own[..., None] * value_wide[0]) / (
        first_old * prefix_total[0] + first_own
    )[..., None]
    second_high = jnp.maximum(jnp.maximum(prefix_top[1], own_score[1]), back_score)
    second_old = jnp.exp(prefix_top[1] - second_high)
    second_back = jnp.exp(back_score - second_high)
    second_own = jnp.exp(own_score[1] - second_high)
    second_num = (
        second_old[..., None] * prefix_sum[1]
        + second_back[..., None] * value_wide[0]
        + second_own[..., None] * value_wide[1]
    )
    second_out = second_num / (second_old * prefix_total[1] + second_back + second_own)[..., None]
    return jnp.stack([first_out, second_out]).astype(jnp.bfloat16)


def ring_order(deep):
    return [*range(0, deep, 2), *range(deep - 1 - deep % 2, 0, -2)]


def mover(groups, devices):
    deep = devices // LINE
    order = ring_order(deep)

    def move(value, step):
        pairs = []
        for g in range(groups):
            for s in range(devices):
                a, b, c = s // LINE, s // 2 % 2, s % 2
                to_g, to_a, to_b, to_c = step(g, a, b, c)
                to_s = (to_a % deep) * LINE + to_b * 2 + to_c
                pairs.append((g * devices + s, to_g * devices + to_s))
        return lax.ppermute(value, ("groups", "sample"), pairs)

    def next_on_ring(a):
        return order[(order.index(a) + 1) % deep]

    along_ring = lambda v: move(v, lambda g, a, b, c: (g, next_on_ring(a), b, c))
    along_z = lambda v, k: move(v, lambda g, a, b, c: (g, a + k, b, c))
    along_y = lambda v: move(v, lambda g, a, b, c: (g, a, 1 - b, c))
    along_x = lambda v: move(v, lambda g, a, b, c: (g ^ 1, a, b, c))
    in_chip = lambda v: move(v, lambda g, a, b, c: (g, a, b, 1 - c))
    return along_ring, along_z, along_y, along_x, in_chip


def after(value, done):
    return lax.optimization_barrier((value, done))[0]


MIB = 1024 * 1024
LIGHT = pl.CostEstimate(flops=1, bytes_accessed=1, transcendentals=0)


def project_queries(steps, weight, cosine, sine):
    count, depth = steps.shape
    parts = 8
    piece = depth // parts

    def body(step_ref, weight_ref, cosine_ref, sine_ref, out_ref, held, sems):
        copies = []
        for i in range(parts):
            copies.append(
                pltpu.make_async_copy(
                    weight_ref.at[pl.ds(i * piece, piece), :], held.at[i], sems.at[i]
                )
            )
            copies[-1].start()
        total = None
        for i in range(parts):
            copies[i].wait()
            product = jnp.dot(
                step_ref[:, i * piece : (i + 1) * piece],
                held[i],
                preferred_element_type=jnp.float32,
            )
            total = product if total is None else total + product
        for start in range(0, weight.shape[1], HEAD_DIM):
            head = total[:, start : start + HEAD_DIM]
            turned = head * cosine_ref[...] + pltpu.roll(head, HEAD_DIM // 2, 1) * sine_ref[...]
            out_ref[:, start : start + HEAD_DIM] = turned.astype(jnp.bfloat16)

    whole = pl.BlockSpec(memory_space=pltpu.VMEM)
    return pl.pallas_call(
        body,
        in_specs=[whole, pl.BlockSpec(memory_space=pltpu.HBM), whole, whole],
        out_specs=whole,
        out_shape=jax.ShapeDtypeStruct((count, weight.shape[1]), jnp.bfloat16),
        scratch_shapes=[
            pltpu.VMEM((parts, piece, weight.shape[1]), weight.dtype),
            pltpu.SemaphoreType.DMA((parts,)),
        ],
        compiler_params=pltpu.CompilerParams(vmem_limit_bytes=10 * MIB),
        cost_estimate=LIGHT,
    )(steps, weight, cosine, sine)


def collect(arrays, first, height):
    columns = arrays[0].shape[1]

    def body(*refs):
        out_ref, sems = refs[-2:]
        copies = [
            pltpu.make_async_copy(ref.at[pl.ds(first, height), :], out_ref.at[i], sems.at[i])
            for i, ref in enumerate(refs[:-2])
        ]
        for copy in copies:
            copy.start()
        for copy in copies:
            copy.wait()

    return pl.pallas_call(
        body,
        in_specs=[pl.BlockSpec(memory_space=pl.ANY)] * len(arrays),
        out_specs=pl.BlockSpec(memory_space=pltpu.VMEM),
        out_shape=jax.ShapeDtypeStruct((len(arrays), height, columns), arrays[0].dtype),
        scratch_shapes=[pltpu.SemaphoreType.DMA((len(arrays),))],
        compiler_params=pltpu.CompilerParams(vmem_limit_bytes=4 * MIB),
        cost_estimate=LIGHT,
    )(*arrays)


def assemble(prompt, got, steps, blocks, width):
    count = blocks.shape[0]
    row_count, step_count = prompt.shape[0], steps.shape[0]
    height = 2 * row_count + step_count

    def body(block_ref, prompt_ref, got_ref, step_ref, out_ref, sems):
        copies = []
        for i in range(count):
            column = pl.ds(pl.multiple_of(block_ref[i] * width, width), width)
            for j, (source, start, rows) in enumerate(
                (
                    (prompt_ref.at[:, column], 0, row_count),
                    (got_ref.at[:, column], row_count, row_count),
                    (step_ref.at[:, column], 2 * row_count, step_count),
                )
            ):
                copies.append(
                    pltpu.make_async_copy(
                        source, out_ref.at[i, pl.ds(start, rows), :], sems.at[i, j]
                    )
                )
                copies[-1].start()
        for copy in copies:
            copy.wait()

    anywhere = pl.BlockSpec(memory_space=pl.ANY)
    return pl.pallas_call(
        body,
        in_specs=[pl.BlockSpec(memory_space=pltpu.SMEM)] + [anywhere] * 3,
        out_specs=pl.BlockSpec(memory_space=pltpu.VMEM),
        out_shape=jax.ShapeDtypeStruct((count, height, width), prompt.dtype),
        scratch_shapes=[pltpu.SemaphoreType.DMA((count, 3))],
        compiler_params=pltpu.CompilerParams(vmem_limit_bytes=16 * MIB),
        cost_estimate=LIGHT,
    )(blocks, prompt, got, steps)


def project(left, which, pieces, acc, kind=jnp.float32):
    arrays = []
    for piece in pieces:
        for array, _ in piece:
            if not any(array is held for held in arrays):
                arrays.append(array)
    _, height, width = left.shape
    columns = sum(array.shape[1] for array, _ in pieces[0])
    extra = [] if acc is None else [acc]

    def body(left_ref, *refs):
        out_ref = refs[-1]
        total = {}
        for i, piece in enumerate(pieces):
            side = 0
            for array, first in piece:
                ref = refs[[array is other for other in arrays].index(True)]
                place = slice(side, side + array.shape[1])
                product = jnp.dot(
                    left_ref[which[i]],
                    ref[first : first + width, :],
                    preferred_element_type=jnp.float32,
                )
                if i:
                    product += total[place.start]
                elif extra:
                    product += refs[len(arrays)][:, place]
                total[place.start] = product
                if i == len(pieces) - 1:
                    out_ref[:, place] = product.astype(kind)
                side += array.shape[1]

    whole = pl.BlockSpec(memory_space=pltpu.VMEM)
    return pl.pallas_call(
        body,
        in_specs=[whole] * (1 + len(arrays) + len(extra)),
        out_specs=whole,
        out_shape=jax.ShapeDtypeStruct((height, columns), kind),
        compiler_params=pltpu.CompilerParams(vmem_limit_bytes=24 * MIB),
        cost_estimate=LIGHT,
    )(left, *arrays, *extra)


def attend(places, turns, queries, own, other, cosine, sine, token_prompt, row_prompt):
    kv_heads = places.shape[0]
    deep, packed, lanes = queries[0].shape
    share = deep // kv_heads
    count = 2 * share * packed * lanes // HEAD_DIM
    tokens = cosine.shape[0]
    half = tokens // 2
    height = own.shape[0]
    masks = [] if token_prompt is None else [token_prompt, row_prompt]

    def body(place_ref, turn_ref, *refs):
        query_refs = refs[: 2 * share]
        own_ref, other_ref, cosine_ref, sine_ref = refs[2 * share : 2 * share + 4]
        mask_refs = refs[2 * share + 4 : -3]
        weight_ref, top_ref, total_ref = refs[-3:]
        keys = jnp.concatenate(
            [
                own_ref[:half, :].astype(jnp.float32) + other_ref[half:tokens, :],
                own_ref[half:tokens, :].astype(jnp.float32) + other_ref[:half, :],
            ],
            axis=0,
        )
        swapped = pltpu.roll(keys, HEAD_DIM // 2, 1)
        wide_cosine = jnp.concatenate([cosine_ref[...], cosine_ref[...]], axis=1)
        wide_sine = jnp.concatenate([-sine_ref[...], sine_ref[...]], axis=1)
        keys = (keys * wide_cosine + swapped * wide_sine).astype(jnp.bfloat16)
        unpacked = []
        for ref in query_refs:
            for low in range(0, packed, packed // 2):
                for left in range(0, lanes, HEAD_DIM):
                    unpacked.append(ref[0, low : low + packed // 2, left : left + HEAD_DIM])
        scores = lax.dot_general(
            keys,
            jnp.concatenate(unpacked, axis=0),
            (((1,), (1,)), ((), ())),
            preferred_element_type=jnp.float32,
        ) * (HEAD_DIM**-0.5)
        if masks:
            scores = jnp.where(mask_refs[0][...] == mask_refs[1][...], scores, -1e30)
        top = jnp.max(scores, axis=0, keepdims=True)
        weights = jnp.exp(scores - top)
        top_ref[0] = top
        total_ref[0] = jnp.sum(weights, axis=0, keepdims=True)
        weight_ref[0] = weights.astype(jnp.bfloat16)

    def query_spec(part):
        return pl.BlockSpec(
            (1, packed, lanes), lambda j, place, turn: (turn[j * share + part], 0, 0)
        )

    row = jax.ShapeDtypeStruct((kv_heads, 1, count), jnp.float32)
    row_spec = pl.BlockSpec((1, 1, count), lambda j, place, turn: (j, 0, 0))
    fixed = lambda j, place, turn: (0, 0)
    column = pl.BlockSpec((height, HEAD_DIM), lambda j, place, turn: (0, place[j]))
    return pl.pallas_call(
        body,
        grid_spec=pltpu.PrefetchScalarGridSpec(
            num_scalar_prefetch=2,
            grid=(kv_heads,),
            in_specs=[query_spec(part) for part in range(share) for _ in queries]
            + [column, column]
            + [pl.BlockSpec(cosine.shape, fixed)] * 2
            + [pl.BlockSpec(mask.shape, fixed) for mask in masks],
            out_specs=[
                pl.BlockSpec((1, tokens, count), lambda j, place, turn: (j, 0, 0)),
                row_spec,
                row_spec,
            ],
        ),
        out_shape=[
            jax.ShapeDtypeStruct((kv_heads, tokens, count), jnp.bfloat16),
            row,
            row,
        ],
        compiler_params=pltpu.CompilerParams(vmem_limit_bytes=14 * MIB),
        cost_estimate=LIGHT,
    )(places, turns, *([*queries] * share), own, other, cosine, sine, *masks)


def apply_weights(places, weights, values):
    kv_heads, tokens, count = weights.shape

    def body(place_ref, weight_ref, value_ref, out_ref):
        summed = lax.dot_general(
            value_ref[:tokens, :],
            weight_ref[0],
            (((0,), (0,)), ((), ())),
            preferred_element_type=jnp.float32,
        )
        out_ref[0] = summed.T.astype(jnp.bfloat16)

    return pl.pallas_call(
        body,
        grid_spec=pltpu.PrefetchScalarGridSpec(
            num_scalar_prefetch=1,
            grid=(kv_heads,),
            in_specs=[
                pl.BlockSpec((1, tokens, count), lambda j, ref: (j, 0, 0)),
                pl.BlockSpec((values.shape[0], HEAD_DIM), lambda j, ref: (0, ref[j])),
            ],
            out_specs=pl.BlockSpec((1, count, HEAD_DIM), lambda j, ref: (j, 0, 0)),
        ),
        out_shape=jax.ShapeDtypeStruct((kv_heads, count, HEAD_DIM), jnp.bfloat16),
        compiler_params=pltpu.CompilerParams(vmem_limit_bytes=8 * MIB),
        cost_estimate=LIGHT,
    )(places, weights, values)


def out_project(blocks, heads, weight, width):
    def body(block_ref, head_ref, weight_ref, out_ref):
        for i in range(blocks.shape[0]):
            start = pl.multiple_of(block_ref[i] * width, width)
            out_ref[:, i * width : (i + 1) * width] = jnp.dot(
                head_ref[...], weight_ref[:, pl.ds(start, width)], preferred_element_type=jnp.float32
            ).astype(jnp.bfloat16)

    whole = pl.BlockSpec(memory_space=pltpu.VMEM)
    shape = (heads.shape[0], weight.shape[1])
    return pl.pallas_call(
        body,
        in_specs=[pl.BlockSpec(memory_space=pltpu.SMEM), whole, whole],
        out_specs=whole,
        out_shape=jax.ShapeDtypeStruct(shape, jnp.bfloat16),
        compiler_params=pltpu.CompilerParams(vmem_limit_bytes=10 * MIB),
        cost_estimate=LIGHT,
    )(blocks, heads, weight)


def on_device(
    prompt_states,
    page_table,
    step_states,
    sample_order,
    key_weight,
    value_weight,
    query_weight,
    out_weight,
):
    devices = lax.axis_size("sample")
    groups = lax.axis_size("groups")
    own_index = lax.axis_index("sample")
    first = lax.axis_index("groups") % 2 == 0
    deep = devices // LINE
    own_a, own_b, own_c = own_index // LINE, own_index // 2 % 2, own_index % 2
    along_ring, along_z, along_y, along_x, in_chip = mover(groups, devices)
    row_count = prompt_states.shape[0]
    chip_rows = 2 * row_count
    pages_here = row_count // PAGE
    heads_here = query_weight.shape[1] // HEAD_DIM
    total_pages = page_table.shape[0]
    prompts = total_pages // PROMPT_PAGES
    samples = sample_order.shape[0]
    steps = 2 * samples
    group_size = samples // prompts
    own_kv = own_index * heads_here // GQA
    wide_states = step_states.reshape(steps, D)
    rows = heads_here * steps
    width = key_weight.shape[0]
    half = key_weight.shape[1] // 2
    kv_places = jnp.where(first, 0, KV_HEADS // 2) + jnp.arange(KV_HEADS, dtype=jnp.int32)
    kv_places = kv_places % KV_HEADS

    order = ring_order(deep)

    def by_place(table):
        return sum(jnp.where(own_a == a, table[a], 0) for a in range(deep))

    own_turn = by_place([order.index(a) for a in range(deep)])

    def block(place_z, flip, core):
        return place_z * LINE + (own_b ^ flip) * 2 + core

    def behind(k):
        return by_place([order[(order.index(a) - k) % deep] for a in range(deep)])

    def halves(weight):
        low, high = weight[:, :half], weight[:, half:]
        return jnp.where(first, low, high), jnp.where(first, high, low)

    key_mine, key_other = halves(key_weight)
    value_mine, value_other = halves(value_weight)

    step_place = PROMPT_PAGES * PAGE + jnp.arange(2, dtype=jnp.int32)
    step_tables = tuple(t[:, None, :] for t in rope_tables(step_place))
    flat_tables = [
        jnp.repeat(jnp.concatenate([sign * table, table], axis=-1)[:, 0], samples, axis=0)
        for sign, table in zip((1, -1), step_tables)
    ]
    queries = project_queries(wide_states, query_weight, *flat_tables)
    packed_queries = jnp.concatenate(
        jnp.split(queries, half // queries.shape[1], axis=0), axis=1
    )
    packed = packed_queries.shape[0]
    queries = queries.reshape(2, samples, heads_here, HEAD_DIM)

    places = [(k, flip) for k in range(deep) for flip in (0, 1)]
    own_blocks = jnp.stack([block(behind(k), flip, own_c) for k, flip in places])
    done = {}

    def send(move, value):
        moved = done.setdefault(move, [])
        moved.append(move(after(value, moved[-2]) if len(moved) > 1 else value))
        return moved[-1]

    got = in_chip(prompt_states)
    key_z, mine, theirs = {0: key_mine}, {0: value_mine}, {}
    key_z[1] = send(along_ring, key_z[0])
    mine[1] = send(along_ring, mine[0])
    value_y = send(along_y, value_mine)
    key_full = {0: jnp.concatenate([key_mine, key_other, packed_queries])}
    key_y = {0: send(along_y, after(key_full[0], (value_y, key_z[1])))}
    theirs[0] = jnp.concatenate([value_y, packed_queries, key_y[0][2 * width :]])
    mine_x, theirs_x = {0: value_other}, {}
    for k in range(1, deep):
        swapped = send(along_x, after(key_z[k], packed_queries))
        mine_x[k] = send(along_x, mine[k])
        if k == 1:
            theirs_x[0] = send(along_x, value_y)
        if k + 1 < deep:
            key_z[k + 1] = send(along_ring, key_z[k])
            mine[k + 1] = send(along_ring, mine[k])
        key_full[k] = jnp.concatenate([key_z[k], swapped])
        if k == deep - 1:
            left = assemble(
                prompt_states, got, wide_states, after(own_blocks, (key_y[1], mine[2])), width
            )
        key_y[k] = send(along_y, after(key_full[k], (key_y[k - 1], left) if k == deep - 1 else key_y[k - 1]))
    for k in range(1, deep):
        theirs[k] = send(along_ring, theirs[k - 1])
        theirs_x[k] = send(along_x, theirs[k])

    ring_queries = collect([theirs[k] for k in range(deep)], width, 2 * packed)
    ring_queries = [ring_queries, in_chip(ring_queries)]
    query_turns = jnp.stack([(own_turn + deep - order.index(a)) % deep for a in range(deep)])
    by_owner = (deep, 2, 2, rows)

    own_pages = jnp.concatenate(
        [
            holder * pages_here + jnp.arange(pages_here, dtype=jnp.int32)
            for holder in (own_index, own_index ^ 1)
        ]
    )
    slots = jnp.sum(
        jnp.where(
            page_table[None, :] == own_pages[:, None],
            jnp.arange(total_pages, dtype=jnp.int32)[None, :],
            0,
        ),
        axis=1,
    )
    positions = (slots % PROMPT_PAGES * PAGE)[:, None] + jnp.arange(PAGE, dtype=jnp.int32)[None, :]
    cosine, sine_part = rope_tables(positions.reshape(chip_rows))

    key_pieces = [
        [((key_y if flip else key_full)[k], start) for start in (0, width)] for k, flip in places
    ]
    value_pieces = [
        [((theirs if flip else mine)[k], 0), ((theirs_x if flip else mine_x)[k], 0)]
        for k, flip in places
    ]

    def project_blocks(pieces, which, acc, ready, kind=jnp.float32):
        return project(after(left, ready), which, [pieces[i] for i in which], acc, kind)

    last = 2 * deep - 2
    key_early = project_blocks(
        key_pieces, range(last), None, (theirs[1], mine_x[deep - 1], key_y[deep - 2])
    )
    early = [*range(0, 2 * deep, 2), 1]
    value_early = project_blocks(value_pieces, early, None, (key_early, theirs_x[1]))
    key_sum = project_blocks(
        key_pieces, [last, last + 1], key_early, (value_early, theirs[deep - 1], theirs_x[deep - 2]), jnp.bfloat16
    )
    key_back = in_chip(key_sum)
    own_place = lax.dynamic_index_in_dim(kv_places, own_kv, 0, False) * HEAD_DIM

    def own_head(sums):
        sums = lax.dynamic_slice_in_dim(sums, own_place, HEAD_DIM, 1)
        return sums.reshape(2, samples, HEAD_DIM).astype(jnp.float32)

    new_keys = own_head(key_sum[chip_rows:]) + own_head(key_back[chip_rows:])
    new_keys = turn(new_keys, step_tables).astype(jnp.bfloat16)
    masks = (None, None)
    if prompts > 1:
        token_prompt = jnp.repeat(slots // PROMPT_PAGES, PAGE)
        row_prompt = jnp.tile(sample_order // group_size, devices // KV_HEADS * rows // samples)
        masks = (token_prompt[:, None], row_prompt[None, :])
    weights, top, total = attend(
        kv_places, query_turns, ring_queries, key_sum, key_back, cosine, sine_part, *masks
    )

    stats = jnp.stack([top.reshape(by_owner), total.reshape(by_owner)])
    stats = jnp.stack([stats, along_y(stats)[:, :, :, ::-1]])
    weights = after(weights, stats)
    stats = jnp.concatenate([stats] + [along_z(stats, k) for k in range(1, deep)])
    prefix_top = jnp.max(stats[:, 0], axis=0)
    prefix_total = jnp.sum(jnp.exp(stats[:, 0] - prefix_top) * stats[:, 1], axis=0)
    factor = jnp.exp(top.reshape(by_owner) - prefix_top)[:, 0]
    prefix_top = lax.dynamic_index_in_dim(prefix_top, own_a, 0, False)[0, 0]
    prefix_total = lax.dynamic_index_in_dim(prefix_total, own_a, 0, False)[0, 0]

    late = [i for i in range(2 * deep) if i not in early]
    value_sum = project_blocks(value_pieces, late, value_early, weights, jnp.bfloat16)
    step_values = own_head(value_sum[chip_rows:])
    step_back = own_head(in_chip(value_sum[chip_rows:]))
    new_values = (step_values + step_back).astype(jnp.bfloat16)
    partial = apply_weights(kv_places, weights, value_sum)
    partial = partial.reshape(by_owner + (HEAD_DIM,))

    def narrow(value):
        return value.astype(jnp.bfloat16)

    def wide(value):
        return value.astype(jnp.float32)

    partial = wide(partial[:, 0]) + wide(in_chip(partial[:, 1]))
    partial = narrow(partial * factor[..., None])
    partial = narrow(wide(partial[:, 0]) + wide(along_y(partial[:, 1])))
    prefix_sum = wide(lax.dynamic_index_in_dim(partial, own_a, 0, False))
    for k in range(1, deep):
        piece = lax.dynamic_index_in_dim(partial, (own_a + k) % deep, 0, False)
        prefix_sum = prefix_sum + wide(along_z(piece, k))

    by_head = (heads_here, 2, samples)
    head_out = finish_heads(
        prefix_top.reshape(by_head).swapaxes(0, 1),
        prefix_total.reshape(by_head).swapaxes(0, 1),
        prefix_sum.reshape(by_head + (HEAD_DIM,)).swapaxes(0, 1),
        queries.transpose(0, 2, 1, 3),
        new_keys[:, None],
        new_values[:, None],
    )
    flat_heads = head_out.transpose(0, 2, 1, 3).reshape(steps, heads_here * HEAD_DIM)

    out_width = out_weight.shape[1] // devices
    out_blocks = jnp.stack(
        [
            block((own_a + k) % deep, flip, own_c ^ turned)
            for turned in (0, 1)
            for flip in (0, 1)
            for k in range(deep)
        ]
    )
    terms = out_project(out_blocks, flat_heads, out_weight, out_width)
    for move in (in_chip, along_y):
        share = terms.shape[1] // 2
        terms = narrow(wide(terms[:, :share]) + wide(move(terms[:, share:])))
    attn_out = wide(terms[:, :out_width])
    for k in range(1, deep):
        attn_out = attn_out + wide(along_z(terms[:, k * out_width : (k + 1) * out_width], k))
    return narrow(attn_out).reshape(2, samples, -1)


def solution(mesh):
    in_specs = (
        P(("groups", "sample"), None),
        P("groups"),
        P(None, "groups", None),
        P("groups"),
        P("sample", None),
        P("sample", None),
        P(None, "sample"),
        P("sample", None),
    )
    out_specs = P(None, "groups", "sample")
    return jax.shard_map(
        on_device, mesh=mesh, in_specs=in_specs, out_specs=out_specs, check_vma=False
    )
```

```python
import jax
import jax.numpy as jnp
from jax import lax
from jax.experimental import pallas as pl
from jax.experimental.pallas import tpu as pltpu
from jax.sharding import PartitionSpec as P

D = 8192
HEAD_DIM = 128
KV_HEADS = 4
GQA = 8
PAGE = 128
PROMPT_PAGES = 64
LINE = 4

rope_base = 1000000.0


def rope_tables(position):
    half_dim = HEAD_DIM // 2
    frequency = rope_base ** (-jnp.arange(half_dim, dtype=jnp.float32) * 2.0 / HEAD_DIM)
    angles = position.astype(jnp.float32)[..., None] * frequency
    return jnp.cos(angles), jnp.sin(angles)


def turn(vector, tables):
    cosine, sine_part = tables
    half_dim = HEAD_DIM // 2
    first_half = vector[..., :half_dim]
    second_half = vector[..., half_dim:]
    return jnp.concatenate(
        [
            first_half * cosine - second_half * sine_part,
            second_half * cosine + first_half * sine_part,
        ],
        axis=-1,
    )


def finish_heads(prefix_top, prefix_total, prefix_sum, queries, new_keys, new_values):
    score_scale = queries.shape[-1] ** (-0.5)
    query_wide = queries.astype(jnp.float32)
    key_wide = new_keys.astype(jnp.float32)
    value_wide = new_values.astype(jnp.float32)
    own_score = jnp.sum(query_wide * key_wide, axis=-1) * score_scale
    back_score = jnp.sum(query_wide[1] * key_wide[0], axis=-1) * score_scale
    first_high = jnp.maximum(prefix_top[0], own_score[0])
    first_old = jnp.exp(prefix_top[0] - first_high)
    first_own = jnp.exp(own_score[0] - first_high)
    first_out = (first_old[..., None] * prefix_sum[0] + first_own[..., None] * value_wide[0]) / (
        first_old * prefix_total[0] + first_own
    )[..., None]
    second_high = jnp.maximum(jnp.maximum(prefix_top[1], own_score[1]), back_score)
    second_old = jnp.exp(prefix_top[1] - second_high)
    second_back = jnp.exp(back_score - second_high)
    second_own = jnp.exp(own_score[1] - second_high)
    second_num = (
        second_old[..., None] * prefix_sum[1]
        + second_back[..., None] * value_wide[0]
        + second_own[..., None] * value_wide[1]
    )
    second_out = second_num / (second_old * prefix_total[1] + second_back + second_own)[..., None]
    return jnp.stack([first_out, second_out]).astype(jnp.bfloat16)


def ring_order(deep):
    return [*range(0, deep, 2), *range(deep - 1 - deep % 2, 0, -2)]


def mover(groups, devices):
    deep = devices // LINE
    order = ring_order(deep)

    def move(value, step):
        pairs = []
        for g in range(groups):
            for s in range(devices):
                a, b, c = s // LINE, s // 2 % 2, s % 2
                to_g, to_a, to_b, to_c = step(g, a, b, c)
                to_s = (to_a % deep) * LINE + to_b * 2 + to_c
                pairs.append((g * devices + s, to_g * devices + to_s))
        return lax.ppermute(value, ("groups", "sample"), pairs)

    def next_on_ring(a):
        return order[(order.index(a) + 1) % deep]

    along_ring = lambda v: move(v, lambda g, a, b, c: (g, next_on_ring(a), b, c))
    along_z = lambda v, k: move(v, lambda g, a, b, c: (g, a + k, b, c))
    along_y = lambda v: move(v, lambda g, a, b, c: (g, a, 1 - b, c))
    along_x = lambda v: move(v, lambda g, a, b, c: (g ^ 1, a, b, c))
    in_chip = lambda v: move(v, lambda g, a, b, c: (g, a, b, 1 - c))
    return along_ring, along_z, along_y, along_x, in_chip


def after(value, done):
    return lax.optimization_barrier((value, done))[0]


MIB = 1024 * 1024
LIGHT = pl.CostEstimate(flops=1, bytes_accessed=1, transcendentals=0)


def project_queries(steps, weight, cosine, sine):
    count, depth = steps.shape
    parts = 8
    piece = depth // parts

    def body(step_ref, weight_ref, cosine_ref, sine_ref, out_ref, held, sems):
        copies = []
        for i in range(parts):
            copies.append(
                pltpu.make_async_copy(
                    weight_ref.at[pl.ds(i * piece, piece), :], held.at[i], sems.at[i]
                )
            )
            copies[-1].start()
        total = None
        for i in range(parts):
            copies[i].wait()
            product = jnp.dot(
                step_ref[:, i * piece : (i + 1) * piece],
                held[i],
                preferred_element_type=jnp.float32,
            )
            total = product if total is None else total + product
        for start in range(0, weight.shape[1], HEAD_DIM):
            head = total[:, start : start + HEAD_DIM]
            turned = head * cosine_ref[...] + pltpu.roll(head, HEAD_DIM // 2, 1) * sine_ref[...]
            out_ref[:, start : start + HEAD_DIM] = turned.astype(jnp.bfloat16)

    whole = pl.BlockSpec(memory_space=pltpu.VMEM)
    return pl.pallas_call(
        body,
        in_specs=[whole, pl.BlockSpec(memory_space=pltpu.HBM), whole, whole],
        out_specs=whole,
        out_shape=jax.ShapeDtypeStruct((count, weight.shape[1]), jnp.bfloat16),
        scratch_shapes=[
            pltpu.VMEM((parts, piece, weight.shape[1]), weight.dtype),
            pltpu.SemaphoreType.DMA((parts,)),
        ],
        compiler_params=pltpu.CompilerParams(vmem_limit_bytes=10 * MIB),
        cost_estimate=LIGHT,
    )(steps, weight, cosine, sine)


def collect(arrays, first, height):
    columns = arrays[0].shape[1]

    def body(*refs):
        out_ref, sems = refs[-2:]
        copies = [
            pltpu.make_async_copy(ref.at[pl.ds(first, height), :], out_ref.at[i], sems.at[i])
            for i, ref in enumerate(refs[:-2])
        ]
        for copy in copies:
            copy.start()
        for copy in copies:
            copy.wait()

    return pl.pallas_call(
        body,
        in_specs=[pl.BlockSpec(memory_space=pl.ANY)] * len(arrays),
        out_specs=pl.BlockSpec(memory_space=pltpu.VMEM),
        out_shape=jax.ShapeDtypeStruct((len(arrays), height, columns), arrays[0].dtype),
        scratch_shapes=[pltpu.SemaphoreType.DMA((len(arrays),))],
        compiler_params=pltpu.CompilerParams(vmem_limit_bytes=4 * MIB),
        cost_estimate=LIGHT,
    )(*arrays)


def assemble(prompt, got, steps, blocks, width):
    count = blocks.shape[0]
    row_count, step_count = prompt.shape[0], steps.shape[0]
    height = 2 * row_count + step_count

    def body(block_ref, prompt_ref, got_ref, step_ref, out_ref, sems):
        copies = []
        for i in range(count):
            column = pl.ds(pl.multiple_of(block_ref[i] * width, width), width)
            for j, (source, start, rows) in enumerate(
                (
                    (prompt_ref.at[:, column], 0, row_count),
                    (got_ref.at[:, column], row_count, row_count),
                    (step_ref.at[:, column], 2 * row_count, step_count),
                )
            ):
                copies.append(
                    pltpu.make_async_copy(
                        source, out_ref.at[i, pl.ds(start, rows), :], sems.at[i, j]
                    )
                )
                copies[-1].start()
        for copy in copies:
            copy.wait()

    anywhere = pl.BlockSpec(memory_space=pl.ANY)
    return pl.pallas_call(
        body,
        in_specs=[pl.BlockSpec(memory_space=pltpu.SMEM)] + [anywhere] * 3,
        out_specs=pl.BlockSpec(memory_space=pltpu.VMEM),
        out_shape=jax.ShapeDtypeStruct((count, height, width), prompt.dtype),
        scratch_shapes=[pltpu.SemaphoreType.DMA((count, 3))],
        compiler_params=pltpu.CompilerParams(vmem_limit_bytes=57 * MIB),
        cost_estimate=LIGHT,
    )(blocks, prompt, got, steps)


def project(left, which, pieces, acc, kind=jnp.float32):
    arrays = []
    for piece in pieces:
        for array, _ in piece:
            if not any(array is held for held in arrays):
                arrays.append(array)
    _, height, width = left.shape
    count = len(pieces)
    columns = sum(array.shape[1] for array, _ in pieces[0])
    extra = [] if acc is None else [acc]

    def body(left_ref, *refs):
        out_ref, blocks, weights, held, sems = refs[-5:]
        groups = []
        for i, piece in enumerate(pieces):
            group = [pltpu.make_async_copy(left_ref.at[which[i]], blocks.at[i], sems.at[i, 0])]
            side = 0
            for j, (array, first) in enumerate(piece):
                ref = refs[[array is other for other in arrays].index(True)]
                group.append(
                    pltpu.make_async_copy(
                        ref.at[pl.ds(first, width), :],
                        weights.at[i, :, pl.ds(side, array.shape[1])],
                        sems.at[i, 1 + j],
                    )
                )
                side += array.shape[1]
            for copy in group:
                copy.start()
            groups.append(group)
        if extra:
            before = pltpu.make_async_copy(refs[len(arrays)], held, sems.at[count, 0])
            before.start()
        total = None
        for i, group in enumerate(groups):
            for copy in group:
                copy.wait()
            product = jnp.dot(blocks[i], weights[i], preferred_element_type=jnp.float32)
            total = product if total is None else total + product
        if extra:
            before.wait()
            total = total + held[...]
        out_ref[...] = total.astype(kind)

    anywhere = pl.BlockSpec(memory_space=pl.ANY)
    return pl.pallas_call(
        body,
        in_specs=[anywhere] * (1 + len(arrays) + len(extra)),
        out_specs=pl.BlockSpec(memory_space=pltpu.VMEM),
        out_shape=jax.ShapeDtypeStruct((height, columns), kind),
        scratch_shapes=[
            pltpu.VMEM((count, height, width), left.dtype),
            pltpu.VMEM((count, width, columns), left.dtype),
            pltpu.VMEM((height, columns) if extra else (8, 128), jnp.float32),
            pltpu.SemaphoreType.DMA((count + 1, 3)),
        ],
        compiler_params=pltpu.CompilerParams(vmem_limit_bytes=57 * MIB),
        cost_estimate=LIGHT,
    )(left, *arrays, *extra)


def attend(places, turns, queries, own, other, cosine, sine, token_prompt, row_prompt):
    kv_heads = places.shape[0]
    deep, packed, lanes = queries[0].shape
    share = deep // kv_heads
    count = 2 * share * packed * lanes // HEAD_DIM
    tokens = cosine.shape[0]
    half = tokens // 2
    height = own.shape[0]
    masks = [] if token_prompt is None else [token_prompt, row_prompt]

    def body(place_ref, turn_ref, *refs):
        query_refs = refs[: 2 * share]
        own_ref, other_ref, cosine_ref, sine_ref = refs[2 * share : 2 * share + 4]
        mask_refs = refs[2 * share + 4 : -3]
        weight_ref, top_ref, total_ref = refs[-3:]
        keys = jnp.concatenate(
            [
                own_ref[:half, :].astype(jnp.float32) + other_ref[half:tokens, :],
                own_ref[half:tokens, :].astype(jnp.float32) + other_ref[:half, :],
            ],
            axis=0,
        )
        swapped = pltpu.roll(keys, HEAD_DIM // 2, 1)
        wide_cosine = jnp.concatenate([cosine_ref[...], cosine_ref[...]], axis=1)
        wide_sine = jnp.concatenate([-sine_ref[...], sine_ref[...]], axis=1)
        keys = (keys * wide_cosine + swapped * wide_sine).astype(jnp.bfloat16)
        unpacked = []
        for ref in query_refs:
            for low in range(0, packed, packed // 2):
                for left in range(0, lanes, HEAD_DIM):
                    unpacked.append(ref[0, low : low + packed // 2, left : left + HEAD_DIM])
        scores = lax.dot_general(
            keys,
            jnp.concatenate(unpacked, axis=0),
            (((1,), (1,)), ((), ())),
            preferred_element_type=jnp.float32,
        ) * (HEAD_DIM**-0.5)
        if masks:
            scores = jnp.where(mask_refs[0][...] == mask_refs[1][...], scores, -1e30)
        top = jnp.max(scores, axis=0, keepdims=True)
        weights = jnp.exp(scores - top)
        top_ref[0] = top
        total_ref[0] = jnp.sum(weights, axis=0, keepdims=True)
        weight_ref[0] = weights.astype(jnp.bfloat16)

    def query_spec(part):
        return pl.BlockSpec(
            (1, packed, lanes), lambda j, place, turn: (turn[j * share + part], 0, 0)
        )

    row = jax.ShapeDtypeStruct((kv_heads, 1, count), jnp.float32)
    row_spec = pl.BlockSpec((1, 1, count), lambda j, place, turn: (j, 0, 0))
    fixed = lambda j, place, turn: (0, 0)
    column = pl.BlockSpec((height, HEAD_DIM), lambda j, place, turn: (0, place[j]))
    return pl.pallas_call(
        body,
        grid_spec=pltpu.PrefetchScalarGridSpec(
            num_scalar_prefetch=2,
            grid=(kv_heads,),
            in_specs=[query_spec(part) for part in range(share) for _ in queries]
            + [column, column]
            + [pl.BlockSpec(cosine.shape, fixed)] * 2
            + [pl.BlockSpec(mask.shape, fixed) for mask in masks],
            out_specs=[
                pl.BlockSpec((1, tokens, count), lambda j, place, turn: (j, 0, 0)),
                row_spec,
                row_spec,
            ],
        ),
        out_shape=[
            jax.ShapeDtypeStruct((kv_heads, tokens, count), jnp.bfloat16),
            row,
            row,
        ],
        compiler_params=pltpu.CompilerParams(vmem_limit_bytes=57 * MIB),
        cost_estimate=LIGHT,
    )(places, turns, *([*queries] * share), own, other, cosine, sine, *masks)


def apply_weights(places, weights, values):
    kv_heads, tokens, count = weights.shape

    def body(place_ref, weight_ref, value_ref, out_ref):
        summed = lax.dot_general(
            value_ref[:tokens, :],
            weight_ref[0],
            (((0,), (0,)), ((), ())),
            preferred_element_type=jnp.float32,
        )
        out_ref[0] = summed.T.astype(jnp.bfloat16)

    return pl.pallas_call(
        body,
        grid_spec=pltpu.PrefetchScalarGridSpec(
            num_scalar_prefetch=1,
            grid=(kv_heads,),
            in_specs=[
                pl.BlockSpec((1, tokens, count), lambda j, ref: (j, 0, 0)),
                pl.BlockSpec((values.shape[0], HEAD_DIM), lambda j, ref: (0, ref[j])),
            ],
            out_specs=pl.BlockSpec((1, count, HEAD_DIM), lambda j, ref: (j, 0, 0)),
        ),
        out_shape=jax.ShapeDtypeStruct((kv_heads, count, HEAD_DIM), jnp.bfloat16),
        compiler_params=pltpu.CompilerParams(vmem_limit_bytes=57 * MIB),
        cost_estimate=LIGHT,
    )(places, weights, values)


def out_project(blocks, heads, weight, width):
    count = blocks.shape[0]
    depth = weight.shape[0]

    def body(block_ref, head_ref, weight_ref, out_ref, held, sems):
        copies = []
        for i in range(count):
            start = pl.multiple_of(block_ref[i] * width, width)
            copies.append(
                pltpu.make_async_copy(
                    weight_ref.at[:, pl.ds(start, width)], held.at[i], sems.at[i]
                )
            )
            copies[-1].start()
        for i, copy in enumerate(copies):
            copy.wait()
            out_ref[:, i * width : (i + 1) * width] = jnp.dot(
                head_ref[...], held[i], preferred_element_type=jnp.float32
            ).astype(jnp.bfloat16)

    whole = pl.BlockSpec(memory_space=pltpu.VMEM)
    return pl.pallas_call(
        body,
        in_specs=[
            pl.BlockSpec(memory_space=pltpu.SMEM),
            whole,
            pl.BlockSpec(memory_space=pl.ANY),
        ],
        out_specs=whole,
        out_shape=jax.ShapeDtypeStruct((heads.shape[0], weight.shape[1]), jnp.bfloat16),
        scratch_shapes=[
            pltpu.VMEM((count, depth, width), weight.dtype),
            pltpu.SemaphoreType.DMA((count,)),
        ],
        compiler_params=pltpu.CompilerParams(vmem_limit_bytes=60 * MIB),
        cost_estimate=LIGHT,
    )(blocks, heads, weight)


def on_device(
    prompt_states,
    page_table,
    step_states,
    sample_order,
    key_weight,
    value_weight,
    query_weight,
    out_weight,
):
    devices = lax.axis_size("sample")
    groups = lax.axis_size("groups")
    own_index = lax.axis_index("sample")
    first = lax.axis_index("groups") % 2 == 0
    deep = devices // LINE
    own_a, own_b, own_c = own_index // LINE, own_index // 2 % 2, own_index % 2
    along_ring, along_z, along_y, along_x, in_chip = mover(groups, devices)
    row_count = prompt_states.shape[0]
    chip_rows = 2 * row_count
    pages_here = row_count // PAGE
    heads_here = query_weight.shape[1] // HEAD_DIM
    total_pages = page_table.shape[0]
    prompts = total_pages // PROMPT_PAGES
    samples = sample_order.shape[0]
    steps = 2 * samples
    group_size = samples // prompts
    own_kv = own_index * heads_here // GQA
    wide_states = step_states.reshape(steps, D)
    rows = heads_here * steps
    width = key_weight.shape[0]
    half = key_weight.shape[1] // 2
    kv_places = jnp.where(first, 0, KV_HEADS // 2) + jnp.arange(KV_HEADS, dtype=jnp.int32)
    kv_places = kv_places % KV_HEADS

    order = ring_order(deep)

    def by_place(table):
        return sum(jnp.where(own_a == a, table[a], 0) for a in range(deep))

    own_turn = by_place([order.index(a) for a in range(deep)])

    def block(place_z, flip, core):
        return place_z * LINE + (own_b ^ flip) * 2 + core

    def behind(k):
        return by_place([order[(order.index(a) - k) % deep] for a in range(deep)])

    def halves(weight):
        low, high = weight[:, :half], weight[:, half:]
        return jnp.where(first, low, high), jnp.where(first, high, low)

    key_mine, key_other = halves(key_weight)
    value_mine, value_other = halves(value_weight)

    step_place = PROMPT_PAGES * PAGE + jnp.arange(2, dtype=jnp.int32)
    step_tables = tuple(t[:, None, :] for t in rope_tables(step_place))
    flat_tables = [
        jnp.repeat(jnp.concatenate([sign * table, table], axis=-1)[:, 0], samples, axis=0)
        for sign, table in zip((1, -1), step_tables)
    ]
    queries = project_queries(wide_states, query_weight, *flat_tables)
    packed_queries = jnp.concatenate(
        jnp.split(queries, half // queries.shape[1], axis=0), axis=1
    )
    packed = packed_queries.shape[0]
    queries = queries.reshape(2, samples, heads_here, HEAD_DIM)

    own_pages = jnp.concatenate(
        [
            holder * pages_here + jnp.arange(pages_here, dtype=jnp.int32)
            for holder in (own_index, own_index ^ 1)
        ]
    )
    slots = jnp.sum(
        jnp.where(
            page_table[None, :] == own_pages[:, None],
            jnp.arange(total_pages, dtype=jnp.int32)[None, :],
            0,
        ),
        axis=1,
    )
    positions = (slots % PROMPT_PAGES * PAGE)[:, None] + jnp.arange(PAGE, dtype=jnp.int32)[None, :]
    cosine, sine_part = rope_tables(positions.reshape(chip_rows))

    places = [(k, flip) for k in range(deep) for flip in (0, 1)]
    own_blocks = jnp.stack([block(behind(k), flip, own_c) for k, flip in places])
    query_turns = jnp.stack([(own_turn + deep - order.index(a)) % deep for a in range(deep)])
    own_place = (own_kv + jnp.where(first, 0, KV_HEADS // 2)) % KV_HEADS * HEAD_DIM
    prepared = (cosine, sine_part, kv_places, query_turns)
    done = {}

    def send(move, value):
        moved = done.setdefault(move, [])
        moved.append(move(after(value, moved[-2]) if len(moved) > 1 else value))
        return moved[-1]

    got = in_chip(prompt_states)
    key_z, mine, theirs = {0: key_mine}, {0: value_mine}, {}
    key_z[1] = send(along_ring, key_z[0])
    mine[1] = send(along_ring, mine[0])
    value_y = send(along_y, value_mine)
    key_full = {0: jnp.concatenate([key_mine, key_other, packed_queries])}
    key_y = {0: send(along_y, after(key_full[0], (value_y, key_z[1])))}
    theirs[0] = jnp.concatenate([value_y, packed_queries, key_y[0][2 * width :]])
    mine_x, theirs_x = {0: value_other}, {}
    for k in range(1, deep):
        swapped = send(along_x, after(key_z[k], packed_queries))
        mine_x[k] = send(along_x, mine[k])
        if k == 1:
            theirs_x[0] = send(along_x, value_y)
        if k + 1 < deep:
            key_z[k + 1] = send(along_ring, key_z[k])
            mine[k + 1] = send(along_ring, mine[k])
        key_full[k] = jnp.concatenate([key_z[k], swapped])
        ready = [key_y[k - 1]]
        if k == 2:
            left = assemble(prompt_states, got, wide_states, after(own_blocks, prepared), width)
            ready.append(left)
        key_y[k] = send(along_y, after(key_full[k], ready))
    for k in range(1, deep):
        theirs[k] = send(along_ring, theirs[k - 1])
        theirs_x[k] = send(along_x, theirs[k])

    ring_queries = collect([theirs[k] for k in range(deep)], width, 2 * packed)
    ring_queries = [ring_queries, in_chip(ring_queries)]
    by_owner = (deep, 2, 2, rows)

    key_pieces = [
        [((key_y if flip else key_full)[k], start) for start in (0, width)] for k, flip in places
    ]
    value_pieces = [
        [((theirs if flip else mine)[k], 0), ((theirs_x if flip else mine_x)[k], 0)]
        for k, flip in places
    ]

    def project_blocks(pieces, which, acc, ready, kind=jnp.float32):
        return project(after(left, ready), which, [pieces[i] for i in which], acc, kind)

    last = 2 * deep - 2
    key_early = project_blocks(
        key_pieces, range(last), None, (theirs[1], mine_x[deep - 1], key_y[deep - 2])
    )
    early = [*range(0, 2 * deep, 2), 1]
    value_early = project_blocks(value_pieces, early, None, (key_early, theirs_x[1]))
    key_sum = project_blocks(
        key_pieces, [last, last + 1], key_early, (value_early, theirs[deep - 1], theirs_x[deep - 2]), jnp.bfloat16
    )
    key_back = in_chip(key_sum)

    def own_head(sums):
        sums = lax.dynamic_slice_in_dim(sums, own_place, HEAD_DIM, 1)
        return sums.reshape(2, samples, HEAD_DIM).astype(jnp.float32)

    new_keys = own_head(key_sum[chip_rows:]) + own_head(key_back[chip_rows:])
    new_keys = turn(new_keys, step_tables).astype(jnp.bfloat16)
    masks = (None, None)
    if prompts > 1:
        token_prompt = jnp.repeat(slots // PROMPT_PAGES, PAGE)
        row_prompt = jnp.tile(sample_order // group_size, devices // KV_HEADS * rows // samples)
        masks = (token_prompt[:, None], row_prompt[None, :])
    weights, top, total = attend(
        kv_places, query_turns, ring_queries, key_sum, key_back, cosine, sine_part, *masks
    )

    stats = jnp.stack([top.reshape(by_owner), total.reshape(by_owner)])
    stats = jnp.stack([stats, along_y(stats)[:, :, :, ::-1]])
    weights = after(weights, stats)
    stats = jnp.concatenate([stats] + [along_z(stats, k) for k in range(1, deep)])
    prefix_top = jnp.max(stats[:, 0], axis=0)
    prefix_total = jnp.sum(jnp.exp(stats[:, 0] - prefix_top) * stats[:, 1], axis=0)
    factor = jnp.exp(top.reshape(by_owner) - prefix_top)[:, 0]
    prefix_top = lax.dynamic_index_in_dim(prefix_top, own_a, 0, False)[0, 0]
    prefix_total = lax.dynamic_index_in_dim(prefix_total, own_a, 0, False)[0, 0]

    late = [i for i in range(2 * deep) if i not in early]
    value_sum = project_blocks(value_pieces, late, value_early, weights, jnp.bfloat16)
    step_values = own_head(value_sum[chip_rows:])
    step_back = own_head(in_chip(value_sum[chip_rows:]))
    new_values = (step_values + step_back).astype(jnp.bfloat16)
    partial = apply_weights(kv_places, weights, value_sum)
    partial = partial.reshape(by_owner + (HEAD_DIM,))

    def narrow(value):
        return value.astype(jnp.bfloat16)

    def wide(value):
        return value.astype(jnp.float32)

    partial = wide(partial[:, 0]) + wide(in_chip(partial[:, 1]))
    partial = narrow(partial * factor[..., None])
    partial = narrow(wide(partial[:, 0]) + wide(along_y(partial[:, 1])))
    prefix_sum = wide(lax.dynamic_index_in_dim(partial, own_a, 0, False))
    for k in range(1, deep):
        piece = lax.dynamic_index_in_dim(partial, (own_a + k) % deep, 0, False)
        prefix_sum = prefix_sum + wide(along_z(piece, k))

    by_head = (heads_here, 2, samples)
    head_out = finish_heads(
        prefix_top.reshape(by_head).swapaxes(0, 1),
        prefix_total.reshape(by_head).swapaxes(0, 1),
        prefix_sum.reshape(by_head + (HEAD_DIM,)).swapaxes(0, 1),
        queries.transpose(0, 2, 1, 3),
        new_keys[:, None],
        new_values[:, None],
    )
    flat_heads = head_out.transpose(0, 2, 1, 3).reshape(steps, heads_here * HEAD_DIM)

    out_width = out_weight.shape[1] // devices
    out_blocks = jnp.stack(
        [
            block((own_a + k) % deep, flip, own_c ^ turned)
            for turned in (0, 1)
            for flip in (0, 1)
            for k in range(deep)
        ]
    )
    terms = out_project(out_blocks, flat_heads, out_weight, out_width)
    for move in (in_chip, along_y):
        share = terms.shape[1] // 2
        terms = narrow(wide(terms[:, :share]) + wide(move(terms[:, share:])))
    attn_out = wide(terms[:, :out_width])
    for k in range(1, deep):
        attn_out = attn_out + wide(along_z(terms[:, k * out_width : (k + 1) * out_width], k))
    return narrow(attn_out).reshape(2, samples, -1)


def solution(mesh):
    in_specs = (
        P(("groups", "sample"), None),
        P("groups"),
        P(None, "groups", None),
        P("groups"),
        P("sample", None),
        P("sample", None),
        P(None, "sample"),
        P("sample", None),
    )
    out_specs = P(None, "groups", "sample")
    return jax.shard_map(
        on_device, mesh=mesh, in_specs=in_specs, out_specs=out_specs, check_vma=False
    )
```

```python
import jax
import jax.numpy as jnp
from jax import lax
from jax.experimental import pallas as pl
from jax.experimental.pallas import tpu as pltpu
from jax.sharding import PartitionSpec as P

D = 8192
HEAD_DIM = 128
KV_HEADS = 4
GQA = 8
PAGE = 128
PROMPT_PAGES = 64
LINE = 4

rope_base = 1000000.0


def rope_tables(position):
    half_dim = HEAD_DIM // 2
    frequency = rope_base ** (-jnp.arange(half_dim, dtype=jnp.float32) * 2.0 / HEAD_DIM)
    angles = position.astype(jnp.float32)[..., None] * frequency
    return jnp.cos(angles), jnp.sin(angles)


def turn(vector, tables):
    cosine, sine_part = tables
    half_dim = HEAD_DIM // 2
    first_half = vector[..., :half_dim]
    second_half = vector[..., half_dim:]
    return jnp.concatenate(
        [
            first_half * cosine - second_half * sine_part,
            second_half * cosine + first_half * sine_part,
        ],
        axis=-1,
    )


def finish_heads(prefix_top, prefix_total, prefix_sum, queries, new_keys, new_values):
    score_scale = queries.shape[-1] ** (-0.5)
    query_wide = queries.astype(jnp.float32)
    key_wide = new_keys.astype(jnp.float32)
    value_wide = new_values.astype(jnp.float32)
    own_score = jnp.sum(query_wide * key_wide, axis=-1) * score_scale
    back_score = jnp.sum(query_wide[1] * key_wide[0], axis=-1) * score_scale
    first_high = jnp.maximum(prefix_top[0], own_score[0])
    first_old = jnp.exp(prefix_top[0] - first_high)
    first_own = jnp.exp(own_score[0] - first_high)
    first_out = (first_old[..., None] * prefix_sum[0] + first_own[..., None] * value_wide[0]) / (
        first_old * prefix_total[0] + first_own
    )[..., None]
    second_high = jnp.maximum(jnp.maximum(prefix_top[1], own_score[1]), back_score)
    second_old = jnp.exp(prefix_top[1] - second_high)
    second_back = jnp.exp(back_score - second_high)
    second_own = jnp.exp(own_score[1] - second_high)
    second_num = (
        second_old[..., None] * prefix_sum[1]
        + second_back[..., None] * value_wide[0]
        + second_own[..., None] * value_wide[1]
    )
    second_out = second_num / (second_old * prefix_total[1] + second_back + second_own)[..., None]
    return jnp.stack([first_out, second_out]).astype(jnp.bfloat16)


def ring_order(deep):
    return [*range(0, deep, 2), *range(deep - 1 - deep % 2, 0, -2)]


def mover(groups, devices):
    deep = devices // LINE
    order = ring_order(deep)

    def move(value, step):
        pairs = []
        for g in range(groups):
            for s in range(devices):
                a, b, c = s // LINE, s // 2 % 2, s % 2
                to_g, to_a, to_b, to_c = step(g, a, b, c)
                to_s = (to_a % deep) * LINE + to_b * 2 + to_c
                pairs.append((g * devices + s, to_g * devices + to_s))
        return lax.ppermute(value, ("groups", "sample"), pairs)

    def next_on_ring(a):
        return order[(order.index(a) + 1) % deep]

    along_ring = lambda v: move(v, lambda g, a, b, c: (g, next_on_ring(a), b, c))
    along_z = lambda v, k: move(v, lambda g, a, b, c: (g, a + k, b, c))
    along_y = lambda v: move(v, lambda g, a, b, c: (g, a, 1 - b, c))
    along_x = lambda v: move(v, lambda g, a, b, c: (g ^ 1, a, b, c))
    in_chip = lambda v: move(v, lambda g, a, b, c: (g, a, b, 1 - c))
    return along_ring, along_z, along_y, along_x, in_chip


def after(value, done):
    return lax.optimization_barrier((value, done))[0]


MIB = 1024 * 1024
LIGHT = pl.CostEstimate(flops=1, bytes_accessed=1, transcendentals=0)


def project_queries(steps, weight, cosine, sine):
    count, depth = steps.shape
    parts = 8
    piece = depth // parts

    def body(step_ref, weight_ref, cosine_ref, sine_ref, out_ref, held, sems):
        copies = []
        for i in range(parts):
            copies.append(
                pltpu.make_async_copy(
                    weight_ref.at[pl.ds(i * piece, piece), :], held.at[i], sems.at[i]
                )
            )
            copies[-1].start()
        total = None
        for i in range(parts):
            copies[i].wait()
            product = jnp.dot(
                step_ref[:, i * piece : (i + 1) * piece],
                held[i],
                preferred_element_type=jnp.float32,
            )
            total = product if total is None else total + product
        for start in range(0, weight.shape[1], HEAD_DIM):
            head = total[:, start : start + HEAD_DIM]
            turned = head * cosine_ref[...] + pltpu.roll(head, HEAD_DIM // 2, 1) * sine_ref[...]
            out_ref[:, start : start + HEAD_DIM] = turned.astype(jnp.bfloat16)

    whole = pl.BlockSpec(memory_space=pltpu.VMEM)
    return pl.pallas_call(
        body,
        in_specs=[whole, pl.BlockSpec(memory_space=pltpu.HBM), whole, whole],
        out_specs=whole,
        out_shape=jax.ShapeDtypeStruct((count, weight.shape[1]), jnp.bfloat16),
        scratch_shapes=[
            pltpu.VMEM((parts, piece, weight.shape[1]), weight.dtype),
            pltpu.SemaphoreType.DMA((parts,)),
        ],
        compiler_params=pltpu.CompilerParams(vmem_limit_bytes=10 * MIB),
        cost_estimate=LIGHT,
    )(steps, weight, cosine, sine)


def collect(arrays, first, height):
    columns = arrays[0].shape[1]

    def body(*refs):
        out_ref, sems = refs[-2:]
        copies = [
            pltpu.make_async_copy(ref.at[pl.ds(first, height), :], out_ref.at[i], sems.at[i])
            for i, ref in enumerate(refs[:-2])
        ]
        for copy in copies:
            copy.start()
        for copy in copies:
            copy.wait()

    return pl.pallas_call(
        body,
        in_specs=[pl.BlockSpec(memory_space=pl.ANY)] * len(arrays),
        out_specs=pl.BlockSpec(memory_space=pltpu.VMEM),
        out_shape=jax.ShapeDtypeStruct((len(arrays), height, columns), arrays[0].dtype),
        scratch_shapes=[pltpu.SemaphoreType.DMA((len(arrays),))],
        compiler_params=pltpu.CompilerParams(vmem_limit_bytes=4 * MIB),
        cost_estimate=LIGHT,
    )(*arrays)


class Blocks:
    def __init__(self, prompt, steps, width, pieces):
        self.arrays = []
        for piece in pieces:
            for array, _ in piece:
                if not any(array is held for held in self.arrays):
                    self.arrays.append(array)
        self.pieces, self.width, self.count = pieces, width, len(pieces)
        self.row_count, self.step_count = prompt.shape[0], steps.shape[0]
        self.height = 2 * self.row_count + self.step_count
        self.columns = sum(array.shape[1] for array, _ in pieces[0])
        self.scratch = [
            pltpu.VMEM((self.count, self.height, width), prompt.dtype),
            pltpu.VMEM((self.count, width, self.columns), prompt.dtype),
            pltpu.SemaphoreType.DMA((self.count, 5)),
        ]

    def copies(self, i, block_ref, sources, weight_refs, scratch):
        left, weights, sems = scratch
        column = pl.ds(pl.multiple_of(block_ref[i] * self.width, self.width), self.width)
        group = []
        start = 0
        for j, (source, rows) in enumerate(
            zip(sources, (self.row_count, self.row_count, self.step_count))
        ):
            group.append(
                pltpu.make_async_copy(
                    source.at[:, column], left.at[i, pl.ds(start, rows), :], sems.at[i, j]
                )
            )
            start += rows
        side = 0
        for j, (array, first) in enumerate(self.pieces[i]):
            ref = weight_refs[[array is other for other in self.arrays].index(True)]
            group.append(
                pltpu.make_async_copy(
                    ref.at[pl.ds(first, self.width), :],
                    weights.at[i, :, pl.ds(side, array.shape[1])],
                    sems.at[i, 3 + j],
                )
            )
            side += array.shape[1]
        return group


AHEAD = 3


def project(prompt, got, steps, blocks, width, pieces, kind):
    held = Blocks(prompt, steps, width, pieces)

    def body(block_ref, prompt_ref, got_ref, step_ref, *refs):
        weight_refs = refs[: len(held.arrays)]
        out_ref, *scratch = refs[len(held.arrays) :]
        left, weights, _ = scratch
        sources = (prompt_ref, got_ref, step_ref)
        groups = [
            held.copies(i, block_ref, sources, weight_refs, scratch) for i in range(held.count)
        ]
        for group in groups[:AHEAD]:
            for copy in group:
                copy.start()
        total = None
        for i, group in enumerate(groups):
            for copy in group:
                copy.wait()
            if i + AHEAD < held.count:
                for copy in groups[i + AHEAD]:
                    copy.start()
            product = jnp.dot(left[i], weights[i], preferred_element_type=jnp.float32)
            total = product if total is None else total + product
        out_ref[...] = total.astype(kind)

    anywhere = pl.BlockSpec(memory_space=pl.ANY)
    return pl.pallas_call(
        body,
        in_specs=[pl.BlockSpec(memory_space=pltpu.SMEM)] + [anywhere] * (3 + len(held.arrays)),
        out_specs=pl.BlockSpec(memory_space=pltpu.VMEM),
        out_shape=jax.ShapeDtypeStruct((held.height, held.columns), kind),
        scratch_shapes=held.scratch,
        compiler_params=pltpu.CompilerParams(vmem_limit_bytes=57 * MIB),
        cost_estimate=LIGHT,
    )(blocks, prompt, got, steps, *held.arrays)


def attend(
    places, turns, queries, own, other, cosine, sine, masks, prompt, got, steps, blocks, width,
    pieces, early,
):
    kv_heads = places.shape[0]
    deep, packed, lanes = queries[0].shape
    share = deep // kv_heads
    count = 2 * share * packed * lanes // HEAD_DIM
    tokens = cosine.shape[0]
    half = tokens // 2
    held = Blocks(prompt, steps, width, pieces)
    inputs = [*queries, own, other, cosine, sine, *masks]

    def body(place_ref, turn_ref, block_ref, *refs):
        query_refs = refs[:2]
        own_ref, other_ref, cosine_ref, sine_ref = refs[2:6]
        mask_refs = refs[6 : len(inputs)]
        prompt_ref, got_ref, step_ref, early_ref = refs[len(inputs) : len(inputs) + 4]
        rest = refs[len(inputs) + 4 :]
        weight_refs, rest = rest[: len(held.arrays)], rest[len(held.arrays) :]
        out_ref, top_ref, total_ref, step_out_ref = rest[:4]
        early_held, weight_held, value_held, early_sem, *scratch = rest[4:]
        left, weight_rows, _ = scratch
        sources = (prompt_ref, got_ref, step_ref)
        groups = [
            held.copies(i, block_ref, sources, weight_refs, scratch) for i in range(held.count)
        ]
        before = pltpu.make_async_copy(early_ref, early_held, early_sem.at[0])
        before.start()
        for group in groups:
            for copy in group:
                copy.start()
        wide_cosine = jnp.concatenate([cosine_ref[...], cosine_ref[...]], axis=1)
        wide_sine = jnp.concatenate([-sine_ref[...], sine_ref[...]], axis=1)

        def one_head(j, _):
            column = pl.ds(pl.multiple_of(place_ref[j] * HEAD_DIM, HEAD_DIM), HEAD_DIM)
            keys = jnp.concatenate(
                [
                    own_ref[:half, column].astype(jnp.float32)
                    + other_ref[half:tokens, column].astype(jnp.float32),
                    own_ref[half:tokens, column].astype(jnp.float32)
                    + other_ref[:half, column].astype(jnp.float32),
                ],
                axis=0,
            )
            swapped = pltpu.roll(keys, HEAD_DIM // 2, 1)
            keys = (keys * wide_cosine + swapped * wide_sine).astype(jnp.bfloat16)
            unpacked = []
            for part in range(share):
                for ref in query_refs:
                    both = ref[turn_ref[j * share + part]]
                    for low in range(0, packed, packed // 2):
                        for left_lane in range(0, lanes, HEAD_DIM):
                            unpacked.append(
                                both[low : low + packed // 2, left_lane : left_lane + HEAD_DIM]
                            )
            scores = lax.dot_general(
                keys,
                jnp.concatenate(unpacked, axis=0),
                (((1,), (1,)), ((), ())),
                preferred_element_type=jnp.float32,
            ) * (HEAD_DIM**-0.5)
            if masks:
                scores = jnp.where(mask_refs[0][...] == mask_refs[1][...], scores, -1e30)
            top = jnp.max(scores, axis=0, keepdims=True)
            weights = jnp.exp(scores - top)
            top_ref[j] = top
            total_ref[j] = jnp.sum(weights, axis=0, keepdims=True)
            weight_held[j] = weights.astype(jnp.bfloat16)
            return 0

        lax.fori_loop(0, kv_heads, one_head, 0)
        before.wait()
        total = early_held[...]
        for i, group in enumerate(groups):
            for copy in group:
                copy.wait()
            total += jnp.dot(left[i], weight_rows[i], preferred_element_type=jnp.float32)
        value_held[...] = total[:tokens].astype(jnp.bfloat16)
        step_out_ref[...] = total[tokens:]

        def one_sum(j, _):
            column = pl.ds(pl.multiple_of(place_ref[j] * HEAD_DIM, HEAD_DIM), HEAD_DIM)
            summed = lax.dot_general(
                value_held[:, column],
                weight_held[j],
                (((0,), (0,)), ((), ())),
                preferred_element_type=jnp.float32,
            )
            out_ref[j] = summed.T.astype(jnp.bfloat16)
            return 0

        lax.fori_loop(0, kv_heads, one_sum, 0)

    anywhere = pl.BlockSpec(memory_space=pl.ANY)
    whole = pl.BlockSpec(memory_space=pltpu.VMEM)
    row = jax.ShapeDtypeStruct((kv_heads, 1, count), jnp.float32)
    return pl.pallas_call(
        body,
        in_specs=[pl.BlockSpec(memory_space=pltpu.SMEM)] * 3
        + [whole] * len(inputs)
        + [anywhere] * (4 + len(held.arrays)),
        out_specs=[whole] * 4,
        out_shape=[
            jax.ShapeDtypeStruct((kv_heads, count, HEAD_DIM), jnp.bfloat16),
            row,
            row,
            jax.ShapeDtypeStruct((held.step_count, held.columns), jnp.float32),
        ],
        scratch_shapes=[
            pltpu.VMEM((held.height, held.columns), jnp.float32),
            pltpu.VMEM((kv_heads, tokens, count), jnp.bfloat16),
            pltpu.VMEM((tokens, held.columns), jnp.bfloat16),
            pltpu.SemaphoreType.DMA((1,)),
            *held.scratch,
        ],
        compiler_params=pltpu.CompilerParams(vmem_limit_bytes=57 * MIB),
        cost_estimate=LIGHT,
    )(places, turns, blocks, *inputs, prompt, got, steps, early, *held.arrays)


def out_project(blocks, heads, weight, width):
    def body(block_ref, head_ref, weight_ref, out_ref):
        for i in range(blocks.shape[0]):
            start = pl.multiple_of(block_ref[i] * width, width)
            out_ref[:, i * width : (i + 1) * width] = jnp.dot(
                head_ref[...], weight_ref[:, pl.ds(start, width)], preferred_element_type=jnp.float32
            ).astype(jnp.bfloat16)

    whole = pl.BlockSpec(memory_space=pltpu.VMEM)
    return pl.pallas_call(
        body,
        in_specs=[pl.BlockSpec(memory_space=pltpu.SMEM), whole, whole],
        out_specs=whole,
        out_shape=jax.ShapeDtypeStruct((heads.shape[0], weight.shape[1]), jnp.bfloat16),
        compiler_params=pltpu.CompilerParams(vmem_limit_bytes=10 * MIB),
        cost_estimate=LIGHT,
    )(blocks, heads, weight)


def on_device(
    prompt_states,
    page_table,
    step_states,
    sample_order,
    key_weight,
    value_weight,
    query_weight,
    out_weight,
):
    devices = lax.axis_size("sample")
    groups = lax.axis_size("groups")
    own_index = lax.axis_index("sample")
    first = lax.axis_index("groups") % 2 == 0
    deep = devices // LINE
    own_a, own_b, own_c = own_index // LINE, own_index // 2 % 2, own_index % 2
    along_ring, along_z, along_y, along_x, in_chip = mover(groups, devices)
    row_count = prompt_states.shape[0]
    chip_rows = 2 * row_count
    pages_here = row_count // PAGE
    heads_here = query_weight.shape[1] // HEAD_DIM
    total_pages = page_table.shape[0]
    prompts = total_pages // PROMPT_PAGES
    samples = sample_order.shape[0]
    steps = 2 * samples
    group_size = samples // prompts
    own_kv = own_index * heads_here // GQA
    wide_states = step_states.reshape(steps, D)
    rows = heads_here * steps
    width = key_weight.shape[0]
    half = key_weight.shape[1] // 2
    kv_places = jnp.where(first, 0, KV_HEADS // 2) + jnp.arange(KV_HEADS, dtype=jnp.int32)
    kv_places = kv_places % KV_HEADS

    order = ring_order(deep)

    def by_place(table):
        return sum(jnp.where(own_a == a, table[a], 0) for a in range(deep))

    own_turn = by_place([order.index(a) for a in range(deep)])

    def block(place_z, flip, core):
        return place_z * LINE + (own_b ^ flip) * 2 + core

    def behind(k):
        return by_place([order[(order.index(a) - k) % deep] for a in range(deep)])

    def halves(weight):
        low, high = weight[:, :half], weight[:, half:]
        return jnp.where(first, low, high), jnp.where(first, high, low)

    key_mine, key_other = halves(key_weight)
    value_mine, value_other = halves(value_weight)

    step_place = PROMPT_PAGES * PAGE + jnp.arange(2, dtype=jnp.int32)
    step_tables = tuple(t[:, None, :] for t in rope_tables(step_place))
    flat_tables = [
        jnp.repeat(jnp.concatenate([sign * table, table], axis=-1)[:, 0], samples, axis=0)
        for sign, table in zip((1, -1), step_tables)
    ]
    queries = project_queries(wide_states, query_weight, *flat_tables)
    packed_queries = jnp.concatenate(
        jnp.split(queries, half // queries.shape[1], axis=0), axis=1
    )
    packed = packed_queries.shape[0]
    queries = queries.reshape(2, samples, heads_here, HEAD_DIM)

    own_pages = jnp.concatenate(
        [
            holder * pages_here + jnp.arange(pages_here, dtype=jnp.int32)
            for holder in (own_index, own_index ^ 1)
        ]
    )
    slots = jnp.sum(
        jnp.where(
            page_table[None, :] == own_pages[:, None],
            jnp.arange(total_pages, dtype=jnp.int32)[None, :],
            0,
        ),
        axis=1,
    )
    positions = (slots % PROMPT_PAGES * PAGE)[:, None] + jnp.arange(PAGE, dtype=jnp.int32)[None, :]
    cosine, sine_part = rope_tables(positions.reshape(chip_rows))

    places = [(k, flip) for k in range(deep) for flip in (0, 1)]
    own_blocks = jnp.stack([block(behind(k), flip, own_c) for k, flip in places])
    query_turns = jnp.stack([(own_turn + deep - order.index(a)) % deep for a in range(deep)])
    own_place = (own_kv + jnp.where(first, 0, KV_HEADS // 2)) % KV_HEADS * HEAD_DIM
    prepared = (cosine, sine_part, kv_places, query_turns)
    done = {}

    def send(move, value):
        moved = done.setdefault(move, [])
        moved.append(move(after(value, moved[-2]) if len(moved) > 1 else value))
        return moved[-1]

    got = in_chip(prompt_states)
    key_z, mine, theirs = {0: key_mine}, {0: value_mine}, {}
    key_z[1] = send(along_ring, key_z[0])
    mine[1] = send(along_ring, mine[0])
    value_y = send(along_y, value_mine)
    key_full = {0: jnp.concatenate([key_mine, key_other, packed_queries])}
    key_y = {0: send(along_y, after(key_full[0], (value_y, key_z[1])))}
    theirs[0] = jnp.concatenate([value_y, packed_queries, key_y[0][2 * width :]])
    mine_x, theirs_x = {0: value_other}, {}
    for k in range(1, deep):
        swapped = send(along_x, after(key_z[k], packed_queries))
        mine_x[k] = send(along_x, mine[k])
        if k == 1:
            theirs_x[0] = send(along_x, value_y)
        if k + 1 < deep:
            key_z[k + 1] = send(along_ring, key_z[k])
            mine[k + 1] = send(along_ring, mine[k])
        key_full[k] = jnp.concatenate([key_z[k], swapped])
        key_y[k] = send(along_y, after(key_full[k], (key_y[k - 1], prepared if k == 2 else ())))
    for k in range(1, deep):
        theirs[k] = send(along_ring, theirs[k - 1])
        theirs_x[k] = send(along_x, theirs[k])

    ring_queries = collect([theirs[k] for k in range(deep)], width, 2 * packed)
    ring_queries = [ring_queries, in_chip(ring_queries)]
    by_owner = (deep, 2, 2, rows)

    key_pieces = [
        [((key_y if flip else key_full)[k], start) for start in (0, width)] for k, flip in places
    ]
    value_pieces = [
        [((theirs if flip else mine)[k], 0), ((theirs_x if flip else mine_x)[k], 0)]
        for k, flip in places
    ]

    def project_blocks(pieces, which, ready, kind):
        taken = after(jnp.stack([own_blocks[i] for i in which]), ready)
        return project(
            prompt_states, got, wide_states, taken, width, [pieces[i] for i in which], kind
        )

    key_sum = project_blocks(
        key_pieces, range(2 * deep), (theirs[deep - 1], [theirs_x[k] for k in range(1, deep - 1)]), jnp.bfloat16
    )
    early = [*range(0, 2 * deep, 2), 1]
    late = [i for i in range(2 * deep) if i not in early]
    value_early = project_blocks(value_pieces, early, key_sum, jnp.float32)
    key_back = in_chip(key_sum)

    def own_head(sums):
        sums = lax.dynamic_slice_in_dim(sums, own_place, HEAD_DIM, 1)
        return sums.reshape(2, samples, HEAD_DIM).astype(jnp.float32)

    new_keys = own_head(key_sum[chip_rows:]) + own_head(key_back[chip_rows:])
    new_keys = turn(new_keys, step_tables).astype(jnp.bfloat16)
    masks = []
    if prompts > 1:
        token_prompt = jnp.repeat(slots // PROMPT_PAGES, PAGE)
        row_prompt = jnp.tile(sample_order // group_size, devices // KV_HEADS * rows // samples)
        masks = [token_prompt[:, None], row_prompt[None, :]]
    partial, top, total, step_values = attend(
        kv_places, query_turns, ring_queries, key_sum, key_back, cosine, sine_part, masks,
        prompt_states, got, wide_states, jnp.stack([own_blocks[i] for i in late]), width,
        [value_pieces[i] for i in late], value_early,
    )
    new_values = own_head(step_values) + own_head(in_chip(step_values))
    new_values = new_values.astype(jnp.bfloat16)

    def narrow(value):
        return value.astype(jnp.bfloat16)

    def wide(value):
        return value.astype(jnp.float32)

    def to_z(value, k):
        return lax.dynamic_index_in_dim(value, (own_a + k) % deep, 0, False)

    stats = jnp.stack([top.reshape(by_owner)[:, 0], total.reshape(by_owner)[:, 0]], axis=2)
    partial = partial.reshape(by_owner + (HEAD_DIM,))
    near = stats[:, 0]
    far = along_y(stats[:, 1])
    top = jnp.maximum(near[:, 0], far[:, 0])
    near_factor, far_factor = jnp.exp(near[:, 0] - top), jnp.exp(far[:, 0] - top)
    stats = jnp.stack([top, near[:, 1] * near_factor + far[:, 1] * far_factor], axis=1)
    stats = jnp.stack([to_z(stats, 0)] + [along_z(to_z(stats, k), k) for k in range(1, deep)])
    prefix_top = jnp.max(stats[:, 0], axis=0)
    factors = jnp.exp(stats[:, 0] - prefix_top)
    prefix_total = jnp.sum(stats[:, 1] * factors, axis=0)

    partial = narrow(wide(partial[:, 0]) + wide(in_chip(partial[:, 1])))
    partial = narrow(
        wide(partial[:, 0]) * near_factor[..., None]
        + wide(along_y(partial[:, 1])) * far_factor[..., None]
    )
    prefix_sum = wide(to_z(partial, 0)) * factors[0][:, None]
    for k in range(1, deep):
        prefix_sum = prefix_sum + wide(along_z(to_z(partial, k), k)) * factors[k][:, None]

    by_head = (heads_here, 2, samples)
    head_out = finish_heads(
        prefix_top.reshape(by_head).swapaxes(0, 1),
        prefix_total.reshape(by_head).swapaxes(0, 1),
        prefix_sum.reshape(by_head + (HEAD_DIM,)).swapaxes(0, 1),
        queries.transpose(0, 2, 1, 3),
        new_keys[:, None],
        new_values[:, None],
    )
    flat_heads = head_out.transpose(0, 2, 1, 3).reshape(steps, heads_here * HEAD_DIM)

    out_width = out_weight.shape[1] // devices
    out_blocks = jnp.stack(
        [
            block((own_a + k) % deep, flip, own_c ^ turned)
            for turned in (0, 1)
            for flip in (0, 1)
            for k in range(deep)
        ]
    )
    terms = out_project(out_blocks, flat_heads, out_weight, out_width)
    for move in (in_chip, along_y):
        share = terms.shape[1] // 2
        terms = narrow(wide(terms[:, :share]) + wide(move(terms[:, share:])))
    attn_out = wide(terms[:, :out_width])
    for k in range(1, deep):
        attn_out = attn_out + wide(along_z(terms[:, k * out_width : (k + 1) * out_width], k))
    return narrow(attn_out).reshape(2, samples, -1)


def solution(mesh):
    in_specs = (
        P(("groups", "sample"), None),
        P("groups"),
        P(None, "groups", None),
        P("groups"),
        P("sample", None),
        P("sample", None),
        P(None, "sample"),
        P("sample", None),
    )
    out_specs = P(None, "groups", "sample")
    return jax.shard_map(
        on_device, mesh=mesh, in_specs=in_specs, out_specs=out_specs, check_vma=False
    )
```

```python
import jax
import jax.numpy as jnp
from jax import lax
from jax.experimental import pallas as pl
from jax.experimental.pallas import tpu as pltpu
from jax.sharding import PartitionSpec as P

D = 8192
HEAD_DIM = 128
KV_HEADS = 4
GQA = 8
PAGE = 128
PROMPT_PAGES = 64
LINE = 4

rope_base = 1000000.0


def rope_tables(position):
    half_dim = HEAD_DIM // 2
    frequency = rope_base ** (-jnp.arange(half_dim, dtype=jnp.float32) * 2.0 / HEAD_DIM)
    angles = position.astype(jnp.float32)[..., None] * frequency
    return jnp.cos(angles), jnp.sin(angles)


def turn(vector, tables):
    cosine, sine_part = tables
    half_dim = HEAD_DIM // 2
    first_half = vector[..., :half_dim]
    second_half = vector[..., half_dim:]
    return jnp.concatenate(
        [
            first_half * cosine - second_half * sine_part,
            second_half * cosine + first_half * sine_part,
        ],
        axis=-1,
    )


def ring_order(deep):
    return [*range(0, deep, 2), *range(deep - 1 - deep % 2, 0, -2)]


def mover(groups, devices):
    deep = devices // LINE
    order = ring_order(deep)

    def move(value, step):
        pairs = []
        for g in range(groups):
            for s in range(devices):
                a, b, c = s // LINE, s // 2 % 2, s % 2
                to_g, to_a, to_b, to_c = step(g, a, b, c)
                to_s = (to_a % deep) * LINE + to_b * 2 + to_c
                pairs.append((g * devices + s, to_g * devices + to_s))
        return lax.ppermute(value, ("groups", "sample"), pairs)

    def next_on_ring(a):
        return order[(order.index(a) + 1) % deep]

    along_ring = lambda v: move(v, lambda g, a, b, c: (g, next_on_ring(a), b, c))
    along_z = lambda v, k: move(v, lambda g, a, b, c: (g, a + k, b, c))
    along_y = lambda v: move(v, lambda g, a, b, c: (g, a, 1 - b, c))
    along_x = lambda v: move(v, lambda g, a, b, c: (g ^ 1, a, b, c))
    in_chip = lambda v: move(v, lambda g, a, b, c: (g, a, b, 1 - c))
    return along_ring, along_z, along_y, along_x, in_chip


def after(value, done):
    return lax.optimization_barrier((value, done))[0]


MIB = 1024 * 1024
LIGHT = pl.CostEstimate(flops=1, bytes_accessed=1, transcendentals=0)


def project_queries(steps, weight, cosine, sine):
    count, depth = steps.shape
    parts = 8
    piece = depth // parts

    def body(step_ref, weight_ref, cosine_ref, sine_ref, out_ref, held, sems):
        copies = []
        for i in range(parts):
            copies.append(
                pltpu.make_async_copy(
                    weight_ref.at[pl.ds(i * piece, piece), :], held.at[i], sems.at[i]
                )
            )
            copies[-1].start()
        total = None
        for i in range(parts):
            copies[i].wait()
            product = jnp.dot(
                step_ref[:, i * piece : (i + 1) * piece],
                held[i],
                preferred_element_type=jnp.float32,
            )
            total = product if total is None else total + product
        for start in range(0, weight.shape[1], HEAD_DIM):
            head = total[:, start : start + HEAD_DIM]
            turned = head * cosine_ref[...] + pltpu.roll(head, HEAD_DIM // 2, 1) * sine_ref[...]
            out_ref[:, start : start + HEAD_DIM] = turned.astype(jnp.bfloat16)

    whole = pl.BlockSpec(memory_space=pltpu.VMEM)
    return pl.pallas_call(
        body,
        in_specs=[whole, pl.BlockSpec(memory_space=pltpu.HBM), whole, whole],
        out_specs=whole,
        out_shape=jax.ShapeDtypeStruct((count, weight.shape[1]), jnp.bfloat16),
        scratch_shapes=[
            pltpu.VMEM((parts, piece, weight.shape[1]), weight.dtype),
            pltpu.SemaphoreType.DMA((parts,)),
        ],
        compiler_params=pltpu.CompilerParams(vmem_limit_bytes=10 * MIB),
        cost_estimate=LIGHT,
    )(steps, weight, cosine, sine)


def collect(arrays, first, height):
    columns = arrays[0].shape[1]

    def body(*refs):
        out_ref, sems = refs[-2:]
        copies = [
            pltpu.make_async_copy(ref.at[pl.ds(first, height), :], out_ref.at[i], sems.at[i])
            for i, ref in enumerate(refs[:-2])
        ]
        for copy in copies:
            copy.start()
        for copy in copies:
            copy.wait()

    return pl.pallas_call(
        body,
        in_specs=[pl.BlockSpec(memory_space=pl.ANY)] * len(arrays),
        out_specs=pl.BlockSpec(memory_space=pltpu.VMEM),
        out_shape=jax.ShapeDtypeStruct((len(arrays), height, columns), arrays[0].dtype),
        scratch_shapes=[pltpu.SemaphoreType.DMA((len(arrays),))],
        compiler_params=pltpu.CompilerParams(vmem_limit_bytes=4 * MIB),
        cost_estimate=LIGHT,
    )(*arrays)


class Blocks:
    def __init__(self, prompt, steps, width, pieces):
        self.arrays = []
        for piece in pieces:
            for array, _ in piece:
                if not any(array is held for held in self.arrays):
                    self.arrays.append(array)
        self.pieces, self.width, self.count = pieces, width, len(pieces)
        self.row_count, self.step_count = prompt.shape[0], steps.shape[0]
        self.height = 2 * self.row_count + self.step_count
        self.columns = sum(array.shape[1] for array, _ in pieces[0])
        self.scratch = [
            pltpu.VMEM((self.count, self.height, width), prompt.dtype),
            pltpu.VMEM((self.count, width, self.columns), prompt.dtype),
            pltpu.SemaphoreType.DMA((self.count, 5)),
        ]

    def copies(self, i, block_ref, sources, weight_refs, scratch):
        left, weights, sems = scratch
        column = pl.ds(pl.multiple_of(block_ref[i] * self.width, self.width), self.width)
        group = []
        start = 0
        for j, (source, rows) in enumerate(
            zip(sources, (self.row_count, self.row_count, self.step_count))
        ):
            group.append(
                pltpu.make_async_copy(
                    source.at[:, column], left.at[i, pl.ds(start, rows), :], sems.at[i, j]
                )
            )
            start += rows
        side = 0
        for j, (array, first) in enumerate(self.pieces[i]):
            ref = weight_refs[[array is other for other in self.arrays].index(True)]
            group.append(
                pltpu.make_async_copy(
                    ref.at[pl.ds(first, self.width), :],
                    weights.at[i, :, pl.ds(side, array.shape[1])],
                    sems.at[i, 3 + j],
                )
            )
            side += array.shape[1]
        return group


AHEAD = 3


def project(prompt, got, steps, blocks, width, pieces, kind):
    held = Blocks(prompt, steps, width, pieces)

    def body(block_ref, prompt_ref, got_ref, step_ref, *refs):
        weight_refs = refs[: len(held.arrays)]
        out_ref, *scratch = refs[len(held.arrays) :]
        left, weights, _ = scratch
        sources = (prompt_ref, got_ref, step_ref)
        groups = [
            held.copies(i, block_ref, sources, weight_refs, scratch) for i in range(held.count)
        ]
        for group in groups[:AHEAD]:
            for copy in group:
                copy.start()
        total = None
        for i, group in enumerate(groups):
            for copy in group:
                copy.wait()
            if i + AHEAD < held.count:
                for copy in groups[i + AHEAD]:
                    copy.start()
            product = jnp.dot(left[i], weights[i], preferred_element_type=jnp.float32)
            total = product if total is None else total + product
        out_ref[...] = total.astype(kind)

    anywhere = pl.BlockSpec(memory_space=pl.ANY)
    return pl.pallas_call(
        body,
        in_specs=[pl.BlockSpec(memory_space=pltpu.SMEM)] + [anywhere] * (3 + len(held.arrays)),
        out_specs=pl.BlockSpec(memory_space=pltpu.VMEM),
        out_shape=jax.ShapeDtypeStruct((held.height, held.columns), kind),
        scratch_shapes=held.scratch,
        compiler_params=pltpu.CompilerParams(vmem_limit_bytes=57 * MIB),
        cost_estimate=LIGHT,
    )(blocks, prompt, got, steps, *held.arrays)


NOTES = 16


def thirds(value):
    parts = []
    for _ in range(3):
        parts.append(value.astype(jnp.bfloat16))
        value = value - parts[-1].astype(jnp.float32)
    return parts


def note_rows(top, total):
    parts = [part.astype(jnp.float32) for part in thirds(top) + thirds(total)]
    rows = jnp.concatenate(parts + [jnp.zeros((NOTES - 6, top.shape[1]), jnp.float32)], axis=0)
    return rows.astype(jnp.bfloat16)


def read_notes(rows):
    rows = rows.astype(jnp.float32)
    return rows[0:1] + rows[1:2] + rows[2:3], rows[3:4] + rows[4:5] + rows[5:6]


def small_call(body, out_shapes, scalars, arrays):
    whole = pl.BlockSpec(memory_space=pltpu.VMEM)
    return pl.pallas_call(
        body,
        in_specs=[pl.BlockSpec(memory_space=pltpu.SMEM)] * len(scalars) + [whole] * len(arrays),
        out_specs=[whole] * len(out_shapes),
        out_shape=[jax.ShapeDtypeStruct(shape, jnp.bfloat16) for shape in out_shapes],
        compiler_params=pltpu.CompilerParams(vmem_limit_bytes=12 * MIB),
        cost_estimate=LIGHT,
    )(*scalars, *arrays)


def merge_cores(own, other):
    deep, _, _, height, lanes = own.shape

    def body(own_ref, other_ref, near_ref, far_ref):
        for z in range(deep):
            for y, out_ref in enumerate((near_ref, far_ref)):
                both = own_ref[z, 0, y, :HEAD_DIM, :].astype(jnp.float32) + other_ref[
                    z, y, :HEAD_DIM, :
                ].astype(jnp.float32)
                out_ref[z, :HEAD_DIM, :] = both.astype(jnp.bfloat16)
                out_ref[z, HEAD_DIM:, :] = own_ref[z, 0, y, HEAD_DIM:, :]

    return small_call(body, [(deep, height, lanes)] * 2, [], [own, other])


def merge_chips(own_place, near, far):
    deep, height, lanes = near.shape

    def body(place_ref, near_ref, far_ref, *out_refs):
        for k, out_ref in enumerate(out_refs):
            z = lax.rem(place_ref[0] + k, deep)
            first, second = near_ref[z], far_ref[z]
            first_top, first_total = read_notes(first[HEAD_DIM:, :])
            second_top, second_total = read_notes(second[HEAD_DIM:, :])
            top = jnp.maximum(first_top, second_top)
            first_factor, second_factor = jnp.exp(first_top - top), jnp.exp(second_top - top)
            out_ref[:HEAD_DIM, :] = (
                first[:HEAD_DIM, :].astype(jnp.float32) * first_factor
                + second[:HEAD_DIM, :].astype(jnp.float32) * second_factor
            ).astype(jnp.bfloat16)
            out_ref[HEAD_DIM:, :] = note_rows(
                top, first_total * first_factor + second_total * second_factor
            )

    return small_call(body, [(height, lanes)] * deep, [own_place], [near, far])


def attend(
    places, turns, queries, own, other, cosine, sine, masks, prompt, got, steps, blocks, width,
    pieces, early,
):
    kv_heads = places.shape[0]
    deep, packed, lanes = queries[0].shape
    share = deep // kv_heads
    count = 2 * share * packed * lanes // HEAD_DIM
    owners = count // HEAD_DIM
    tokens = cosine.shape[0]
    half = tokens // 2
    held = Blocks(prompt, steps, width, pieces)
    inputs = [*queries, own, other, cosine, sine, *masks]

    def body(place_ref, turn_ref, block_ref, *refs):
        query_refs = refs[:2]
        own_ref, other_ref, cosine_ref, sine_ref = refs[2:6]
        mask_refs = refs[6 : len(inputs)]
        prompt_ref, got_ref, step_ref, early_ref = refs[len(inputs) : len(inputs) + 4]
        rest = refs[len(inputs) + 4 :]
        weight_refs, rest = rest[: len(held.arrays)], rest[len(held.arrays) :]
        out_ref, step_out_ref = rest[:2]
        early_held, weight_held, value_held, early_sem, *scratch = rest[2:]
        left, weight_rows, _ = scratch
        sources = (prompt_ref, got_ref, step_ref)
        groups = [
            held.copies(i, block_ref, sources, weight_refs, scratch) for i in range(held.count)
        ]
        before = pltpu.make_async_copy(early_ref, early_held, early_sem.at[0])
        before.start()
        for group in groups:
            for copy in group:
                copy.start()
        wide_cosine = jnp.concatenate([cosine_ref[...], cosine_ref[...]], axis=1)
        wide_sine = jnp.concatenate([-sine_ref[...], sine_ref[...]], axis=1)

        def one_head(j, _):
            column = pl.ds(pl.multiple_of(place_ref[j] * HEAD_DIM, HEAD_DIM), HEAD_DIM)
            keys = jnp.concatenate(
                [
                    own_ref[:half, column].astype(jnp.float32)
                    + other_ref[half:tokens, column].astype(jnp.float32),
                    own_ref[half:tokens, column].astype(jnp.float32)
                    + other_ref[:half, column].astype(jnp.float32),
                ],
                axis=0,
            )
            swapped = pltpu.roll(keys, HEAD_DIM // 2, 1)
            keys = (keys * wide_cosine + swapped * wide_sine).astype(jnp.bfloat16)
            unpacked = []
            for part in range(share):
                for ref in query_refs:
                    both = ref[turn_ref[j * share + part]]
                    for low in range(0, packed, packed // 2):
                        for left_lane in range(0, lanes, HEAD_DIM):
                            unpacked.append(
                                both[low : low + packed // 2, left_lane : left_lane + HEAD_DIM]
                            )
            scores = lax.dot_general(
                keys,
                jnp.concatenate(unpacked, axis=0),
                (((1,), (1,)), ((), ())),
                preferred_element_type=jnp.float32,
            ) * (HEAD_DIM**-0.5)
            if masks:
                scores = jnp.where(mask_refs[0][...] == mask_refs[1][...], scores, -1e30)
            top = jnp.max(scores, axis=0, keepdims=True)
            weights = jnp.exp(scores - top)
            total = jnp.sum(weights, axis=0, keepdims=True)
            for i in range(owners):
                lane = slice(i * HEAD_DIM, (i + 1) * HEAD_DIM)
                out_ref[j, i, HEAD_DIM:, :] = note_rows(top[:, lane], total[:, lane])
            weight_held[j] = weights.astype(jnp.bfloat16)
            return 0

        lax.fori_loop(0, kv_heads, one_head, 0)
        before.wait()
        total = early_held[...]
        for i, group in enumerate(groups):
            for copy in group:
                copy.wait()
            total += jnp.dot(left[i], weight_rows[i], preferred_element_type=jnp.float32)
        value_held[...] = total[:tokens].astype(jnp.bfloat16)
        step_out_ref[...] = total[tokens:]

        def one_sum(j, _):
            column = pl.ds(pl.multiple_of(place_ref[j] * HEAD_DIM, HEAD_DIM), HEAD_DIM)
            summed = lax.dot_general(
                value_held[:, column],
                weight_held[j],
                (((0,), (0,)), ((), ())),
                preferred_element_type=jnp.float32,
            )
            for i in range(owners):
                lane = slice(i * HEAD_DIM, (i + 1) * HEAD_DIM)
                out_ref[j, i, :HEAD_DIM, :] = summed[:, lane].astype(jnp.bfloat16)
            return 0

        lax.fori_loop(0, kv_heads, one_sum, 0)

    anywhere = pl.BlockSpec(memory_space=pl.ANY)
    whole = pl.BlockSpec(memory_space=pltpu.VMEM)
    return pl.pallas_call(
        body,
        in_specs=[pl.BlockSpec(memory_space=pltpu.SMEM)] * 3
        + [whole] * len(inputs)
        + [anywhere] * (4 + len(held.arrays)),
        out_specs=[whole] * 2,
        out_shape=[
            jax.ShapeDtypeStruct((kv_heads, owners, HEAD_DIM + NOTES, HEAD_DIM), jnp.bfloat16),
            jax.ShapeDtypeStruct((held.step_count, held.columns), jnp.float32),
        ],
        scratch_shapes=[
            pltpu.VMEM((held.height, held.columns), jnp.float32),
            pltpu.VMEM((kv_heads, tokens, count), jnp.bfloat16),
            pltpu.VMEM((tokens, held.columns), jnp.bfloat16),
            pltpu.SemaphoreType.DMA((1,)),
            *held.scratch,
        ],
        compiler_params=pltpu.CompilerParams(vmem_limit_bytes=57 * MIB),
        cost_estimate=LIGHT,
    )(places, turns, blocks, *inputs, prompt, got, steps, early, *held.arrays)


def out_project(blocks, parts, queries, new_keys, new_values, weight, width):
    count = len(parts)
    steps = queries.shape[0]
    samples = steps // 2

    def body(block_ref, *refs):
        part_refs = refs[:count]
        query_ref, key_ref, value_ref, weight_ref, out_ref = refs[count:]
        notes = [read_notes(ref[HEAD_DIM:, :]) for ref in part_refs]
        top = notes[0][0]
        for other, _ in notes[1:]:
            top = jnp.maximum(top, other)
        sums = total = 0.0
        for ref, (part_top, part_total) in zip(part_refs, notes):
            factor = jnp.exp(part_top - top)
            sums = sums + ref[:HEAD_DIM, :].astype(jnp.float32) * factor
            total = total + part_total * factor
        sums = sums.T
        both = jnp.concatenate([top, total, jnp.zeros((6, HEAD_DIM), jnp.float32)], axis=0).T
        keys, values = key_ref[...], value_ref[...]
        heads = []
        for h in range(queries.shape[1] // HEAD_DIM):
            query = query_ref[:, h * HEAD_DIM : (h + 1) * HEAD_DIM].astype(jnp.float32)
            own_score = jnp.sum(query * keys, axis=1, keepdims=True) * (HEAD_DIM**-0.5)
            back_score = jnp.sum(
                query[samples:] * keys[:samples], axis=1, keepdims=True
            ) * (HEAD_DIM**-0.5)
            ends = []
            for step in (0, 1):
                place = slice((2 * h + step) * samples, (2 * h + step + 1) * samples)
                here = slice(step * samples, (step + 1) * samples)
                old_top, old_total = both[place, 0:1], both[place, 1:2]
                scores = [(own_score[here], values[here])]
                if step:
                    scores.append((back_score, values[:samples]))
                high = old_top
                for score, _ in scores:
                    high = jnp.maximum(high, score)
                old = jnp.exp(old_top - high)
                numerator, denominator = old * sums[place], old * old_total
                for score, value in scores:
                    new = jnp.exp(score - high)
                    numerator, denominator = numerator + new * value, denominator + new
                ends.append(numerator / denominator)
            heads.append(jnp.concatenate(ends, axis=0).astype(jnp.bfloat16))
        heads = jnp.concatenate(heads, axis=1)
        for i in range(blocks.shape[0]):
            start = pl.multiple_of(block_ref[i] * width, width)
            out_ref[:, i * width : (i + 1) * width] = jnp.dot(
                heads, weight_ref[:, pl.ds(start, width)], preferred_element_type=jnp.float32
            ).astype(jnp.bfloat16)

    return small_call(
        body, [(steps, weight.shape[1])], [blocks], [*parts, queries, new_keys, new_values, weight]
    )[0]


def on_device(
    prompt_states,
    page_table,
    step_states,
    sample_order,
    key_weight,
    value_weight,
    query_weight,
    out_weight,
):
    devices = lax.axis_size("sample")
    groups = lax.axis_size("groups")
    own_index = lax.axis_index("sample")
    first = lax.axis_index("groups") % 2 == 0
    deep = devices // LINE
    own_a, own_b, own_c = own_index // LINE, own_index // 2 % 2, own_index % 2
    along_ring, along_z, along_y, along_x, in_chip = mover(groups, devices)
    row_count = prompt_states.shape[0]
    chip_rows = 2 * row_count
    pages_here = row_count // PAGE
    heads_here = query_weight.shape[1] // HEAD_DIM
    total_pages = page_table.shape[0]
    prompts = total_pages // PROMPT_PAGES
    samples = sample_order.shape[0]
    steps = 2 * samples
    group_size = samples // prompts
    own_kv = own_index * heads_here // GQA
    wide_states = step_states.reshape(steps, D)
    rows = heads_here * steps
    width = key_weight.shape[0]
    half = key_weight.shape[1] // 2
    kv_places = jnp.where(first, 0, KV_HEADS // 2) + jnp.arange(KV_HEADS, dtype=jnp.int32)
    kv_places = kv_places % KV_HEADS

    order = ring_order(deep)

    def by_place(table):
        return sum(jnp.where(own_a == a, table[a], 0) for a in range(deep))

    own_turn = by_place([order.index(a) for a in range(deep)])

    def block(place_z, flip, core):
        return place_z * LINE + (own_b ^ flip) * 2 + core

    def behind(k):
        return by_place([order[(order.index(a) - k) % deep] for a in range(deep)])

    def halves(weight):
        low, high = weight[:, :half], weight[:, half:]
        return jnp.where(first, low, high), jnp.where(first, high, low)

    key_mine, key_other = halves(key_weight)
    value_mine, value_other = halves(value_weight)

    step_place = PROMPT_PAGES * PAGE + jnp.arange(2, dtype=jnp.int32)
    step_tables = tuple(t[:, None, :] for t in rope_tables(step_place))
    flat_tables = [
        jnp.repeat(jnp.concatenate([sign * table, table], axis=-1)[:, 0], samples, axis=0)
        for sign, table in zip((1, -1), step_tables)
    ]
    queries = project_queries(wide_states, query_weight, *flat_tables)
    packed_queries = jnp.concatenate(
        jnp.split(queries, half // queries.shape[1], axis=0), axis=1
    )
    packed = packed_queries.shape[0]

    own_pages = jnp.concatenate(
        [
            holder * pages_here + jnp.arange(pages_here, dtype=jnp.int32)
            for holder in (own_index, own_index ^ 1)
        ]
    )
    slots = jnp.sum(
        jnp.where(
            page_table[None, :] == own_pages[:, None],
            jnp.arange(total_pages, dtype=jnp.int32)[None, :],
            0,
        ),
        axis=1,
    )
    positions = (slots % PROMPT_PAGES * PAGE)[:, None] + jnp.arange(PAGE, dtype=jnp.int32)[None, :]
    cosine, sine_part = rope_tables(positions.reshape(chip_rows))

    places = [(k, flip) for k in range(deep) for flip in (0, 1)]
    own_blocks = jnp.stack([block(behind(k), flip, own_c) for k, flip in places])
    query_turns = jnp.stack([(own_turn + deep - order.index(a)) % deep for a in range(deep)])
    own_place = (own_kv + jnp.where(first, 0, KV_HEADS // 2)) % KV_HEADS * HEAD_DIM
    prepared = (cosine, sine_part, kv_places, query_turns)
    done = {}

    def send(move, value):
        moved = done.setdefault(move, [])
        moved.append(move(after(value, moved[-2]) if len(moved) > 1 else value))
        return moved[-1]

    got = in_chip(prompt_states)
    key_z, mine, theirs = {0: key_mine}, {0: value_mine}, {}
    key_z[1] = send(along_ring, key_z[0])
    mine[1] = send(along_ring, mine[0])
    value_y = send(along_y, value_mine)
    key_full = {0: jnp.concatenate([key_mine, key_other, packed_queries])}
    key_y = {0: send(along_y, after(key_full[0], (value_y, key_z[1])))}
    theirs[0] = jnp.concatenate([value_y, packed_queries, key_y[0][2 * width :]])
    mine_x, theirs_x = {0: value_other}, {}
    for k in range(1, deep):
        swapped = send(along_x, after(key_z[k], packed_queries))
        mine_x[k] = send(along_x, mine[k])
        if k == 1:
            theirs_x[0] = send(along_x, value_y)
        if k + 1 < deep:
            key_z[k + 1] = send(along_ring, key_z[k])
            mine[k + 1] = send(along_ring, mine[k])
        key_full[k] = jnp.concatenate([key_z[k], swapped])
        key_y[k] = send(along_y, after(key_full[k], (key_y[k - 1], prepared if k == 2 else ())))
    for k in range(1, deep):
        theirs[k] = send(along_ring, theirs[k - 1])
        theirs_x[k] = send(along_x, theirs[k])

    ring_queries = collect([theirs[k] for k in range(deep)], width, 2 * packed)
    ring_queries = [ring_queries, in_chip(ring_queries)]
    by_owner = (deep, 2, 2, rows)

    key_pieces = [
        [((key_y if flip else key_full)[k], start) for start in (0, width)] for k, flip in places
    ]
    value_pieces = [
        [((theirs if flip else mine)[k], 0), ((theirs_x if flip else mine_x)[k], 0)]
        for k, flip in places
    ]

    def project_blocks(pieces, which, ready, kind):
        taken = after(jnp.stack([own_blocks[i] for i in which]), ready)
        return project(
            prompt_states, got, wide_states, taken, width, [pieces[i] for i in which], kind
        )

    early = [*range(0, 2 * deep, 2), 1]
    late = [i for i in range(2 * deep) if i not in early]
    value_early = project_blocks(value_pieces, early, (theirs_x[1], theirs[deep - 2]), jnp.float32)
    awaited = (value_early, theirs[deep - 1], [theirs_x[k] for k in range(1, deep - 1)])
    key_sum = project_blocks(key_pieces, range(2 * deep), awaited, jnp.bfloat16)
    key_back = in_chip(key_sum)

    def own_head(sums):
        sums = lax.dynamic_slice_in_dim(sums, own_place, HEAD_DIM, 1)
        return sums.reshape(2, samples, HEAD_DIM).astype(jnp.float32)

    new_keys = own_head(key_sum[chip_rows:]) + own_head(key_back[chip_rows:])
    new_keys = turn(new_keys, step_tables).astype(jnp.bfloat16).astype(jnp.float32)
    new_keys = new_keys.reshape(steps, HEAD_DIM)
    masks = []
    if prompts > 1:
        token_prompt = jnp.repeat(slots // PROMPT_PAGES, PAGE)
        row_prompt = jnp.tile(sample_order // group_size, devices // KV_HEADS * rows // samples)
        masks = [token_prompt[:, None], row_prompt[None, :]]
    partial, step_values = attend(
        kv_places, query_turns, ring_queries, key_sum, key_back, cosine, sine_part, masks,
        prompt_states, got, wide_states, jnp.stack([own_blocks[i] for i in late]), width,
        [value_pieces[i] for i in late], value_early,
    )
    new_values = own_head(step_values) + own_head(in_chip(step_values))
    new_values = new_values.astype(jnp.bfloat16).astype(jnp.float32).reshape(steps, HEAD_DIM)

    partial = partial.reshape(by_owner[:3] + partial.shape[2:])
    near, far = merge_cores(partial, in_chip(partial[:, 1]))
    merged = merge_chips(own_a[None], near, along_y(far))
    parts = [merged[0]] + [along_z(merged[k], k) for k in range(1, deep)]

    out_width = out_weight.shape[1] // devices
    out_blocks = jnp.stack(
        [
            block((own_a + k) % deep, flip, own_c ^ turned)
            for turned in (0, 1)
            for flip in (0, 1)
            for k in range(deep)
        ]
    )
    terms = out_project(out_blocks, parts, queries, new_keys, new_values, out_weight, out_width)

    def narrow(value):
        return value.astype(jnp.bfloat16)

    def wide(value):
        return value.astype(jnp.float32)

    for move in (in_chip, along_y):
        share = terms.shape[1] // 2
        terms = narrow(wide(terms[:, :share]) + wide(move(terms[:, share:])))
    attn_out = wide(terms[:, :out_width])
    for k in range(1, deep):
        attn_out = attn_out + wide(along_z(terms[:, k * out_width : (k + 1) * out_width], k))
    return narrow(attn_out).reshape(2, samples, -1)


def solution(mesh):
    in_specs = (
        P(("groups", "sample"), None),
        P("groups"),
        P(None, "groups", None),
        P("groups"),
        P("sample", None),
        P("sample", None),
        P(None, "sample"),
        P("sample", None),
    )
    out_specs = P(None, "groups", "sample")
    return jax.shard_map(
        on_device, mesh=mesh, in_specs=in_specs, out_specs=out_specs, check_vma=False
    )
```

```python
import jax
import jax.numpy as jnp
from jax import lax
from jax.experimental import pallas as pl
from jax.experimental.pallas import tpu as pltpu
from jax.sharding import PartitionSpec as P

D = 8192
HEAD_DIM = 128
KV_HEADS = 4
GQA = 8
PAGE = 128
PROMPT_PAGES = 64
LINE = 4

rope_base = 1000000.0


def rope_tables(position):
    half_dim = HEAD_DIM // 2
    frequency = rope_base ** (-jnp.arange(half_dim, dtype=jnp.float32) * 2.0 / HEAD_DIM)
    angles = position.astype(jnp.float32)[..., None] * frequency
    return jnp.cos(angles), jnp.sin(angles)


def turn(vector, tables):
    cosine, sine_part = tables
    half_dim = HEAD_DIM // 2
    first_half = vector[..., :half_dim]
    second_half = vector[..., half_dim:]
    return jnp.concatenate(
        [
            first_half * cosine - second_half * sine_part,
            second_half * cosine + first_half * sine_part,
        ],
        axis=-1,
    )


def ring_order(deep):
    return [*range(0, deep, 2), *range(deep - 1 - deep % 2, 0, -2)]


def mover(groups, devices):
    deep = devices // LINE
    order = ring_order(deep)

    def move(value, step):
        pairs = []
        for g in range(groups):
            for s in range(devices):
                a, b, c = s // LINE, s // 2 % 2, s % 2
                to_g, to_a, to_b, to_c = step(g, a, b, c)
                to_s = (to_a % deep) * LINE + to_b * 2 + to_c
                pairs.append((g * devices + s, to_g * devices + to_s))
        return lax.ppermute(value, ("groups", "sample"), pairs)

    def next_on_ring(a):
        return order[(order.index(a) + 1) % deep]

    along_ring = lambda v: move(v, lambda g, a, b, c: (g, next_on_ring(a), b, c))
    along_z = lambda v, k: move(v, lambda g, a, b, c: (g, a + k, b, c))
    along_y = lambda v: move(v, lambda g, a, b, c: (g, a, 1 - b, c))
    along_x = lambda v: move(v, lambda g, a, b, c: (g ^ 1, a, b, c))
    in_chip = lambda v: move(v, lambda g, a, b, c: (g, a, b, 1 - c))
    return along_ring, along_z, along_y, along_x, in_chip


def after(value, done):
    return lax.optimization_barrier((value, done))[0]


MIB = 1024 * 1024
LIGHT = pl.CostEstimate(flops=1, bytes_accessed=1, transcendentals=0)


def project_queries(steps, weight, cosine, sine):
    count, depth = steps.shape
    parts = 8
    piece = depth // parts

    def body(step_ref, weight_ref, cosine_ref, sine_ref, out_ref, held, sems):
        copies = []
        for i in range(parts):
            copies.append(
                pltpu.make_async_copy(
                    weight_ref.at[pl.ds(i * piece, piece), :], held.at[i], sems.at[i]
                )
            )
            copies[-1].start()
        total = None
        for i in range(parts):
            copies[i].wait()
            product = jnp.dot(
                step_ref[:, i * piece : (i + 1) * piece],
                held[i],
                preferred_element_type=jnp.float32,
            )
            total = product if total is None else total + product
        for start in range(0, weight.shape[1], HEAD_DIM):
            head = total[:, start : start + HEAD_DIM]
            turned = head * cosine_ref[...] + pltpu.roll(head, HEAD_DIM // 2, 1) * sine_ref[...]
            out_ref[:, start : start + HEAD_DIM] = turned.astype(jnp.bfloat16)

    whole = pl.BlockSpec(memory_space=pltpu.VMEM)
    return pl.pallas_call(
        body,
        in_specs=[whole, pl.BlockSpec(memory_space=pltpu.HBM), whole, whole],
        out_specs=whole,
        out_shape=jax.ShapeDtypeStruct((count, weight.shape[1]), jnp.bfloat16),
        scratch_shapes=[
            pltpu.VMEM((parts, piece, weight.shape[1]), weight.dtype),
            pltpu.SemaphoreType.DMA((parts,)),
        ],
        compiler_params=pltpu.CompilerParams(vmem_limit_bytes=10 * MIB),
        cost_estimate=LIGHT,
    )(steps, weight, cosine, sine)


def collect(arrays, first, height):
    columns = arrays[0].shape[1]

    def body(*refs):
        out_ref, sems = refs[-2:]
        copies = [
            pltpu.make_async_copy(ref.at[pl.ds(first, height), :], out_ref.at[i], sems.at[i])
            for i, ref in enumerate(refs[:-2])
        ]
        for copy in copies:
            copy.start()
        for copy in copies:
            copy.wait()

    return pl.pallas_call(
        body,
        in_specs=[pl.BlockSpec(memory_space=pl.ANY)] * len(arrays),
        out_specs=pl.BlockSpec(memory_space=pltpu.VMEM),
        out_shape=jax.ShapeDtypeStruct((len(arrays), height, columns), arrays[0].dtype),
        scratch_shapes=[pltpu.SemaphoreType.DMA((len(arrays),))],
        compiler_params=pltpu.CompilerParams(vmem_limit_bytes=4 * MIB),
        cost_estimate=LIGHT,
    )(*arrays)


class Blocks:
    def __init__(self, prompt, steps, width, pieces):
        self.arrays = []
        for piece in pieces:
            for array, _ in piece:
                if not any(array is held for held in self.arrays):
                    self.arrays.append(array)
        self.pieces, self.width, self.count = pieces, width, len(pieces)
        self.row_count, self.step_count = prompt.shape[0], steps.shape[0]
        self.height = 2 * self.row_count + self.step_count
        self.columns = sum(array.shape[1] for array, _ in pieces[0])
        self.scratch = [
            pltpu.VMEM((self.count, self.height, width), prompt.dtype),
            pltpu.VMEM((self.count, width, self.columns), prompt.dtype),
            pltpu.SemaphoreType.DMA((self.count, 5)),
        ]

    def copies(self, i, block_ref, sources, weight_refs, scratch):
        left, weights, sems = scratch
        column = pl.ds(pl.multiple_of(block_ref[i] * self.width, self.width), self.width)
        group = []
        start = 0
        for j, (source, rows) in enumerate(
            zip(sources, (self.row_count, self.row_count, self.step_count))
        ):
            group.append(
                pltpu.make_async_copy(
                    source.at[:, column], left.at[i, pl.ds(start, rows), :], sems.at[i, j]
                )
            )
            start += rows
        side = 0
        for j, (array, first) in enumerate(self.pieces[i]):
            ref = weight_refs[[array is other for other in self.arrays].index(True)]
            group.append(
                pltpu.make_async_copy(
                    ref.at[pl.ds(first, self.width), :],
                    weights.at[i, :, pl.ds(side, array.shape[1])],
                    sems.at[i, 3 + j],
                )
            )
            side += array.shape[1]
        return group


AHEAD = 3


def project(prompt, got, steps, blocks, width, pieces, acc, kind):
    held = Blocks(prompt, steps, width, pieces)
    extra = [] if acc is None else [acc]

    def body(block_ref, prompt_ref, got_ref, step_ref, *refs):
        weight_refs = refs[: len(held.arrays)]
        out_ref, acc_held, acc_sem, *scratch = refs[len(held.arrays) + len(extra) :]
        left, weights, _ = scratch
        sources = (prompt_ref, got_ref, step_ref)
        groups = [
            held.copies(i, block_ref, sources, weight_refs, scratch) for i in range(held.count)
        ]
        for group in groups[:AHEAD]:
            for copy in group:
                copy.start()
        if extra:
            before = pltpu.make_async_copy(refs[len(held.arrays)], acc_held, acc_sem.at[0])
            before.start()
        total = None
        for i, group in enumerate(groups):
            for copy in group:
                copy.wait()
            if i + AHEAD < held.count:
                for copy in groups[i + AHEAD]:
                    copy.start()
            product = jnp.dot(left[i], weights[i], preferred_element_type=jnp.float32)
            total = product if total is None else total + product
        if extra:
            before.wait()
            total = total + acc_held[...]
        out_ref[...] = total.astype(kind)

    anywhere = pl.BlockSpec(memory_space=pl.ANY)
    return pl.pallas_call(
        body,
        in_specs=[pl.BlockSpec(memory_space=pltpu.SMEM)] + [anywhere] * (3 + len(held.arrays) + len(extra)),
        out_specs=pl.BlockSpec(memory_space=pltpu.VMEM),
        out_shape=jax.ShapeDtypeStruct((held.height, held.columns), kind),
        scratch_shapes=[
            pltpu.VMEM((held.height, held.columns) if extra else (8, HEAD_DIM), jnp.float32),
            pltpu.SemaphoreType.DMA((1,)),
            *held.scratch,
        ],
        compiler_params=pltpu.CompilerParams(vmem_limit_bytes=57 * MIB),
        cost_estimate=LIGHT,
    )(blocks, prompt, got, steps, *held.arrays, *extra)


NOTES = 16


def thirds(value):
    parts = []
    for _ in range(3):
        parts.append(value.astype(jnp.bfloat16))
        value = value - parts[-1].astype(jnp.float32)
    return parts


def note_rows(top, total):
    parts = [part.astype(jnp.float32) for part in thirds(top) + thirds(total)]
    rows = jnp.concatenate(parts + [jnp.zeros((NOTES - 6, top.shape[1]), jnp.float32)], axis=0)
    return rows.astype(jnp.bfloat16)


def read_notes(rows):
    rows = rows.astype(jnp.float32)
    return rows[0:1] + rows[1:2] + rows[2:3], rows[3:4] + rows[4:5] + rows[5:6]


def small_call(body, out_shapes, scalars, arrays):
    whole = pl.BlockSpec(memory_space=pltpu.VMEM)
    return pl.pallas_call(
        body,
        in_specs=[pl.BlockSpec(memory_space=pltpu.SMEM)] * len(scalars) + [whole] * len(arrays),
        out_specs=[whole] * len(out_shapes),
        out_shape=[jax.ShapeDtypeStruct(shape, jnp.bfloat16) for shape in out_shapes],
        compiler_params=pltpu.CompilerParams(vmem_limit_bytes=12 * MIB),
        cost_estimate=LIGHT,
    )(*scalars, *arrays)


def merge_cores(own, other):
    deep, _, _, height, lanes = own.shape

    def body(own_ref, other_ref, near_ref, far_ref):
        for z in range(deep):
            for y, out_ref in enumerate((near_ref, far_ref)):
                both = own_ref[z, 0, y, :HEAD_DIM, :].astype(jnp.float32) + other_ref[
                    z, y, :HEAD_DIM, :
                ].astype(jnp.float32)
                out_ref[z, :HEAD_DIM, :] = both.astype(jnp.bfloat16)
                out_ref[z, HEAD_DIM:, :] = own_ref[z, 0, y, HEAD_DIM:, :]

    return small_call(body, [(deep, height, lanes)] * 2, [], [own, other])


def merge_chips(own_place, near, far):
    deep, height, lanes = near.shape

    def body(place_ref, near_ref, far_ref, *out_refs):
        for k, out_ref in enumerate(out_refs):
            z = lax.rem(place_ref[0] + k, deep)
            first, second = near_ref[z], far_ref[z]
            first_top, first_total = read_notes(first[HEAD_DIM:, :])
            second_top, second_total = read_notes(second[HEAD_DIM:, :])
            top = jnp.maximum(first_top, second_top)
            first_factor, second_factor = jnp.exp(first_top - top), jnp.exp(second_top - top)
            out_ref[:HEAD_DIM, :] = (
                first[:HEAD_DIM, :].astype(jnp.float32) * first_factor
                + second[:HEAD_DIM, :].astype(jnp.float32) * second_factor
            ).astype(jnp.bfloat16)
            out_ref[HEAD_DIM:, :] = note_rows(
                top, first_total * first_factor + second_total * second_factor
            )

    return small_call(body, [(height, lanes)] * deep, [own_place], [near, far])


def attend(
    places, turns, queries, own, other, cosine, sine, masks, prompt, got, steps, blocks, width,
    pieces, early,
):
    kv_heads = places.shape[0]
    deep, packed, lanes = queries[0].shape
    share = deep // kv_heads
    count = 2 * share * packed * lanes // HEAD_DIM
    owners = count // HEAD_DIM
    tokens = cosine.shape[0]
    half = tokens // 2
    held = Blocks(prompt, steps, width, pieces)
    inputs = [*queries, own, other, cosine, sine, *masks]

    def body(place_ref, turn_ref, block_ref, *refs):
        query_refs = refs[:2]
        own_ref, other_ref, cosine_ref, sine_ref = refs[2:6]
        mask_refs = refs[6 : len(inputs)]
        prompt_ref, got_ref, step_ref, early_ref = refs[len(inputs) : len(inputs) + 4]
        rest = refs[len(inputs) + 4 :]
        weight_refs, rest = rest[: len(held.arrays)], rest[len(held.arrays) :]
        out_ref, step_out_ref = rest[:2]
        early_held, weight_held, value_held, early_sem, *scratch = rest[2:]
        left, weight_rows, _ = scratch
        sources = (prompt_ref, got_ref, step_ref)
        groups = [
            held.copies(i, block_ref, sources, weight_refs, scratch) for i in range(held.count)
        ]
        before = pltpu.make_async_copy(early_ref, early_held, early_sem.at[0])
        before.start()
        for group in groups:
            for copy in group:
                copy.start()
        wide_cosine = jnp.concatenate([cosine_ref[...], cosine_ref[...]], axis=1)
        wide_sine = jnp.concatenate([-sine_ref[...], sine_ref[...]], axis=1)

        def one_head(j, _):
            column = pl.ds(pl.multiple_of(place_ref[j] * HEAD_DIM, HEAD_DIM), HEAD_DIM)
            keys = jnp.concatenate(
                [
                    own_ref[:half, column].astype(jnp.float32)
                    + other_ref[half:tokens, column].astype(jnp.float32),
                    own_ref[half:tokens, column].astype(jnp.float32)
                    + other_ref[:half, column].astype(jnp.float32),
                ],
                axis=0,
            )
            swapped = pltpu.roll(keys, HEAD_DIM // 2, 1)
            keys = (keys * wide_cosine + swapped * wide_sine).astype(jnp.bfloat16)
            unpacked = []
            for part in range(share):
                for ref in query_refs:
                    both = ref[turn_ref[j * share + part]]
                    for low in range(0, packed, packed // 2):
                        for left_lane in range(0, lanes, HEAD_DIM):
                            unpacked.append(
                                both[low : low + packed // 2, left_lane : left_lane + HEAD_DIM]
                            )
            scores = lax.dot_general(
                keys,
                jnp.concatenate(unpacked, axis=0),
                (((1,), (1,)), ((), ())),
                preferred_element_type=jnp.float32,
            ) * (HEAD_DIM**-0.5)
            if masks:
                scores = jnp.where(mask_refs[0][...] == mask_refs[1][...], scores, -1e30)
            top = jnp.max(scores, axis=0, keepdims=True)
            weights = jnp.exp(scores - top)
            total = jnp.sum(weights, axis=0, keepdims=True)
            for i in range(owners):
                lane = slice(i * HEAD_DIM, (i + 1) * HEAD_DIM)
                out_ref[j, i, HEAD_DIM:, :] = note_rows(top[:, lane], total[:, lane])
            weight_held[j] = weights.astype(jnp.bfloat16)
            return 0

        lax.fori_loop(0, kv_heads, one_head, 0)
        before.wait()
        total = early_held[...]
        for i, group in enumerate(groups):
            for copy in group:
                copy.wait()
            total += jnp.dot(left[i], weight_rows[i], preferred_element_type=jnp.float32)
        value_held[...] = total[:tokens].astype(jnp.bfloat16)
        step_out_ref[...] = total[tokens:]

        def one_sum(j, _):
            column = pl.ds(pl.multiple_of(place_ref[j] * HEAD_DIM, HEAD_DIM), HEAD_DIM)
            summed = lax.dot_general(
                value_held[:, column],
                weight_held[j],
                (((0,), (0,)), ((), ())),
                preferred_element_type=jnp.float32,
            )
            for i in range(owners):
                lane = slice(i * HEAD_DIM, (i + 1) * HEAD_DIM)
                out_ref[j, i, :HEAD_DIM, :] = summed[:, lane].astype(jnp.bfloat16)
            return 0

        lax.fori_loop(0, kv_heads, one_sum, 0)

    anywhere = pl.BlockSpec(memory_space=pl.ANY)
    whole = pl.BlockSpec(memory_space=pltpu.VMEM)
    return pl.pallas_call(
        body,
        in_specs=[pl.BlockSpec(memory_space=pltpu.SMEM)] * 3
        + [whole] * len(inputs)
        + [anywhere] * (4 + len(held.arrays)),
        out_specs=[whole] * 2,
        out_shape=[
            jax.ShapeDtypeStruct((kv_heads, owners, HEAD_DIM + NOTES, HEAD_DIM), jnp.bfloat16),
            jax.ShapeDtypeStruct((held.step_count, held.columns), jnp.float32),
        ],
        scratch_shapes=[
            pltpu.VMEM((held.height, held.columns), jnp.float32),
            pltpu.VMEM((kv_heads, tokens, count), jnp.bfloat16),
            pltpu.VMEM((tokens, held.columns), jnp.bfloat16),
            pltpu.SemaphoreType.DMA((1,)),
            *held.scratch,
        ],
        compiler_params=pltpu.CompilerParams(vmem_limit_bytes=57 * MIB),
        cost_estimate=LIGHT,
    )(places, turns, blocks, *inputs, prompt, got, steps, early, *held.arrays)


def out_project(blocks, parts, queries, new_keys, new_values, weight, width):
    count = len(parts)
    steps = queries.shape[0]
    samples = steps // 2

    def body(block_ref, *refs):
        part_refs = refs[:count]
        query_ref, key_ref, value_ref, weight_ref, out_ref = refs[count:]
        notes = [read_notes(ref[HEAD_DIM:, :]) for ref in part_refs]
        top = notes[0][0]
        for other, _ in notes[1:]:
            top = jnp.maximum(top, other)
        sums = total = 0.0
        for ref, (part_top, part_total) in zip(part_refs, notes):
            factor = jnp.exp(part_top - top)
            sums = sums + ref[:HEAD_DIM, :].astype(jnp.float32) * factor
            total = total + part_total * factor
        sums = sums.T
        both = jnp.concatenate([top, total, jnp.zeros((6, HEAD_DIM), jnp.float32)], axis=0).T
        keys, values = key_ref[...], value_ref[...]
        heads = []
        for h in range(queries.shape[1] // HEAD_DIM):
            query = query_ref[:, h * HEAD_DIM : (h + 1) * HEAD_DIM].astype(jnp.float32)
            own_score = jnp.sum(query * keys, axis=1, keepdims=True) * (HEAD_DIM**-0.5)
            back_score = jnp.sum(
                query[samples:] * keys[:samples], axis=1, keepdims=True
            ) * (HEAD_DIM**-0.5)
            ends = []
            for step in (0, 1):
                place = slice((2 * h + step) * samples, (2 * h + step + 1) * samples)
                here = slice(step * samples, (step + 1) * samples)
                old_top, old_total = both[place, 0:1], both[place, 1:2]
                scores = [(own_score[here], values[here])]
                if step:
                    scores.append((back_score, values[:samples]))
                high = old_top
                for score, _ in scores:
                    high = jnp.maximum(high, score)
                old = jnp.exp(old_top - high)
                numerator, denominator = old * sums[place], old * old_total
                for score, value in scores:
                    new = jnp.exp(score - high)
                    numerator, denominator = numerator + new * value, denominator + new
                ends.append(numerator / denominator)
            heads.append(jnp.concatenate(ends, axis=0).astype(jnp.bfloat16))
        heads = jnp.concatenate(heads, axis=1)
        for i in range(blocks.shape[0]):
            start = pl.multiple_of(block_ref[i] * width, width)
            out_ref[:, i * width : (i + 1) * width] = jnp.dot(
                heads, weight_ref[:, pl.ds(start, width)], preferred_element_type=jnp.float32
            ).astype(jnp.bfloat16)

    return small_call(
        body, [(steps, weight.shape[1])], [blocks], [*parts, queries, new_keys, new_values, weight]
    )[0]


def on_device(
    prompt_states,
    page_table,
    step_states,
    sample_order,
    key_weight,
    value_weight,
    query_weight,
    out_weight,
):
    devices = lax.axis_size("sample")
    groups = lax.axis_size("groups")
    own_index = lax.axis_index("sample")
    first = lax.axis_index("groups") % 2 == 0
    deep = devices // LINE
    own_a, own_b, own_c = own_index // LINE, own_index // 2 % 2, own_index % 2
    along_ring, along_z, along_y, along_x, in_chip = mover(groups, devices)
    row_count = prompt_states.shape[0]
    chip_rows = 2 * row_count
    pages_here = row_count // PAGE
    heads_here = query_weight.shape[1] // HEAD_DIM
    total_pages = page_table.shape[0]
    prompts = total_pages // PROMPT_PAGES
    samples = sample_order.shape[0]
    steps = 2 * samples
    group_size = samples // prompts
    own_kv = own_index * heads_here // GQA
    wide_states = step_states.reshape(steps, D)
    rows = heads_here * steps
    width = key_weight.shape[0]
    half = key_weight.shape[1] // 2
    kv_places = jnp.where(first, 0, KV_HEADS // 2) + jnp.arange(KV_HEADS, dtype=jnp.int32)
    kv_places = kv_places % KV_HEADS

    order = ring_order(deep)

    def by_place(table):
        return sum(jnp.where(own_a == a, table[a], 0) for a in range(deep))

    own_turn = by_place([order.index(a) for a in range(deep)])

    def block(place_z, flip, core):
        return place_z * LINE + (own_b ^ flip) * 2 + core

    def behind(k):
        return by_place([order[(order.index(a) - k) % deep] for a in range(deep)])

    low = jnp.concatenate([key_weight[:, :half], value_weight[:, :half]])
    high = jnp.concatenate([key_weight[:, half:], value_weight[:, half:]])
    both_mine, both_other = jnp.where(first, low, high), jnp.where(first, high, low)

    own_pages = jnp.concatenate(
        [
            holder * pages_here + jnp.arange(pages_here, dtype=jnp.int32)
            for holder in (own_index, own_index ^ 1)
        ]
    )
    slots = jnp.sum(
        jnp.where(
            page_table[None, :] == own_pages[:, None],
            jnp.arange(total_pages, dtype=jnp.int32)[None, :],
            0,
        ),
        axis=1,
    )
    positions = (slots % PROMPT_PAGES * PAGE)[:, None] + jnp.arange(PAGE, dtype=jnp.int32)[None, :]
    cosine, sine_part = rope_tables(positions.reshape(chip_rows))

    step_place = PROMPT_PAGES * PAGE + jnp.arange(2, dtype=jnp.int32)
    step_tables = tuple(t[:, None, :] for t in rope_tables(step_place))
    flat_tables = [
        jnp.repeat(jnp.concatenate([sign * table, table], axis=-1)[:, 0], samples, axis=0)
        for sign, table in zip((1, -1), step_tables)
    ]
    queries = project_queries(
        after(wide_states, (cosine, sine_part)), query_weight, *flat_tables
    )
    packed_queries = jnp.concatenate(
        jnp.split(queries, half // queries.shape[1], axis=0), axis=1
    )
    packed = packed_queries.shape[0]

    places = [(k, flip) for k in range(deep) for flip in (0, 1)]
    own_blocks = jnp.stack([block(behind(k), flip, own_c) for k, flip in places])
    query_turns = jnp.stack([(own_turn + deep - order.index(a)) % deep for a in range(deep)])
    own_place = (own_kv + jnp.where(first, 0, KV_HEADS // 2)) % KV_HEADS * HEAD_DIM
    done = {}

    def send(move, value):
        moved = done.setdefault(move, [])
        moved.append(move(after(value, moved[-2]) if len(moved) > 1 else value))
        return moved[-1]

    got = in_chip(prompt_states)
    both_z, both_x, theirs, theirs_x = {0: both_mine}, {0: both_other}, {}, {}
    both_z[1] = send(along_ring, both_mine)
    value_y = send(along_y, both_mine[width:])
    key_full = {0: jnp.concatenate([both_mine[:width], both_other[:width], packed_queries])}
    key_y = {0: send(along_y, after(key_full[0], value_y))}
    theirs[0] = jnp.concatenate([value_y, packed_queries, key_y[0][2 * width :]])
    for k in range(1, deep):
        if k + 1 < deep:
            both_z[k + 1] = send(along_ring, both_z[k])
        both_x[k] = send(along_x, both_z[k])
        if k == 1:
            theirs_x[0] = send(along_x, value_y)
        key_full[k] = jnp.concatenate([both_z[k][:width], both_x[k][:width]])
        key_y[k] = send(along_y, after(key_full[k], key_y[k - 1]))
    for k in range(1, deep):
        theirs[k] = send(along_ring, theirs[k - 1])
        theirs_x[k] = send(along_x, theirs[k])

    ring_queries = collect([theirs[k] for k in range(deep)], width, 2 * packed)
    ring_queries = [ring_queries, in_chip(ring_queries)]
    by_owner = (deep, 2, 2, rows)

    key_pieces = [
        [((key_y if flip else key_full)[k], start) for start in (0, width)] for k, flip in places
    ]
    value_pieces = [
        [(theirs[k], 0), (theirs_x[k], 0)] if flip else [(both_z[k], width), (both_x[k], width)]
        for k, flip in places
    ]

    def project_blocks(pieces, which, acc, ready, kind):
        taken = after(jnp.stack([own_blocks[i] for i in which]), ready)
        return project(
            prompt_states, got, wide_states, taken, width, [pieces[i] for i in which], acc, kind
        )

    last = 2 * deep - 2
    key_early = project_blocks(
        key_pieces, range(last), None, (theirs_x[1], theirs[deep - 2]), jnp.float32
    )
    awaited = [theirs_x[k] for k in range(1, deep)]
    key_sum = project_blocks(key_pieces, [last, last + 1], key_early, awaited, jnp.bfloat16)
    early = [*range(0, 2 * deep, 2), 1]
    late = [i for i in range(2 * deep) if i not in early]
    value_early = project_blocks(value_pieces, early, None, key_sum, jnp.float32)
    key_back = in_chip(key_sum)

    def own_head(sums):
        sums = lax.dynamic_slice_in_dim(sums, own_place, HEAD_DIM, 1)
        return sums.reshape(2, samples, HEAD_DIM).astype(jnp.float32)

    new_keys = own_head(key_sum[chip_rows:]) + own_head(key_back[chip_rows:])
    new_keys = turn(new_keys, step_tables).astype(jnp.bfloat16).astype(jnp.float32)
    new_keys = new_keys.reshape(steps, HEAD_DIM)
    masks = []
    if prompts > 1:
        token_prompt = jnp.repeat(slots // PROMPT_PAGES, PAGE)
        row_prompt = jnp.tile(sample_order // group_size, devices // KV_HEADS * rows // samples)
        masks = [token_prompt[:, None], row_prompt[None, :]]
    partial, step_values = attend(
        kv_places, query_turns, ring_queries, key_sum, key_back, cosine, sine_part, masks,
        prompt_states, got, wide_states, jnp.stack([own_blocks[i] for i in late]), width,
        [value_pieces[i] for i in late], value_early,
    )
    new_values = own_head(step_values) + own_head(in_chip(step_values))
    new_values = new_values.astype(jnp.bfloat16).astype(jnp.float32).reshape(steps, HEAD_DIM)

    partial = partial.reshape(by_owner[:3] + partial.shape[2:])
    near, far = merge_cores(partial, in_chip(partial[:, 1]))
    merged = merge_chips(own_a[None], near, along_y(far))
    parts = [merged[0]] + [along_z(merged[k], k) for k in range(1, deep)]

    out_width = out_weight.shape[1] // devices
    out_blocks = jnp.stack(
        [
            block((own_a + k) % deep, flip, own_c ^ turned)
            for turned in (0, 1)
            for flip in (0, 1)
            for k in range(deep)
        ]
    )
    terms = out_project(out_blocks, parts, queries, new_keys, new_values, out_weight, out_width)

    def narrow(value):
        return value.astype(jnp.bfloat16)

    def wide(value):
        return value.astype(jnp.float32)

    for move in (in_chip, along_y):
        share = terms.shape[1] // 2
        terms = narrow(wide(terms[:, :share]) + wide(move(terms[:, share:])))
    attn_out = wide(terms[:, :out_width])
    for k in range(1, deep):
        attn_out = attn_out + wide(along_z(terms[:, k * out_width : (k + 1) * out_width], k))
    return narrow(attn_out).reshape(2, samples, -1)


def solution(mesh):
    in_specs = (
        P(("groups", "sample"), None),
        P("groups"),
        P(None, "groups", None),
        P("groups"),
        P("sample", None),
        P("sample", None),
        P(None, "sample"),
        P("sample", None),
    )
    out_specs = P(None, "groups", "sample")
    return jax.shard_map(
        on_device, mesh=mesh, in_specs=in_specs, out_specs=out_specs, check_vma=False
    )
```

```python
import jax
import jax.numpy as jnp
from jax import lax
from jax.experimental import pallas as pl
from jax.experimental.pallas import tpu as pltpu
from jax.sharding import PartitionSpec as P

D = 8192
HEAD_DIM = 128
KV_HEADS = 4
GQA = 8
PAGE = 128
PROMPT_PAGES = 64
LINE = 4

rope_base = 1000000.0


def rope_tables(position):
    half_dim = HEAD_DIM // 2
    frequency = rope_base ** (-jnp.arange(half_dim, dtype=jnp.float32) * 2.0 / HEAD_DIM)
    angles = position.astype(jnp.float32)[..., None] * frequency
    return jnp.cos(angles), jnp.sin(angles)


def turn(vector, tables):
    cosine, sine_part = tables
    half_dim = HEAD_DIM // 2
    first_half = vector[..., :half_dim]
    second_half = vector[..., half_dim:]
    return jnp.concatenate(
        [
            first_half * cosine - second_half * sine_part,
            second_half * cosine + first_half * sine_part,
        ],
        axis=-1,
    )


def ring_order(deep):
    return [*range(0, deep, 2), *range(deep - 1 - deep % 2, 0, -2)]


def mover(groups, devices):
    deep = devices // LINE
    order = ring_order(deep)

    def move(value, step):
        pairs = []
        for g in range(groups):
            for s in range(devices):
                a, b, c = s // LINE, s // 2 % 2, s % 2
                to_g, to_a, to_b, to_c = step(g, a, b, c)
                to_s = (to_a % deep) * LINE + to_b * 2 + to_c
                pairs.append((g * devices + s, to_g * devices + to_s))
        return lax.ppermute(value, ("groups", "sample"), pairs)

    def next_on_ring(a):
        return order[(order.index(a) + 1) % deep]

    along_ring = lambda v: move(v, lambda g, a, b, c: (g, next_on_ring(a), b, c))
    along_z = lambda v, k: move(v, lambda g, a, b, c: (g, a + k, b, c))
    along_y = lambda v: move(v, lambda g, a, b, c: (g, a, 1 - b, c))
    along_x = lambda v: move(v, lambda g, a, b, c: (g ^ 1, a, b, c))
    in_chip = lambda v: move(v, lambda g, a, b, c: (g, a, b, 1 - c))
    return along_ring, along_z, along_y, along_x, in_chip


def after(value, done):
    return lax.optimization_barrier((value, done))[0]


MIB = 1024 * 1024
LIGHT = pl.CostEstimate(flops=1, bytes_accessed=1, transcendentals=0)


def project_queries(steps, weight, cosine, sine):
    count, depth = steps.shape
    parts = 8
    piece = depth // parts

    def body(step_ref, weight_ref, cosine_ref, sine_ref, out_ref, held, sems):
        copies = []
        for i in range(parts):
            copies.append(
                pltpu.make_async_copy(
                    weight_ref.at[pl.ds(i * piece, piece), :], held.at[i], sems.at[i]
                )
            )
            copies[-1].start()
        total = None
        for i in range(parts):
            copies[i].wait()
            product = jnp.dot(
                step_ref[:, i * piece : (i + 1) * piece],
                held[i],
                preferred_element_type=jnp.float32,
            )
            total = product if total is None else total + product
        for start in range(0, weight.shape[1], HEAD_DIM):
            head = total[:, start : start + HEAD_DIM]
            turned = head * cosine_ref[...] + pltpu.roll(head, HEAD_DIM // 2, 1) * sine_ref[...]
            out_ref[:, start : start + HEAD_DIM] = turned.astype(jnp.bfloat16)

    whole = pl.BlockSpec(memory_space=pltpu.VMEM)
    return pl.pallas_call(
        body,
        in_specs=[whole, pl.BlockSpec(memory_space=pltpu.HBM), whole, whole],
        out_specs=whole,
        out_shape=jax.ShapeDtypeStruct((count, weight.shape[1]), jnp.bfloat16),
        scratch_shapes=[
            pltpu.VMEM((parts, piece, weight.shape[1]), weight.dtype),
            pltpu.SemaphoreType.DMA((parts,)),
        ],
        compiler_params=pltpu.CompilerParams(vmem_limit_bytes=10 * MIB),
        cost_estimate=LIGHT,
    )(steps, weight, cosine, sine)


def collect(arrays, first, height):
    columns = arrays[0].shape[1]

    def body(*refs):
        out_ref, sems = refs[-2:]
        copies = [
            pltpu.make_async_copy(ref.at[pl.ds(first, height), :], out_ref.at[i], sems.at[i])
            for i, ref in enumerate(refs[:-2])
        ]
        for copy in copies:
            copy.start()
        for copy in copies:
            copy.wait()

    return pl.pallas_call(
        body,
        in_specs=[pl.BlockSpec(memory_space=pl.ANY)] * len(arrays),
        out_specs=pl.BlockSpec(memory_space=pltpu.VMEM),
        out_shape=jax.ShapeDtypeStruct((len(arrays), height, columns), arrays[0].dtype),
        scratch_shapes=[pltpu.SemaphoreType.DMA((len(arrays),))],
        compiler_params=pltpu.CompilerParams(vmem_limit_bytes=4 * MIB),
        cost_estimate=LIGHT,
    )(*arrays)


class Blocks:
    def __init__(self, prompt, steps, width, pieces):
        self.arrays = []
        for piece in pieces:
            for array, _ in piece:
                if not any(array is held for held in self.arrays):
                    self.arrays.append(array)
        self.pieces, self.width, self.count = pieces, width, len(pieces)
        self.row_count, self.step_count = prompt.shape[0], steps.shape[0]
        self.height = 2 * self.row_count + self.step_count
        self.columns = sum(array.shape[1] for array, _ in pieces[0])
        self.scratch = [
            pltpu.VMEM((self.count, self.height, width), prompt.dtype),
            pltpu.VMEM((self.count, width, self.columns), prompt.dtype),
            pltpu.SemaphoreType.DMA((self.count, 5)),
        ]

    def copies(self, i, block_ref, sources, weight_refs, scratch):
        left, weights, sems = scratch
        column = pl.ds(pl.multiple_of(block_ref[i] * self.width, self.width), self.width)
        group = []
        start = 0
        for j, (source, rows) in enumerate(
            zip(sources, (self.row_count, self.row_count, self.step_count))
        ):
            group.append(
                pltpu.make_async_copy(
                    source.at[:, column], left.at[i, pl.ds(start, rows), :], sems.at[i, j]
                )
            )
            start += rows
        side = 0
        for j, (array, first) in enumerate(self.pieces[i]):
            ref = weight_refs[[array is other for other in self.arrays].index(True)]
            group.append(
                pltpu.make_async_copy(
                    ref.at[pl.ds(first, self.width), :],
                    weights.at[i, :, pl.ds(side, array.shape[1])],
                    sems.at[i, 3 + j],
                )
            )
            side += array.shape[1]
        return group


AHEAD = 3


def project(prompt, got, steps, blocks, width, pieces, acc, kind):
    held = Blocks(prompt, steps, width, pieces)
    extra = [] if acc is None else [acc]

    def body(block_ref, prompt_ref, got_ref, step_ref, *refs):
        weight_refs = refs[: len(held.arrays)]
        out_ref, acc_held, acc_sem, *scratch = refs[len(held.arrays) + len(extra) :]
        left, weights, _ = scratch
        sources = (prompt_ref, got_ref, step_ref)
        groups = [
            held.copies(i, block_ref, sources, weight_refs, scratch) for i in range(held.count)
        ]
        for group in groups[:AHEAD]:
            for copy in group:
                copy.start()
        if extra:
            before = pltpu.make_async_copy(refs[len(held.arrays)], acc_held, acc_sem.at[0])
            before.start()
        total = None
        for i, group in enumerate(groups):
            for copy in group:
                copy.wait()
            if i + AHEAD < held.count:
                for copy in groups[i + AHEAD]:
                    copy.start()
            product = jnp.dot(left[i], weights[i], preferred_element_type=jnp.float32)
            total = product if total is None else total + product
        if extra:
            before.wait()
            total = total + acc_held[...]
        out_ref[...] = total.astype(kind)

    anywhere = pl.BlockSpec(memory_space=pl.ANY)
    return pl.pallas_call(
        body,
        in_specs=[pl.BlockSpec(memory_space=pltpu.SMEM)] + [anywhere] * (3 + len(held.arrays) + len(extra)),
        out_specs=pl.BlockSpec(memory_space=pltpu.VMEM),
        out_shape=jax.ShapeDtypeStruct((held.height, held.columns), kind),
        scratch_shapes=[
            pltpu.VMEM((held.height, held.columns) if extra else (8, HEAD_DIM), jnp.float32),
            pltpu.SemaphoreType.DMA((1,)),
            *held.scratch,
        ],
        compiler_params=pltpu.CompilerParams(vmem_limit_bytes=57 * MIB),
        cost_estimate=LIGHT,
    )(blocks, prompt, got, steps, *held.arrays, *extra)


NOTES = 16


def thirds(value):
    parts = []
    for _ in range(3):
        parts.append(value.astype(jnp.bfloat16))
        value = value - parts[-1].astype(jnp.float32)
    return parts


def note_rows(top, total):
    parts = [part.astype(jnp.float32) for part in thirds(top) + thirds(total)]
    rows = jnp.concatenate(parts + [jnp.zeros((NOTES - 6, top.shape[1]), jnp.float32)], axis=0)
    return rows.astype(jnp.bfloat16)


def read_notes(rows):
    rows = rows.astype(jnp.float32)
    return rows[0:1] + rows[1:2] + rows[2:3], rows[3:4] + rows[4:5] + rows[5:6]


def small_call(body, out_shapes, scalars, arrays):
    whole = pl.BlockSpec(memory_space=pltpu.VMEM)
    return pl.pallas_call(
        body,
        in_specs=[pl.BlockSpec(memory_space=pltpu.SMEM)] * len(scalars) + [whole] * len(arrays),
        out_specs=[whole] * len(out_shapes),
        out_shape=[jax.ShapeDtypeStruct(shape, jnp.bfloat16) for shape in out_shapes],
        compiler_params=pltpu.CompilerParams(vmem_limit_bytes=12 * MIB),
        cost_estimate=LIGHT,
    )(*scalars, *arrays)


def merge_cores(own, other):
    deep, _, height, lanes = own.shape

    def body(own_ref, other_ref, near_ref, far_ref):
        for z in range(deep):
            for y, out_ref in enumerate((near_ref, far_ref)):
                both = own_ref[z, y, :HEAD_DIM, :].astype(jnp.float32) + other_ref[
                    z, y, :HEAD_DIM, :
                ].astype(jnp.float32)
                out_ref[z, :HEAD_DIM, :] = both.astype(jnp.bfloat16)
                out_ref[z, HEAD_DIM:, :] = own_ref[z, y, HEAD_DIM:, :]

    return small_call(body, [(deep, height, lanes)] * 2, [], [own, other])


def merge_chips(own_place, near, far):
    deep, height, lanes = near.shape

    def body(place_ref, near_ref, far_ref, *out_refs):
        for k, out_ref in enumerate(out_refs):
            z = lax.rem(place_ref[0] + k, deep)
            first, second = near_ref[z], far_ref[z]
            first_top, first_total = read_notes(first[HEAD_DIM:, :])
            second_top, second_total = read_notes(second[HEAD_DIM:, :])
            top = jnp.maximum(first_top, second_top)
            first_factor, second_factor = jnp.exp(first_top - top), jnp.exp(second_top - top)
            out_ref[:HEAD_DIM, :] = (
                first[:HEAD_DIM, :].astype(jnp.float32) * first_factor
                + second[:HEAD_DIM, :].astype(jnp.float32) * second_factor
            ).astype(jnp.bfloat16)
            out_ref[HEAD_DIM:, :] = note_rows(
                top, first_total * first_factor + second_total * second_factor
            )

    return small_call(body, [(height, lanes)] * deep, [own_place], [near, far])


def attend(
    places, turns, queries, own, other, cosine, sine, masks, prompt, got, steps, blocks, width,
    pieces, early,
):
    kv_heads = places.shape[0]
    deep, packed, lanes = queries[0].shape
    share = deep // kv_heads
    count = 2 * share * packed * lanes // HEAD_DIM
    owners = count // HEAD_DIM
    tokens = cosine.shape[0]
    half = tokens // 2
    held = Blocks(prompt, steps, width, pieces)
    inputs = [*queries, own, other, cosine, sine, *masks]

    def body(place_ref, turn_ref, block_ref, *refs):
        query_refs = refs[:2]
        own_ref, other_ref, cosine_ref, sine_ref = refs[2:6]
        mask_refs = refs[6 : len(inputs)]
        prompt_ref, got_ref, step_ref, early_ref = refs[len(inputs) : len(inputs) + 4]
        rest = refs[len(inputs) + 4 :]
        weight_refs, rest = rest[: len(held.arrays)], rest[len(held.arrays) :]
        *out_refs, step_out_ref = rest[:3]
        early_held, weight_held, value_held, early_sem, *scratch = rest[3:]
        left, weight_rows, _ = scratch
        sources = (prompt_ref, got_ref, step_ref)
        groups = [
            held.copies(i, block_ref, sources, weight_refs, scratch) for i in range(held.count)
        ]
        before = pltpu.make_async_copy(early_ref, early_held, early_sem.at[0])
        before.start()
        for group in groups:
            for copy in group:
                copy.start()
        wide_cosine = jnp.concatenate([cosine_ref[...], cosine_ref[...]], axis=1)
        wide_sine = jnp.concatenate([-sine_ref[...], sine_ref[...]], axis=1)

        def one_head(j, _):
            column = pl.ds(pl.multiple_of(place_ref[j] * HEAD_DIM, HEAD_DIM), HEAD_DIM)
            keys = jnp.concatenate(
                [
                    own_ref[:half, column].astype(jnp.float32)
                    + other_ref[half:tokens, column].astype(jnp.float32),
                    own_ref[half:tokens, column].astype(jnp.float32)
                    + other_ref[:half, column].astype(jnp.float32),
                ],
                axis=0,
            )
            swapped = pltpu.roll(keys, HEAD_DIM // 2, 1)
            keys = (keys * wide_cosine + swapped * wide_sine).astype(jnp.bfloat16)
            unpacked = []
            for part in range(share):
                for ref in query_refs:
                    both = ref[turn_ref[j * share + part]]
                    for low in range(0, packed, packed // 2):
                        for left_lane in range(0, lanes, HEAD_DIM):
                            unpacked.append(
                                both[low : low + packed // 2, left_lane : left_lane + HEAD_DIM]
                            )
            scores = lax.dot_general(
                keys,
                jnp.concatenate(unpacked, axis=0),
                (((1,), (1,)), ((), ())),
                preferred_element_type=jnp.float32,
            ) * (HEAD_DIM**-0.5)
            if masks:
                scores = jnp.where(mask_refs[0][...] == mask_refs[1][...], scores, -1e30)
            top = jnp.max(scores, axis=0, keepdims=True)
            weights = jnp.exp(scores - top)
            total = jnp.sum(weights, axis=0, keepdims=True)
            for i in range(owners):
                lane = slice(i * HEAD_DIM, (i + 1) * HEAD_DIM)
                out_ref = out_refs[i // 2 % 2]
                out_ref[j, i // 4 * 2 + i % 2, HEAD_DIM:, :] = note_rows(
                    top[:, lane], total[:, lane]
                )
            weight_held[j] = weights.astype(jnp.bfloat16)
            return 0

        lax.fori_loop(0, kv_heads, one_head, 0)
        before.wait()
        total = early_held[...]
        for i, group in enumerate(groups):
            for copy in group:
                copy.wait()
            total += jnp.dot(left[i], weight_rows[i], preferred_element_type=jnp.float32)
        value_held[...] = total[:tokens].astype(jnp.bfloat16)
        step_out_ref[...] = total[tokens:]

        def one_sum(j, _):
            column = pl.ds(pl.multiple_of(place_ref[j] * HEAD_DIM, HEAD_DIM), HEAD_DIM)
            summed = lax.dot_general(
                value_held[:, column],
                weight_held[j],
                (((0,), (0,)), ((), ())),
                preferred_element_type=jnp.float32,
            )
            for i in range(owners):
                lane = slice(i * HEAD_DIM, (i + 1) * HEAD_DIM)
                out_ref = out_refs[i // 2 % 2]
                out_ref[j, i // 4 * 2 + i % 2, :HEAD_DIM, :] = summed[:, lane].astype(jnp.bfloat16)
            return 0

        lax.fori_loop(0, kv_heads, one_sum, 0)

    anywhere = pl.BlockSpec(memory_space=pl.ANY)
    whole = pl.BlockSpec(memory_space=pltpu.VMEM)
    return pl.pallas_call(
        body,
        in_specs=[pl.BlockSpec(memory_space=pltpu.SMEM)] * 3
        + [whole] * len(inputs)
        + [anywhere] * (4 + len(held.arrays)),
        out_specs=[whole] * 3,
        out_shape=[
            *[
                jax.ShapeDtypeStruct(
                    (kv_heads, owners // 2, HEAD_DIM + NOTES, HEAD_DIM), jnp.bfloat16
                )
            ]
            * 2,
            jax.ShapeDtypeStruct((held.step_count, held.columns), jnp.float32),
        ],
        scratch_shapes=[
            pltpu.VMEM((held.height, held.columns), jnp.float32),
            pltpu.VMEM((kv_heads, tokens, count), jnp.bfloat16),
            pltpu.VMEM((tokens, held.columns), jnp.bfloat16),
            pltpu.SemaphoreType.DMA((1,)),
            *held.scratch,
        ],
        compiler_params=pltpu.CompilerParams(vmem_limit_bytes=57 * MIB),
        cost_estimate=LIGHT,
    )(places, turns, blocks, *inputs, prompt, got, steps, early, *held.arrays)


def out_project(blocks, parts, queries, new_keys, new_values, weight, width):
    count = len(parts)
    steps = queries.shape[0]
    samples = steps // 2

    def body(block_ref, *refs):
        part_refs = refs[:count]
        query_ref, key_ref, value_ref, weight_ref, out_ref = refs[count:]
        notes = [read_notes(ref[HEAD_DIM:, :]) for ref in part_refs]
        top = notes[0][0]
        for other, _ in notes[1:]:
            top = jnp.maximum(top, other)
        sums = total = 0.0
        for ref, (part_top, part_total) in zip(part_refs, notes):
            factor = jnp.exp(part_top - top)
            sums = sums + ref[:HEAD_DIM, :].astype(jnp.float32) * factor
            total = total + part_total * factor
        sums = sums.T
        both = jnp.concatenate([top, total, jnp.zeros((6, HEAD_DIM), jnp.float32)], axis=0).T
        keys, values = key_ref[...], value_ref[...]
        heads = []
        for h in range(queries.shape[1] // HEAD_DIM):
            query = query_ref[:, h * HEAD_DIM : (h + 1) * HEAD_DIM].astype(jnp.float32)
            own_score = jnp.sum(query * keys, axis=1, keepdims=True) * (HEAD_DIM**-0.5)
            back_score = jnp.sum(
                query[samples:] * keys[:samples], axis=1, keepdims=True
            ) * (HEAD_DIM**-0.5)
            ends = []
            for step in (0, 1):
                place = slice((2 * h + step) * samples, (2 * h + step + 1) * samples)
                here = slice(step * samples, (step + 1) * samples)
                old_top, old_total = both[place, 0:1], both[place, 1:2]
                scores = [(own_score[here], values[here])]
                if step:
                    scores.append((back_score, values[:samples]))
                high = old_top
                for score, _ in scores:
                    high = jnp.maximum(high, score)
                old = jnp.exp(old_top - high)
                numerator, denominator = old * sums[place], old * old_total
                for score, value in scores:
                    new = jnp.exp(score - high)
                    numerator, denominator = numerator + new * value, denominator + new
                ends.append(numerator / denominator)
            heads.append(jnp.concatenate(ends, axis=0).astype(jnp.bfloat16))
        heads = jnp.concatenate(heads, axis=1)
        for i in range(blocks.shape[0]):
            start = pl.multiple_of(block_ref[i] * width, width)
            out_ref[:, i * width : (i + 1) * width] = jnp.dot(
                heads, weight_ref[:, pl.ds(start, width)], preferred_element_type=jnp.float32
            ).astype(jnp.bfloat16)

    return small_call(
        body, [(steps, weight.shape[1])], [blocks], [*parts, queries, new_keys, new_values, weight]
    )[0]


def on_device(
    prompt_states,
    page_table,
    step_states,
    sample_order,
    key_weight,
    value_weight,
    query_weight,
    out_weight,
):
    devices = lax.axis_size("sample")
    groups = lax.axis_size("groups")
    own_index = lax.axis_index("sample")
    first = lax.axis_index("groups") % 2 == 0
    deep = devices // LINE
    own_a, own_b, own_c = own_index // LINE, own_index // 2 % 2, own_index % 2
    along_ring, along_z, along_y, along_x, in_chip = mover(groups, devices)
    row_count = prompt_states.shape[0]
    chip_rows = 2 * row_count
    pages_here = row_count // PAGE
    heads_here = query_weight.shape[1] // HEAD_DIM
    total_pages = page_table.shape[0]
    prompts = total_pages // PROMPT_PAGES
    samples = sample_order.shape[0]
    steps = 2 * samples
    group_size = samples // prompts
    own_kv = own_index * heads_here // GQA
    wide_states = step_states.reshape(steps, D)
    rows = heads_here * steps
    width = key_weight.shape[0]
    half = key_weight.shape[1] // 2
    kv_places = jnp.where(first, 0, KV_HEADS // 2) + jnp.arange(KV_HEADS, dtype=jnp.int32)
    kv_places = kv_places % KV_HEADS

    order = ring_order(deep)

    def by_place(table):
        return sum(jnp.where(own_a == a, table[a], 0) for a in range(deep))

    own_turn = by_place([order.index(a) for a in range(deep)])

    def block(place_z, flip, core):
        return place_z * LINE + (own_b ^ flip) * 2 + core

    def behind(k):
        return by_place([order[(order.index(a) - k) % deep] for a in range(deep)])

    low = jnp.concatenate([key_weight[:, :half], value_weight[:, :half]])
    high = jnp.concatenate([key_weight[:, half:], value_weight[:, half:]])
    both_mine, both_other = jnp.where(first, low, high), jnp.where(first, high, low)

    own_pages = jnp.concatenate(
        [
            holder * pages_here + jnp.arange(pages_here, dtype=jnp.int32)
            for holder in (own_index, own_index ^ 1)
        ]
    )
    slots = jnp.sum(
        jnp.where(
            page_table[None, :] == own_pages[:, None],
            jnp.arange(total_pages, dtype=jnp.int32)[None, :],
            0,
        ),
        axis=1,
    )
    positions = (slots % PROMPT_PAGES * PAGE)[:, None] + jnp.arange(PAGE, dtype=jnp.int32)[None, :]
    cosine, sine_part = rope_tables(positions.reshape(chip_rows))

    step_place = PROMPT_PAGES * PAGE + jnp.arange(2, dtype=jnp.int32)
    step_tables = tuple(t[:, None, :] for t in rope_tables(step_place))
    flat_tables = [
        jnp.repeat(jnp.concatenate([sign * table, table], axis=-1)[:, 0], samples, axis=0)
        for sign, table in zip((1, -1), step_tables)
    ]
    queries = project_queries(
        after(wide_states, (cosine, sine_part)), query_weight, *flat_tables
    )
    packed_queries = jnp.concatenate(
        jnp.split(queries, half // queries.shape[1], axis=0), axis=1
    )
    packed = packed_queries.shape[0]

    places = [(k, flip) for k in range(deep) for flip in (0, 1)]
    own_blocks = jnp.stack([block(behind(k), flip, own_c) for k, flip in places])
    query_turns = jnp.stack([(own_turn + deep - order.index(a)) % deep for a in range(deep)])
    own_place = (own_kv + jnp.where(first, 0, KV_HEADS // 2)) % KV_HEADS * HEAD_DIM
    done = {}

    def send(move, value):
        moved = done.setdefault(move, [])
        moved.append(move(after(value, moved[-2]) if len(moved) > 1 else value))
        return moved[-1]

    got = in_chip(prompt_states)
    both_z, both_x, theirs, theirs_x = {0: both_mine}, {0: both_other}, {}, {}
    both_z[1] = send(along_ring, both_mine)
    value_y = send(along_y, both_mine[width:])
    key_full = {0: jnp.concatenate([both_mine[:width], both_other[:width], packed_queries])}
    key_y = {0: send(along_y, after(key_full[0], value_y))}
    theirs[0] = jnp.concatenate([value_y, packed_queries, key_y[0][2 * width :]])
    for k in range(1, deep):
        if k + 1 < deep:
            both_z[k + 1] = send(along_ring, both_z[k])
        if k == 1:
            theirs_x[0] = send(along_x, value_y)
        both_x[k] = send(along_x, after(both_z[k], theirs_x[0]))
        key_full[k] = jnp.concatenate([both_z[k][:width], both_x[k][:width]])
        key_y[k] = send(along_y, after(key_full[k], key_y[k - 1]))
    for k in range(1, deep):
        theirs[k] = send(along_ring, theirs[k - 1])
        theirs_x[k] = send(along_x, theirs[k][:width])

    ring_queries = collect([theirs[k] for k in range(deep)], width, 2 * packed)
    ring_queries = [ring_queries, in_chip(ring_queries)]

    key_pieces = [
        [((key_y if flip else key_full)[k], start) for start in (0, width)] for k, flip in places
    ]
    value_pieces = [
        [(theirs[k], 0), (theirs_x[k], 0)] if flip else [(both_z[k], width), (both_x[k], width)]
        for k, flip in places
    ]

    def project_blocks(pieces, which, acc, ready, kind):
        taken = after(jnp.stack([own_blocks[i] for i in which]), ready)
        return project(
            prompt_states, got, wide_states, taken, width, [pieces[i] for i in which], acc, kind
        )

    early = [*range(0, 2 * deep, 2), 1]
    late = [i for i in range(2 * deep) if i not in early]
    value_early = project_blocks(
        value_pieces, early, None, (theirs_x[1], theirs[deep - 1]), jnp.float32
    )
    awaited = (value_early, [theirs_x[k] for k in range(1, deep)])
    key_sum = project_blocks(key_pieces, range(2 * deep), None, awaited, jnp.bfloat16)
    key_back = in_chip(key_sum)

    def own_head(sums):
        sums = lax.dynamic_slice_in_dim(sums, own_place, HEAD_DIM, 1)
        return sums.reshape(2, samples, HEAD_DIM).astype(jnp.float32)

    new_keys = own_head(key_sum[chip_rows:]) + own_head(key_back[chip_rows:])
    new_keys = turn(new_keys, step_tables).astype(jnp.bfloat16).astype(jnp.float32)
    new_keys = new_keys.reshape(steps, HEAD_DIM)
    masks = []
    if prompts > 1:
        token_prompt = jnp.repeat(slots // PROMPT_PAGES, PAGE)
        row_prompt = jnp.tile(sample_order // group_size, devices // KV_HEADS * rows // samples)
        masks = [token_prompt[:, None], row_prompt[None, :]]
    kept, sent, step_values = attend(
        kv_places, query_turns, ring_queries, key_sum, key_back, cosine, sine_part, masks,
        prompt_states, got, wide_states, jnp.stack([own_blocks[i] for i in late]), width,
        [value_pieces[i] for i in late], value_early,
    )
    new_values = own_head(step_values) + own_head(in_chip(step_values))
    new_values = new_values.astype(jnp.bfloat16).astype(jnp.float32).reshape(steps, HEAD_DIM)

    by_owner = (deep, 2, *kept.shape[2:])
    near, far = merge_cores(kept.reshape(by_owner), in_chip(sent.reshape(by_owner)))
    merged = merge_chips(own_a[None], near, along_y(far))
    parts = [merged[0]] + [along_z(merged[k], k) for k in range(1, deep)]

    out_width = out_weight.shape[1] // devices
    out_blocks = jnp.stack(
        [
            block((own_a + k) % deep, flip, own_c ^ turned)
            for turned in (0, 1)
            for flip in (0, 1)
            for k in range(deep)
        ]
    )
    terms = out_project(out_blocks, parts, queries, new_keys, new_values, out_weight, out_width)

    def narrow(value):
        return value.astype(jnp.bfloat16)

    def wide(value):
        return value.astype(jnp.float32)

    for move in (in_chip, along_y):
        share = terms.shape[1] // 2
        terms = narrow(wide(terms[:, :share]) + wide(move(terms[:, share:])))
    attn_out = wide(terms[:, :out_width])
    for k in range(1, deep):
        attn_out = attn_out + wide(along_z(terms[:, k * out_width : (k + 1) * out_width], k))
    return narrow(attn_out).reshape(2, samples, -1)


def solution(mesh):
    in_specs = (
        P(("groups", "sample"), None),
        P("groups"),
        P(None, "groups", None),
        P("groups"),
        P("sample", None),
        P("sample", None),
        P(None, "sample"),
        P("sample", None),
    )
    out_specs = P(None, "groups", "sample")
    return jax.shard_map(
        on_device, mesh=mesh, in_specs=in_specs, out_specs=out_specs, check_vma=False
    )
```

```python
import jax
import jax.numpy as jnp
from jax import lax
from jax.experimental import pallas as pl
from jax.experimental.pallas import tpu as pltpu
from jax.sharding import PartitionSpec as P

D = 8192
HEAD_DIM = 128
KV_HEADS = 4
GQA = 8
PAGE = 128
PROMPT_PAGES = 64
LINE = 4

rope_base = 1000000.0


def rope_tables(position):
    half_dim = HEAD_DIM // 2
    frequency = rope_base ** (-jnp.arange(half_dim, dtype=jnp.float32) * 2.0 / HEAD_DIM)
    angles = position.astype(jnp.float32)[..., None] * frequency
    return jnp.cos(angles), jnp.sin(angles)


def turn(vector, tables):
    cosine, sine_part = tables
    half_dim = HEAD_DIM // 2
    first_half = vector[..., :half_dim]
    second_half = vector[..., half_dim:]
    return jnp.concatenate(
        [
            first_half * cosine - second_half * sine_part,
            second_half * cosine + first_half * sine_part,
        ],
        axis=-1,
    )


def ring_order(deep):
    return [*range(0, deep, 2), *range(deep - 1 - deep % 2, 0, -2)]


def mover(groups, devices):
    deep = devices // LINE
    order = ring_order(deep)

    def move(value, step):
        pairs = []
        for g in range(groups):
            for s in range(devices):
                a, b, c = s // LINE, s // 2 % 2, s % 2
                to_g, to_a, to_b, to_c = step(g, a, b, c)
                to_s = (to_a % deep) * LINE + to_b * 2 + to_c
                pairs.append((g * devices + s, to_g * devices + to_s))
        return lax.ppermute(value, ("groups", "sample"), pairs)

    def next_on_ring(a):
        return order[(order.index(a) + 1) % deep]

    along_ring = lambda v: move(v, lambda g, a, b, c: (g, next_on_ring(a), b, c))
    along_z = lambda v, k: move(v, lambda g, a, b, c: (g, a ^ k, b, c))
    along_y = lambda v: move(v, lambda g, a, b, c: (g, a, 1 - b, c))
    along_x = lambda v: move(v, lambda g, a, b, c: (g ^ 1, a, b, c))
    in_chip = lambda v: move(v, lambda g, a, b, c: (g, a, b, 1 - c))
    return along_ring, along_z, along_y, along_x, in_chip


def after(value, done):
    return lax.optimization_barrier((value, done))[0]


MIB = 1024 * 1024
LIGHT = pl.CostEstimate(flops=1, bytes_accessed=1, transcendentals=0)


def project_queries(steps, weight, cosine, sine):
    count, depth = steps.shape
    parts = 8
    piece = depth // parts

    def body(step_ref, weight_ref, cosine_ref, sine_ref, out_ref, held, sems):
        copies = []
        for i in range(parts):
            copies.append(
                pltpu.make_async_copy(
                    weight_ref.at[pl.ds(i * piece, piece), :], held.at[i], sems.at[i]
                )
            )
            copies[-1].start()
        total = None
        for i in range(parts):
            copies[i].wait()
            product = jnp.dot(
                step_ref[:, i * piece : (i + 1) * piece],
                held[i],
                preferred_element_type=jnp.float32,
            )
            total = product if total is None else total + product
        for start in range(0, weight.shape[1], HEAD_DIM):
            head = total[:, start : start + HEAD_DIM]
            turned = head * cosine_ref[...] + pltpu.roll(head, HEAD_DIM // 2, 1) * sine_ref[...]
            out_ref[:, start : start + HEAD_DIM] = turned.astype(jnp.bfloat16)

    whole = pl.BlockSpec(memory_space=pltpu.VMEM)
    return pl.pallas_call(
        body,
        in_specs=[whole, pl.BlockSpec(memory_space=pltpu.HBM), whole, whole],
        out_specs=whole,
        out_shape=jax.ShapeDtypeStruct((count, weight.shape[1]), jnp.bfloat16),
        scratch_shapes=[
            pltpu.VMEM((parts, piece, weight.shape[1]), weight.dtype),
            pltpu.SemaphoreType.DMA((parts,)),
        ],
        compiler_params=pltpu.CompilerParams(vmem_limit_bytes=61 * MIB),
        cost_estimate=LIGHT,
    )(steps, weight, cosine, sine)


def collect(arrays, first, height):
    columns = arrays[0].shape[1]

    def body(*refs):
        out_ref, sems = refs[-2:]
        copies = [
            pltpu.make_async_copy(ref.at[pl.ds(first, height), :], out_ref.at[i], sems.at[i])
            for i, ref in enumerate(refs[:-2])
        ]
        for copy in copies:
            copy.start()
        for copy in copies:
            copy.wait()

    return pl.pallas_call(
        body,
        in_specs=[pl.BlockSpec(memory_space=pl.ANY)] * len(arrays),
        out_specs=pl.BlockSpec(memory_space=pltpu.VMEM),
        out_shape=jax.ShapeDtypeStruct((len(arrays), height, columns), arrays[0].dtype),
        scratch_shapes=[pltpu.SemaphoreType.DMA((len(arrays),))],
        compiler_params=pltpu.CompilerParams(vmem_limit_bytes=4 * MIB),
        cost_estimate=LIGHT,
    )(*arrays)


class Blocks:
    def __init__(self, prompt, steps, width, pieces):
        self.arrays = []
        for piece in pieces:
            for array, _ in piece:
                if not any(array is held for held in self.arrays):
                    self.arrays.append(array)
        self.pieces, self.width, self.count = pieces, width, len(pieces)
        self.row_count, self.step_count = prompt.shape[0], steps.shape[0]
        self.height = 2 * self.row_count + self.step_count
        self.columns = sum(array.shape[1] for array, _ in pieces[0])
        self.scratch = [
            pltpu.VMEM((self.count, self.height, width), prompt.dtype),
            pltpu.VMEM((self.count, width, self.columns), prompt.dtype),
            pltpu.SemaphoreType.DMA((self.count, 5)),
        ]

    def copies(self, i, block_ref, sources, weight_refs, scratch):
        left, weights, sems = scratch
        column = pl.ds(pl.multiple_of(block_ref[i] * self.width, self.width), self.width)
        group = []
        start = 0
        for j, (source, rows) in enumerate(
            zip(sources, (self.row_count, self.row_count, self.step_count))
        ):
            group.append(
                pltpu.make_async_copy(
                    source.at[:, column], left.at[i, pl.ds(start, rows), :], sems.at[i, j]
                )
            )
            start += rows
        side = 0
        for j, (array, first) in enumerate(self.pieces[i]):
            ref = weight_refs[[array is other for other in self.arrays].index(True)]
            group.append(
                pltpu.make_async_copy(
                    ref.at[pl.ds(first, self.width), :],
                    weights.at[i, :, pl.ds(side, array.shape[1])],
                    sems.at[i, 3 + j],
                )
            )
            side += array.shape[1]
        return group


AHEAD = 3


def project(prompt, got, steps, blocks, width, pieces, acc, kind):
    held = Blocks(prompt, steps, width, pieces)
    extra = [] if acc is None else [acc]

    def body(block_ref, prompt_ref, got_ref, step_ref, *refs):
        weight_refs = refs[: len(held.arrays)]
        out_ref, acc_held, acc_sem, *scratch = refs[len(held.arrays) + len(extra) :]
        left, weights, _ = scratch
        sources = (prompt_ref, got_ref, step_ref)
        groups = [
            held.copies(i, block_ref, sources, weight_refs, scratch) for i in range(held.count)
        ]
        for group in groups[:AHEAD]:
            for copy in group:
                copy.start()
        if extra:
            before = pltpu.make_async_copy(refs[len(held.arrays)], acc_held, acc_sem.at[0])
            before.start()
        total = None
        for i, group in enumerate(groups):
            for copy in group:
                copy.wait()
            if i + AHEAD < held.count:
                for copy in groups[i + AHEAD]:
                    copy.start()
            product = jnp.dot(left[i], weights[i], preferred_element_type=jnp.float32)
            total = product if total is None else total + product
        if extra:
            before.wait()
            total = total + acc_held[...]
        out_ref[...] = total.astype(kind)

    anywhere = pl.BlockSpec(memory_space=pl.ANY)
    return pl.pallas_call(
        body,
        in_specs=[pl.BlockSpec(memory_space=pltpu.SMEM)] + [anywhere] * (3 + len(held.arrays) + len(extra)),
        out_specs=pl.BlockSpec(memory_space=pltpu.VMEM),
        out_shape=jax.ShapeDtypeStruct((held.height, held.columns), kind),
        scratch_shapes=[
            pltpu.VMEM((held.height, held.columns) if extra else (8, HEAD_DIM), jnp.float32),
            pltpu.SemaphoreType.DMA((1,)),
            *held.scratch,
        ],
        compiler_params=pltpu.CompilerParams(vmem_limit_bytes=57 * MIB),
        cost_estimate=LIGHT,
    )(blocks, prompt, got, steps, *held.arrays, *extra)


NOTES = 16


def thirds(value):
    parts = []
    for _ in range(3):
        parts.append(value.astype(jnp.bfloat16))
        value = value - parts[-1].astype(jnp.float32)
    return parts


def note_rows(top, total):
    parts = [part.astype(jnp.float32) for part in thirds(top) + thirds(total)]
    rows = jnp.concatenate(parts + [jnp.zeros((NOTES - 6, top.shape[1]), jnp.float32)], axis=0)
    return rows.astype(jnp.bfloat16)


def read_notes(rows):
    rows = rows.astype(jnp.float32)
    return rows[0:1] + rows[1:2] + rows[2:3], rows[3:4] + rows[4:5] + rows[5:6]


def small_call(body, out_shapes, scalars, arrays):
    whole = pl.BlockSpec(memory_space=pltpu.VMEM)
    return pl.pallas_call(
        body,
        in_specs=[pl.BlockSpec(memory_space=pltpu.SMEM)] * len(scalars) + [whole] * len(arrays),
        out_specs=[whole] * len(out_shapes),
        out_shape=[jax.ShapeDtypeStruct(shape, jnp.bfloat16) for shape in out_shapes],
        compiler_params=pltpu.CompilerParams(vmem_limit_bytes=12 * MIB),
        cost_estimate=LIGHT,
    )(*scalars, *arrays)


def merge_cores(own, other):
    deep, _, height, lanes = own.shape

    def body(own_ref, other_ref, near_ref, far_ref):
        for z in range(deep):
            for y, out_ref in enumerate((near_ref, far_ref)):
                both = own_ref[z, y, :HEAD_DIM, :].astype(jnp.float32) + other_ref[
                    z, y, :HEAD_DIM, :
                ].astype(jnp.float32)
                out_ref[z, :HEAD_DIM, :] = both.astype(jnp.bfloat16)
                out_ref[z, HEAD_DIM:, :] = own_ref[z, y, HEAD_DIM:, :]

    return small_call(body, [(deep, height, lanes)] * 2, [], [own, other])


def merge_chips(own_place, near, far):
    deep, height, lanes = near.shape

    def body(place_ref, near_ref, far_ref, *out_refs):
        for k, out_ref in enumerate(out_refs):
            z = place_ref[0] ^ k
            first, second = near_ref[z], far_ref[z]
            first_top, first_total = read_notes(first[HEAD_DIM:, :])
            second_top, second_total = read_notes(second[HEAD_DIM:, :])
            top = jnp.maximum(first_top, second_top)
            first_factor, second_factor = jnp.exp(first_top - top), jnp.exp(second_top - top)
            out_ref[:HEAD_DIM, :] = (
                first[:HEAD_DIM, :].astype(jnp.float32) * first_factor
                + second[:HEAD_DIM, :].astype(jnp.float32) * second_factor
            ).astype(jnp.bfloat16)
            out_ref[HEAD_DIM:, :] = note_rows(
                top, first_total * first_factor + second_total * second_factor
            )

    return small_call(body, [(height, lanes)] * deep, [own_place], [near, far])


def attend(
    places, turns, queries, own, other, cosine, sine, masks, prompt, got, steps, blocks, width,
    pieces, early,
):
    kv_heads = places.shape[0]
    deep, packed, lanes = queries[0].shape
    share = deep // kv_heads
    count = 2 * share * packed * lanes // HEAD_DIM
    owners = count // HEAD_DIM
    tokens = cosine.shape[0]
    half = tokens // 2
    held = Blocks(prompt, steps, width, pieces)
    inputs = [*queries, own, other, cosine, sine, *masks]

    def body(place_ref, turn_ref, block_ref, *refs):
        query_refs = refs[:2]
        own_ref, other_ref, cosine_ref, sine_ref = refs[2:6]
        mask_refs = refs[6 : len(inputs)]
        prompt_ref, got_ref, step_ref, early_ref = refs[len(inputs) : len(inputs) + 4]
        rest = refs[len(inputs) + 4 :]
        weight_refs, rest = rest[: len(held.arrays)], rest[len(held.arrays) :]
        *out_refs, step_out_ref = rest[:3]
        early_held, weight_held, value_held, early_sem, *scratch = rest[3:]
        left, weight_rows, _ = scratch
        sources = (prompt_ref, got_ref, step_ref)
        groups = [
            held.copies(i, block_ref, sources, weight_refs, scratch) for i in range(held.count)
        ]
        before = pltpu.make_async_copy(early_ref, early_held, early_sem.at[0])
        before.start()
        for group in groups:
            for copy in group:
                copy.start()
        wide_cosine = jnp.concatenate([cosine_ref[...], cosine_ref[...]], axis=1)
        wide_sine = jnp.concatenate([-sine_ref[...], sine_ref[...]], axis=1)

        def one_head(j, _):
            column = pl.ds(pl.multiple_of(place_ref[j] * HEAD_DIM, HEAD_DIM), HEAD_DIM)
            keys = jnp.concatenate(
                [
                    own_ref[:half, column].astype(jnp.float32)
                    + other_ref[half:tokens, column].astype(jnp.float32),
                    own_ref[half:tokens, column].astype(jnp.float32)
                    + other_ref[:half, column].astype(jnp.float32),
                ],
                axis=0,
            )
            swapped = pltpu.roll(keys, HEAD_DIM // 2, 1)
            keys = (keys * wide_cosine + swapped * wide_sine).astype(jnp.bfloat16)
            unpacked = []
            for part in range(share):
                for ref in query_refs:
                    both = ref[turn_ref[j * share + part]]
                    for low in range(0, packed, packed // 2):
                        for left_lane in range(0, lanes, HEAD_DIM):
                            unpacked.append(
                                both[low : low + packed // 2, left_lane : left_lane + HEAD_DIM]
                            )
            scores = lax.dot_general(
                keys,
                jnp.concatenate(unpacked, axis=0),
                (((1,), (1,)), ((), ())),
                preferred_element_type=jnp.float32,
            ) * (HEAD_DIM**-0.5)
            if masks:
                scores = jnp.where(mask_refs[0][...] == mask_refs[1][...], scores, -1e30)
            top = jnp.max(scores, axis=0, keepdims=True)
            weights = jnp.exp(scores - top)
            total = jnp.sum(weights, axis=0, keepdims=True)
            for i in range(owners):
                lane = slice(i * HEAD_DIM, (i + 1) * HEAD_DIM)
                out_ref = out_refs[i // 2 % 2]
                out_ref[j, i // 4 * 2 + i % 2, HEAD_DIM:, :] = note_rows(
                    top[:, lane], total[:, lane]
                )
            weight_held[j] = weights.astype(jnp.bfloat16)
            return 0

        lax.fori_loop(0, kv_heads, one_head, 0)
        before.wait()
        total = early_held[...]
        for i, group in enumerate(groups):
            for copy in group:
                copy.wait()
            total += jnp.dot(left[i], weight_rows[i], preferred_element_type=jnp.float32)
        value_held[...] = total[:tokens].astype(jnp.bfloat16)
        step_out_ref[...] = total[tokens:]

        def one_sum(j, _):
            column = pl.ds(pl.multiple_of(place_ref[j] * HEAD_DIM, HEAD_DIM), HEAD_DIM)
            summed = lax.dot_general(
                value_held[:, column],
                weight_held[j],
                (((0,), (0,)), ((), ())),
                preferred_element_type=jnp.float32,
            )
            for i in range(owners):
                lane = slice(i * HEAD_DIM, (i + 1) * HEAD_DIM)
                out_ref = out_refs[i // 2 % 2]
                out_ref[j, i // 4 * 2 + i % 2, :HEAD_DIM, :] = summed[:, lane].astype(jnp.bfloat16)
            return 0

        lax.fori_loop(0, kv_heads, one_sum, 0)

    anywhere = pl.BlockSpec(memory_space=pl.ANY)
    whole = pl.BlockSpec(memory_space=pltpu.VMEM)
    return pl.pallas_call(
        body,
        in_specs=[pl.BlockSpec(memory_space=pltpu.SMEM)] * 3
        + [whole] * len(inputs)
        + [anywhere] * (4 + len(held.arrays)),
        out_specs=[whole] * 3,
        out_shape=[
            *[
                jax.ShapeDtypeStruct(
                    (kv_heads, owners // 2, HEAD_DIM + NOTES, HEAD_DIM), jnp.bfloat16
                )
            ]
            * 2,
            jax.ShapeDtypeStruct((held.step_count, held.columns), jnp.float32),
        ],
        scratch_shapes=[
            pltpu.VMEM((held.height, held.columns), jnp.float32),
            pltpu.VMEM((kv_heads, tokens, count), jnp.bfloat16),
            pltpu.VMEM((tokens, held.columns), jnp.bfloat16),
            pltpu.SemaphoreType.DMA((1,)),
            *held.scratch,
        ],
        compiler_params=pltpu.CompilerParams(vmem_limit_bytes=57 * MIB),
        cost_estimate=LIGHT,
    )(places, turns, blocks, *inputs, prompt, got, steps, early, *held.arrays)


def out_project(blocks, parts, queries, new_keys, new_values, weight, width):
    count = len(parts)
    steps = queries.shape[0]
    samples = steps // 2

    def body(block_ref, *refs):
        part_refs = refs[:count]
        query_ref, key_ref, value_ref, weight_ref, out_ref = refs[count:]
        notes = [read_notes(ref[HEAD_DIM:, :]) for ref in part_refs]
        top = notes[0][0]
        for other, _ in notes[1:]:
            top = jnp.maximum(top, other)
        sums = total = 0.0
        for ref, (part_top, part_total) in zip(part_refs, notes):
            factor = jnp.exp(part_top - top)
            sums = sums + ref[:HEAD_DIM, :].astype(jnp.float32) * factor
            total = total + part_total * factor
        sums = sums.T
        both = jnp.concatenate([top, total, jnp.zeros((6, HEAD_DIM), jnp.float32)], axis=0).T
        keys, values = key_ref[...], value_ref[...]
        heads = []
        for h in range(queries.shape[1] // HEAD_DIM):
            query = query_ref[:, h * HEAD_DIM : (h + 1) * HEAD_DIM].astype(jnp.float32)
            own_score = jnp.sum(query * keys, axis=1, keepdims=True) * (HEAD_DIM**-0.5)
            back_score = jnp.sum(
                query[samples:] * keys[:samples], axis=1, keepdims=True
            ) * (HEAD_DIM**-0.5)
            ends = []
            for step in (0, 1):
                place = slice((2 * h + step) * samples, (2 * h + step + 1) * samples)
                here = slice(step * samples, (step + 1) * samples)
                old_top, old_total = both[place, 0:1], both[place, 1:2]
                scores = [(own_score[here], values[here])]
                if step:
                    scores.append((back_score, values[:samples]))
                high = old_top
                for score, _ in scores:
                    high = jnp.maximum(high, score)
                old = jnp.exp(old_top - high)
                numerator, denominator = old * sums[place], old * old_total
                for score, value in scores:
                    new = jnp.exp(score - high)
                    numerator, denominator = numerator + new * value, denominator + new
                ends.append(numerator / denominator)
            heads.append(jnp.concatenate(ends, axis=0).astype(jnp.bfloat16))
        heads = jnp.concatenate(heads, axis=1)
        for i in range(blocks.shape[0]):
            start = pl.multiple_of(block_ref[i] * width, width)
            out_ref[:, i * width : (i + 1) * width] = jnp.dot(
                heads, weight_ref[:, pl.ds(start, width)], preferred_element_type=jnp.float32
            ).astype(jnp.bfloat16)

    return small_call(
        body, [(steps, weight.shape[1])], [blocks], [*parts, queries, new_keys, new_values, weight]
    )[0]


def on_device(
    prompt_states,
    page_table,
    step_states,
    sample_order,
    key_weight,
    value_weight,
    query_weight,
    out_weight,
):
    devices = lax.axis_size("sample")
    groups = lax.axis_size("groups")
    own_index = lax.axis_index("sample")
    first = lax.axis_index("groups") % 2 == 0
    deep = devices // LINE
    own_a, own_b, own_c = own_index // LINE, own_index // 2 % 2, own_index % 2
    along_ring, along_z, along_y, along_x, in_chip = mover(groups, devices)
    row_count = prompt_states.shape[0]
    chip_rows = 2 * row_count
    pages_here = row_count // PAGE
    heads_here = query_weight.shape[1] // HEAD_DIM
    total_pages = page_table.shape[0]
    prompts = total_pages // PROMPT_PAGES
    samples = sample_order.shape[0]
    steps = 2 * samples
    group_size = samples // prompts
    own_kv = own_index * heads_here // GQA
    wide_states = step_states.reshape(steps, D)
    rows = heads_here * steps
    width = key_weight.shape[0]
    half = key_weight.shape[1] // 2
    kv_places = jnp.where(first, 0, KV_HEADS // 2) + jnp.arange(KV_HEADS, dtype=jnp.int32)
    kv_places = kv_places % KV_HEADS

    order = ring_order(deep)

    def by_place(table):
        return sum(jnp.where(own_a == a, table[a], 0) for a in range(deep))

    own_turn = by_place([order.index(a) for a in range(deep)])

    def block(place_z, flip, core):
        return place_z * LINE + (own_b ^ flip) * 2 + core

    def behind(k):
        return by_place([order[(order.index(a) - k) % deep] for a in range(deep)])

    low = jnp.concatenate([key_weight[:, :half], value_weight[:, :half]])
    high = jnp.concatenate([key_weight[:, half:], value_weight[:, half:]])
    both_mine, both_other = jnp.where(first, low, high), jnp.where(first, high, low)

    own_pages = jnp.concatenate(
        [
            holder * pages_here + jnp.arange(pages_here, dtype=jnp.int32)
            for holder in (own_index, own_index ^ 1)
        ]
    )
    slots = jnp.sum(
        jnp.where(
            page_table[None, :] == own_pages[:, None],
            jnp.arange(total_pages, dtype=jnp.int32)[None, :],
            0,
        ),
        axis=1,
    )
    positions = (slots % PROMPT_PAGES * PAGE)[:, None] + jnp.arange(PAGE, dtype=jnp.int32)[None, :]
    cosine, sine_part = rope_tables(positions.reshape(chip_rows))

    step_place = PROMPT_PAGES * PAGE + jnp.arange(2, dtype=jnp.int32)
    step_tables = tuple(t[:, None, :] for t in rope_tables(step_place))
    flat_tables = [
        jnp.repeat(jnp.concatenate([sign * table, table], axis=-1)[:, 0], samples, axis=0)
        for sign, table in zip((1, -1), step_tables)
    ]
    queries = project_queries(
        after(wide_states, (cosine, sine_part)), query_weight, *flat_tables
    )
    packed_queries = jnp.concatenate(
        jnp.split(queries, half // queries.shape[1], axis=0), axis=1
    )
    packed = packed_queries.shape[0]

    places = [(k, flip) for k in range(deep) for flip in (0, 1)]
    own_blocks = jnp.stack([block(behind(k), flip, own_c) for k, flip in places])
    query_turns = jnp.stack([(own_turn + deep - order.index(a)) % deep for a in range(deep)])
    own_place = (own_kv + jnp.where(first, 0, KV_HEADS // 2)) % KV_HEADS * HEAD_DIM
    done = {}

    def send(move, value):
        moved = done.setdefault(move, [])
        moved.append(move(after(value, moved[-2]) if len(moved) > 1 else value))
        return moved[-1]

    got = in_chip(prompt_states)
    both_z, both_x, theirs, theirs_x = {0: both_mine}, {0: both_other}, {}, {}
    both_z[1] = send(along_ring, both_mine)
    value_y = send(along_y, both_mine[width:])
    key_full = {0: jnp.concatenate([both_mine[:width], both_other[:width], packed_queries])}
    key_y = {0: send(along_y, after(key_full[0], value_y))}
    theirs[0] = jnp.concatenate([value_y, packed_queries, key_y[0][2 * width :]])
    for k in range(1, deep):
        if k + 1 < deep:
            both_z[k + 1] = send(along_ring, both_z[k])
        if k == 1:
            theirs_x[0] = send(along_x, value_y)
        both_x[k] = send(along_x, both_z[k])
        key_full[k] = jnp.concatenate([both_z[k][:width], both_x[k][:width]])
        key_y[k] = send(along_y, after(key_full[k], key_y[k - 1]))
    for k in range(1, deep):
        theirs[k] = send(along_ring, theirs[k - 1])
        theirs_x[k] = send(along_x, theirs[k][:width])

    ring_queries = collect([theirs[k] for k in range(deep)], width, 2 * packed)
    ring_queries = [ring_queries, in_chip(ring_queries)]

    key_pieces = [
        [((key_y if flip else key_full)[k], start) for start in (0, width)] for k, flip in places
    ]
    value_pieces = [
        [(theirs[k], 0), (theirs_x[k], 0)] if flip else [(both_z[k], width), (both_x[k], width)]
        for k, flip in places
    ]

    def project_blocks(pieces, which, acc, ready, kind):
        taken = after(jnp.stack([own_blocks[i] for i in which]), ready)
        return project(
            prompt_states, got, wide_states, taken, width, [pieces[i] for i in which], acc, kind
        )

    early = [*range(0, 2 * deep, 2), 1]
    late = [i for i in range(2 * deep) if i not in early]
    value_early = project_blocks(
        value_pieces, early, None, (theirs_x[1], theirs[deep - 1]), jnp.float32
    )
    awaited = (value_early, [theirs_x[k] for k in range(1, deep)])
    key_sum = project_blocks(key_pieces, range(2 * deep), None, awaited, jnp.bfloat16)
    key_back = in_chip(key_sum)

    def own_head(sums):
        sums = lax.dynamic_slice_in_dim(sums, own_place, HEAD_DIM, 1)
        return sums.reshape(2, samples, HEAD_DIM).astype(jnp.float32)

    new_keys = own_head(key_sum[chip_rows:]) + own_head(key_back[chip_rows:])
    new_keys = turn(new_keys, step_tables).astype(jnp.bfloat16).astype(jnp.float32)
    new_keys = new_keys.reshape(steps, HEAD_DIM)
    masks = []
    if prompts > 1:
        token_prompt = jnp.repeat(slots // PROMPT_PAGES, PAGE)
        row_prompt = jnp.tile(sample_order // group_size, devices // KV_HEADS * rows // samples)
        masks = [token_prompt[:, None], row_prompt[None, :]]
    kept, sent, step_values = attend(
        kv_places, query_turns, ring_queries, key_sum, key_back, cosine, sine_part, masks,
        prompt_states, got, wide_states, jnp.stack([own_blocks[i] for i in late]), width,
        [value_pieces[i] for i in late], value_early,
    )
    new_values = own_head(step_values) + own_head(in_chip(step_values))
    new_values = new_values.astype(jnp.bfloat16).astype(jnp.float32).reshape(steps, HEAD_DIM)

    by_owner = (deep, 2, *kept.shape[2:])
    near, far = merge_cores(kept.reshape(by_owner), in_chip(sent.reshape(by_owner)))
    merged = merge_chips(own_a[None], near, along_y(far))
    parts = [merged[0]] + [along_z(merged[k], k) for k in range(1, deep)]

    out_width = out_weight.shape[1] // devices
    out_blocks = jnp.stack(
        [
            block(own_a ^ k, flip, own_c ^ turned)
            for turned in (0, 1)
            for flip in (0, 1)
            for k in range(deep)
        ]
    )
    terms = out_project(out_blocks, parts, queries, new_keys, new_values, out_weight, out_width)

    def narrow(value):
        return value.astype(jnp.bfloat16)

    def wide(value):
        return value.astype(jnp.float32)

    for move in (in_chip, along_y):
        share = terms.shape[1] // 2
        terms = narrow(wide(terms[:, :share]) + wide(move(terms[:, share:])))
    attn_out = wide(terms[:, :out_width])
    for k in range(1, deep):
        attn_out = attn_out + wide(along_z(terms[:, k * out_width : (k + 1) * out_width], k))
    return narrow(attn_out).reshape(2, samples, -1)


def solution(mesh):
    in_specs = (
        P(("groups", "sample"), None),
        P("groups"),
        P(None, "groups", None),
        P("groups"),
        P("sample", None),
        P("sample", None),
        P(None, "sample"),
        P("sample", None),
    )
    out_specs = P(None, "groups", "sample")
    return jax.shard_map(
        on_device, mesh=mesh, in_specs=in_specs, out_specs=out_specs, check_vma=False
    )
```

```python
import jax
import jax.numpy as jnp
from jax import lax
from jax.experimental import pallas as pl
from jax.experimental.pallas import tpu as pltpu
from jax.sharding import PartitionSpec as P

D = 8192
HEAD_DIM = 128
KV_HEADS = 4
GQA = 8
PAGE = 128
PROMPT_PAGES = 64
LINE = 4

rope_base = 1000000.0


def rope_tables(position):
    half_dim = HEAD_DIM // 2
    frequency = rope_base ** (-jnp.arange(half_dim, dtype=jnp.float32) * 2.0 / HEAD_DIM)
    angles = position.astype(jnp.float32)[..., None] * frequency
    return jnp.cos(angles), jnp.sin(angles)


def turn(vector, tables):
    cosine, sine_part = tables
    half_dim = HEAD_DIM // 2
    first_half = vector[..., :half_dim]
    second_half = vector[..., half_dim:]
    return jnp.concatenate(
        [
            first_half * cosine - second_half * sine_part,
            second_half * cosine + first_half * sine_part,
        ],
        axis=-1,
    )


def ring_order(deep):
    return [*range(0, deep, 2), *range(deep - 1 - deep % 2, 0, -2)]


def mover(groups, devices):
    deep = devices // LINE
    order = ring_order(deep)

    def move(value, step):
        pairs = []
        for g in range(groups):
            for s in range(devices):
                a, b, c = s // LINE, s // 2 % 2, s % 2
                to_g, to_a, to_b, to_c = step(g, a, b, c)
                to_s = (to_a % deep) * LINE + to_b * 2 + to_c
                pairs.append((g * devices + s, to_g * devices + to_s))
        return lax.ppermute(value, ("groups", "sample"), pairs)

    def next_on_ring(a):
        return order[(order.index(a) + 1) % deep]

    along_ring = lambda v: move(v, lambda g, a, b, c: (g, next_on_ring(a), b, c))
    along_z = lambda v, k: move(v, lambda g, a, b, c: (g, a ^ k, b, c))
    along_y = lambda v: move(v, lambda g, a, b, c: (g, a, 1 - b, c))
    along_x = lambda v: move(v, lambda g, a, b, c: (g ^ 1, a, b, c))
    in_chip = lambda v: move(v, lambda g, a, b, c: (g, a, b, 1 - c))
    return along_ring, along_z, along_y, along_x, in_chip


def after(value, done):
    return lax.optimization_barrier((value, done))[0]


MIB = 1024 * 1024
LIGHT = pl.CostEstimate(flops=1, bytes_accessed=1, transcendentals=0)


def project_queries(steps, weight, cosine, sine):
    count, depth = steps.shape
    parts = 8
    piece = depth // parts

    def body(step_ref, weight_ref, cosine_ref, sine_ref, out_ref, held, sems):
        copies = []
        for i in range(parts):
            copies.append(
                pltpu.make_async_copy(
                    weight_ref.at[pl.ds(i * piece, piece), :], held.at[i], sems.at[i]
                )
            )
            copies[-1].start()
        total = None
        for i in range(parts):
            copies[i].wait()
            product = jnp.dot(
                step_ref[:, i * piece : (i + 1) * piece],
                held[i],
                preferred_element_type=jnp.float32,
            )
            total = product if total is None else total + product
        for start in range(0, weight.shape[1], HEAD_DIM):
            head = total[:, start : start + HEAD_DIM]
            turned = head * cosine_ref[...] + pltpu.roll(head, HEAD_DIM // 2, 1) * sine_ref[...]
            out_ref[:, start : start + HEAD_DIM] = turned.astype(jnp.bfloat16)

    whole = pl.BlockSpec(memory_space=pltpu.VMEM)
    return pl.pallas_call(
        body,
        in_specs=[whole, pl.BlockSpec(memory_space=pltpu.HBM), whole, whole],
        out_specs=whole,
        out_shape=jax.ShapeDtypeStruct((count, weight.shape[1]), jnp.bfloat16),
        scratch_shapes=[
            pltpu.VMEM((parts, piece, weight.shape[1]), weight.dtype),
            pltpu.SemaphoreType.DMA((parts,)),
        ],
        compiler_params=pltpu.CompilerParams(vmem_limit_bytes=61 * MIB),
        cost_estimate=LIGHT,
    )(steps, weight, cosine, sine)


def collect(arrays, first, height):
    columns = arrays[0].shape[1]

    def body(*refs):
        out_ref, sems = refs[-2:]
        copies = [
            pltpu.make_async_copy(ref.at[pl.ds(first, height), :], out_ref.at[i], sems.at[i])
            for i, ref in enumerate(refs[:-2])
        ]
        for copy in copies:
            copy.start()
        for copy in copies:
            copy.wait()

    return pl.pallas_call(
        body,
        in_specs=[pl.BlockSpec(memory_space=pl.ANY)] * len(arrays),
        out_specs=pl.BlockSpec(memory_space=pltpu.VMEM),
        out_shape=jax.ShapeDtypeStruct((len(arrays), height, columns), arrays[0].dtype),
        scratch_shapes=[pltpu.SemaphoreType.DMA((len(arrays),))],
        compiler_params=pltpu.CompilerParams(vmem_limit_bytes=4 * MIB),
        cost_estimate=LIGHT,
    )(*arrays)


class Blocks:
    def __init__(self, prompt, steps, width, pieces):
        self.arrays = []
        for piece in pieces:
            for array, _ in piece:
                if not any(array is held for held in self.arrays):
                    self.arrays.append(array)
        self.pieces, self.width, self.count = pieces, width, len(pieces)
        self.row_count, self.step_count = prompt.shape[0], steps.shape[0]
        self.height = 2 * self.row_count + self.step_count
        self.columns = sum(array.shape[1] for array, _ in pieces[0])
        self.scratch = [
            pltpu.VMEM((self.count, self.height, width), prompt.dtype),
            pltpu.VMEM((self.count, width, self.columns), prompt.dtype),
            pltpu.SemaphoreType.DMA((self.count, 5)),
        ]

    def copies(self, i, block_ref, sources, weight_refs, scratch):
        left, weights, sems = scratch
        column = pl.ds(pl.multiple_of(block_ref[i] * self.width, self.width), self.width)
        group = []
        start = 0
        for j, (source, rows) in enumerate(
            zip(sources, (self.row_count, self.row_count, self.step_count))
        ):
            group.append(
                pltpu.make_async_copy(
                    source.at[:, column], left.at[i, pl.ds(start, rows), :], sems.at[i, j]
                )
            )
            start += rows
        side = 0
        for j, (array, first) in enumerate(self.pieces[i]):
            ref = weight_refs[[array is other for other in self.arrays].index(True)]
            group.append(
                pltpu.make_async_copy(
                    ref.at[pl.ds(first, self.width), :],
                    weights.at[i, :, pl.ds(side, array.shape[1])],
                    sems.at[i, 3 + j],
                )
            )
            side += array.shape[1]
        return group


AHEAD = 3


def project(prompt, got, steps, blocks, width, pieces, acc, kind):
    held = Blocks(prompt, steps, width, pieces)
    extra = [] if acc is None else [acc]

    def body(block_ref, prompt_ref, got_ref, step_ref, *refs):
        weight_refs = refs[: len(held.arrays)]
        out_ref, acc_held, acc_sem, *scratch = refs[len(held.arrays) + len(extra) :]
        left, weights, _ = scratch
        sources = (prompt_ref, got_ref, step_ref)
        groups = [
            held.copies(i, block_ref, sources, weight_refs, scratch) for i in range(held.count)
        ]
        for group in groups[:AHEAD]:
            for copy in group:
                copy.start()
        if extra:
            before = pltpu.make_async_copy(refs[len(held.arrays)], acc_held, acc_sem.at[0])
            before.start()
        total = None
        for i, group in enumerate(groups):
            for copy in group:
                copy.wait()
            if i + AHEAD < held.count:
                for copy in groups[i + AHEAD]:
                    copy.start()
            product = jnp.dot(left[i], weights[i], preferred_element_type=jnp.float32)
            total = product if total is None else total + product
        if extra:
            before.wait()
            total = total + acc_held[...]
        out_ref[...] = total.astype(kind)

    anywhere = pl.BlockSpec(memory_space=pl.ANY)
    return pl.pallas_call(
        body,
        in_specs=[pl.BlockSpec(memory_space=pltpu.SMEM)] + [anywhere] * (3 + len(held.arrays) + len(extra)),
        out_specs=pl.BlockSpec(memory_space=pltpu.VMEM),
        out_shape=jax.ShapeDtypeStruct((held.height, held.columns), kind),
        scratch_shapes=[
            pltpu.VMEM((held.height, held.columns) if extra else (8, HEAD_DIM), jnp.float32),
            pltpu.SemaphoreType.DMA((1,)),
            *held.scratch,
        ],
        compiler_params=pltpu.CompilerParams(vmem_limit_bytes=57 * MIB),
        cost_estimate=LIGHT,
    )(blocks, prompt, got, steps, *held.arrays, *extra)


NOTES = 16


def thirds(value):
    parts = []
    for _ in range(3):
        parts.append(value.astype(jnp.bfloat16))
        value = value - parts[-1].astype(jnp.float32)
    return parts


def note_rows(top, total):
    parts = [part.astype(jnp.float32) for part in thirds(top) + thirds(total)]
    rows = jnp.concatenate(parts + [jnp.zeros((NOTES - 6, top.shape[1]), jnp.float32)], axis=0)
    return rows.astype(jnp.bfloat16)


def read_notes(rows):
    rows = rows.astype(jnp.float32)
    return rows[0:1] + rows[1:2] + rows[2:3], rows[3:4] + rows[4:5] + rows[5:6]


def small_call(body, out_shapes, scalars, arrays):
    whole = pl.BlockSpec(memory_space=pltpu.VMEM)
    return pl.pallas_call(
        body,
        in_specs=[pl.BlockSpec(memory_space=pltpu.SMEM)] * len(scalars) + [whole] * len(arrays),
        out_specs=[whole] * len(out_shapes),
        out_shape=[jax.ShapeDtypeStruct(shape, jnp.bfloat16) for shape in out_shapes],
        compiler_params=pltpu.CompilerParams(vmem_limit_bytes=12 * MIB),
        cost_estimate=LIGHT,
    )(*scalars, *arrays)


def merge_cores(own, other):
    deep, _, height, lanes = own.shape

    def body(own_ref, other_ref, near_ref, far_ref):
        for z in range(deep):
            for y, out_ref in enumerate((near_ref, far_ref)):
                both = own_ref[z, y, :HEAD_DIM, :].astype(jnp.float32) + other_ref[
                    z, y, :HEAD_DIM, :
                ].astype(jnp.float32)
                out_ref[z, :HEAD_DIM, :] = both.astype(jnp.bfloat16)
                out_ref[z, HEAD_DIM:, :] = own_ref[z, y, HEAD_DIM:, :]

    return small_call(body, [(deep, height, lanes)] * 2, [], [own, other])


def merge_chips(own_place, near, far):
    deep, height, lanes = near.shape

    def body(place_ref, near_ref, far_ref, *out_refs):
        for k, out_ref in enumerate(out_refs):
            z = place_ref[0] ^ k
            first, second = near_ref[z], far_ref[z]
            first_top, first_total = read_notes(first[HEAD_DIM:, :])
            second_top, second_total = read_notes(second[HEAD_DIM:, :])
            top = jnp.maximum(first_top, second_top)
            first_factor, second_factor = jnp.exp(first_top - top), jnp.exp(second_top - top)
            out_ref[:HEAD_DIM, :] = (
                first[:HEAD_DIM, :].astype(jnp.float32) * first_factor
                + second[:HEAD_DIM, :].astype(jnp.float32) * second_factor
            ).astype(jnp.bfloat16)
            out_ref[HEAD_DIM:, :] = note_rows(
                top, first_total * first_factor + second_total * second_factor
            )

    return small_call(body, [(height, lanes)] * deep, [own_place], [near, far])


def attend(
    places, turns, queries, own, other, cosine, sine, masks, prompt, got, steps, blocks, width,
    pieces, early,
):
    kv_heads = places.shape[0]
    deep, packed, lanes = queries[0].shape
    share = deep // kv_heads
    count = 2 * share * packed * lanes // HEAD_DIM
    owners = count // HEAD_DIM
    tokens = cosine.shape[0]
    half = tokens // 2
    held = Blocks(prompt, steps, width, pieces)
    inputs = [*queries, own, other, cosine, sine, *masks]

    def body(place_ref, turn_ref, block_ref, *refs):
        query_refs = refs[:2]
        own_ref, other_ref, cosine_ref, sine_ref = refs[2:6]
        mask_refs = refs[6 : len(inputs)]
        prompt_ref, got_ref, step_ref, early_ref = refs[len(inputs) : len(inputs) + 4]
        rest = refs[len(inputs) + 4 :]
        weight_refs, rest = rest[: len(held.arrays)], rest[len(held.arrays) :]
        *out_refs, step_out_ref = rest[:3]
        early_held, weight_held, value_held, early_sem, *scratch = rest[3:]
        left, weight_rows, _ = scratch
        sources = (prompt_ref, got_ref, step_ref)
        groups = [
            held.copies(i, block_ref, sources, weight_refs, scratch) for i in range(held.count)
        ]
        before = pltpu.make_async_copy(early_ref, early_held, early_sem.at[0])
        before.start()
        for group in groups:
            for copy in group:
                copy.start()
        wide_cosine = jnp.concatenate([cosine_ref[...], cosine_ref[...]], axis=1)
        wide_sine = jnp.concatenate([-sine_ref[...], sine_ref[...]], axis=1)

        def one_head(j, _):
            column = pl.ds(pl.multiple_of(place_ref[j] * HEAD_DIM, HEAD_DIM), HEAD_DIM)
            keys = jnp.concatenate(
                [
                    own_ref[:half, column].astype(jnp.float32)
                    + other_ref[half:tokens, column].astype(jnp.float32),
                    own_ref[half:tokens, column].astype(jnp.float32)
                    + other_ref[:half, column].astype(jnp.float32),
                ],
                axis=0,
            )
            swapped = pltpu.roll(keys, HEAD_DIM // 2, 1)
            keys = (keys * wide_cosine + swapped * wide_sine).astype(jnp.bfloat16)
            unpacked = []
            for part in range(share):
                for ref in query_refs:
                    both = ref[turn_ref[j * share + part]]
                    for low in range(0, packed, packed // 2):
                        for left_lane in range(0, lanes, HEAD_DIM):
                            unpacked.append(
                                both[low : low + packed // 2, left_lane : left_lane + HEAD_DIM]
                            )
            scores = lax.dot_general(
                keys,
                jnp.concatenate(unpacked, axis=0),
                (((1,), (1,)), ((), ())),
                preferred_element_type=jnp.float32,
            ) * (HEAD_DIM**-0.5)
            if masks:
                scores = jnp.where(mask_refs[0][...] == mask_refs[1][...], scores, -1e30)
            top = jnp.max(scores, axis=0, keepdims=True)
            weights = jnp.exp(scores - top)
            total = jnp.sum(weights, axis=0, keepdims=True)
            for i in range(owners):
                lane = slice(i * HEAD_DIM, (i + 1) * HEAD_DIM)
                out_ref = out_refs[i // 2 % 2]
                out_ref[j, i // 4 * 2 + i % 2, HEAD_DIM:, :] = note_rows(
                    top[:, lane], total[:, lane]
                )
            weight_held[j] = weights.astype(jnp.bfloat16)
            return 0

        lax.fori_loop(0, kv_heads, one_head, 0)
        before.wait()
        total = early_held[...]
        for i, group in enumerate(groups):
            for copy in group:
                copy.wait()
            total += jnp.dot(left[i], weight_rows[i], preferred_element_type=jnp.float32)
        value_held[...] = total[:tokens].astype(jnp.bfloat16)
        step_out_ref[...] = total[tokens:]

        def one_sum(j, _):
            column = pl.ds(pl.multiple_of(place_ref[j] * HEAD_DIM, HEAD_DIM), HEAD_DIM)
            summed = lax.dot_general(
                value_held[:, column],
                weight_held[j],
                (((0,), (0,)), ((), ())),
                preferred_element_type=jnp.float32,
            )
            for i in range(owners):
                lane = slice(i * HEAD_DIM, (i + 1) * HEAD_DIM)
                out_ref = out_refs[i // 2 % 2]
                out_ref[j, i // 4 * 2 + i % 2, :HEAD_DIM, :] = summed[:, lane].astype(jnp.bfloat16)
            return 0

        lax.fori_loop(0, kv_heads, one_sum, 0)

    anywhere = pl.BlockSpec(memory_space=pl.ANY)
    whole = pl.BlockSpec(memory_space=pltpu.VMEM)
    return pl.pallas_call(
        body,
        in_specs=[pl.BlockSpec(memory_space=pltpu.SMEM)] * 3
        + [whole] * len(inputs)
        + [anywhere] * (4 + len(held.arrays)),
        out_specs=[whole] * 3,
        out_shape=[
            *[
                jax.ShapeDtypeStruct(
                    (kv_heads, owners // 2, HEAD_DIM + NOTES, HEAD_DIM), jnp.bfloat16
                )
            ]
            * 2,
            jax.ShapeDtypeStruct((held.step_count, held.columns), jnp.float32),
        ],
        scratch_shapes=[
            pltpu.VMEM((held.height, held.columns), jnp.float32),
            pltpu.VMEM((kv_heads, tokens, count), jnp.bfloat16),
            pltpu.VMEM((tokens, held.columns), jnp.bfloat16),
            pltpu.SemaphoreType.DMA((1,)),
            *held.scratch,
        ],
        compiler_params=pltpu.CompilerParams(vmem_limit_bytes=57 * MIB),
        cost_estimate=LIGHT,
    )(places, turns, blocks, *inputs, prompt, got, steps, early, *held.arrays)


def out_project(blocks, parts, queries, new_keys, new_values, weight, width):
    count = len(parts)
    steps = queries.shape[0]
    samples = steps // 2

    def body(block_ref, *refs):
        part_refs = refs[:count]
        query_ref, key_ref, value_ref, weight_ref, out_ref = refs[count:]
        notes = [read_notes(ref[HEAD_DIM:, :]) for ref in part_refs]
        top = notes[0][0]
        for other, _ in notes[1:]:
            top = jnp.maximum(top, other)
        sums = total = 0.0
        for ref, (part_top, part_total) in zip(part_refs, notes):
            factor = jnp.exp(part_top - top)
            sums = sums + ref[:HEAD_DIM, :].astype(jnp.float32) * factor
            total = total + part_total * factor
        sums = sums.T
        both = jnp.concatenate([top, total, jnp.zeros((6, HEAD_DIM), jnp.float32)], axis=0).T
        keys, values = key_ref[...], value_ref[...]
        heads = []
        for h in range(queries.shape[1] // HEAD_DIM):
            query = query_ref[:, h * HEAD_DIM : (h + 1) * HEAD_DIM].astype(jnp.float32)
            own_score = jnp.sum(query * keys, axis=1, keepdims=True) * (HEAD_DIM**-0.5)
            back_score = jnp.sum(
                query[samples:] * keys[:samples], axis=1, keepdims=True
            ) * (HEAD_DIM**-0.5)
            ends = []
            for step in (0, 1):
                place = slice((2 * h + step) * samples, (2 * h + step + 1) * samples)
                here = slice(step * samples, (step + 1) * samples)
                old_top, old_total = both[place, 0:1], both[place, 1:2]
                scores = [(own_score[here], values[here])]
                if step:
                    scores.append((back_score, values[:samples]))
                high = old_top
                for score, _ in scores:
                    high = jnp.maximum(high, score)
                old = jnp.exp(old_top - high)
                numerator, denominator = old * sums[place], old * old_total
                for score, value in scores:
                    new = jnp.exp(score - high)
                    numerator, denominator = numerator + new * value, denominator + new
                ends.append(numerator / denominator)
            heads.append(jnp.concatenate(ends, axis=0).astype(jnp.bfloat16))
        heads = jnp.concatenate(heads, axis=1)
        for i in range(blocks.shape[0]):
            start = pl.multiple_of(block_ref[i] * width, width)
            out_ref[:, i * width : (i + 1) * width] = jnp.dot(
                heads, weight_ref[:, pl.ds(start, width)], preferred_element_type=jnp.float32
            ).astype(jnp.bfloat16)

    return small_call(
        body, [(steps, weight.shape[1])], [blocks], [*parts, queries, new_keys, new_values, weight]
    )[0]


def on_device(
    prompt_states,
    page_table,
    step_states,
    sample_order,
    key_weight,
    value_weight,
    query_weight,
    out_weight,
):
    devices = lax.axis_size("sample")
    groups = lax.axis_size("groups")
    own_index = lax.axis_index("sample")
    first = lax.axis_index("groups") % 2 == 0
    deep = devices // LINE
    own_a, own_b, own_c = own_index // LINE, own_index // 2 % 2, own_index % 2
    along_ring, along_z, along_y, along_x, in_chip = mover(groups, devices)
    row_count = prompt_states.shape[0]
    chip_rows = 2 * row_count
    pages_here = row_count // PAGE
    heads_here = query_weight.shape[1] // HEAD_DIM
    total_pages = page_table.shape[0]
    prompts = total_pages // PROMPT_PAGES
    samples = sample_order.shape[0]
    steps = 2 * samples
    group_size = samples // prompts
    own_kv = own_index * heads_here // GQA
    wide_states = step_states.reshape(steps, D)
    rows = heads_here * steps
    width = key_weight.shape[0]
    half = key_weight.shape[1] // 2
    kv_places = jnp.where(first, 0, KV_HEADS // 2) + jnp.arange(KV_HEADS, dtype=jnp.int32)
    kv_places = kv_places % KV_HEADS

    order = ring_order(deep)

    def by_place(table):
        return sum(jnp.where(own_a == a, table[a], 0) for a in range(deep))

    own_turn = by_place([order.index(a) for a in range(deep)])

    def block(place_z, flip, core):
        return place_z * LINE + (own_b ^ flip) * 2 + core

    def behind(k):
        return by_place([order[(order.index(a) - k) % deep] for a in range(deep)])

    low = jnp.concatenate([key_weight[:, :half], value_weight[:, :half]])
    high = jnp.concatenate([key_weight[:, half:], value_weight[:, half:]])
    both_mine, both_other = jnp.where(first, low, high), jnp.where(first, high, low)

    own_pages = jnp.concatenate(
        [
            holder * pages_here + jnp.arange(pages_here, dtype=jnp.int32)
            for holder in (own_index, own_index ^ 1)
        ]
    )
    slots = jnp.sum(
        jnp.where(
            page_table[None, :] == own_pages[:, None],
            jnp.arange(total_pages, dtype=jnp.int32)[None, :],
            0,
        ),
        axis=1,
    )
    positions = (slots % PROMPT_PAGES * PAGE)[:, None] + jnp.arange(PAGE, dtype=jnp.int32)[None, :]
    cosine, sine_part = rope_tables(positions.reshape(chip_rows))

    step_place = PROMPT_PAGES * PAGE + jnp.arange(2, dtype=jnp.int32)
    step_tables = tuple(t[:, None, :] for t in rope_tables(step_place))
    flat_tables = [
        jnp.repeat(jnp.concatenate([sign * table, table], axis=-1)[:, 0], samples, axis=0)
        for sign, table in zip((1, -1), step_tables)
    ]
    queries = project_queries(
        after(wide_states, (cosine, sine_part)), query_weight, *flat_tables
    )
    packed_queries = jnp.concatenate(
        jnp.split(queries, half // queries.shape[1], axis=0), axis=1
    )
    packed = packed_queries.shape[0]

    places = [(k, flip) for k in range(deep) for flip in (0, 1)]
    own_blocks = jnp.stack([block(behind(k), flip, own_c) for k, flip in places])
    query_turns = jnp.stack([(own_turn + deep - order.index(a)) % deep for a in range(deep)])
    own_place = (own_kv + jnp.where(first, 0, KV_HEADS // 2)) % KV_HEADS * HEAD_DIM
    done = {}

    def send(move, value):
        moved = done.setdefault(move, [])
        moved.append(move(after(value, moved[-2]) if len(moved) > 1 else value))
        return moved[-1]

    got = in_chip(prompt_states)
    both_z, both_x, theirs, theirs_x = {0: both_mine}, {0: both_other}, {}, {}
    value_y = send(along_y, value_weight)
    both_z[1] = send(along_ring, both_mine)
    theirs_x[0] = jnp.where(first, value_y[:, half:], value_y[:, :half])
    value_y = jnp.where(first, value_y[:, :half], value_y[:, half:])
    key_full = {0: jnp.concatenate([both_mine[:width], both_other[:width], packed_queries])}
    key_y = {0: send(along_y, after(key_full[0], value_y))}
    theirs[0] = jnp.concatenate([value_y, packed_queries, key_y[0][2 * width :]])
    for k in range(1, deep):
        if k + 1 < deep:
            both_z[k + 1] = send(along_ring, both_z[k])
        both_x[k] = send(along_x, both_z[k])
        key_full[k] = jnp.concatenate([both_z[k][:width], both_x[k][:width]])
        key_y[k] = send(along_y, after(key_full[k], key_y[k - 1]))
    for k in range(1, deep):
        theirs[k] = send(along_ring, theirs[k - 1])
        theirs_x[k] = send(along_x, theirs[k][:width])

    ring_queries = collect([theirs[k] for k in range(deep)], width, 2 * packed)
    ring_queries = [ring_queries, in_chip(ring_queries)]

    key_pieces = [
        [((key_y if flip else key_full)[k], start) for start in (0, width)] for k, flip in places
    ]
    value_pieces = [
        [(theirs[k], 0), (theirs_x[k], 0)] if flip else [(both_z[k], width), (both_x[k], width)]
        for k, flip in places
    ]

    def project_blocks(pieces, which, acc, ready, kind):
        taken = after(jnp.stack([own_blocks[i] for i in which]), ready)
        return project(
            prompt_states, got, wide_states, taken, width, [pieces[i] for i in which], acc, kind
        )

    early = [*range(0, 2 * deep, 2), 1]
    late = [i for i in range(2 * deep) if i not in early]
    value_early = project_blocks(
        value_pieces, early, None, (theirs_x[1], theirs[deep - 1]), jnp.float32
    )
    awaited = (value_early, [theirs_x[k] for k in range(1, deep)])
    key_sum = project_blocks(key_pieces, range(2 * deep), None, awaited, jnp.bfloat16)
    key_back = in_chip(key_sum)

    def own_head(sums):
        sums = lax.dynamic_slice_in_dim(sums, own_place, HEAD_DIM, 1)
        return sums.reshape(2, samples, HEAD_DIM).astype(jnp.float32)

    new_keys = own_head(key_sum[chip_rows:]) + own_head(key_back[chip_rows:])
    new_keys = turn(new_keys, step_tables).astype(jnp.bfloat16).astype(jnp.float32)
    new_keys = new_keys.reshape(steps, HEAD_DIM)
    masks = []
    if prompts > 1:
        token_prompt = jnp.repeat(slots // PROMPT_PAGES, PAGE)
        row_prompt = jnp.tile(sample_order // group_size, devices // KV_HEADS * rows // samples)
        masks = [token_prompt[:, None], row_prompt[None, :]]
    kept, sent, step_values = attend(
        kv_places, query_turns, ring_queries, key_sum, key_back, cosine, sine_part, masks,
        prompt_states, got, wide_states, jnp.stack([own_blocks[i] for i in late]), width,
        [value_pieces[i] for i in late], value_early,
    )
    new_values = own_head(step_values) + own_head(in_chip(step_values))
    new_values = new_values.astype(jnp.bfloat16).astype(jnp.float32).reshape(steps, HEAD_DIM)

    by_owner = (deep, 2, *kept.shape[2:])
    near, far = merge_cores(kept.reshape(by_owner), in_chip(sent.reshape(by_owner)))
    merged = merge_chips(own_a[None], near, along_y(far))
    parts = [merged[0]] + [along_z(merged[k], k) for k in range(1, deep)]

    out_width = out_weight.shape[1] // devices
    out_blocks = jnp.stack(
        [
            block(own_a ^ k, flip, own_c ^ turned)
            for turned in (0, 1)
            for flip in (0, 1)
            for k in range(deep)
        ]
    )
    terms = out_project(out_blocks, parts, queries, new_keys, new_values, out_weight, out_width)

    def narrow(value):
        return value.astype(jnp.bfloat16)

    def wide(value):
        return value.astype(jnp.float32)

    for move in (in_chip, along_y):
        share = terms.shape[1] // 2
        terms = narrow(wide(terms[:, :share]) + wide(move(terms[:, share:])))
    attn_out = wide(terms[:, :out_width])
    for k in range(1, deep):
        attn_out = attn_out + wide(along_z(terms[:, k * out_width : (k + 1) * out_width], k))
    return narrow(attn_out).reshape(2, samples, -1)


def solution(mesh):
    in_specs = (
        P(("groups", "sample"), None),
        P("groups"),
        P(None, "groups", None),
        P("groups"),
        P("sample", None),
        P("sample", None),
        P(None, "sample"),
        P("sample", None),
    )
    out_specs = P(None, "groups", "sample")
    return jax.shard_map(
        on_device, mesh=mesh, in_specs=in_specs, out_specs=out_specs, check_vma=False
    )
```

```python
import jax
import jax.numpy as jnp
from jax import lax
from jax.experimental import pallas as pl
from jax.experimental.pallas import tpu as pltpu
from jax.sharding import PartitionSpec as P

D = 8192
HEAD_DIM = 128
KV_HEADS = 4
GQA = 8
PAGE = 128
PROMPT_PAGES = 64
LINE = 4

rope_base = 1000000.0


def rope_tables(position):
    half_dim = HEAD_DIM // 2
    frequency = rope_base ** (-jnp.arange(half_dim, dtype=jnp.float32) * 2.0 / HEAD_DIM)
    angles = position.astype(jnp.float32)[..., None] * frequency
    return jnp.cos(angles), jnp.sin(angles)


def turn(vector, tables):
    cosine, sine_part = tables
    half_dim = HEAD_DIM // 2
    first_half = vector[..., :half_dim]
    second_half = vector[..., half_dim:]
    return jnp.concatenate(
        [
            first_half * cosine - second_half * sine_part,
            second_half * cosine + first_half * sine_part,
        ],
        axis=-1,
    )


def ring_order(deep):
    return [*range(0, deep, 2), *range(deep - 1 - deep % 2, 0, -2)]


def mover(groups, devices):
    deep = devices // LINE
    order = ring_order(deep)

    def move(value, step):
        pairs = []
        for g in range(groups):
            for s in range(devices):
                a, b, c = s // LINE, s // 2 % 2, s % 2
                to_g, to_a, to_b, to_c = step(g, a, b, c)
                to_s = (to_a % deep) * LINE + to_b * 2 + to_c
                pairs.append((g * devices + s, to_g * devices + to_s))
        return lax.ppermute(value, ("groups", "sample"), pairs)

    def next_on_ring(a):
        return order[(order.index(a) + 1) % deep]

    along_ring = lambda v: move(v, lambda g, a, b, c: (g, next_on_ring(a), b, c))
    along_z = lambda v, k: move(v, lambda g, a, b, c: (g, a ^ k, b, c))
    along_y = lambda v: move(v, lambda g, a, b, c: (g, a, 1 - b, c))
    along_x = lambda v: move(v, lambda g, a, b, c: (g ^ 1, a, b, c))
    in_chip = lambda v: move(v, lambda g, a, b, c: (g, a, b, 1 - c))
    return along_ring, along_z, along_y, along_x, in_chip


def after(value, done):
    return lax.optimization_barrier((value, done))[0]


MIB = 1024 * 1024
LIGHT = pl.CostEstimate(flops=1, bytes_accessed=1, transcendentals=0)


def project_queries(steps, weight, cosine, sine):
    count, depth = steps.shape
    parts = 8
    piece = depth // parts

    def body(step_ref, weight_ref, cosine_ref, sine_ref, out_ref, held, sems):
        copies = []
        for i in range(parts):
            copies.append(
                pltpu.make_async_copy(
                    weight_ref.at[pl.ds(i * piece, piece), :], held.at[i], sems.at[i]
                )
            )
            copies[-1].start()
        total = None
        for i in range(parts):
            copies[i].wait()
            product = jnp.dot(
                step_ref[:, i * piece : (i + 1) * piece],
                held[i],
                preferred_element_type=jnp.float32,
            )
            total = product if total is None else total + product
        for start in range(0, weight.shape[1], HEAD_DIM):
            head = total[:, start : start + HEAD_DIM]
            turned = head * cosine_ref[...] + pltpu.roll(head, HEAD_DIM // 2, 1) * sine_ref[...]
            out_ref[:, start : start + HEAD_DIM] = turned.astype(jnp.bfloat16)

    whole = pl.BlockSpec(memory_space=pltpu.VMEM)
    return pl.pallas_call(
        body,
        in_specs=[whole, pl.BlockSpec(memory_space=pltpu.HBM), whole, whole],
        out_specs=whole,
        out_shape=jax.ShapeDtypeStruct((count, weight.shape[1]), jnp.bfloat16),
        scratch_shapes=[
            pltpu.VMEM((parts, piece, weight.shape[1]), weight.dtype),
            pltpu.SemaphoreType.DMA((parts,)),
        ],
        compiler_params=pltpu.CompilerParams(vmem_limit_bytes=61 * MIB),
        cost_estimate=LIGHT,
    )(steps, weight, cosine, sine)


def collect(arrays, first, height):
    columns = arrays[0].shape[1]

    def body(*refs):
        out_ref, sems = refs[-2:]
        copies = [
            pltpu.make_async_copy(ref.at[pl.ds(first, height), :], out_ref.at[i], sems.at[i])
            for i, ref in enumerate(refs[:-2])
        ]
        for copy in copies:
            copy.start()
        for copy in copies:
            copy.wait()

    return pl.pallas_call(
        body,
        in_specs=[pl.BlockSpec(memory_space=pl.ANY)] * len(arrays),
        out_specs=pl.BlockSpec(memory_space=pltpu.VMEM),
        out_shape=jax.ShapeDtypeStruct((len(arrays), height, columns), arrays[0].dtype),
        scratch_shapes=[pltpu.SemaphoreType.DMA((len(arrays),))],
        compiler_params=pltpu.CompilerParams(vmem_limit_bytes=4 * MIB),
        cost_estimate=LIGHT,
    )(*arrays)


class Blocks:
    def __init__(self, prompt, steps, width, pieces):
        self.arrays = []
        for piece in pieces:
            for array, _ in piece:
                if not any(array is held for held in self.arrays):
                    self.arrays.append(array)
        self.pieces, self.width, self.count = pieces, width, len(pieces)
        self.row_count, self.step_count = prompt.shape[0], steps.shape[0]
        self.height = 2 * self.row_count + self.step_count
        self.columns = sum(array.shape[1] for array, _ in pieces[0])
        self.scratch = [
            pltpu.VMEM((self.count, self.height, width), prompt.dtype),
            pltpu.VMEM((self.count, width, self.columns), prompt.dtype),
            pltpu.SemaphoreType.DMA((self.count, 5)),
        ]

    def copies(self, i, block_ref, sources, weight_refs, scratch):
        left, weights, sems = scratch
        column = pl.ds(pl.multiple_of(block_ref[i] * self.width, self.width), self.width)
        group = []
        start = 0
        for j, (source, rows) in enumerate(
            zip(sources, (self.row_count, self.row_count, self.step_count))
        ):
            group.append(
                pltpu.make_async_copy(
                    source.at[:, column], left.at[i, pl.ds(start, rows), :], sems.at[i, j]
                )
            )
            start += rows
        side = 0
        for j, (array, first) in enumerate(self.pieces[i]):
            ref = weight_refs[[array is other for other in self.arrays].index(True)]
            group.append(
                pltpu.make_async_copy(
                    ref.at[pl.ds(first, self.width), :],
                    weights.at[i, :, pl.ds(side, array.shape[1])],
                    sems.at[i, 3 + j],
                )
            )
            side += array.shape[1]
        return group


AHEAD = 3


def project(prompt, got, steps, blocks, width, pieces, acc, kind):
    held = Blocks(prompt, steps, width, pieces)
    extra = [] if acc is None else [acc]

    def body(block_ref, prompt_ref, got_ref, step_ref, *refs):
        weight_refs = refs[: len(held.arrays)]
        out_ref, acc_held, acc_sem, *scratch = refs[len(held.arrays) + len(extra) :]
        left, weights, _ = scratch
        sources = (prompt_ref, got_ref, step_ref)
        groups = [
            held.copies(i, block_ref, sources, weight_refs, scratch) for i in range(held.count)
        ]
        for group in groups[:AHEAD]:
            for copy in group:
                copy.start()
        if extra:
            before = pltpu.make_async_copy(refs[len(held.arrays)], acc_held, acc_sem.at[0])
            before.start()
        total = None
        for i, group in enumerate(groups):
            for copy in group:
                copy.wait()
            if i + AHEAD < held.count:
                for copy in groups[i + AHEAD]:
                    copy.start()
            product = jnp.dot(left[i], weights[i], preferred_element_type=jnp.float32)
            total = product if total is None else total + product
        if extra:
            before.wait()
            total = total + acc_held[...]
        out_ref[...] = total.astype(kind)

    anywhere = pl.BlockSpec(memory_space=pl.ANY)
    return pl.pallas_call(
        body,
        in_specs=[pl.BlockSpec(memory_space=pltpu.SMEM)] + [anywhere] * (3 + len(held.arrays) + len(extra)),
        out_specs=pl.BlockSpec(memory_space=pltpu.VMEM),
        out_shape=jax.ShapeDtypeStruct((held.height, held.columns), kind),
        scratch_shapes=[
            pltpu.VMEM((held.height, held.columns) if extra else (8, HEAD_DIM), jnp.float32),
            pltpu.SemaphoreType.DMA((1,)),
            *held.scratch,
        ],
        compiler_params=pltpu.CompilerParams(vmem_limit_bytes=57 * MIB),
        cost_estimate=LIGHT,
    )(blocks, prompt, got, steps, *held.arrays, *extra)


NOTES = 16


def thirds(value):
    parts = []
    for _ in range(3):
        parts.append(value.astype(jnp.bfloat16))
        value = value - parts[-1].astype(jnp.float32)
    return parts


def note_rows(top, total):
    parts = [part.astype(jnp.float32) for part in thirds(top) + thirds(total)]
    rows = jnp.concatenate(parts + [jnp.zeros((NOTES - 6, top.shape[1]), jnp.float32)], axis=0)
    return rows.astype(jnp.bfloat16)


def read_notes(rows):
    rows = rows.astype(jnp.float32)
    return rows[0:1] + rows[1:2] + rows[2:3], rows[3:4] + rows[4:5] + rows[5:6]


def small_call(body, out_shapes, scalars, arrays):
    whole = pl.BlockSpec(memory_space=pltpu.VMEM)
    return pl.pallas_call(
        body,
        in_specs=[pl.BlockSpec(memory_space=pltpu.SMEM)] * len(scalars) + [whole] * len(arrays),
        out_specs=[whole] * len(out_shapes),
        out_shape=[jax.ShapeDtypeStruct(shape, jnp.bfloat16) for shape in out_shapes],
        compiler_params=pltpu.CompilerParams(vmem_limit_bytes=12 * MIB),
        cost_estimate=LIGHT,
    )(*scalars, *arrays)


def merge_cores(own, other):
    deep, _, height, lanes = own.shape

    def body(own_ref, other_ref, near_ref, far_ref):
        for z in range(deep):
            for y, out_ref in enumerate((near_ref, far_ref)):
                both = own_ref[z, y, :HEAD_DIM, :].astype(jnp.float32) + other_ref[
                    z, y, :HEAD_DIM, :
                ].astype(jnp.float32)
                out_ref[z, :HEAD_DIM, :] = both.astype(jnp.bfloat16)
                out_ref[z, HEAD_DIM:, :] = own_ref[z, y, HEAD_DIM:, :]

    return small_call(body, [(deep, height, lanes)] * 2, [], [own, other])


def merge_chips(own_place, near, far):
    deep, height, lanes = near.shape

    def body(place_ref, near_ref, far_ref, *out_refs):
        for k, out_ref in enumerate(out_refs):
            z = place_ref[0] ^ k
            first, second = near_ref[z], far_ref[z]
            first_top, first_total = read_notes(first[HEAD_DIM:, :])
            second_top, second_total = read_notes(second[HEAD_DIM:, :])
            top = jnp.maximum(first_top, second_top)
            first_factor, second_factor = jnp.exp(first_top - top), jnp.exp(second_top - top)
            out_ref[:HEAD_DIM, :] = (
                first[:HEAD_DIM, :].astype(jnp.float32) * first_factor
                + second[:HEAD_DIM, :].astype(jnp.float32) * second_factor
            ).astype(jnp.bfloat16)
            out_ref[HEAD_DIM:, :] = note_rows(
                top, first_total * first_factor + second_total * second_factor
            )

    return small_call(body, [(height, lanes)] * deep, [own_place], [near, far])


def attend(
    places, turns, queries, own, other, cosine, sine, masks, prompt, got, steps, blocks, width,
    pieces, early,
):
    kv_heads = places.shape[0]
    deep, packed, lanes = queries[0].shape
    share = deep // kv_heads
    count = 2 * share * packed * lanes // HEAD_DIM
    owners = count // HEAD_DIM
    tokens = cosine.shape[0]
    half = tokens // 2
    held = Blocks(prompt, steps, width, pieces)
    inputs = [*queries, own, other, cosine, sine, *masks]

    def body(place_ref, turn_ref, block_ref, *refs):
        query_refs = refs[:2]
        own_ref, other_ref, cosine_ref, sine_ref = refs[2:6]
        mask_refs = refs[6 : len(inputs)]
        prompt_ref, got_ref, step_ref = refs[len(inputs) : len(inputs) + 3]
        early_refs = refs[len(inputs) + 3 : len(inputs) + 3 + len(early)]
        rest = refs[len(inputs) + 3 + len(early) :]
        weight_refs, rest = rest[: len(held.arrays)], rest[len(held.arrays) :]
        *out_refs, step_out_ref = rest[:3]
        early_held, weight_held, value_held, early_sem, *scratch = rest[3:]
        left, weight_rows, _ = scratch
        sources = (prompt_ref, got_ref, step_ref)
        groups = [
            held.copies(i, block_ref, sources, weight_refs, scratch) for i in range(held.count)
        ]
        before = [
            pltpu.make_async_copy(ref, early_held.at[i], early_sem.at[i])
            for i, ref in enumerate(early_refs)
        ]
        for copy in before:
            copy.start()
        for group in groups:
            for copy in group:
                copy.start()
        wide_cosine = jnp.concatenate([cosine_ref[...], cosine_ref[...]], axis=1)
        wide_sine = jnp.concatenate([-sine_ref[...], sine_ref[...]], axis=1)

        def one_head(j, _):
            column = pl.ds(pl.multiple_of(place_ref[j] * HEAD_DIM, HEAD_DIM), HEAD_DIM)
            keys = jnp.concatenate(
                [
                    own_ref[:half, column].astype(jnp.float32)
                    + other_ref[half:tokens, column].astype(jnp.float32),
                    own_ref[half:tokens, column].astype(jnp.float32)
                    + other_ref[:half, column].astype(jnp.float32),
                ],
                axis=0,
            )
            swapped = pltpu.roll(keys, HEAD_DIM // 2, 1)
            keys = (keys * wide_cosine + swapped * wide_sine).astype(jnp.bfloat16)
            unpacked = []
            for part in range(share):
                for ref in query_refs:
                    both = ref[turn_ref[j * share + part]]
                    for low in range(0, packed, packed // 2):
                        for left_lane in range(0, lanes, HEAD_DIM):
                            unpacked.append(
                                both[low : low + packed // 2, left_lane : left_lane + HEAD_DIM]
                            )
            scores = lax.dot_general(
                keys,
                jnp.concatenate(unpacked, axis=0),
                (((1,), (1,)), ((), ())),
                preferred_element_type=jnp.float32,
            ) * (HEAD_DIM**-0.5)
            if masks:
                scores = jnp.where(mask_refs[0][...] == mask_refs[1][...], scores, -1e30)
            top = jnp.max(scores, axis=0, keepdims=True)
            weights = jnp.exp(scores - top)
            total = jnp.sum(weights, axis=0, keepdims=True)
            for i in range(owners):
                lane = slice(i * HEAD_DIM, (i + 1) * HEAD_DIM)
                out_ref = out_refs[i // 2 % 2]
                out_ref[j, i // 4 * 2 + i % 2, HEAD_DIM:, :] = note_rows(
                    top[:, lane], total[:, lane]
                )
            weight_held[j] = weights.astype(jnp.bfloat16)
            return 0

        lax.fori_loop(0, kv_heads, one_head, 0)
        for copy in before:
            copy.wait()
        total = sum(early_held[i] for i in range(len(early)))
        for i, group in enumerate(groups):
            for copy in group:
                copy.wait()
            total += jnp.dot(left[i], weight_rows[i], preferred_element_type=jnp.float32)
        value_held[...] = total[:tokens].astype(jnp.bfloat16)
        step_out_ref[...] = total[tokens:]

        def one_sum(j, _):
            column = pl.ds(pl.multiple_of(place_ref[j] * HEAD_DIM, HEAD_DIM), HEAD_DIM)
            summed = lax.dot_general(
                value_held[:, column],
                weight_held[j],
                (((0,), (0,)), ((), ())),
                preferred_element_type=jnp.float32,
            )
            for i in range(owners):
                lane = slice(i * HEAD_DIM, (i + 1) * HEAD_DIM)
                out_ref = out_refs[i // 2 % 2]
                out_ref[j, i // 4 * 2 + i % 2, :HEAD_DIM, :] = summed[:, lane].astype(jnp.bfloat16)
            return 0

        lax.fori_loop(0, kv_heads, one_sum, 0)

    anywhere = pl.BlockSpec(memory_space=pl.ANY)
    whole = pl.BlockSpec(memory_space=pltpu.VMEM)
    return pl.pallas_call(
        body,
        in_specs=[pl.BlockSpec(memory_space=pltpu.SMEM)] * 3
        + [whole] * len(inputs)
        + [anywhere] * (3 + len(early) + len(held.arrays)),
        out_specs=[whole] * 3,
        out_shape=[
            *[
                jax.ShapeDtypeStruct(
                    (kv_heads, owners // 2, HEAD_DIM + NOTES, HEAD_DIM), jnp.bfloat16
                )
            ]
            * 2,
            jax.ShapeDtypeStruct((held.step_count, held.columns), jnp.float32),
        ],
        scratch_shapes=[
            pltpu.VMEM((len(early), held.height, held.columns), jnp.float32),
            pltpu.VMEM((kv_heads, tokens, count), jnp.bfloat16),
            pltpu.VMEM((tokens, held.columns), jnp.bfloat16),
            pltpu.SemaphoreType.DMA((len(early),)),
            *held.scratch,
        ],
        compiler_params=pltpu.CompilerParams(vmem_limit_bytes=57 * MIB),
        cost_estimate=LIGHT,
    )(places, turns, blocks, *inputs, prompt, got, steps, *early, *held.arrays)


def out_project(blocks, parts, queries, new_keys, new_values, weight, width):
    count = len(parts)
    steps = queries.shape[0]
    samples = steps // 2

    def body(block_ref, *refs):
        part_refs = refs[:count]
        query_ref, key_ref, value_ref, weight_ref, out_ref = refs[count:]
        notes = [read_notes(ref[HEAD_DIM:, :]) for ref in part_refs]
        top = notes[0][0]
        for other, _ in notes[1:]:
            top = jnp.maximum(top, other)
        sums = total = 0.0
        for ref, (part_top, part_total) in zip(part_refs, notes):
            factor = jnp.exp(part_top - top)
            sums = sums + ref[:HEAD_DIM, :].astype(jnp.float32) * factor
            total = total + part_total * factor
        sums = sums.T
        both = jnp.concatenate([top, total, jnp.zeros((6, HEAD_DIM), jnp.float32)], axis=0).T
        keys, values = key_ref[...], value_ref[...]
        heads = []
        for h in range(queries.shape[1] // HEAD_DIM):
            query = query_ref[:, h * HEAD_DIM : (h + 1) * HEAD_DIM].astype(jnp.float32)
            own_score = jnp.sum(query * keys, axis=1, keepdims=True) * (HEAD_DIM**-0.5)
            back_score = jnp.sum(
                query[samples:] * keys[:samples], axis=1, keepdims=True
            ) * (HEAD_DIM**-0.5)
            ends = []
            for step in (0, 1):
                place = slice((2 * h + step) * samples, (2 * h + step + 1) * samples)
                here = slice(step * samples, (step + 1) * samples)
                old_top, old_total = both[place, 0:1], both[place, 1:2]
                scores = [(own_score[here], values[here])]
                if step:
                    scores.append((back_score, values[:samples]))
                high = old_top
                for score, _ in scores:
                    high = jnp.maximum(high, score)
                old = jnp.exp(old_top - high)
                numerator, denominator = old * sums[place], old * old_total
                for score, value in scores:
                    new = jnp.exp(score - high)
                    numerator, denominator = numerator + new * value, denominator + new
                ends.append(numerator / denominator)
            heads.append(jnp.concatenate(ends, axis=0).astype(jnp.bfloat16))
        heads = jnp.concatenate(heads, axis=1)
        for i in range(blocks.shape[0]):
            start = pl.multiple_of(block_ref[i] * width, width)
            out_ref[:, i * width : (i + 1) * width] = jnp.dot(
                heads, weight_ref[:, pl.ds(start, width)], preferred_element_type=jnp.float32
            ).astype(jnp.bfloat16)

    return small_call(
        body, [(steps, weight.shape[1])], [blocks], [*parts, queries, new_keys, new_values, weight]
    )[0]


def on_device(
    prompt_states,
    page_table,
    step_states,
    sample_order,
    key_weight,
    value_weight,
    query_weight,
    out_weight,
):
    devices = lax.axis_size("sample")
    groups = lax.axis_size("groups")
    own_index = lax.axis_index("sample")
    first = lax.axis_index("groups") % 2 == 0
    deep = devices // LINE
    own_a, own_b, own_c = own_index // LINE, own_index // 2 % 2, own_index % 2
    along_ring, along_z, along_y, along_x, in_chip = mover(groups, devices)
    row_count = prompt_states.shape[0]
    chip_rows = 2 * row_count
    pages_here = row_count // PAGE
    heads_here = query_weight.shape[1] // HEAD_DIM
    total_pages = page_table.shape[0]
    prompts = total_pages // PROMPT_PAGES
    samples = sample_order.shape[0]
    steps = 2 * samples
    group_size = samples // prompts
    own_kv = own_index * heads_here // GQA
    wide_states = step_states.reshape(steps, D)
    rows = heads_here * steps
    width = key_weight.shape[0]
    half = key_weight.shape[1] // 2
    kv_places = jnp.where(first, 0, KV_HEADS // 2) + jnp.arange(KV_HEADS, dtype=jnp.int32)
    kv_places = kv_places % KV_HEADS

    order = ring_order(deep)

    def by_place(table):
        return sum(jnp.where(own_a == a, table[a], 0) for a in range(deep))

    own_turn = by_place([order.index(a) for a in range(deep)])

    def block(place_z, flip, core):
        return place_z * LINE + (own_b ^ flip) * 2 + core

    def behind(k):
        return by_place([order[(order.index(a) - k) % deep] for a in range(deep)])

    low = jnp.concatenate([key_weight[:, :half], value_weight[:, :half]])
    high = jnp.concatenate([key_weight[:, half:], value_weight[:, half:]])
    both_mine, both_other = jnp.where(first, low, high), jnp.where(first, high, low)

    own_pages = jnp.concatenate(
        [
            holder * pages_here + jnp.arange(pages_here, dtype=jnp.int32)
            for holder in (own_index, own_index ^ 1)
        ]
    )
    slots = jnp.sum(
        jnp.where(
            page_table[None, :] == own_pages[:, None],
            jnp.arange(total_pages, dtype=jnp.int32)[None, :],
            0,
        ),
        axis=1,
    )
    positions = (slots % PROMPT_PAGES * PAGE)[:, None] + jnp.arange(PAGE, dtype=jnp.int32)[None, :]
    cosine, sine_part = rope_tables(positions.reshape(chip_rows))

    step_place = PROMPT_PAGES * PAGE + jnp.arange(2, dtype=jnp.int32)
    step_tables = tuple(t[:, None, :] for t in rope_tables(step_place))
    flat_tables = [
        jnp.repeat(jnp.concatenate([sign * table, table], axis=-1)[:, 0], samples, axis=0)
        for sign, table in zip((1, -1), step_tables)
    ]
    queries = project_queries(
        after(wide_states, (cosine, sine_part)), query_weight, *flat_tables
    )
    packed_queries = jnp.concatenate(
        jnp.split(queries, half // queries.shape[1], axis=0), axis=1
    )
    packed = packed_queries.shape[0]

    places = [(k, flip) for k in range(deep) for flip in (0, 1)]
    parts_of = [
        tuple(range(0, 2 * deep, 2)),
        tuple(range(1, 2 * deep - 4, 2)),
        tuple(range(2 * deep - 3, 2 * deep, 2)),
    ]
    taken_blocks = {
        which: jnp.stack([block(behind(places[i][0]), places[i][1], own_c) for i in which])
        for which in (tuple(range(2 * deep)), *parts_of)
    }
    query_turns = jnp.stack([(own_turn + deep - order.index(a)) % deep for a in range(deep)])
    own_place = (own_kv + jnp.where(first, 0, KV_HEADS // 2)) % KV_HEADS * HEAD_DIM
    done = {}

    def send(move, value):
        moved = done.setdefault(move, [])
        moved.append(move(after(value, moved[-2]) if len(moved) > 1 else value))
        return moved[-1]

    got = in_chip(prompt_states)
    both_z, both_x, theirs, theirs_x = {0: both_mine}, {0: both_other}, {}, {}
    value_y = send(along_y, value_weight)
    both_z[1] = send(along_ring, both_mine)
    theirs_x[0] = jnp.where(first, value_y[:, half:], value_y[:, :half])
    value_y = jnp.where(first, value_y[:, :half], value_y[:, half:])
    key_full = {0: jnp.concatenate([both_mine[:width], both_other[:width], packed_queries])}
    key_y = {0: send(along_y, after(key_full[0], value_y))}
    theirs[0] = jnp.concatenate([value_y, packed_queries, key_y[0][2 * width :]])
    for k in range(1, deep):
        if k + 1 < deep:
            both_z[k + 1] = send(along_ring, both_z[k])
        both_x[k] = send(along_x, both_z[k])
        key_full[k] = jnp.concatenate([both_z[k][:width], both_x[k][:width]])
        early_work = (taken_blocks, kv_places, query_turns) if k == 2 else ()
        key_y[k] = send(along_y, after(key_full[k], (key_y[k - 1], early_work)))
    for k in range(1, deep):
        theirs[k] = send(along_ring, theirs[k - 1])
        theirs_x[k] = send(along_x, theirs[k][:width])

    ring_queries = collect([theirs[k] for k in range(deep)], width, 2 * packed)
    ring_queries = [ring_queries, in_chip(ring_queries)]

    key_pieces = [
        [((key_y if flip else key_full)[k], start) for start in (0, width)] for k, flip in places
    ]
    value_pieces = [
        [(theirs[k], 0), (theirs_x[k], 0)] if flip else [(both_z[k], width), (both_x[k], width)]
        for k, flip in places
    ]

    def project_blocks(pieces, which, acc, ready, kind):
        taken = after(taken_blocks[tuple(which)], ready)
        return project(
            prompt_states, got, wide_states, taken, width, [pieces[i] for i in which], acc, kind
        )

    value_early = project_blocks(
        value_pieces, parts_of[0], None, (theirs_x[1], theirs[deep - 1]), jnp.float32
    )
    awaited = (value_early, [theirs_x[k] for k in range(1, deep)])
    key_sum = project_blocks(key_pieces, range(2 * deep), None, awaited, jnp.bfloat16)
    value_next = project_blocks(value_pieces, parts_of[1], None, key_sum, jnp.float32)
    key_back = in_chip(key_sum)

    def own_head(sums):
        sums = lax.dynamic_slice_in_dim(sums, own_place, HEAD_DIM, 1)
        return sums.reshape(2, samples, HEAD_DIM).astype(jnp.float32)

    new_keys = own_head(key_sum[chip_rows:]) + own_head(key_back[chip_rows:])
    new_keys = turn(new_keys, step_tables).astype(jnp.bfloat16).astype(jnp.float32)
    new_keys = new_keys.reshape(steps, HEAD_DIM)
    masks = []
    if prompts > 1:
        token_prompt = jnp.repeat(slots // PROMPT_PAGES, PAGE)
        row_prompt = jnp.tile(sample_order // group_size, devices // KV_HEADS * rows // samples)
        masks = [token_prompt[:, None], row_prompt[None, :]]
    kept, sent, step_values = attend(
        kv_places, query_turns, ring_queries, key_sum, key_back, cosine, sine_part, masks,
        prompt_states, got, wide_states, taken_blocks[parts_of[2]], width,
        [value_pieces[i] for i in parts_of[2]], [value_early, value_next],
    )
    new_values = own_head(step_values) + own_head(in_chip(step_values))
    new_values = new_values.astype(jnp.bfloat16).astype(jnp.float32).reshape(steps, HEAD_DIM)

    by_owner = (deep, 2, *kept.shape[2:])
    near, far = merge_cores(kept.reshape(by_owner), in_chip(sent.reshape(by_owner)))
    merged = merge_chips(own_a[None], near, along_y(far))
    parts = [merged[0]] + [along_z(merged[k], k) for k in range(1, deep)]

    out_width = out_weight.shape[1] // devices
    out_blocks = jnp.stack(
        [
            block(own_a ^ k, flip, own_c ^ turned)
            for turned in (0, 1)
            for flip in (0, 1)
            for k in range(deep)
        ]
    )
    terms = out_project(out_blocks, parts, queries, new_keys, new_values, out_weight, out_width)

    def narrow(value):
        return value.astype(jnp.bfloat16)

    def wide(value):
        return value.astype(jnp.float32)

    for move in (in_chip, along_y):
        share = terms.shape[1] // 2
        terms = narrow(wide(terms[:, :share]) + wide(move(terms[:, share:])))
    attn_out = wide(terms[:, :out_width])
    for k in range(1, deep):
        attn_out = attn_out + wide(along_z(terms[:, k * out_width : (k + 1) * out_width], k))
    return narrow(attn_out).reshape(2, samples, -1)


def solution(mesh):
    in_specs = (
        P(("groups", "sample"), None),
        P("groups"),
        P(None, "groups", None),
        P("groups"),
        P("sample", None),
        P("sample", None),
        P(None, "sample"),
        P("sample", None),
    )
    out_specs = P(None, "groups", "sample")
    return jax.shard_map(
        on_device, mesh=mesh, in_specs=in_specs, out_specs=out_specs, check_vma=False
    )
```

```python
import jax
import jax.numpy as jnp
from jax import lax
from jax.experimental import pallas as pl
from jax.experimental.pallas import tpu as pltpu
from jax.sharding import PartitionSpec as P

D = 8192
HEAD_DIM = 128
KV_HEADS = 4
GQA = 8
PAGE = 128
PROMPT_PAGES = 64
LINE = 4

rope_base = 1000000.0


def rope_tables(position):
    half_dim = HEAD_DIM // 2
    frequency = rope_base ** (-jnp.arange(half_dim, dtype=jnp.float32) * 2.0 / HEAD_DIM)
    angles = position.astype(jnp.float32)[..., None] * frequency
    return jnp.cos(angles), jnp.sin(angles)


def turn(vector, tables):
    cosine, sine_part = tables
    half_dim = HEAD_DIM // 2
    first_half = vector[..., :half_dim]
    second_half = vector[..., half_dim:]
    return jnp.concatenate(
        [
            first_half * cosine - second_half * sine_part,
            second_half * cosine + first_half * sine_part,
        ],
        axis=-1,
    )


def ring_order(deep):
    return [*range(0, deep, 2), *range(deep - 1 - deep % 2, 0, -2)]


def mover(groups, devices):
    deep = devices // LINE
    order = ring_order(deep)

    def move(value, step):
        pairs = []
        for g in range(groups):
            for s in range(devices):
                a, b, c = s // LINE, s // 2 % 2, s % 2
                to_g, to_a, to_b, to_c = step(g, a, b, c)
                to_s = (to_a % deep) * LINE + to_b * 2 + to_c
                pairs.append((g * devices + s, to_g * devices + to_s))
        return lax.ppermute(value, ("groups", "sample"), pairs)

    def next_on_ring(a):
        return order[(order.index(a) + 1) % deep]

    along_ring = lambda v: move(v, lambda g, a, b, c: (g, next_on_ring(a), b, c))
    along_z = lambda v, k: move(v, lambda g, a, b, c: (g, a ^ k, b, c))
    along_y = lambda v: move(v, lambda g, a, b, c: (g, a, 1 - b, c))
    along_x = lambda v: move(v, lambda g, a, b, c: (g ^ 1, a, b, c))
    in_chip = lambda v: move(v, lambda g, a, b, c: (g, a, b, 1 - c))
    return along_ring, along_z, along_y, along_x, in_chip


def after(value, done):
    return lax.optimization_barrier((value, done))[0]


MIB = 1024 * 1024
LIGHT = pl.CostEstimate(flops=1, bytes_accessed=1, transcendentals=0)


def project_queries(steps, weight, cosine, sine):
    count, depth = steps.shape
    parts = 8
    piece = depth // parts

    def body(step_ref, weight_ref, cosine_ref, sine_ref, out_ref, held, sems):
        copies = []
        for i in range(parts):
            copies.append(
                pltpu.make_async_copy(
                    weight_ref.at[pl.ds(i * piece, piece), :], held.at[i], sems.at[i]
                )
            )
            copies[-1].start()
        total = None
        for i in range(parts):
            copies[i].wait()
            product = jnp.dot(
                step_ref[:, i * piece : (i + 1) * piece],
                held[i],
                preferred_element_type=jnp.float32,
            )
            total = product if total is None else total + product
        for start in range(0, weight.shape[1], HEAD_DIM):
            head = total[:, start : start + HEAD_DIM]
            turned = head * cosine_ref[...] + pltpu.roll(head, HEAD_DIM // 2, 1) * sine_ref[...]
            out_ref[:, start : start + HEAD_DIM] = turned.astype(jnp.bfloat16)

    whole = pl.BlockSpec(memory_space=pltpu.VMEM)
    return pl.pallas_call(
        body,
        in_specs=[whole, pl.BlockSpec(memory_space=pltpu.HBM), whole, whole],
        out_specs=whole,
        out_shape=jax.ShapeDtypeStruct((count, weight.shape[1]), jnp.bfloat16),
        scratch_shapes=[
            pltpu.VMEM((parts, piece, weight.shape[1]), weight.dtype),
            pltpu.SemaphoreType.DMA((parts,)),
        ],
        compiler_params=pltpu.CompilerParams(vmem_limit_bytes=61 * MIB),
        cost_estimate=LIGHT,
    )(steps, weight, cosine, sine)


def collect(arrays, first, height):
    columns = arrays[0].shape[1]

    def body(*refs):
        out_ref, sems = refs[-2:]
        copies = [
            pltpu.make_async_copy(ref.at[pl.ds(first, height), :], out_ref.at[i], sems.at[i])
            for i, ref in enumerate(refs[:-2])
        ]
        for copy in copies:
            copy.start()
        for copy in copies:
            copy.wait()

    return pl.pallas_call(
        body,
        in_specs=[pl.BlockSpec(memory_space=pl.ANY)] * len(arrays),
        out_specs=pl.BlockSpec(memory_space=pltpu.VMEM),
        out_shape=jax.ShapeDtypeStruct((len(arrays), height, columns), arrays[0].dtype),
        scratch_shapes=[pltpu.SemaphoreType.DMA((len(arrays),))],
        compiler_params=pltpu.CompilerParams(vmem_limit_bytes=4 * MIB),
        cost_estimate=LIGHT,
    )(*arrays)


class Blocks:
    def __init__(self, prompt, steps, width, pieces):
        self.arrays = []
        for piece in pieces:
            for array, _ in piece:
                if not any(array is held for held in self.arrays):
                    self.arrays.append(array)
        self.pieces, self.width, self.count = pieces, width, len(pieces)
        self.row_count, self.step_count = prompt.shape[0], steps.shape[0]
        self.height = 2 * self.row_count + self.step_count
        self.columns = sum(array.shape[1] for array, _ in pieces[0])
        self.scratch = [
            pltpu.VMEM((self.count, self.height, width), prompt.dtype),
            pltpu.VMEM((self.count, width, self.columns), prompt.dtype),
            pltpu.SemaphoreType.DMA((self.count, 5)),
        ]

    def copies(self, i, block_ref, sources, weight_refs, scratch):
        left, weights, sems = scratch
        column = pl.ds(pl.multiple_of(block_ref[i] * self.width, self.width), self.width)
        group = []
        start = 0
        for j, (source, rows) in enumerate(
            zip(sources, (self.row_count, self.row_count, self.step_count))
        ):
            group.append(
                pltpu.make_async_copy(
                    source.at[:, column], left.at[i, pl.ds(start, rows), :], sems.at[i, j]
                )
            )
            start += rows
        side = 0
        for j, (array, first) in enumerate(self.pieces[i]):
            ref = weight_refs[[array is other for other in self.arrays].index(True)]
            group.append(
                pltpu.make_async_copy(
                    ref.at[pl.ds(first, self.width), :],
                    weights.at[i, :, pl.ds(side, array.shape[1])],
                    sems.at[i, 3 + j],
                )
            )
            side += array.shape[1]
        return group


AHEAD = 3


def project(prompt, got, steps, blocks, width, pieces, acc, kind):
    held = Blocks(prompt, steps, width, pieces)
    extra = [] if acc is None else [acc]

    def body(block_ref, prompt_ref, got_ref, step_ref, *refs):
        weight_refs = refs[: len(held.arrays)]
        out_ref, acc_held, acc_sem, *scratch = refs[len(held.arrays) + len(extra) :]
        left, weights, _ = scratch
        sources = (prompt_ref, got_ref, step_ref)
        groups = [
            held.copies(i, block_ref, sources, weight_refs, scratch) for i in range(held.count)
        ]
        for group in groups[:AHEAD]:
            for copy in group:
                copy.start()
        if extra:
            before = pltpu.make_async_copy(refs[len(held.arrays)], acc_held, acc_sem.at[0])
            before.start()
        total = None
        for i, group in enumerate(groups):
            for copy in group:
                copy.wait()
            if i + AHEAD < held.count:
                for copy in groups[i + AHEAD]:
                    copy.start()
            product = jnp.dot(left[i], weights[i], preferred_element_type=jnp.float32)
            total = product if total is None else total + product
        if extra:
            before.wait()
            total = total + acc_held[...]
        out_ref[...] = total.astype(kind)

    anywhere = pl.BlockSpec(memory_space=pl.ANY)
    return pl.pallas_call(
        body,
        in_specs=[pl.BlockSpec(memory_space=pltpu.SMEM)] + [anywhere] * (3 + len(held.arrays) + len(extra)),
        out_specs=pl.BlockSpec(memory_space=pltpu.VMEM),
        out_shape=jax.ShapeDtypeStruct((held.height, held.columns), kind),
        scratch_shapes=[
            pltpu.VMEM((held.height, held.columns) if extra else (8, HEAD_DIM), jnp.float32),
            pltpu.SemaphoreType.DMA((1,)),
            *held.scratch,
        ],
        compiler_params=pltpu.CompilerParams(vmem_limit_bytes=57 * MIB),
        cost_estimate=LIGHT,
    )(blocks, prompt, got, steps, *held.arrays, *extra)


NOTES = 16


def thirds(value):
    parts = []
    for _ in range(3):
        parts.append(value.astype(jnp.bfloat16))
        value = value - parts[-1].astype(jnp.float32)
    return parts


def note_rows(top, total):
    parts = [part.astype(jnp.float32) for part in thirds(top) + thirds(total)]
    rows = jnp.concatenate(parts + [jnp.zeros((NOTES - 6, top.shape[1]), jnp.float32)], axis=0)
    return rows.astype(jnp.bfloat16)


def read_notes(rows):
    rows = rows.astype(jnp.float32)
    return rows[0:1] + rows[1:2] + rows[2:3], rows[3:4] + rows[4:5] + rows[5:6]


def small_call(body, out_shapes, scalars, arrays):
    whole = pl.BlockSpec(memory_space=pltpu.VMEM)
    return pl.pallas_call(
        body,
        in_specs=[pl.BlockSpec(memory_space=pltpu.SMEM)] * len(scalars) + [whole] * len(arrays),
        out_specs=[whole] * len(out_shapes),
        out_shape=[jax.ShapeDtypeStruct(shape, jnp.bfloat16) for shape in out_shapes],
        compiler_params=pltpu.CompilerParams(vmem_limit_bytes=12 * MIB),
        cost_estimate=LIGHT,
    )(*scalars, *arrays)


def merge_cores(own, other):
    deep, _, height, lanes = own.shape

    def body(own_ref, other_ref, near_ref, far_ref):
        for z in range(deep):
            for y, out_ref in enumerate((near_ref, far_ref)):
                both = own_ref[z, y, :HEAD_DIM, :].astype(jnp.float32) + other_ref[
                    z, y, :HEAD_DIM, :
                ].astype(jnp.float32)
                out_ref[z, :HEAD_DIM, :] = both.astype(jnp.bfloat16)
                out_ref[z, HEAD_DIM:, :] = own_ref[z, y, HEAD_DIM:, :]

    return small_call(body, [(deep, height, lanes)] * 2, [], [own, other])


def merge_chips(own_place, near, far):
    deep, height, lanes = near.shape

    def body(place_ref, near_ref, far_ref, *out_refs):
        for k, out_ref in enumerate(out_refs):
            z = place_ref[0] ^ k
            first, second = near_ref[z], far_ref[z]
            first_top, first_total = read_notes(first[HEAD_DIM:, :])
            second_top, second_total = read_notes(second[HEAD_DIM:, :])
            top = jnp.maximum(first_top, second_top)
            first_factor, second_factor = jnp.exp(first_top - top), jnp.exp(second_top - top)
            out_ref[:HEAD_DIM, :] = (
                first[:HEAD_DIM, :].astype(jnp.float32) * first_factor
                + second[:HEAD_DIM, :].astype(jnp.float32) * second_factor
            ).astype(jnp.bfloat16)
            out_ref[HEAD_DIM:, :] = note_rows(
                top, first_total * first_factor + second_total * second_factor
            )

    return small_call(body, [(height, lanes)] * deep, [own_place], [near, far])


def attend(
    places, turns, queries, own, other, cosine, sine, masks, prompt, got, steps, blocks, width,
    pieces, early,
):
    kv_heads = places.shape[0]
    deep, packed, lanes = queries[0].shape
    share = deep // kv_heads
    count = 2 * share * packed * lanes // HEAD_DIM
    owners = count // HEAD_DIM
    tokens = cosine.shape[0]
    half = tokens // 2
    held = Blocks(prompt, steps, width, pieces)
    inputs = [*queries, own, other, cosine, sine, *masks]

    def body(place_ref, turn_ref, block_ref, *refs):
        query_refs = refs[:2]
        own_ref, other_ref, cosine_ref, sine_ref = refs[2:6]
        mask_refs = refs[6 : len(inputs)]
        prompt_ref, got_ref, step_ref = refs[len(inputs) : len(inputs) + 3]
        early_refs = refs[len(inputs) + 3 : len(inputs) + 3 + len(early)]
        rest = refs[len(inputs) + 3 + len(early) :]
        weight_refs, rest = rest[: len(held.arrays)], rest[len(held.arrays) :]
        *out_refs, step_out_ref = rest[:3]
        early_held, weight_held, value_held, early_sem, *scratch = rest[3:]
        left, weight_rows, _ = scratch
        sources = (prompt_ref, got_ref, step_ref)
        groups = [
            held.copies(i, block_ref, sources, weight_refs, scratch) for i in range(held.count)
        ]
        before = [
            pltpu.make_async_copy(ref, early_held.at[i], early_sem.at[i])
            for i, ref in enumerate(early_refs)
        ]
        for copy in before:
            copy.start()
        for group in groups:
            for copy in group:
                copy.start()
        wide_cosine = jnp.concatenate([cosine_ref[...], cosine_ref[...]], axis=1)
        wide_sine = jnp.concatenate([-sine_ref[...], sine_ref[...]], axis=1)

        def one_head(j, _):
            column = pl.ds(pl.multiple_of(place_ref[j] * HEAD_DIM, HEAD_DIM), HEAD_DIM)
            keys = jnp.concatenate(
                [
                    own_ref[:half, column].astype(jnp.float32)
                    + other_ref[half:tokens, column].astype(jnp.float32),
                    own_ref[half:tokens, column].astype(jnp.float32)
                    + other_ref[:half, column].astype(jnp.float32),
                ],
                axis=0,
            )
            swapped = pltpu.roll(keys, HEAD_DIM // 2, 1)
            keys = (keys * wide_cosine + swapped * wide_sine).astype(jnp.bfloat16)
            unpacked = []
            for part in range(share):
                for ref in query_refs:
                    both = ref[turn_ref[j * share + part]]
                    for low in range(0, packed, packed // 2):
                        for left_lane in range(0, lanes, HEAD_DIM):
                            unpacked.append(
                                both[low : low + packed // 2, left_lane : left_lane + HEAD_DIM]
                            )
            scores = lax.dot_general(
                keys,
                jnp.concatenate(unpacked, axis=0),
                (((1,), (1,)), ((), ())),
                preferred_element_type=jnp.float32,
            )
            if masks:
                scores = jnp.where(mask_refs[0][...] == mask_refs[1][...], scores, -1e30)
            top = jnp.max(scores, axis=0, keepdims=True)
            weights = jnp.exp(scores - top)
            total = jnp.sum(weights, axis=0, keepdims=True)
            for i in range(owners):
                lane = slice(i * HEAD_DIM, (i + 1) * HEAD_DIM)
                out_ref = out_refs[i // 2 % 2]
                out_ref[j, i // 4 * 2 + i % 2, HEAD_DIM:, :] = note_rows(
                    top[:, lane], total[:, lane]
                )
            weight_held[j] = weights.astype(jnp.bfloat16)
            return 0

        lax.fori_loop(0, kv_heads, one_head, 0)
        for copy in before:
            copy.wait()
        total = sum(early_held[i].astype(jnp.float32) for i in range(len(early)))
        for i, group in enumerate(groups):
            for copy in group:
                copy.wait()
            total += jnp.dot(left[i], weight_rows[i], preferred_element_type=jnp.float32)
        value_held[...] = total[:tokens].astype(jnp.bfloat16)
        step_out_ref[...] = total[tokens:]

        def one_sum(j, _):
            column = pl.ds(pl.multiple_of(place_ref[j] * HEAD_DIM, HEAD_DIM), HEAD_DIM)
            summed = lax.dot_general(
                value_held[:, column],
                weight_held[j],
                (((0,), (0,)), ((), ())),
                preferred_element_type=jnp.float32,
            )
            for i in range(owners):
                lane = slice(i * HEAD_DIM, (i + 1) * HEAD_DIM)
                out_ref = out_refs[i // 2 % 2]
                out_ref[j, i // 4 * 2 + i % 2, :HEAD_DIM, :] = summed[:, lane].astype(jnp.bfloat16)
            return 0

        lax.fori_loop(0, kv_heads, one_sum, 0)

    anywhere = pl.BlockSpec(memory_space=pl.ANY)
    whole = pl.BlockSpec(memory_space=pltpu.VMEM)
    return pl.pallas_call(
        body,
        in_specs=[pl.BlockSpec(memory_space=pltpu.SMEM)] * 3
        + [whole] * len(inputs)
        + [anywhere] * (3 + len(early) + len(held.arrays)),
        out_specs=[whole] * 3,
        out_shape=[
            *[
                jax.ShapeDtypeStruct(
                    (kv_heads, owners // 2, HEAD_DIM + NOTES, HEAD_DIM), jnp.bfloat16
                )
            ]
            * 2,
            jax.ShapeDtypeStruct((held.step_count, held.columns), jnp.float32),
        ],
        scratch_shapes=[
            pltpu.VMEM((len(early), held.height, held.columns), jnp.bfloat16),
            pltpu.VMEM((kv_heads, tokens, count), jnp.bfloat16),
            pltpu.VMEM((tokens, held.columns), jnp.bfloat16),
            pltpu.SemaphoreType.DMA((len(early),)),
            *held.scratch,
        ],
        compiler_params=pltpu.CompilerParams(vmem_limit_bytes=57 * MIB),
        cost_estimate=LIGHT,
    )(places, turns, blocks, *inputs, prompt, got, steps, *early, *held.arrays)


def out_project(blocks, parts, queries, new_keys, new_values, weight, width):
    count = len(parts)
    steps = queries.shape[0]
    samples = steps // 2

    def body(block_ref, *refs):
        part_refs = refs[:count]
        query_ref, key_ref, value_ref, weight_ref, out_ref = refs[count:]
        notes = [read_notes(ref[HEAD_DIM:, :]) for ref in part_refs]
        top = notes[0][0]
        for other, _ in notes[1:]:
            top = jnp.maximum(top, other)
        sums = total = 0.0
        for ref, (part_top, part_total) in zip(part_refs, notes):
            factor = jnp.exp(part_top - top)
            sums = sums + ref[:HEAD_DIM, :].astype(jnp.float32) * factor
            total = total + part_total * factor
        sums = sums.T
        both = jnp.concatenate([top, total, jnp.zeros((6, HEAD_DIM), jnp.float32)], axis=0).T
        keys, values = key_ref[...], value_ref[...]
        heads = []
        for h in range(queries.shape[1] // HEAD_DIM):
            query = query_ref[:, h * HEAD_DIM : (h + 1) * HEAD_DIM].astype(jnp.float32)
            own_score = jnp.sum(query * keys, axis=1, keepdims=True) * (HEAD_DIM**-0.5)
            back_score = jnp.sum(
                query[samples:] * keys[:samples], axis=1, keepdims=True
            ) * (HEAD_DIM**-0.5)
            ends = []
            for step in (0, 1):
                place = slice((2 * h + step) * samples, (2 * h + step + 1) * samples)
                here = slice(step * samples, (step + 1) * samples)
                old_top, old_total = both[place, 0:1], both[place, 1:2]
                scores = [(own_score[here], values[here])]
                if step:
                    scores.append((back_score, values[:samples]))
                high = old_top
                for score, _ in scores:
                    high = jnp.maximum(high, score)
                old = jnp.exp(old_top - high)
                numerator, denominator = old * sums[place], old * old_total
                for score, value in scores:
                    new = jnp.exp(score - high)
                    numerator, denominator = numerator + new * value, denominator + new
                ends.append(numerator / denominator)
            heads.append(jnp.concatenate(ends, axis=0).astype(jnp.bfloat16))
        heads = jnp.concatenate(heads, axis=1)
        for i in range(blocks.shape[0]):
            start = pl.multiple_of(block_ref[i] * width, width)
            out_ref[:, i * width : (i + 1) * width] = jnp.dot(
                heads, weight_ref[:, pl.ds(start, width)], preferred_element_type=jnp.float32
            ).astype(jnp.bfloat16)

    return small_call(
        body, [(steps, weight.shape[1])], [blocks], [*parts, queries, new_keys, new_values, weight]
    )[0]


def on_device(
    prompt_states,
    page_table,
    step_states,
    sample_order,
    key_weight,
    value_weight,
    query_weight,
    out_weight,
):
    devices = lax.axis_size("sample")
    groups = lax.axis_size("groups")
    own_index = lax.axis_index("sample")
    first = lax.axis_index("groups") % 2 == 0
    deep = devices // LINE
    own_a, own_b, own_c = own_index // LINE, own_index // 2 % 2, own_index % 2
    along_ring, along_z, along_y, along_x, in_chip = mover(groups, devices)
    row_count = prompt_states.shape[0]
    chip_rows = 2 * row_count
    pages_here = row_count // PAGE
    heads_here = query_weight.shape[1] // HEAD_DIM
    total_pages = page_table.shape[0]
    prompts = total_pages // PROMPT_PAGES
    samples = sample_order.shape[0]
    steps = 2 * samples
    group_size = samples // prompts
    own_kv = own_index * heads_here // GQA
    wide_states = step_states.reshape(steps, D)
    rows = heads_here * steps
    width = key_weight.shape[0]
    half = key_weight.shape[1] // 2
    kv_places = jnp.where(first, 0, KV_HEADS // 2) + jnp.arange(KV_HEADS, dtype=jnp.int32)
    kv_places = kv_places % KV_HEADS

    order = ring_order(deep)

    def by_place(table):
        return sum(jnp.where(own_a == a, table[a], 0) for a in range(deep))

    own_turn = by_place([order.index(a) for a in range(deep)])

    def block(place_z, flip, core):
        return place_z * LINE + (own_b ^ flip) * 2 + core

    def behind(k):
        return by_place([order[(order.index(a) - k) % deep] for a in range(deep)])

    low = jnp.concatenate([key_weight[:, :half], value_weight[:, :half]])
    high = jnp.concatenate([key_weight[:, half:], value_weight[:, half:]])
    both_mine, both_other = jnp.where(first, low, high), jnp.where(first, high, low)

    own_pages = jnp.concatenate(
        [
            holder * pages_here + jnp.arange(pages_here, dtype=jnp.int32)
            for holder in (own_index, own_index ^ 1)
        ]
    )
    slots = jnp.sum(
        jnp.where(
            page_table[None, :] == own_pages[:, None],
            jnp.arange(total_pages, dtype=jnp.int32)[None, :],
            0,
        ),
        axis=1,
    )
    positions = (slots % PROMPT_PAGES * PAGE)[:, None] + jnp.arange(PAGE, dtype=jnp.int32)[None, :]
    scaled_tables = tuple(
        table * HEAD_DIM ** (-0.5) for table in rope_tables(positions.reshape(chip_rows))
    )

    step_place = PROMPT_PAGES * PAGE + jnp.arange(2, dtype=jnp.int32)
    step_tables = tuple(t[:, None, :] for t in rope_tables(step_place))
    flat_tables = [
        jnp.repeat(jnp.concatenate([sign * table, table], axis=-1)[:, 0], samples, axis=0)
        for sign, table in zip((1, -1), step_tables)
    ]
    queries = project_queries(
        after(wide_states, scaled_tables), query_weight, *flat_tables
    )
    packed_queries = jnp.concatenate(
        jnp.split(queries, half // queries.shape[1], axis=0), axis=1
    )
    packed = packed_queries.shape[0]

    places = [(k, flip) for k in range(deep) for flip in (0, 1)]
    parts_of = [
        (*range(0, 2 * deep, 2), 1),
        tuple(range(3, 2 * deep, 2)),
    ]
    taken_blocks = {
        which: jnp.stack([block(behind(places[i][0]), places[i][1], own_c) for i in which])
        for which in (tuple(range(2 * deep)), *parts_of)
    }
    query_turns = jnp.stack([(own_turn + deep - order.index(a)) % deep for a in range(deep)])
    own_place = (own_kv + jnp.where(first, 0, KV_HEADS // 2)) % KV_HEADS * HEAD_DIM
    done = {}

    def send(move, value):
        moved = done.setdefault(move, [])
        moved.append(move(after(value, moved[-2]) if len(moved) > 1 else value))
        return moved[-1]

    got = in_chip(prompt_states)
    both_z, both_x, theirs, theirs_x = {0: both_mine}, {0: both_other}, {}, {}
    value_y = send(along_y, value_weight)
    both_z[1] = send(along_ring, both_mine)
    theirs_x[0] = jnp.where(first, value_y[:, half:], value_y[:, :half])
    value_y = jnp.where(first, value_y[:, :half], value_y[:, half:])
    key_full = {0: jnp.concatenate([both_mine[:width], both_other[:width], packed_queries])}
    key_y = {0: send(along_y, after(key_full[0], value_y))}
    theirs[0] = jnp.concatenate([value_y, packed_queries, key_y[0][2 * width :]])
    for k in range(1, deep):
        if k + 1 < deep:
            both_z[k + 1] = send(along_ring, both_z[k])
        both_x[k] = send(along_x, both_z[k])
        key_full[k] = jnp.concatenate([both_z[k][:width], both_x[k][:width]])
        early_work = (taken_blocks, kv_places, query_turns) if k == 2 else ()
        key_y[k] = send(along_y, after(key_full[k], (key_y[k - 1], early_work)))
    for k in range(1, deep):
        theirs[k] = send(along_ring, theirs[k - 1])
        theirs_x[k] = send(along_x, theirs[k][:width])

    ring_queries = collect([theirs[k] for k in range(deep)], width, 2 * packed)
    ring_queries = [ring_queries, in_chip(ring_queries)]

    key_pieces = [
        [((key_y if flip else key_full)[k], start) for start in (0, width)] for k, flip in places
    ]
    value_pieces = [
        [(theirs[k], 0), (theirs_x[k], 0)] if flip else [(both_z[k], width), (both_x[k], width)]
        for k, flip in places
    ]

    def project_blocks(pieces, which, acc, ready, kind):
        taken = after(taken_blocks[tuple(which)], ready)
        return project(
            prompt_states, got, wide_states, taken, width, [pieces[i] for i in which], acc, kind
        )

    value_early = project_blocks(
        value_pieces, parts_of[0], None, (theirs_x[1], theirs[deep - 1]), jnp.bfloat16
    )
    awaited = (value_early, [theirs_x[k] for k in range(1, deep)])
    key_sum = project_blocks(key_pieces, range(2 * deep), None, awaited, jnp.bfloat16)
    key_back = in_chip(key_sum)

    def own_head(sums):
        sums = lax.dynamic_slice_in_dim(sums, own_place, HEAD_DIM, 1)
        return sums.reshape(2, samples, HEAD_DIM).astype(jnp.float32)

    new_keys = own_head(key_sum[chip_rows:]) + own_head(key_back[chip_rows:])
    new_keys = turn(new_keys, step_tables).astype(jnp.bfloat16).astype(jnp.float32)
    new_keys = new_keys.reshape(steps, HEAD_DIM)
    masks = []
    if prompts > 1:
        token_prompt = jnp.repeat(slots // PROMPT_PAGES, PAGE)
        row_prompt = jnp.tile(sample_order // group_size, devices // KV_HEADS * rows // samples)
        masks = [token_prompt[:, None], row_prompt[None, :]]
    kept, sent, step_values = attend(
        kv_places, query_turns, ring_queries, key_sum, key_back, *scaled_tables, masks,
        prompt_states, got, wide_states, taken_blocks[parts_of[1]], width,
        [value_pieces[i] for i in parts_of[1]], [value_early],
    )
    new_values = own_head(step_values) + own_head(in_chip(step_values))
    new_values = new_values.astype(jnp.bfloat16).astype(jnp.float32).reshape(steps, HEAD_DIM)

    by_owner = (deep, 2, *kept.shape[2:])
    near, far = merge_cores(kept.reshape(by_owner), in_chip(sent.reshape(by_owner)))
    merged = merge_chips(own_a[None], near, along_y(far))
    parts = [merged[0]] + [along_z(merged[k], k) for k in range(1, deep)]

    out_width = out_weight.shape[1] // devices
    out_blocks = jnp.stack(
        [
            block(own_a ^ k, flip, own_c ^ turned)
            for turned in (0, 1)
            for flip in (0, 1)
            for k in range(deep)
        ]
    )
    terms = out_project(out_blocks, parts, queries, new_keys, new_values, out_weight, out_width)

    def narrow(value):
        return value.astype(jnp.bfloat16)

    def wide(value):
        return value.astype(jnp.float32)

    for move in (in_chip, along_y):
        share = terms.shape[1] // 2
        terms = narrow(wide(terms[:, :share]) + wide(move(terms[:, share:])))
    attn_out = wide(terms[:, :out_width])
    for k in range(1, deep):
        attn_out = attn_out + wide(along_z(terms[:, k * out_width : (k + 1) * out_width], k))
    return narrow(attn_out).reshape(2, samples, -1)


def solution(mesh):
    in_specs = (
        P(("groups", "sample"), None),
        P("groups"),
        P(None, "groups", None),
        P("groups"),
        P("sample", None),
        P("sample", None),
        P(None, "sample"),
        P("sample", None),
    )
    out_specs = P(None, "groups", "sample")
    return jax.shard_map(
        on_device, mesh=mesh, in_specs=in_specs, out_specs=out_specs, check_vma=False
    )
```

```python
import jax
import jax.numpy as jnp
from jax import lax
from jax.experimental import pallas as pl
from jax.experimental.pallas import tpu as pltpu
from jax.sharding import PartitionSpec as P

D = 8192
HEAD_DIM = 128
KV_HEADS = 4
GQA = 8
PAGE = 128
PROMPT_PAGES = 64
LINE = 4

rope_base = 1000000.0


def rope_tables(position):
    half_dim = HEAD_DIM // 2
    frequency = rope_base ** (-jnp.arange(half_dim, dtype=jnp.float32) * 2.0 / HEAD_DIM)
    angles = position.astype(jnp.float32)[..., None] * frequency
    return jnp.cos(angles), jnp.sin(angles)


def turn(vector, tables):
    cosine, sine_part = tables
    half_dim = HEAD_DIM // 2
    first_half = vector[..., :half_dim]
    second_half = vector[..., half_dim:]
    return jnp.concatenate(
        [
            first_half * cosine - second_half * sine_part,
            second_half * cosine + first_half * sine_part,
        ],
        axis=-1,
    )


def ring_order(deep):
    return [*range(0, deep, 2), *range(deep - 1 - deep % 2, 0, -2)]


def mover(groups, devices):
    deep = devices // LINE
    order = ring_order(deep)

    def move(value, step):
        pairs = []
        for g in range(groups):
            for s in range(devices):
                a, b, c = s // LINE, s // 2 % 2, s % 2
                to_g, to_a, to_b, to_c = step(g, a, b, c)
                to_s = (to_a % deep) * LINE + to_b * 2 + to_c
                pairs.append((g * devices + s, to_g * devices + to_s))
        return lax.ppermute(value, ("groups", "sample"), pairs)

    def next_on_ring(a):
        return order[(order.index(a) + 1) % deep]

    along_ring = lambda v: move(v, lambda g, a, b, c: (g, next_on_ring(a), b, c))
    along_z = lambda v, k: move(v, lambda g, a, b, c: (g, a ^ k, b, c))
    along_y = lambda v: move(v, lambda g, a, b, c: (g, a, 1 - b, c))
    along_x = lambda v: move(v, lambda g, a, b, c: (g ^ 1, a, b, c))
    in_chip = lambda v: move(v, lambda g, a, b, c: (g, a, b, 1 - c))
    return along_ring, along_z, along_y, along_x, in_chip


def after(value, done):
    return lax.optimization_barrier((value, done))[0]


MIB = 1024 * 1024
LIGHT = pl.CostEstimate(flops=1, bytes_accessed=1, transcendentals=0)


def project_queries(steps, weight, cosine, sine):
    count, depth = steps.shape
    parts = 8
    piece = depth // parts

    def body(step_ref, weight_ref, cosine_ref, sine_ref, out_ref, held, sems):
        copies = []
        for i in range(parts):
            copies.append(
                pltpu.make_async_copy(
                    weight_ref.at[pl.ds(i * piece, piece), :], held.at[i], sems.at[i]
                )
            )
            copies[-1].start()
        total = None
        for i in range(parts):
            copies[i].wait()
            product = jnp.dot(
                step_ref[:, i * piece : (i + 1) * piece],
                held[i],
                preferred_element_type=jnp.float32,
            )
            total = product if total is None else total + product
        tables = [
            jnp.concatenate(
                [jnp.broadcast_to(ref[i : i + 1, :], (count // 2, HEAD_DIM)) for i in (0, 1)],
                axis=0,
            )
            for ref in (cosine_ref, sine_ref)
        ]
        for start in range(0, weight.shape[1], HEAD_DIM):
            head = total[:, start : start + HEAD_DIM]
            turned = head * tables[0] + pltpu.roll(head, HEAD_DIM // 2, 1) * tables[1]
            out_ref[:, start : start + HEAD_DIM] = turned.astype(jnp.bfloat16)

    whole = pl.BlockSpec(memory_space=pltpu.VMEM)
    return pl.pallas_call(
        body,
        in_specs=[whole, pl.BlockSpec(memory_space=pltpu.HBM), whole, whole],
        out_specs=whole,
        out_shape=jax.ShapeDtypeStruct((count, weight.shape[1]), jnp.bfloat16),
        scratch_shapes=[
            pltpu.VMEM((parts, piece, weight.shape[1]), weight.dtype),
            pltpu.SemaphoreType.DMA((parts,)),
        ],
        compiler_params=pltpu.CompilerParams(vmem_limit_bytes=61 * MIB),
        cost_estimate=LIGHT,
    )(steps, weight, cosine, sine)


def collect(arrays, first, height):
    columns = arrays[0].shape[1]

    def body(*refs):
        out_ref, sems = refs[-2:]
        copies = [
            pltpu.make_async_copy(ref.at[pl.ds(first, height), :], out_ref.at[i], sems.at[i])
            for i, ref in enumerate(refs[:-2])
        ]
        for copy in copies:
            copy.start()
        for copy in copies:
            copy.wait()

    return pl.pallas_call(
        body,
        in_specs=[pl.BlockSpec(memory_space=pl.ANY)] * len(arrays),
        out_specs=pl.BlockSpec(memory_space=pltpu.VMEM),
        out_shape=jax.ShapeDtypeStruct((len(arrays), height, columns), arrays[0].dtype),
        scratch_shapes=[pltpu.SemaphoreType.DMA((len(arrays),))],
        compiler_params=pltpu.CompilerParams(vmem_limit_bytes=4 * MIB),
        cost_estimate=LIGHT,
    )(*arrays)


class Blocks:
    def __init__(self, prompt, steps, width, pieces):
        self.arrays = []
        for piece in pieces:
            for array, _ in piece:
                if not any(array is held for held in self.arrays):
                    self.arrays.append(array)
        self.pieces, self.width, self.count = pieces, width, len(pieces)
        self.row_count, self.step_count = prompt.shape[0], steps.shape[0]
        self.height = 2 * self.row_count + self.step_count
        self.columns = sum(array.shape[1] for array, _ in pieces[0])
        self.scratch = [
            pltpu.VMEM((self.count, self.height, width), prompt.dtype),
            pltpu.VMEM((self.count, width, self.columns), prompt.dtype),
            pltpu.SemaphoreType.DMA((self.count, 5)),
        ]

    def copies(self, i, block_ref, sources, weight_refs, scratch):
        left, weights, sems = scratch
        column = pl.ds(pl.multiple_of(block_ref[i] * self.width, self.width), self.width)
        group = []
        start = 0
        for j, (source, rows) in enumerate(
            zip(sources, (self.row_count, self.row_count, self.step_count))
        ):
            group.append(
                pltpu.make_async_copy(
                    source.at[:, column], left.at[i, pl.ds(start, rows), :], sems.at[i, j]
                )
            )
            start += rows
        side = 0
        for j, (array, first) in enumerate(self.pieces[i]):
            ref = weight_refs[[array is other for other in self.arrays].index(True)]
            group.append(
                pltpu.make_async_copy(
                    ref.at[pl.ds(first, self.width), :],
                    weights.at[i, :, pl.ds(side, array.shape[1])],
                    sems.at[i, 3 + j],
                )
            )
            side += array.shape[1]
        return group


AHEAD = 3


def project(prompt, got, steps, blocks, width, pieces, acc, kind):
    held = Blocks(prompt, steps, width, pieces)
    extra = [] if acc is None else [acc]

    def body(block_ref, prompt_ref, got_ref, step_ref, *refs):
        weight_refs = refs[: len(held.arrays)]
        out_ref, acc_held, acc_sem, *scratch = refs[len(held.arrays) + len(extra) :]
        left, weights, _ = scratch
        sources = (prompt_ref, got_ref, step_ref)
        groups = [
            held.copies(i, block_ref, sources, weight_refs, scratch) for i in range(held.count)
        ]
        for group in groups[:AHEAD]:
            for copy in group:
                copy.start()
        if extra:
            before = pltpu.make_async_copy(refs[len(held.arrays)], acc_held, acc_sem.at[0])
            before.start()
        total = None
        for i, group in enumerate(groups):
            for copy in group:
                copy.wait()
            if i + AHEAD < held.count:
                for copy in groups[i + AHEAD]:
                    copy.start()
            product = jnp.dot(left[i], weights[i], preferred_element_type=jnp.float32)
            total = product if total is None else total + product
        if extra:
            before.wait()
            total = total + acc_held[...]
        out_ref[...] = total.astype(kind)

    anywhere = pl.BlockSpec(memory_space=pl.ANY)
    return pl.pallas_call(
        body,
        in_specs=[pl.BlockSpec(memory_space=pltpu.SMEM)] + [anywhere] * (3 + len(held.arrays) + len(extra)),
        out_specs=pl.BlockSpec(memory_space=pltpu.VMEM),
        out_shape=jax.ShapeDtypeStruct((held.height, held.columns), kind),
        scratch_shapes=[
            pltpu.VMEM((held.height, held.columns) if extra else (8, HEAD_DIM), jnp.float32),
            pltpu.SemaphoreType.DMA((1,)),
            *held.scratch,
        ],
        compiler_params=pltpu.CompilerParams(vmem_limit_bytes=57 * MIB),
        cost_estimate=LIGHT,
    )(blocks, prompt, got, steps, *held.arrays, *extra)


NOTES = 16


def thirds(value):
    parts = []
    for _ in range(3):
        parts.append(value.astype(jnp.bfloat16))
        value = value - parts[-1].astype(jnp.float32)
    return parts


def note_rows(top, total):
    parts = [part.astype(jnp.float32) for part in thirds(top) + thirds(total)]
    rows = jnp.concatenate(parts + [jnp.zeros((NOTES - 6, top.shape[1]), jnp.float32)], axis=0)
    return rows.astype(jnp.bfloat16)


def read_notes(rows):
    rows = rows.astype(jnp.float32)
    return rows[0:1] + rows[1:2] + rows[2:3], rows[3:4] + rows[4:5] + rows[5:6]


def small_call(body, out_shapes, scalars, arrays):
    whole = pl.BlockSpec(memory_space=pltpu.VMEM)
    return pl.pallas_call(
        body,
        in_specs=[pl.BlockSpec(memory_space=pltpu.SMEM)] * len(scalars) + [whole] * len(arrays),
        out_specs=[whole] * len(out_shapes),
        out_shape=[jax.ShapeDtypeStruct(shape, jnp.bfloat16) for shape in out_shapes],
        compiler_params=pltpu.CompilerParams(vmem_limit_bytes=12 * MIB),
        cost_estimate=LIGHT,
    )(*scalars, *arrays)


def merge_cores(own, other):
    deep, _, height, lanes = own.shape

    def body(own_ref, other_ref, near_ref, far_ref):
        for z in range(deep):
            for y, out_ref in enumerate((near_ref, far_ref)):
                both = own_ref[z, y, :HEAD_DIM, :].astype(jnp.float32) + other_ref[
                    z, y, :HEAD_DIM, :
                ].astype(jnp.float32)
                out_ref[z, :HEAD_DIM, :] = both.astype(jnp.bfloat16)
                out_ref[z, HEAD_DIM:, :] = own_ref[z, y, HEAD_DIM:, :]

    return small_call(body, [(deep, height, lanes)] * 2, [], [own, other])


def merge_chips(own_place, near, far):
    deep, height, lanes = near.shape

    def body(place_ref, near_ref, far_ref, *out_refs):
        for k, out_ref in enumerate(out_refs):
            z = place_ref[0] ^ k
            first, second = near_ref[z], far_ref[z]
            first_top, first_total = read_notes(first[HEAD_DIM:, :])
            second_top, second_total = read_notes(second[HEAD_DIM:, :])
            top = jnp.maximum(first_top, second_top)
            first_factor, second_factor = jnp.exp(first_top - top), jnp.exp(second_top - top)
            out_ref[:HEAD_DIM, :] = (
                first[:HEAD_DIM, :].astype(jnp.float32) * first_factor
                + second[:HEAD_DIM, :].astype(jnp.float32) * second_factor
            ).astype(jnp.bfloat16)
            out_ref[HEAD_DIM:, :] = note_rows(
                top, first_total * first_factor + second_total * second_factor
            )

    return small_call(body, [(height, lanes)] * deep, [own_place], [near, far])


def attend(
    places, turns, queries, own, other, cosine, sine, masks, prompt, got, steps, blocks, width,
    pieces, early,
):
    kv_heads = places.shape[0]
    deep, packed, lanes = queries[0].shape
    share = deep // kv_heads
    count = 2 * share * packed * lanes // HEAD_DIM
    owners = count // HEAD_DIM
    tokens = cosine.shape[0]
    half = tokens // 2
    held = Blocks(prompt, steps, width, pieces)
    inputs = [*queries, own, other, cosine, sine, *masks]

    def body(place_ref, turn_ref, block_ref, *refs):
        query_refs = refs[:2]
        own_ref, other_ref, cosine_ref, sine_ref = refs[2:6]
        mask_refs = refs[6 : len(inputs)]
        prompt_ref, got_ref, step_ref = refs[len(inputs) : len(inputs) + 3]
        early_refs = refs[len(inputs) + 3 : len(inputs) + 3 + len(early)]
        rest = refs[len(inputs) + 3 + len(early) :]
        weight_refs, rest = rest[: len(held.arrays)], rest[len(held.arrays) :]
        *out_refs, step_out_ref = rest[:3]
        early_held, weight_held, value_held, early_sem, *scratch = rest[3:]
        left, weight_rows, _ = scratch
        sources = (prompt_ref, got_ref, step_ref)
        groups = [
            held.copies(i, block_ref, sources, weight_refs, scratch) for i in range(held.count)
        ]
        before = [
            pltpu.make_async_copy(ref, early_held.at[i], early_sem.at[i])
            for i, ref in enumerate(early_refs)
        ]
        for copy in before:
            copy.start()
        for group in groups:
            for copy in group:
                copy.start()
        wide_cosine = jnp.concatenate([cosine_ref[...], cosine_ref[...]], axis=1)
        wide_sine = jnp.concatenate([-sine_ref[...], sine_ref[...]], axis=1)

        def one_head(j, _):
            column = pl.ds(pl.multiple_of(place_ref[j] * HEAD_DIM, HEAD_DIM), HEAD_DIM)
            keys = jnp.concatenate(
                [
                    own_ref[:half, column].astype(jnp.float32)
                    + other_ref[half:tokens, column].astype(jnp.float32),
                    own_ref[half:tokens, column].astype(jnp.float32)
                    + other_ref[:half, column].astype(jnp.float32),
                ],
                axis=0,
            )
            swapped = pltpu.roll(keys, HEAD_DIM // 2, 1)
            keys = (keys * wide_cosine + swapped * wide_sine).astype(jnp.bfloat16)
            unpacked = []
            for part in range(share):
                for ref in query_refs:
                    both = ref[turn_ref[j * share + part]]
                    for low in range(0, packed, packed // 2):
                        for left_lane in range(0, lanes, HEAD_DIM):
                            unpacked.append(
                                both[low : low + packed // 2, left_lane : left_lane + HEAD_DIM]
                            )
            scores = lax.dot_general(
                keys,
                jnp.concatenate(unpacked, axis=0),
                (((1,), (1,)), ((), ())),
                preferred_element_type=jnp.float32,
            )
            if masks:
                scores = jnp.where(mask_refs[0][...] == mask_refs[1][...], scores, -1e30)
            top = jnp.max(scores, axis=0, keepdims=True)
            weights = jnp.exp(scores - top)
            total = jnp.sum(weights, axis=0, keepdims=True)
            for i in range(owners):
                lane = slice(i * HEAD_DIM, (i + 1) * HEAD_DIM)
                out_ref = out_refs[i // 2 % 2]
                out_ref[j, i // 4 * 2 + i % 2, HEAD_DIM:, :] = note_rows(
                    top[:, lane], total[:, lane]
                )
            weight_held[j] = weights.astype(jnp.bfloat16)
            return 0

        lax.fori_loop(0, kv_heads, one_head, 0)
        for copy in before:
            copy.wait()
        total = sum(early_held[i].astype(jnp.float32) for i in range(len(early)))
        for i, group in enumerate(groups):
            for copy in group:
                copy.wait()
            total += jnp.dot(left[i], weight_rows[i], preferred_element_type=jnp.float32)
        value_held[...] = total[:tokens].astype(jnp.bfloat16)
        step_out_ref[...] = total[tokens:]

        def one_sum(j, _):
            column = pl.ds(pl.multiple_of(place_ref[j] * HEAD_DIM, HEAD_DIM), HEAD_DIM)
            summed = lax.dot_general(
                value_held[:, column],
                weight_held[j],
                (((0,), (0,)), ((), ())),
                preferred_element_type=jnp.float32,
            )
            for i in range(owners):
                lane = slice(i * HEAD_DIM, (i + 1) * HEAD_DIM)
                out_ref = out_refs[i // 2 % 2]
                out_ref[j, i // 4 * 2 + i % 2, :HEAD_DIM, :] = summed[:, lane].astype(jnp.bfloat16)
            return 0

        lax.fori_loop(0, kv_heads, one_sum, 0)

    anywhere = pl.BlockSpec(memory_space=pl.ANY)
    whole = pl.BlockSpec(memory_space=pltpu.VMEM)
    return pl.pallas_call(
        body,
        in_specs=[pl.BlockSpec(memory_space=pltpu.SMEM)] * 3
        + [whole] * len(inputs)
        + [anywhere] * (3 + len(early) + len(held.arrays)),
        out_specs=[whole] * 3,
        out_shape=[
            *[
                jax.ShapeDtypeStruct(
                    (kv_heads, owners // 2, HEAD_DIM + NOTES, HEAD_DIM), jnp.bfloat16
                )
            ]
            * 2,
            jax.ShapeDtypeStruct((held.step_count, held.columns), jnp.float32),
        ],
        scratch_shapes=[
            pltpu.VMEM((len(early), held.height, held.columns), jnp.bfloat16),
            pltpu.VMEM((kv_heads, tokens, count), jnp.bfloat16),
            pltpu.VMEM((tokens, held.columns), jnp.bfloat16),
            pltpu.SemaphoreType.DMA((len(early),)),
            *held.scratch,
        ],
        compiler_params=pltpu.CompilerParams(vmem_limit_bytes=57 * MIB),
        cost_estimate=LIGHT,
    )(places, turns, blocks, *inputs, prompt, got, steps, *early, *held.arrays)


def out_project(blocks, parts, queries, new_keys, new_values, weight, width):
    count = len(parts)
    steps = queries.shape[0]
    samples = steps // 2

    def body(block_ref, *refs):
        part_refs = refs[:count]
        query_ref, key_ref, value_ref, weight_ref, out_ref = refs[count:]
        notes = [read_notes(ref[HEAD_DIM:, :]) for ref in part_refs]
        top = notes[0][0]
        for other, _ in notes[1:]:
            top = jnp.maximum(top, other)
        sums = total = 0.0
        for ref, (part_top, part_total) in zip(part_refs, notes):
            factor = jnp.exp(part_top - top)
            sums = sums + ref[:HEAD_DIM, :].astype(jnp.float32) * factor
            total = total + part_total * factor
        sums = sums.T
        both = jnp.concatenate([top, total, jnp.zeros((6, HEAD_DIM), jnp.float32)], axis=0).T
        keys, values = key_ref[...], value_ref[...]
        heads = []
        for h in range(queries.shape[1] // HEAD_DIM):
            query = query_ref[:, h * HEAD_DIM : (h + 1) * HEAD_DIM].astype(jnp.float32)
            own_score = jnp.sum(query * keys, axis=1, keepdims=True) * (HEAD_DIM**-0.5)
            back_score = jnp.sum(
                query[samples:] * keys[:samples], axis=1, keepdims=True
            ) * (HEAD_DIM**-0.5)
            ends = []
            for step in (0, 1):
                place = slice((2 * h + step) * samples, (2 * h + step + 1) * samples)
                here = slice(step * samples, (step + 1) * samples)
                old_top, old_total = both[place, 0:1], both[place, 1:2]
                scores = [(own_score[here], values[here])]
                if step:
                    scores.append((back_score, values[:samples]))
                high = old_top
                for score, _ in scores:
                    high = jnp.maximum(high, score)
                old = jnp.exp(old_top - high)
                numerator, denominator = old * sums[place], old * old_total
                for score, value in scores:
                    new = jnp.exp(score - high)
                    numerator, denominator = numerator + new * value, denominator + new
                ends.append(numerator / denominator)
            heads.append(jnp.concatenate(ends, axis=0).astype(jnp.bfloat16))
        heads = jnp.concatenate(heads, axis=1)
        for i in range(blocks.shape[0]):
            start = pl.multiple_of(block_ref[i] * width, width)
            out_ref[:, i * width : (i + 1) * width] = jnp.dot(
                heads, weight_ref[:, pl.ds(start, width)], preferred_element_type=jnp.float32
            ).astype(jnp.bfloat16)

    return small_call(
        body, [(steps, weight.shape[1])], [blocks], [*parts, queries, new_keys, new_values, weight]
    )[0]


def on_device(
    prompt_states,
    page_table,
    step_states,
    sample_order,
    key_weight,
    value_weight,
    query_weight,
    out_weight,
):
    devices = lax.axis_size("sample")
    groups = lax.axis_size("groups")
    own_index = lax.axis_index("sample")
    first = lax.axis_index("groups") % 2 == 0
    deep = devices // LINE
    own_a, own_b, own_c = own_index // LINE, own_index // 2 % 2, own_index % 2
    along_ring, along_z, along_y, along_x, in_chip = mover(groups, devices)
    row_count = prompt_states.shape[0]
    chip_rows = 2 * row_count
    pages_here = row_count // PAGE
    heads_here = query_weight.shape[1] // HEAD_DIM
    total_pages = page_table.shape[0]
    prompts = total_pages // PROMPT_PAGES
    samples = sample_order.shape[0]
    steps = 2 * samples
    group_size = samples // prompts
    own_kv = own_index * heads_here // GQA
    wide_states = step_states.reshape(steps, D)
    rows = heads_here * steps
    width = key_weight.shape[0]
    half = key_weight.shape[1] // 2
    kv_places = jnp.where(first, 0, KV_HEADS // 2) + jnp.arange(KV_HEADS, dtype=jnp.int32)
    kv_places = kv_places % KV_HEADS

    order = ring_order(deep)

    def by_place(table):
        return sum(jnp.where(own_a == a, table[a], 0) for a in range(deep))

    own_turn = by_place([order.index(a) for a in range(deep)])

    def block(place_z, flip, core):
        return place_z * LINE + (own_b ^ flip) * 2 + core

    def behind(k):
        return by_place([order[(order.index(a) - k) % deep] for a in range(deep)])

    low = jnp.concatenate([key_weight[:, :half], value_weight[:, :half]])
    high = jnp.concatenate([key_weight[:, half:], value_weight[:, half:]])
    both_mine, both_other = jnp.where(first, low, high), jnp.where(first, high, low)

    own_pages = jnp.concatenate(
        [
            holder * pages_here + jnp.arange(pages_here, dtype=jnp.int32)
            for holder in (own_index, own_index ^ 1)
        ]
    )
    slots = jnp.sum(
        jnp.where(
            page_table[None, :] == own_pages[:, None],
            jnp.arange(total_pages, dtype=jnp.int32)[None, :],
            0,
        ),
        axis=1,
    )
    positions = (slots % PROMPT_PAGES * PAGE)[:, None] + jnp.arange(PAGE, dtype=jnp.int32)[None, :]
    scaled_tables = tuple(
        table * HEAD_DIM ** (-0.5) for table in rope_tables(positions.reshape(chip_rows))
    )

    step_place = PROMPT_PAGES * PAGE + jnp.arange(2, dtype=jnp.int32)
    step_tables = tuple(t[:, None, :] for t in rope_tables(step_place))
    flat_tables = [
        jnp.concatenate([sign * table, table], axis=-1)[:, 0]
        for sign, table in zip((1, -1), step_tables)
    ]
    queries = project_queries(
        after(wide_states, scaled_tables), query_weight, *flat_tables
    )
    packed_queries = jnp.concatenate(
        jnp.split(queries, half // queries.shape[1], axis=0), axis=1
    )
    packed = packed_queries.shape[0]

    places = [(k, flip) for k in range(deep) for flip in (0, 1)]
    parts_of = [
        (*range(0, 2 * deep, 2), 1),
        tuple(range(3, 2 * deep, 2)),
    ]
    taken_blocks = {
        which: jnp.stack([block(behind(places[i][0]), places[i][1], own_c) for i in which])
        for which in (tuple(range(2 * deep)), *parts_of)
    }
    query_turns = jnp.stack([(own_turn + deep - order.index(a)) % deep for a in range(deep)])
    own_place = (own_kv + jnp.where(first, 0, KV_HEADS // 2)) % KV_HEADS * HEAD_DIM
    done = {}

    def send(move, value):
        moved = done.setdefault(move, [])
        moved.append(move(after(value, moved[-2]) if len(moved) > 1 else value))
        return moved[-1]

    got = in_chip(prompt_states)
    both_z, both_x, theirs, theirs_x = {0: both_mine}, {0: both_other}, {}, {}
    value_y = send(along_y, after(value_weight, both_mine))
    both_z[1] = send(along_ring, both_mine)
    theirs_x[0] = jnp.where(first, value_y[:, half:], value_y[:, :half])
    value_y = jnp.where(first, value_y[:, :half], value_y[:, half:])
    key_full = {0: jnp.concatenate([both_mine[:width], both_other[:width], packed_queries])}
    key_y = {0: send(along_y, after(key_full[0], value_y))}
    theirs[0] = jnp.concatenate([value_y, packed_queries, key_y[0][2 * width :]])
    for k in range(1, deep):
        if k + 1 < deep:
            both_z[k + 1] = send(along_ring, both_z[k])
        both_x[k] = send(along_x, both_z[k])
        key_full[k] = jnp.concatenate([both_z[k][:width], both_x[k][:width]])
        early_work = (taken_blocks, kv_places, query_turns) if k == 2 else ()
        key_y[k] = send(along_y, after(key_full[k], (key_y[k - 1], early_work)))
    for k in range(1, deep):
        theirs[k] = send(along_ring, theirs[k - 1])
        theirs_x[k] = send(along_x, theirs[k][:width])

    ring_queries = collect([theirs[k] for k in range(deep)], width, 2 * packed)
    ring_queries = [ring_queries, in_chip(ring_queries)]

    key_pieces = [
        [((key_y if flip else key_full)[k], start) for start in (0, width)] for k, flip in places
    ]
    value_pieces = [
        [(theirs[k], 0), (theirs_x[k], 0)] if flip else [(both_z[k], width), (both_x[k], width)]
        for k, flip in places
    ]

    def project_blocks(pieces, which, acc, ready, kind):
        taken = after(taken_blocks[tuple(which)], ready)
        return project(
            prompt_states, got, wide_states, taken, width, [pieces[i] for i in which], acc, kind
        )

    value_early = project_blocks(
        value_pieces, parts_of[0], None, (theirs_x[1], theirs[deep - 1]), jnp.bfloat16
    )
    awaited = (value_early, [theirs_x[k] for k in range(1, deep)])
    key_sum = project_blocks(key_pieces, range(2 * deep), None, awaited, jnp.bfloat16)
    key_back = in_chip(key_sum)

    def own_head(sums):
        sums = lax.dynamic_slice_in_dim(sums, own_place, HEAD_DIM, 1)
        return sums.reshape(2, samples, HEAD_DIM).astype(jnp.float32)

    new_keys = own_head(key_sum[chip_rows:]) + own_head(key_back[chip_rows:])
    new_keys = turn(new_keys, step_tables).astype(jnp.bfloat16).astype(jnp.float32)
    new_keys = new_keys.reshape(steps, HEAD_DIM)
    masks = []
    if prompts > 1:
        token_prompt = jnp.repeat(slots // PROMPT_PAGES, PAGE)
        row_prompt = jnp.tile(sample_order // group_size, devices // KV_HEADS * rows // samples)
        masks = [token_prompt[:, None], row_prompt[None, :]]
    kept, sent, step_values = attend(
        kv_places, query_turns, ring_queries, key_sum, key_back, *scaled_tables, masks,
        prompt_states, got, wide_states, taken_blocks[parts_of[1]], width,
        [value_pieces[i] for i in parts_of[1]], [value_early],
    )
    new_values = own_head(step_values) + own_head(in_chip(step_values))
    new_values = new_values.astype(jnp.bfloat16).astype(jnp.float32).reshape(steps, HEAD_DIM)

    by_owner = (deep, 2, *kept.shape[2:])
    near, far = merge_cores(kept.reshape(by_owner), in_chip(sent.reshape(by_owner)))
    merged = merge_chips(own_a[None], near, along_y(far))
    parts = [merged[0]] + [along_z(merged[k], k) for k in range(1, deep)]

    out_width = out_weight.shape[1] // devices
    out_blocks = jnp.stack(
        [
            block(own_a ^ k, flip, own_c ^ turned)
            for turned in (0, 1)
            for flip in (0, 1)
            for k in range(deep)
        ]
    )
    terms = out_project(out_blocks, parts, queries, new_keys, new_values, out_weight, out_width)

    def narrow(value):
        return value.astype(jnp.bfloat16)

    def wide(value):
        return value.astype(jnp.float32)

    for move in (in_chip, along_y):
        share = terms.shape[1] // 2
        terms = narrow(wide(terms[:, :share]) + wide(move(terms[:, share:])))
    attn_out = wide(terms[:, :out_width])
    for k in range(1, deep):
        attn_out = attn_out + wide(along_z(terms[:, k * out_width : (k + 1) * out_width], k))
    return narrow(attn_out).reshape(2, samples, -1)


def solution(mesh):
    in_specs = (
        P(("groups", "sample"), None),
        P("groups"),
        P(None, "groups", None),
        P("groups"),
        P("sample", None),
        P("sample", None),
        P(None, "sample"),
        P("sample", None),
    )
    out_specs = P(None, "groups", "sample")
    return jax.shard_map(
        on_device, mesh=mesh, in_specs=in_specs, out_specs=out_specs, check_vma=False
    )
```

```python
import jax
import jax.numpy as jnp
from jax import lax
from jax.experimental import pallas as pl
from jax.experimental.pallas import tpu as pltpu
from jax.sharding import PartitionSpec as P

D = 8192
HEAD_DIM = 128
KV_HEADS = 4
GQA = 8
PAGE = 128
PROMPT_PAGES = 64
LINE = 4

rope_base = 1000000.0


def rope_tables(position):
    half_dim = HEAD_DIM // 2
    frequency = rope_base ** (-jnp.arange(half_dim, dtype=jnp.float32) * 2.0 / HEAD_DIM)
    angles = position.astype(jnp.float32)[..., None] * frequency
    return jnp.cos(angles), jnp.sin(angles)


def turn(vector, tables):
    cosine, sine_part = tables
    half_dim = HEAD_DIM // 2
    first_half = vector[..., :half_dim]
    second_half = vector[..., half_dim:]
    return jnp.concatenate(
        [
            first_half * cosine - second_half * sine_part,
            second_half * cosine + first_half * sine_part,
        ],
        axis=-1,
    )


def ring_order(deep):
    return [*range(0, deep, 2), *range(deep - 1 - deep % 2, 0, -2)]


def mover(groups, devices):
    deep = devices // LINE
    order = ring_order(deep)

    def move(value, step):
        pairs = []
        for g in range(groups):
            for s in range(devices):
                a, b, c = s // LINE, s // 2 % 2, s % 2
                to_g, to_a, to_b, to_c = step(g, a, b, c)
                to_s = (to_a % deep) * LINE + to_b * 2 + to_c
                pairs.append((g * devices + s, to_g * devices + to_s))
        return lax.ppermute(value, ("groups", "sample"), pairs)

    def next_on_ring(a):
        return order[(order.index(a) + 1) % deep]

    along_ring = lambda v: move(v, lambda g, a, b, c: (g, next_on_ring(a), b, c))
    along_z = lambda v, k: move(v, lambda g, a, b, c: (g, a ^ k, b, c))
    along_y = lambda v: move(v, lambda g, a, b, c: (g, a, 1 - b, c))
    along_x = lambda v: move(v, lambda g, a, b, c: (g ^ 1, a, b, c))
    in_chip = lambda v: move(v, lambda g, a, b, c: (g, a, b, 1 - c))
    return along_ring, along_z, along_y, along_x, in_chip


def after(value, done):
    return lax.optimization_barrier((value, done))[0]


MIB = 1024 * 1024
LIGHT = pl.CostEstimate(flops=1, bytes_accessed=1, transcendentals=0)


def project_queries(steps, weight, cosine, sine):
    count, depth = steps.shape
    parts = 8
    piece = depth // parts

    def body(step_ref, weight_ref, cosine_ref, sine_ref, out_ref, held, sems):
        copies = []
        for i in range(parts):
            copies.append(
                pltpu.make_async_copy(
                    weight_ref.at[pl.ds(i * piece, piece), :], held.at[i], sems.at[i]
                )
            )
            copies[-1].start()
        total = None
        for i in range(parts):
            copies[i].wait()
            product = jnp.dot(
                step_ref[:, i * piece : (i + 1) * piece],
                held[i],
                preferred_element_type=jnp.float32,
            )
            total = product if total is None else total + product
        tables = [
            jnp.concatenate(
                [jnp.broadcast_to(ref[i : i + 1, :], (count // 2, HEAD_DIM)) for i in (0, 1)],
                axis=0,
            )
            for ref in (cosine_ref, sine_ref)
        ]
        for start in range(0, weight.shape[1], HEAD_DIM):
            head = total[:, start : start + HEAD_DIM]
            turned = head * tables[0] + pltpu.roll(head, HEAD_DIM // 2, 1) * tables[1]
            out_ref[:, start : start + HEAD_DIM] = turned.astype(jnp.bfloat16)

    whole = pl.BlockSpec(memory_space=pltpu.VMEM)
    return pl.pallas_call(
        body,
        in_specs=[whole, pl.BlockSpec(memory_space=pltpu.HBM), whole, whole],
        out_specs=whole,
        out_shape=jax.ShapeDtypeStruct((count, weight.shape[1]), jnp.bfloat16),
        scratch_shapes=[
            pltpu.VMEM((parts, piece, weight.shape[1]), weight.dtype),
            pltpu.SemaphoreType.DMA((parts,)),
        ],
        compiler_params=pltpu.CompilerParams(vmem_limit_bytes=61 * MIB),
        cost_estimate=LIGHT,
    )(steps, weight, cosine, sine)


def collect(arrays, first, height):
    columns = arrays[0].shape[1]

    def body(*refs):
        out_ref, sems = refs[-2:]
        copies = [
            pltpu.make_async_copy(ref.at[pl.ds(first, height), :], out_ref.at[i], sems.at[i])
            for i, ref in enumerate(refs[:-2])
        ]
        for copy in copies:
            copy.start()
        for copy in copies:
            copy.wait()

    return pl.pallas_call(
        body,
        in_specs=[pl.BlockSpec(memory_space=pl.ANY)] * len(arrays),
        out_specs=pl.BlockSpec(memory_space=pltpu.VMEM),
        out_shape=jax.ShapeDtypeStruct((len(arrays), height, columns), arrays[0].dtype),
        scratch_shapes=[pltpu.SemaphoreType.DMA((len(arrays),))],
        compiler_params=pltpu.CompilerParams(vmem_limit_bytes=4 * MIB),
        cost_estimate=LIGHT,
    )(*arrays)


class Blocks:
    def __init__(self, prompt, steps, width, pieces):
        self.arrays = []
        for piece in pieces:
            for array, _ in piece:
                if not any(array is held for held in self.arrays):
                    self.arrays.append(array)
        self.pieces, self.width, self.count = pieces, width, len(pieces)
        self.row_count, self.step_count = prompt.shape[0], steps.shape[0]
        self.height = 2 * self.row_count + self.step_count
        self.columns = sum(array.shape[1] for array, _ in pieces[0])
        self.scratch = [
            pltpu.VMEM((self.count, self.height, width), prompt.dtype),
            pltpu.VMEM((self.count, width, self.columns), prompt.dtype),
            pltpu.SemaphoreType.DMA((self.count, 5)),
        ]

    def copies(self, i, block_ref, sources, weight_refs, scratch):
        left, weights, sems = scratch
        column = pl.ds(pl.multiple_of(block_ref[i] * self.width, self.width), self.width)
        group = []
        start = 0
        for j, (source, rows) in enumerate(
            zip(sources, (self.row_count, self.row_count, self.step_count))
        ):
            group.append(
                pltpu.make_async_copy(
                    source.at[:, column], left.at[i, pl.ds(start, rows), :], sems.at[i, j]
                )
            )
            start += rows
        side = 0
        for j, (array, first) in enumerate(self.pieces[i]):
            ref = weight_refs[[array is other for other in self.arrays].index(True)]
            group.append(
                pltpu.make_async_copy(
                    ref.at[pl.ds(first, self.width), :],
                    weights.at[i, :, pl.ds(side, array.shape[1])],
                    sems.at[i, 3 + j],
                )
            )
            side += array.shape[1]
        return group


AHEAD = 2


def project(prompt, got, steps, blocks, width, pieces, acc, kind):
    held = Blocks(prompt, steps, width, pieces)
    extra = [] if acc is None else [acc]

    def body(block_ref, prompt_ref, got_ref, step_ref, *refs):
        weight_refs = refs[: len(held.arrays)]
        out_ref, acc_held, acc_sem, *scratch = refs[len(held.arrays) + len(extra) :]
        left, weights, _ = scratch
        sources = (prompt_ref, got_ref, step_ref)
        groups = [
            held.copies(i, block_ref, sources, weight_refs, scratch) for i in range(held.count)
        ]
        for group in groups[:AHEAD]:
            for copy in group:
                copy.start()
        if extra:
            before = pltpu.make_async_copy(refs[len(held.arrays)], acc_held, acc_sem.at[0])
            before.start()
        total = None
        for i, group in enumerate(groups):
            for copy in group:
                copy.wait()
            if i + AHEAD < held.count:
                for copy in groups[i + AHEAD]:
                    copy.start()
            product = jnp.dot(left[i], weights[i], preferred_element_type=jnp.float32)
            total = product if total is None else total + product
        if extra:
            before.wait()
            total = total + acc_held[...]
        out_ref[...] = total.astype(kind)

    anywhere = pl.BlockSpec(memory_space=pl.ANY)
    return pl.pallas_call(
        body,
        in_specs=[pl.BlockSpec(memory_space=pltpu.SMEM)] + [anywhere] * (3 + len(held.arrays) + len(extra)),
        out_specs=pl.BlockSpec(memory_space=pltpu.VMEM),
        out_shape=jax.ShapeDtypeStruct((held.height, held.columns), kind),
        scratch_shapes=[
            pltpu.VMEM((held.height, held.columns) if extra else (8, HEAD_DIM), jnp.float32),
            pltpu.SemaphoreType.DMA((1,)),
            *held.scratch,
        ],
        compiler_params=pltpu.CompilerParams(vmem_limit_bytes=57 * MIB),
        cost_estimate=LIGHT,
    )(blocks, prompt, got, steps, *held.arrays, *extra)


NOTES = 16


def thirds(value):
    parts = []
    for _ in range(3):
        parts.append(value.astype(jnp.bfloat16))
        value = value - parts[-1].astype(jnp.float32)
    return parts


def note_rows(top, total):
    parts = [part.astype(jnp.float32) for part in thirds(top) + thirds(total)]
    rows = jnp.concatenate(parts + [jnp.zeros((NOTES - 6, top.shape[1]), jnp.float32)], axis=0)
    return rows.astype(jnp.bfloat16)


def read_notes(rows):
    rows = rows.astype(jnp.float32)
    return rows[0:1] + rows[1:2] + rows[2:3], rows[3:4] + rows[4:5] + rows[5:6]


def small_call(body, out_shapes, scalars, arrays):
    whole = pl.BlockSpec(memory_space=pltpu.VMEM)
    return pl.pallas_call(
        body,
        in_specs=[pl.BlockSpec(memory_space=pltpu.SMEM)] * len(scalars) + [whole] * len(arrays),
        out_specs=[whole] * len(out_shapes),
        out_shape=[jax.ShapeDtypeStruct(shape, jnp.bfloat16) for shape in out_shapes],
        compiler_params=pltpu.CompilerParams(vmem_limit_bytes=12 * MIB),
        cost_estimate=LIGHT,
    )(*scalars, *arrays)


def merge_cores(own, other):
    deep, _, height, lanes = own.shape

    def body(own_ref, other_ref, near_ref, far_ref):
        for z in range(deep):
            for y, out_ref in enumerate((near_ref, far_ref)):
                both = own_ref[z, y, :HEAD_DIM, :].astype(jnp.float32) + other_ref[
                    z, y, :HEAD_DIM, :
                ].astype(jnp.float32)
                out_ref[z, :HEAD_DIM, :] = both.astype(jnp.bfloat16)
                out_ref[z, HEAD_DIM:, :] = own_ref[z, y, HEAD_DIM:, :]

    return small_call(body, [(deep, height, lanes)] * 2, [], [own, other])


def merge_chips(own_place, near, far):
    deep, height, lanes = near.shape

    def body(place_ref, near_ref, far_ref, *out_refs):
        for k, out_ref in enumerate(out_refs):
            z = place_ref[0] ^ k
            first, second = near_ref[z], far_ref[z]
            first_top, first_total = read_notes(first[HEAD_DIM:, :])
            second_top, second_total = read_notes(second[HEAD_DIM:, :])
            top = jnp.maximum(first_top, second_top)
            first_factor, second_factor = jnp.exp(first_top - top), jnp.exp(second_top - top)
            out_ref[:HEAD_DIM, :] = (
                first[:HEAD_DIM, :].astype(jnp.float32) * first_factor
                + second[:HEAD_DIM, :].astype(jnp.float32) * second_factor
            ).astype(jnp.bfloat16)
            out_ref[HEAD_DIM:, :] = note_rows(
                top, first_total * first_factor + second_total * second_factor
            )

    return small_call(body, [(height, lanes)] * deep, [own_place], [near, far])


def attend(
    places, turns, queries, own, other, cosine, sine, masks, prompt, got, steps, blocks, width,
    pieces, early,
):
    kv_heads = places.shape[0]
    deep, packed, lanes = queries[0].shape
    share = deep // kv_heads
    count = 2 * share * packed * lanes // HEAD_DIM
    owners = count // HEAD_DIM
    tokens = cosine.shape[0]
    half = tokens // 2
    held = Blocks(prompt, steps, width, pieces)
    inputs = [*queries, own, other, cosine, sine, *masks]

    def body(place_ref, turn_ref, block_ref, *refs):
        query_refs = refs[:2]
        own_ref, other_ref, cosine_ref, sine_ref = refs[2:6]
        mask_refs = refs[6 : len(inputs)]
        prompt_ref, got_ref, step_ref = refs[len(inputs) : len(inputs) + 3]
        early_refs = refs[len(inputs) + 3 : len(inputs) + 3 + len(early)]
        rest = refs[len(inputs) + 3 + len(early) :]
        weight_refs, rest = rest[: len(held.arrays)], rest[len(held.arrays) :]
        *out_refs, step_out_ref = rest[:3]
        early_held, weight_held, value_held, early_sem, *scratch = rest[3:]
        left, weight_rows, _ = scratch
        sources = (prompt_ref, got_ref, step_ref)
        groups = [
            held.copies(i, block_ref, sources, weight_refs, scratch) for i in range(held.count)
        ]
        before = [
            pltpu.make_async_copy(ref, early_held.at[i], early_sem.at[i])
            for i, ref in enumerate(early_refs)
        ]
        for copy in before:
            copy.start()
        for group in groups:
            for copy in group:
                copy.start()
        wide_cosine = jnp.concatenate([cosine_ref[...], cosine_ref[...]], axis=1)
        wide_sine = jnp.concatenate([-sine_ref[...], sine_ref[...]], axis=1)

        def one_head(j, _):
            column = pl.ds(pl.multiple_of(place_ref[j] * HEAD_DIM, HEAD_DIM), HEAD_DIM)
            keys = jnp.concatenate(
                [
                    own_ref[:half, column].astype(jnp.float32)
                    + other_ref[half:tokens, column].astype(jnp.float32),
                    own_ref[half:tokens, column].astype(jnp.float32)
                    + other_ref[:half, column].astype(jnp.float32),
                ],
                axis=0,
            )
            swapped = pltpu.roll(keys, HEAD_DIM // 2, 1)
            keys = (keys * wide_cosine + swapped * wide_sine).astype(jnp.bfloat16)
            unpacked = []
            for part in range(share):
                for ref in query_refs:
                    both = ref[turn_ref[j * share + part]]
                    for low in range(0, packed, packed // 2):
                        for left_lane in range(0, lanes, HEAD_DIM):
                            unpacked.append(
                                both[low : low + packed // 2, left_lane : left_lane + HEAD_DIM]
                            )
            scores = lax.dot_general(
                keys,
                jnp.concatenate(unpacked, axis=0),
                (((1,), (1,)), ((), ())),
                preferred_element_type=jnp.float32,
            )
            if masks:
                scores = jnp.where(mask_refs[0][...] == mask_refs[1][...], scores, -1e30)
            top = jnp.max(scores, axis=0, keepdims=True)
            weights = jnp.exp(scores - top)
            total = jnp.sum(weights, axis=0, keepdims=True)
            for i in range(owners):
                lane = slice(i * HEAD_DIM, (i + 1) * HEAD_DIM)
                out_ref = out_refs[i // 2 % 2]
                out_ref[j, i // 4 * 2 + i % 2, HEAD_DIM:, :] = note_rows(
                    top[:, lane], total[:, lane]
                )
            weight_held[j] = weights.astype(jnp.bfloat16)
            return 0

        lax.fori_loop(0, kv_heads, one_head, 0)
        for copy in before:
            copy.wait()
        total = sum(early_held[i].astype(jnp.float32) for i in range(len(early)))
        for i, group in enumerate(groups):
            for copy in group:
                copy.wait()
            total += jnp.dot(left[i], weight_rows[i], preferred_element_type=jnp.float32)
        value_held[...] = total[:tokens].astype(jnp.bfloat16)
        step_out_ref[...] = total[tokens:]

        def one_sum(j, _):
            column = pl.ds(pl.multiple_of(place_ref[j] * HEAD_DIM, HEAD_DIM), HEAD_DIM)
            summed = lax.dot_general(
                value_held[:, column],
                weight_held[j],
                (((0,), (0,)), ((), ())),
                preferred_element_type=jnp.float32,
            )
            for i in range(owners):
                lane = slice(i * HEAD_DIM, (i + 1) * HEAD_DIM)
                out_ref = out_refs[i // 2 % 2]
                out_ref[j, i // 4 * 2 + i % 2, :HEAD_DIM, :] = summed[:, lane].astype(jnp.bfloat16)
            return 0

        lax.fori_loop(0, kv_heads, one_sum, 0)

    anywhere = pl.BlockSpec(memory_space=pl.ANY)
    whole = pl.BlockSpec(memory_space=pltpu.VMEM)
    return pl.pallas_call(
        body,
        in_specs=[pl.BlockSpec(memory_space=pltpu.SMEM)] * 3
        + [whole] * len(inputs)
        + [anywhere] * (3 + len(early) + len(held.arrays)),
        out_specs=[whole] * 3,
        out_shape=[
            *[
                jax.ShapeDtypeStruct(
                    (kv_heads, owners // 2, HEAD_DIM + NOTES, HEAD_DIM), jnp.bfloat16
                )
            ]
            * 2,
            jax.ShapeDtypeStruct((held.step_count, held.columns), jnp.float32),
        ],
        scratch_shapes=[
            pltpu.VMEM((len(early), held.height, held.columns), jnp.bfloat16),
            pltpu.VMEM((kv_heads, tokens, count), jnp.bfloat16),
            pltpu.VMEM((tokens, held.columns), jnp.bfloat16),
            pltpu.SemaphoreType.DMA((len(early),)),
            *held.scratch,
        ],
        compiler_params=pltpu.CompilerParams(vmem_limit_bytes=57 * MIB),
        cost_estimate=LIGHT,
    )(places, turns, blocks, *inputs, prompt, got, steps, *early, *held.arrays)


def out_project(blocks, parts, queries, new_keys, new_values, weight, width):
    count = len(parts)
    steps = queries.shape[0]
    samples = steps // 2

    def body(block_ref, *refs):
        part_refs = refs[:count]
        query_ref, key_ref, value_ref, weight_ref, out_ref = refs[count:]
        notes = [read_notes(ref[HEAD_DIM:, :]) for ref in part_refs]
        top = notes[0][0]
        for other, _ in notes[1:]:
            top = jnp.maximum(top, other)
        sums = total = 0.0
        for ref, (part_top, part_total) in zip(part_refs, notes):
            factor = jnp.exp(part_top - top)
            sums = sums + ref[:HEAD_DIM, :].astype(jnp.float32) * factor
            total = total + part_total * factor
        sums = sums.T
        both = jnp.concatenate([top, total, jnp.zeros((6, HEAD_DIM), jnp.float32)], axis=0).T
        keys, values = key_ref[...], value_ref[...]
        heads = []
        for h in range(queries.shape[1] // HEAD_DIM):
            query = query_ref[:, h * HEAD_DIM : (h + 1) * HEAD_DIM].astype(jnp.float32)
            own_score = jnp.sum(query * keys, axis=1, keepdims=True) * (HEAD_DIM**-0.5)
            back_score = jnp.sum(
                query[samples:] * keys[:samples], axis=1, keepdims=True
            ) * (HEAD_DIM**-0.5)
            ends = []
            for step in (0, 1):
                place = slice((2 * h + step) * samples, (2 * h + step + 1) * samples)
                here = slice(step * samples, (step + 1) * samples)
                old_top, old_total = both[place, 0:1], both[place, 1:2]
                scores = [(own_score[here], values[here])]
                if step:
                    scores.append((back_score, values[:samples]))
                high = old_top
                for score, _ in scores:
                    high = jnp.maximum(high, score)
                old = jnp.exp(old_top - high)
                numerator, denominator = old * sums[place], old * old_total
                for score, value in scores:
                    new = jnp.exp(score - high)
                    numerator, denominator = numerator + new * value, denominator + new
                ends.append(numerator / denominator)
            heads.append(jnp.concatenate(ends, axis=0).astype(jnp.bfloat16))
        heads = jnp.concatenate(heads, axis=1)
        for i in range(blocks.shape[0]):
            start = pl.multiple_of(block_ref[i] * width, width)
            out_ref[:, i * width : (i + 1) * width] = jnp.dot(
                heads, weight_ref[:, pl.ds(start, width)], preferred_element_type=jnp.float32
            ).astype(jnp.bfloat16)

    return small_call(
        body, [(steps, weight.shape[1])], [blocks], [*parts, queries, new_keys, new_values, weight]
    )[0]


def on_device(
    prompt_states,
    page_table,
    step_states,
    sample_order,
    key_weight,
    value_weight,
    query_weight,
    out_weight,
):
    devices = lax.axis_size("sample")
    groups = lax.axis_size("groups")
    own_index = lax.axis_index("sample")
    first = lax.axis_index("groups") % 2 == 0
    deep = devices // LINE
    own_a, own_b, own_c = own_index // LINE, own_index // 2 % 2, own_index % 2
    along_ring, along_z, along_y, along_x, in_chip = mover(groups, devices)
    row_count = prompt_states.shape[0]
    chip_rows = 2 * row_count
    pages_here = row_count // PAGE
    heads_here = query_weight.shape[1] // HEAD_DIM
    total_pages = page_table.shape[0]
    prompts = total_pages // PROMPT_PAGES
    samples = sample_order.shape[0]
    steps = 2 * samples
    group_size = samples // prompts
    own_kv = own_index * heads_here // GQA
    wide_states = step_states.reshape(steps, D)
    rows = heads_here * steps
    width = key_weight.shape[0]
    half = key_weight.shape[1] // 2
    kv_places = jnp.where(first, 0, KV_HEADS // 2) + jnp.arange(KV_HEADS, dtype=jnp.int32)
    kv_places = kv_places % KV_HEADS

    order = ring_order(deep)

    def by_place(table):
        return sum(jnp.where(own_a == a, table[a], 0) for a in range(deep))

    own_turn = by_place([order.index(a) for a in range(deep)])

    def block(place_z, flip, core):
        return place_z * LINE + (own_b ^ flip) * 2 + core

    def behind(k):
        return by_place([order[(order.index(a) - k) % deep] for a in range(deep)])

    low = jnp.concatenate([key_weight[:, :half], value_weight[:, :half]])
    high = jnp.concatenate([key_weight[:, half:], value_weight[:, half:]])
    both_mine, both_other = jnp.where(first, low, high), jnp.where(first, high, low)

    own_pages = jnp.concatenate(
        [
            holder * pages_here + jnp.arange(pages_here, dtype=jnp.int32)
            for holder in (own_index, own_index ^ 1)
        ]
    )
    slots = jnp.sum(
        jnp.where(
            page_table[None, :] == own_pages[:, None],
            jnp.arange(total_pages, dtype=jnp.int32)[None, :],
            0,
        ),
        axis=1,
    )
    positions = (slots % PROMPT_PAGES * PAGE)[:, None] + jnp.arange(PAGE, dtype=jnp.int32)[None, :]
    scaled_tables = tuple(
        table * HEAD_DIM ** (-0.5) for table in rope_tables(positions.reshape(chip_rows))
    )

    step_place = PROMPT_PAGES * PAGE + jnp.arange(2, dtype=jnp.int32)
    step_tables = tuple(t[:, None, :] for t in rope_tables(step_place))
    flat_tables = [
        jnp.concatenate([sign * table, table], axis=-1)[:, 0]
        for sign, table in zip((1, -1), step_tables)
    ]
    queries = project_queries(
        after(wide_states, scaled_tables), query_weight, *flat_tables
    )
    packed_queries = jnp.concatenate(
        jnp.split(queries, half // queries.shape[1], axis=0), axis=1
    )
    packed = packed_queries.shape[0]

    places = [(k, flip) for k in range(deep) for flip in (0, 1)]
    parts_of = [
        (*range(0, 2 * deep, 2), 1),
        tuple(range(3, 2 * deep, 2)),
    ]
    taken_blocks = {
        which: jnp.stack([block(behind(places[i][0]), places[i][1], own_c) for i in which])
        for which in (tuple(range(2 * deep)), *parts_of)
    }
    query_turns = jnp.stack([(own_turn + deep - order.index(a)) % deep for a in range(deep)])
    own_place = (own_kv + jnp.where(first, 0, KV_HEADS // 2)) % KV_HEADS * HEAD_DIM
    done = {}

    def send(move, value):
        moved = done.setdefault(move, [])
        moved.append(move(after(value, moved[-2]) if len(moved) > 1 else value))
        return moved[-1]

    got = in_chip(prompt_states)
    both_z, both_x, theirs, theirs_x = {0: both_mine}, {0: both_other}, {}, {}
    value_y = send(along_y, after(value_weight, both_mine))
    both_z[1] = send(along_ring, both_mine)
    theirs_x[0] = jnp.where(first, value_y[:, half:], value_y[:, :half])
    value_y = jnp.where(first, value_y[:, :half], value_y[:, half:])
    key_full = {0: jnp.concatenate([both_mine[:width], both_other[:width], packed_queries])}
    key_y = {0: send(along_y, after(key_full[0], value_y))}
    theirs[0] = jnp.concatenate([value_y, packed_queries, key_y[0][2 * width :]])
    for k in range(1, deep):
        if k + 1 < deep:
            both_z[k + 1] = send(along_ring, both_z[k])
        both_x[k] = send(along_x, both_z[k])
        key_full[k] = jnp.concatenate([both_z[k][:width], both_x[k][:width]])
        early_work = (taken_blocks, kv_places, query_turns) if k == 2 else ()
        key_y[k] = send(along_y, after(key_full[k], (key_y[k - 1], early_work)))
    for k in range(1, deep):
        theirs[k] = send(along_ring, theirs[k - 1])
        theirs_x[k] = send(along_x, theirs[k][:width])

    ring_queries = collect([theirs[k] for k in range(deep)], width, 2 * packed)
    ring_queries = [ring_queries, in_chip(ring_queries)]

    key_pieces = [
        [((key_y if flip else key_full)[k], start) for start in (0, width)] for k, flip in places
    ]
    value_pieces = [
        [(theirs[k], 0), (theirs_x[k], 0)] if flip else [(both_z[k], width), (both_x[k], width)]
        for k, flip in places
    ]

    def project_blocks(pieces, which, acc, ready, kind):
        taken = after(taken_blocks[tuple(which)], ready)
        return project(
            prompt_states, got, wide_states, taken, width, [pieces[i] for i in which], acc, kind
        )

    value_early = project_blocks(
        value_pieces, parts_of[0], None, (theirs_x[1], theirs[deep - 1]), jnp.bfloat16
    )
    awaited = (value_early, [theirs_x[k] for k in range(1, deep)])
    key_sum = project_blocks(key_pieces, range(2 * deep), None, awaited, jnp.bfloat16)
    key_back = in_chip(key_sum)

    def own_head(sums):
        sums = lax.dynamic_slice_in_dim(sums, own_place, HEAD_DIM, 1)
        return sums.reshape(2, samples, HEAD_DIM).astype(jnp.float32)

    new_keys = own_head(key_sum[chip_rows:]) + own_head(key_back[chip_rows:])
    new_keys = turn(new_keys, step_tables).astype(jnp.bfloat16).astype(jnp.float32)
    new_keys = new_keys.reshape(steps, HEAD_DIM)
    masks = []
    if prompts > 1:
        token_prompt = jnp.repeat(slots // PROMPT_PAGES, PAGE)
        row_prompt = jnp.tile(sample_order // group_size, devices // KV_HEADS * rows // samples)
        masks = [token_prompt[:, None], row_prompt[None, :]]
    kept, sent, step_values = attend(
        kv_places, query_turns, ring_queries, key_sum, key_back, *scaled_tables, masks,
        prompt_states, got, wide_states, taken_blocks[parts_of[1]], width,
        [value_pieces[i] for i in parts_of[1]], [value_early],
    )
    new_values = own_head(step_values) + own_head(in_chip(step_values))
    new_values = new_values.astype(jnp.bfloat16).astype(jnp.float32).reshape(steps, HEAD_DIM)

    by_owner = (deep, 2, *kept.shape[2:])
    near, far = merge_cores(kept.reshape(by_owner), in_chip(sent.reshape(by_owner)))
    merged = merge_chips(own_a[None], near, along_y(far))
    parts = [merged[0]] + [along_z(merged[k], k) for k in range(1, deep)]

    out_width = out_weight.shape[1] // devices
    out_blocks = jnp.stack(
        [
            block(own_a ^ k, flip, own_c ^ turned)
            for turned in (0, 1)
            for flip in (0, 1)
            for k in range(deep)
        ]
    )
    terms = out_project(out_blocks, parts, queries, new_keys, new_values, out_weight, out_width)

    def narrow(value):
        return value.astype(jnp.bfloat16)

    def wide(value):
        return value.astype(jnp.float32)

    for move in (in_chip, along_y):
        share = terms.shape[1] // 2
        terms = narrow(wide(terms[:, :share]) + wide(move(terms[:, share:])))
    attn_out = wide(terms[:, :out_width])
    for k in range(1, deep):
        attn_out = attn_out + wide(along_z(terms[:, k * out_width : (k + 1) * out_width], k))
    return narrow(attn_out).reshape(2, samples, -1)


def solution(mesh):
    in_specs = (
        P(("groups", "sample"), None),
        P("groups"),
        P(None, "groups", None),
        P("groups"),
        P("sample", None),
        P("sample", None),
        P(None, "sample"),
        P("sample", None),
    )
    out_specs = P(None, "groups", "sample")
    return jax.shard_map(
        on_device, mesh=mesh, in_specs=in_specs, out_specs=out_specs, check_vma=False
    )
```

```python
import jax
import jax.numpy as jnp
from jax import lax
from jax.experimental import pallas as pl
from jax.experimental.pallas import tpu as pltpu
from jax.sharding import PartitionSpec as P

D = 8192
HEAD_DIM = 128
KV_HEADS = 4
GQA = 8
PAGE = 128
PROMPT_PAGES = 64
LINE = 4

rope_base = 1000000.0


def rope_tables(position):
    half_dim = HEAD_DIM // 2
    frequency = rope_base ** (-jnp.arange(half_dim, dtype=jnp.float32) * 2.0 / HEAD_DIM)
    angles = position.astype(jnp.float32)[..., None] * frequency
    return jnp.cos(angles), jnp.sin(angles)


def turn(vector, tables):
    cosine, sine_part = tables
    half_dim = HEAD_DIM // 2
    first_half = vector[..., :half_dim]
    second_half = vector[..., half_dim:]
    return jnp.concatenate(
        [
            first_half * cosine - second_half * sine_part,
            second_half * cosine + first_half * sine_part,
        ],
        axis=-1,
    )


def ring_order(deep):
    return [*range(0, deep, 2), *range(deep - 1 - deep % 2, 0, -2)]


def mover(groups, devices):
    deep = devices // LINE
    order = ring_order(deep)

    def move(value, step):
        pairs = []
        for g in range(groups):
            for s in range(devices):
                a, b, c = s // LINE, s // 2 % 2, s % 2
                to_g, to_a, to_b, to_c = step(g, a, b, c)
                to_s = (to_a % deep) * LINE + to_b * 2 + to_c
                pairs.append((g * devices + s, to_g * devices + to_s))
        return lax.ppermute(value, ("groups", "sample"), pairs)

    def next_on_ring(a):
        return order[(order.index(a) + 1) % deep]

    along_ring = lambda v: move(v, lambda g, a, b, c: (g, next_on_ring(a), b, c))
    along_z = lambda v, k: move(v, lambda g, a, b, c: (g, a ^ k, b, c))
    along_y = lambda v: move(v, lambda g, a, b, c: (g, a, 1 - b, c))
    along_x = lambda v: move(v, lambda g, a, b, c: (g ^ 1, a, b, c))
    in_chip = lambda v: move(v, lambda g, a, b, c: (g, a, b, 1 - c))
    return along_ring, along_z, along_y, along_x, in_chip


def after(value, done):
    return lax.optimization_barrier((value, done))[0]


MIB = 1024 * 1024
LIGHT = pl.CostEstimate(flops=1, bytes_accessed=1, transcendentals=0)


def project_queries(steps, weight, cosine, sine):
    count, depth = steps.shape
    parts = 8
    piece = depth // parts

    def body(step_ref, weight_ref, cosine_ref, sine_ref, out_ref, held, sems):
        copies = []
        for i in range(parts):
            copies.append(
                pltpu.make_async_copy(
                    weight_ref.at[pl.ds(i * piece, piece), :], held.at[i], sems.at[i]
                )
            )
            copies[-1].start()
        total = None
        for i in range(parts):
            copies[i].wait()
            product = jnp.dot(
                step_ref[:, i * piece : (i + 1) * piece],
                held[i],
                preferred_element_type=jnp.float32,
            )
            total = product if total is None else total + product
        tables = [
            jnp.concatenate(
                [jnp.broadcast_to(ref[i : i + 1, :], (count // 2, HEAD_DIM)) for i in (0, 1)],
                axis=0,
            )
            for ref in (cosine_ref, sine_ref)
        ]
        for start in range(0, weight.shape[1], HEAD_DIM):
            head = total[:, start : start + HEAD_DIM]
            turned = head * tables[0] + pltpu.roll(head, HEAD_DIM // 2, 1) * tables[1]
            out_ref[:, start : start + HEAD_DIM] = turned.astype(jnp.bfloat16)

    whole = pl.BlockSpec(memory_space=pltpu.VMEM)
    return pl.pallas_call(
        body,
        in_specs=[whole, pl.BlockSpec(memory_space=pltpu.HBM), whole, whole],
        out_specs=whole,
        out_shape=jax.ShapeDtypeStruct((count, weight.shape[1]), jnp.bfloat16),
        scratch_shapes=[
            pltpu.VMEM((parts, piece, weight.shape[1]), weight.dtype),
            pltpu.SemaphoreType.DMA((parts,)),
        ],
        compiler_params=pltpu.CompilerParams(vmem_limit_bytes=61 * MIB),
        cost_estimate=LIGHT,
    )(steps, weight, cosine, sine)


def collect(arrays, first, height):
    columns = arrays[0].shape[1]

    def body(*refs):
        out_ref, sems = refs[-2:]
        copies = [
            pltpu.make_async_copy(ref.at[pl.ds(first, height), :], out_ref.at[i], sems.at[i])
            for i, ref in enumerate(refs[:-2])
        ]
        for copy in copies:
            copy.start()
        for copy in copies:
            copy.wait()

    return pl.pallas_call(
        body,
        in_specs=[pl.BlockSpec(memory_space=pl.ANY)] * len(arrays),
        out_specs=pl.BlockSpec(memory_space=pltpu.VMEM),
        out_shape=jax.ShapeDtypeStruct((len(arrays), height, columns), arrays[0].dtype),
        scratch_shapes=[pltpu.SemaphoreType.DMA((len(arrays),))],
        compiler_params=pltpu.CompilerParams(vmem_limit_bytes=4 * MIB),
        cost_estimate=LIGHT,
    )(*arrays)


class Blocks:
    def __init__(self, prompt, steps, width, pieces):
        self.arrays = []
        for piece in pieces:
            for array, _ in piece:
                if not any(array is held for held in self.arrays):
                    self.arrays.append(array)
        self.pieces, self.width, self.count = pieces, width, len(pieces)
        self.row_count, self.step_count = prompt.shape[0], steps.shape[0]
        self.height = 2 * self.row_count + self.step_count
        self.columns = sum(array.shape[1] for array, _ in pieces[0])
        self.scratch = [
            pltpu.VMEM((self.height, self.count * width), prompt.dtype),
            pltpu.VMEM((self.count * width, self.columns), prompt.dtype),
            pltpu.SemaphoreType.DMA((self.count, 5)),
        ]

    def copies(self, i, block_ref, sources, weight_refs, scratch):
        left, weights, sems = scratch
        column = pl.ds(pl.multiple_of(block_ref[i] * self.width, self.width), self.width)
        group = []
        start = 0
        for j, (source, rows) in enumerate(
            zip(sources, (self.row_count, self.row_count, self.step_count))
        ):
            group.append(
                pltpu.make_async_copy(
                    source.at[:, column],
                    left.at[pl.ds(start, rows), pl.ds(i * self.width, self.width)],
                    sems.at[i, j],
                )
            )
            start += rows
        side = 0
        for j, (array, first) in enumerate(self.pieces[i]):
            ref = weight_refs[[array is other for other in self.arrays].index(True)]
            group.append(
                pltpu.make_async_copy(
                    ref.at[pl.ds(first, self.width), :],
                    weights.at[pl.ds(i * self.width, self.width), pl.ds(side, array.shape[1])],
                    sems.at[i, 3 + j],
                )
            )
            side += array.shape[1]
        return group


AHEAD = 4


def project(prompt, got, steps, blocks, width, pieces, acc, kind):
    held = Blocks(prompt, steps, width, pieces)
    extra = [] if acc is None else [acc]

    def body(block_ref, prompt_ref, got_ref, step_ref, *refs):
        weight_refs = refs[: len(held.arrays)]
        out_ref, acc_held, acc_sem, *scratch = refs[len(held.arrays) + len(extra) :]
        left, weights, _ = scratch
        sources = (prompt_ref, got_ref, step_ref)
        groups = [
            held.copies(i, block_ref, sources, weight_refs, scratch) for i in range(held.count)
        ]
        for group in groups[:AHEAD]:
            for copy in group:
                copy.start()
        if extra:
            before = pltpu.make_async_copy(refs[len(held.arrays)], acc_held, acc_sem.at[0])
            before.start()
        total = None
        for i in range(0, held.count, 2):
            for group in groups[i : i + 2]:
                for copy in group:
                    copy.wait()
            for group in groups[i + AHEAD : i + AHEAD + 2]:
                for copy in group:
                    copy.start()
            depth = slice(i * width, min(i + 2, held.count) * width)
            product = jnp.dot(left[:, depth], weights[depth, :], preferred_element_type=jnp.float32)
            total = product if total is None else total + product
        if extra:
            before.wait()
            total = total + acc_held[...]
        out_ref[...] = total.astype(kind)

    anywhere = pl.BlockSpec(memory_space=pl.ANY)
    return pl.pallas_call(
        body,
        in_specs=[pl.BlockSpec(memory_space=pltpu.SMEM)] + [anywhere] * (3 + len(held.arrays) + len(extra)),
        out_specs=pl.BlockSpec(memory_space=pltpu.VMEM),
        out_shape=jax.ShapeDtypeStruct((held.height, held.columns), kind),
        scratch_shapes=[
            pltpu.VMEM((held.height, held.columns) if extra else (8, HEAD_DIM), jnp.float32),
            pltpu.SemaphoreType.DMA((1,)),
            *held.scratch,
        ],
        compiler_params=pltpu.CompilerParams(vmem_limit_bytes=57 * MIB),
        cost_estimate=LIGHT,
    )(blocks, prompt, got, steps, *held.arrays, *extra)


NOTES = 16


def thirds(value):
    parts = []
    for _ in range(3):
        parts.append(value.astype(jnp.bfloat16))
        value = value - parts[-1].astype(jnp.float32)
    return parts


def note_rows(top, total):
    parts = [part.astype(jnp.float32) for part in thirds(top) + thirds(total)]
    rows = jnp.concatenate(parts + [jnp.zeros((NOTES - 6, top.shape[1]), jnp.float32)], axis=0)
    return rows.astype(jnp.bfloat16)


def read_notes(rows):
    rows = rows.astype(jnp.float32)
    return rows[0:1] + rows[1:2] + rows[2:3], rows[3:4] + rows[4:5] + rows[5:6]


def small_call(body, out_shapes, scalars, arrays):
    whole = pl.BlockSpec(memory_space=pltpu.VMEM)
    return pl.pallas_call(
        body,
        in_specs=[pl.BlockSpec(memory_space=pltpu.SMEM)] * len(scalars) + [whole] * len(arrays),
        out_specs=[whole] * len(out_shapes),
        out_shape=[jax.ShapeDtypeStruct(shape, jnp.bfloat16) for shape in out_shapes],
        compiler_params=pltpu.CompilerParams(vmem_limit_bytes=12 * MIB),
        cost_estimate=LIGHT,
    )(*scalars, *arrays)


def merge_cores(own, other):
    deep, _, height, lanes = own.shape

    def body(own_ref, other_ref, near_ref, far_ref):
        for z in range(deep):
            for y, out_ref in enumerate((near_ref, far_ref)):
                both = own_ref[z, y, :HEAD_DIM, :].astype(jnp.float32) + other_ref[
                    z, y, :HEAD_DIM, :
                ].astype(jnp.float32)
                out_ref[z, :HEAD_DIM, :] = both.astype(jnp.bfloat16)
                out_ref[z, HEAD_DIM:, :] = own_ref[z, y, HEAD_DIM:, :]

    return small_call(body, [(deep, height, lanes)] * 2, [], [own, other])


def merge_chips(own_place, near, far):
    deep, height, lanes = near.shape

    def body(place_ref, near_ref, far_ref, *out_refs):
        for k, out_ref in enumerate(out_refs):
            z = place_ref[0] ^ k
            first, second = near_ref[z], far_ref[z]
            first_top, first_total = read_notes(first[HEAD_DIM:, :])
            second_top, second_total = read_notes(second[HEAD_DIM:, :])
            top = jnp.maximum(first_top, second_top)
            first_factor, second_factor = jnp.exp(first_top - top), jnp.exp(second_top - top)
            out_ref[:HEAD_DIM, :] = (
                first[:HEAD_DIM, :].astype(jnp.float32) * first_factor
                + second[:HEAD_DIM, :].astype(jnp.float32) * second_factor
            ).astype(jnp.bfloat16)
            out_ref[HEAD_DIM:, :] = note_rows(
                top, first_total * first_factor + second_total * second_factor
            )

    return small_call(body, [(height, lanes)] * deep, [own_place], [near, far])


def attend(
    places, turns, queries, own, other, cosine, sine, masks, prompt, got, steps, blocks, width,
    pieces, early,
):
    kv_heads = places.shape[0]
    deep, packed, lanes = queries[0].shape
    share = deep // kv_heads
    count = 2 * share * packed * lanes // HEAD_DIM
    owners = count // HEAD_DIM
    tokens = cosine.shape[0]
    half = tokens // 2
    held = Blocks(prompt, steps, width, pieces)
    inputs = [*queries, own, other, cosine, sine, *masks]

    def body(place_ref, turn_ref, block_ref, *refs):
        query_refs = refs[:2]
        own_ref, other_ref, cosine_ref, sine_ref = refs[2:6]
        mask_refs = refs[6 : len(inputs)]
        prompt_ref, got_ref, step_ref = refs[len(inputs) : len(inputs) + 3]
        early_refs = refs[len(inputs) + 3 : len(inputs) + 3 + len(early)]
        rest = refs[len(inputs) + 3 + len(early) :]
        weight_refs, rest = rest[: len(held.arrays)], rest[len(held.arrays) :]
        *out_refs, step_out_ref = rest[:3]
        early_held, weight_held, value_held, early_sem, *scratch = rest[3:]
        left, weight_rows, _ = scratch
        sources = (prompt_ref, got_ref, step_ref)
        groups = [
            held.copies(i, block_ref, sources, weight_refs, scratch) for i in range(held.count)
        ]
        before = [
            pltpu.make_async_copy(ref, early_held.at[i], early_sem.at[i])
            for i, ref in enumerate(early_refs)
        ]
        for copy in before:
            copy.start()
        for group in groups:
            for copy in group:
                copy.start()
        wide_cosine = jnp.concatenate([cosine_ref[...], cosine_ref[...]], axis=1)
        wide_sine = jnp.concatenate([-sine_ref[...], sine_ref[...]], axis=1)

        def one_head(j, _):
            column = pl.ds(pl.multiple_of(place_ref[j] * HEAD_DIM, HEAD_DIM), HEAD_DIM)
            keys = jnp.concatenate(
                [
                    own_ref[:half, column].astype(jnp.float32)
                    + other_ref[half:tokens, column].astype(jnp.float32),
                    own_ref[half:tokens, column].astype(jnp.float32)
                    + other_ref[:half, column].astype(jnp.float32),
                ],
                axis=0,
            )
            swapped = pltpu.roll(keys, HEAD_DIM // 2, 1)
            keys = (keys * wide_cosine + swapped * wide_sine).astype(jnp.bfloat16)
            unpacked = []
            for part in range(share):
                for ref in query_refs:
                    both = ref[turn_ref[j * share + part]]
                    for low in range(0, packed, packed // 2):
                        for left_lane in range(0, lanes, HEAD_DIM):
                            unpacked.append(
                                both[low : low + packed // 2, left_lane : left_lane + HEAD_DIM]
                            )
            scores = lax.dot_general(
                keys,
                jnp.concatenate(unpacked, axis=0),
                (((1,), (1,)), ((), ())),
                preferred_element_type=jnp.float32,
            )
            if masks:
                scores = jnp.where(mask_refs[0][...] == mask_refs[1][...], scores, -1e30)
            top = jnp.max(scores, axis=0, keepdims=True)
            weights = jnp.exp(scores - top)
            total = jnp.sum(weights, axis=0, keepdims=True)
            for i in range(owners):
                lane = slice(i * HEAD_DIM, (i + 1) * HEAD_DIM)
                out_ref = out_refs[i // 2 % 2]
                out_ref[j, i // 4 * 2 + i % 2, HEAD_DIM:, :] = note_rows(
                    top[:, lane], total[:, lane]
                )
            weight_held[j] = weights.astype(jnp.bfloat16)
            return 0

        lax.fori_loop(0, kv_heads, one_head, 0)
        for copy in before:
            copy.wait()
        total = sum(early_held[i].astype(jnp.float32) for i in range(len(early)))
        for i in range(0, held.count, 2):
            for group in groups[i : i + 2]:
                for copy in group:
                    copy.wait()
            depth = slice(i * width, min(i + 2, held.count) * width)
            total += jnp.dot(
                left[:, depth], weight_rows[depth, :], preferred_element_type=jnp.float32
            )
        value_held[...] = total[:tokens].astype(jnp.bfloat16)
        step_out_ref[...] = total[tokens:]

        def one_sum(j, _):
            column = pl.ds(pl.multiple_of(place_ref[j] * HEAD_DIM, HEAD_DIM), HEAD_DIM)
            summed = lax.dot_general(
                value_held[:, column],
                weight_held[j],
                (((0,), (0,)), ((), ())),
                preferred_element_type=jnp.float32,
            )
            for i in range(owners):
                lane = slice(i * HEAD_DIM, (i + 1) * HEAD_DIM)
                out_ref = out_refs[i // 2 % 2]
                out_ref[j, i // 4 * 2 + i % 2, :HEAD_DIM, :] = summed[:, lane].astype(jnp.bfloat16)
            return 0

        lax.fori_loop(0, kv_heads, one_sum, 0)

    anywhere = pl.BlockSpec(memory_space=pl.ANY)
    whole = pl.BlockSpec(memory_space=pltpu.VMEM)
    return pl.pallas_call(
        body,
        in_specs=[pl.BlockSpec(memory_space=pltpu.SMEM)] * 3
        + [whole] * len(inputs)
        + [anywhere] * (3 + len(early) + len(held.arrays)),
        out_specs=[whole] * 3,
        out_shape=[
            *[
                jax.ShapeDtypeStruct(
                    (kv_heads, owners // 2, HEAD_DIM + NOTES, HEAD_DIM), jnp.bfloat16
                )
            ]
            * 2,
            jax.ShapeDtypeStruct((held.step_count, held.columns), jnp.float32),
        ],
        scratch_shapes=[
            pltpu.VMEM((len(early), held.height, held.columns), jnp.bfloat16),
            pltpu.VMEM((kv_heads, tokens, count), jnp.bfloat16),
            pltpu.VMEM((tokens, held.columns), jnp.bfloat16),
            pltpu.SemaphoreType.DMA((len(early),)),
            *held.scratch,
        ],
        compiler_params=pltpu.CompilerParams(vmem_limit_bytes=57 * MIB),
        cost_estimate=LIGHT,
    )(places, turns, blocks, *inputs, prompt, got, steps, *early, *held.arrays)


def out_project(blocks, parts, queries, new_keys, new_values, weight, width):
    count = len(parts)
    steps = queries.shape[0]
    samples = steps // 2

    def body(block_ref, *refs):
        part_refs = refs[:count]
        query_ref, key_ref, value_ref, weight_ref, out_ref = refs[count:]
        notes = [read_notes(ref[HEAD_DIM:, :]) for ref in part_refs]
        top = notes[0][0]
        for other, _ in notes[1:]:
            top = jnp.maximum(top, other)
        sums = total = 0.0
        for ref, (part_top, part_total) in zip(part_refs, notes):
            factor = jnp.exp(part_top - top)
            sums = sums + ref[:HEAD_DIM, :].astype(jnp.float32) * factor
            total = total + part_total * factor
        sums = sums.T
        both = jnp.concatenate([top, total, jnp.zeros((6, HEAD_DIM), jnp.float32)], axis=0).T
        keys, values = key_ref[...], value_ref[...]
        heads = []
        for h in range(queries.shape[1] // HEAD_DIM):
            query = query_ref[:, h * HEAD_DIM : (h + 1) * HEAD_DIM].astype(jnp.float32)
            own_score = jnp.sum(query * keys, axis=1, keepdims=True) * (HEAD_DIM**-0.5)
            back_score = jnp.sum(
                query[samples:] * keys[:samples], axis=1, keepdims=True
            ) * (HEAD_DIM**-0.5)
            ends = []
            for step in (0, 1):
                place = slice((2 * h + step) * samples, (2 * h + step + 1) * samples)
                here = slice(step * samples, (step + 1) * samples)
                old_top, old_total = both[place, 0:1], both[place, 1:2]
                scores = [(own_score[here], values[here])]
                if step:
                    scores.append((back_score, values[:samples]))
                high = old_top
                for score, _ in scores:
                    high = jnp.maximum(high, score)
                old = jnp.exp(old_top - high)
                numerator, denominator = old * sums[place], old * old_total
                for score, value in scores:
                    new = jnp.exp(score - high)
                    numerator, denominator = numerator + new * value, denominator + new
                ends.append(numerator / denominator)
            heads.append(jnp.concatenate(ends, axis=0).astype(jnp.bfloat16))
        heads = jnp.concatenate(heads, axis=1)
        for i in range(blocks.shape[0]):
            start = pl.multiple_of(block_ref[i] * width, width)
            out_ref[:, i * width : (i + 1) * width] = jnp.dot(
                heads, weight_ref[:, pl.ds(start, width)], preferred_element_type=jnp.float32
            ).astype(jnp.bfloat16)

    return small_call(
        body, [(steps, weight.shape[1])], [blocks], [*parts, queries, new_keys, new_values, weight]
    )[0]


def on_device(
    prompt_states,
    page_table,
    step_states,
    sample_order,
    key_weight,
    value_weight,
    query_weight,
    out_weight,
):
    devices = lax.axis_size("sample")
    groups = lax.axis_size("groups")
    own_index = lax.axis_index("sample")
    first = lax.axis_index("groups") % 2 == 0
    deep = devices // LINE
    own_a, own_b, own_c = own_index // LINE, own_index // 2 % 2, own_index % 2
    along_ring, along_z, along_y, along_x, in_chip = mover(groups, devices)
    row_count = prompt_states.shape[0]
    chip_rows = 2 * row_count
    pages_here = row_count // PAGE
    heads_here = query_weight.shape[1] // HEAD_DIM
    total_pages = page_table.shape[0]
    prompts = total_pages // PROMPT_PAGES
    samples = sample_order.shape[0]
    steps = 2 * samples
    group_size = samples // prompts
    own_kv = own_index * heads_here // GQA
    wide_states = step_states.reshape(steps, D)
    rows = heads_here * steps
    width = key_weight.shape[0]
    half = key_weight.shape[1] // 2
    kv_places = jnp.where(first, 0, KV_HEADS // 2) + jnp.arange(KV_HEADS, dtype=jnp.int32)
    kv_places = kv_places % KV_HEADS

    order = ring_order(deep)

    def by_place(table):
        return sum(jnp.where(own_a == a, table[a], 0) for a in range(deep))

    own_turn = by_place([order.index(a) for a in range(deep)])

    def block(place_z, flip, core):
        return place_z * LINE + (own_b ^ flip) * 2 + core

    def behind(k):
        return by_place([order[(order.index(a) - k) % deep] for a in range(deep)])

    low = jnp.concatenate([key_weight[:, :half], value_weight[:, :half]])
    high = jnp.concatenate([key_weight[:, half:], value_weight[:, half:]])
    both_mine, both_other = jnp.where(first, low, high), jnp.where(first, high, low)

    own_pages = jnp.concatenate(
        [
            holder * pages_here + jnp.arange(pages_here, dtype=jnp.int32)
            for holder in (own_index, own_index ^ 1)
        ]
    )
    slots = jnp.sum(
        jnp.where(
            page_table[None, :] == own_pages[:, None],
            jnp.arange(total_pages, dtype=jnp.int32)[None, :],
            0,
        ),
        axis=1,
    )
    positions = (slots % PROMPT_PAGES * PAGE)[:, None] + jnp.arange(PAGE, dtype=jnp.int32)[None, :]
    scaled_tables = tuple(
        table * HEAD_DIM ** (-0.5) for table in rope_tables(positions.reshape(chip_rows))
    )

    step_place = PROMPT_PAGES * PAGE + jnp.arange(2, dtype=jnp.int32)
    step_tables = tuple(t[:, None, :] for t in rope_tables(step_place))
    flat_tables = [
        jnp.concatenate([sign * table, table], axis=-1)[:, 0]
        for sign, table in zip((1, -1), step_tables)
    ]
    queries = project_queries(
        after(wide_states, scaled_tables), query_weight, *flat_tables
    )
    packed_queries = jnp.concatenate(
        jnp.split(queries, half // queries.shape[1], axis=0), axis=1
    )
    packed = packed_queries.shape[0]

    places = [(k, flip) for k in range(deep) for flip in (0, 1)]
    parts_of = [
        (*range(0, 2 * deep, 2), 1),
        tuple(range(3, 2 * deep, 2)),
    ]
    taken_blocks = {
        which: jnp.stack([block(behind(places[i][0]), places[i][1], own_c) for i in which])
        for which in (tuple(range(2 * deep)), *parts_of)
    }
    query_turns = jnp.stack([(own_turn + deep - order.index(a)) % deep for a in range(deep)])
    own_place = (own_kv + jnp.where(first, 0, KV_HEADS // 2)) % KV_HEADS * HEAD_DIM
    done = {}

    def send(move, value):
        moved = done.setdefault(move, [])
        moved.append(move(after(value, moved[-2]) if len(moved) > 1 else value))
        return moved[-1]

    got = in_chip(prompt_states)
    both_z, both_x, theirs, theirs_x = {0: both_mine}, {0: both_other}, {}, {}
    value_y = send(along_y, after(value_weight, both_mine))
    both_z[1] = send(along_ring, both_mine)
    theirs_x[0] = jnp.where(first, value_y[:, half:], value_y[:, :half])
    value_y = jnp.where(first, value_y[:, :half], value_y[:, half:])
    key_full = {0: jnp.concatenate([both_mine[:width], both_other[:width], packed_queries])}
    key_y = {0: send(along_y, after(key_full[0], value_y))}
    theirs[0] = jnp.concatenate([value_y, packed_queries, key_y[0][2 * width :]])
    for k in range(1, deep):
        if k + 1 < deep:
            both_z[k + 1] = send(along_ring, both_z[k])
        both_x[k] = send(along_x, both_z[k])
        key_full[k] = jnp.concatenate([both_z[k][:width], both_x[k][:width]])
        early_work = (taken_blocks, kv_places, query_turns) if k == 2 else ()
        key_y[k] = send(along_y, after(key_full[k], (key_y[k - 1], early_work)))
    for k in range(1, deep):
        theirs[k] = send(along_ring, theirs[k - 1])
        theirs_x[k] = send(along_x, theirs[k][:width])

    ring_queries = collect([theirs[k] for k in range(deep)], width, 2 * packed)
    ring_queries = [ring_queries, in_chip(ring_queries)]

    key_pieces = [
        [((key_y if flip else key_full)[k], start) for start in (0, width)] for k, flip in places
    ]
    value_pieces = [
        [(theirs[k], 0), (theirs_x[k], 0)] if flip else [(both_z[k], width), (both_x[k], width)]
        for k, flip in places
    ]

    def project_blocks(pieces, which, acc, ready, kind):
        taken = after(taken_blocks[tuple(which)], ready)
        return project(
            prompt_states, got, wide_states, taken, width, [pieces[i] for i in which], acc, kind
        )

    value_early = project_blocks(
        value_pieces, parts_of[0], None, (theirs_x[1], theirs[deep - 1]), jnp.bfloat16
    )
    awaited = (value_early, [theirs_x[k] for k in range(1, deep)])
    key_sum = project_blocks(key_pieces, range(2 * deep), None, awaited, jnp.bfloat16)
    key_back = in_chip(key_sum)

    def own_head(sums):
        sums = lax.dynamic_slice_in_dim(sums, own_place, HEAD_DIM, 1)
        return sums.reshape(2, samples, HEAD_DIM).astype(jnp.float32)

    new_keys = own_head(key_sum[chip_rows:]) + own_head(key_back[chip_rows:])
    new_keys = turn(new_keys, step_tables).astype(jnp.bfloat16).astype(jnp.float32)
    new_keys = new_keys.reshape(steps, HEAD_DIM)
    masks = []
    if prompts > 1:
        token_prompt = jnp.repeat(slots // PROMPT_PAGES, PAGE)
        row_prompt = jnp.tile(sample_order // group_size, devices // KV_HEADS * rows // samples)
        masks = [token_prompt[:, None], row_prompt[None, :]]
    kept, sent, step_values = attend(
        kv_places, query_turns, ring_queries, key_sum, key_back, *scaled_tables, masks,
        prompt_states, got, wide_states, taken_blocks[parts_of[1]], width,
        [value_pieces[i] for i in parts_of[1]], [value_early],
    )
    new_values = own_head(step_values) + own_head(in_chip(step_values))
    new_values = new_values.astype(jnp.bfloat16).astype(jnp.float32).reshape(steps, HEAD_DIM)

    by_owner = (deep, 2, *kept.shape[2:])
    near, far = merge_cores(kept.reshape(by_owner), in_chip(sent.reshape(by_owner)))
    merged = merge_chips(own_a[None], near, along_y(far))
    parts = [merged[0]] + [along_z(merged[k], k) for k in range(1, deep)]

    out_width = out_weight.shape[1] // devices
    out_blocks = jnp.stack(
        [
            block(own_a ^ k, flip, own_c ^ turned)
            for turned in (0, 1)
            for flip in (0, 1)
            for k in range(deep)
        ]
    )
    terms = out_project(out_blocks, parts, queries, new_keys, new_values, out_weight, out_width)

    def narrow(value):
        return value.astype(jnp.bfloat16)

    def wide(value):
        return value.astype(jnp.float32)

    for move in (in_chip, along_y):
        share = terms.shape[1] // 2
        terms = narrow(wide(terms[:, :share]) + wide(move(terms[:, share:])))
    attn_out = wide(terms[:, :out_width])
    for k in range(1, deep):
        attn_out = attn_out + wide(along_z(terms[:, k * out_width : (k + 1) * out_width], k))
    return narrow(attn_out).reshape(2, samples, -1)


def solution(mesh):
    in_specs = (
        P(("groups", "sample"), None),
        P("groups"),
        P(None, "groups", None),
        P("groups"),
        P("sample", None),
        P("sample", None),
        P(None, "sample"),
        P("sample", None),
    )
    out_specs = P(None, "groups", "sample")
    return jax.shard_map(
        on_device, mesh=mesh, in_specs=in_specs, out_specs=out_specs, check_vma=False
    )
```
